32 devices in a mesh: section: 4 (over y, core), dp: 8 (over z, x).
Axes of the slice: x: 2, y: 2, z: 4, core: 2. Of those that a mesh axis runs over, the one named last changes fastest.
Arguments:
- tokens_in: bfloat16 [16, 1024, 768], P('dp', 'section'), may hold values from -6 to 6
- seg_starts: int32 [16, 6], P('dp'), may hold values from 0 to 1023, as said below
- pad_mask: int32 [16, 1024], P('dp'), may hold values from 0 to 1, as said below
- w_qkv: bfloat16 [4, 768, 2304], P('section'), may hold values from -0.21875 to 0.21875
- b_qv: float32 [4, 1536], P('section'), may hold values from -3 to 3
- w_attn_out: bfloat16 [4, 768, 768], P('section'), may hold values from -0.875 to 0.875
- b_attn_out: float32 [4, 768], P('section'), may hold values from -3 to 3
- ln_gain: float32 [4, 2, 768], P('section'), may hold values from 0.5 to 1.5
- ln_bias: float32 [4, 2, 768], P('section'), may hold values from -2 to 2
- w_up: bfloat16 [4, 768, 3072], P('section'), may hold values from -0.21875 to 0.21875
- b_up: float32 [4, 3072], P('section'), may hold values from -3 to 3
- w_down: bfloat16 [4, 3072, 768], P('section'), may hold values from -0.109375 to 0.109375
- b_down: float32 [4, 768], P('section'), may hold values from -3 to 3
- w_proj: bfloat16 [768, 128], P(None, 'section'), may hold values from -0.21875 to 0.21875
- cotangent: bfloat16 [16, 1024, 128], P('dp', None, 'section'), may hold values from -6 to 6
Outputs:
- embedded: bfloat16 [16, 1024, 128], P('dp', None, 'section')
- grad_in: float32 [16, 1024, 768], P('dp', 'section')
- grad_w_qkv: float32 [4, 768, 2304], P('section', 'dp')
- grad_b_qv: float32 [4, 1536], P('section', 'dp')
- grad_w_attn_out: float32 [4, 768, 768], P('section', 'dp')
- grad_b_attn_out: float32 [4, 768], P('section', 'dp')
- grad_ln_gain: float32 [4, 2, 768], P('section', None, 'dp')
- grad_ln_bias: float32 [4, 2, 768], P('section', None, 'dp')
- grad_w_up: float32 [4, 768, 3072], P('section', 'dp')
- grad_b_up: float32 [4, 3072], P('section', 'dp')
- grad_w_down: float32 [4, 3072, 768], P('section', 'dp')
- grad_b_down: float32 [4, 768], P('section', 'dp')
- grad_w_proj: float32 [768, 128], P('dp', 'section')
The draws below stay inside these ranges and needn't reach their ends.
Inputs may be any that keep to these rules, and one draw needn't show every extreme that they name: `seg_starts`: in each row the 6 starts rise strictly and the first is 0. `pad_mask`: in each row the zeros form a tail of at most 256 positions.
All inputs are finite; a program needn't handle non-finite values.
Results may differ from the reference program's by a relative error of at most 0.025.
Values may be sent and summed in bfloat16 or wider, within the bound.
No kernel may reach another device: no remote copies, remote signals or barrier semaphores. Data moves between devices by JAX's collectives and lax.ppermute only.
A program may use at most 512 MiB of HBM per device.

```python
import jax
import jax.numpy as jnp
from jax import lax

D = 768
HEADS = 12
HEAD = 64
FF = 3072
DIM = 128
L = 1024
SEGS = 6
ROWS = 16
N_SECTION = 4


def draw_seg_starts(key, part):
    key = jax.random.fold_in(key, 11)

    def one_row(row_key):
        picks = jax.random.permutation(row_key, L - 1)[:SEGS - 1] + 1
        return jnp.concatenate([jnp.zeros((1,), jnp.int32), jnp.sort(picks).astype(jnp.int32)])
    return jax.vmap(one_row)(jax.random.split(key, ROWS))


def draw_pad_mask(key, part):
    key = jax.random.fold_in(key, 23)
    tails = jax.random.randint(key, (ROWS, 1), 0, L // 4 + 1)
    places = jnp.arange(L, dtype=jnp.int32)[None, :]
    return (places < L - tails).astype(jnp.int32)


def block_scale(stream_key, dims, shards, smallest, largest):
    factor_of, own = 1.0, jax.random.fold_in(stream_key, 6)
    for axis_at, blocks in shards:
        heights = jnp.exp(jax.random.uniform(jax.random.fold_in(own, axis_at), (blocks,), jnp.float32, smallest / len(shards), largest / len(shards)))
        factor_of = factor_of * jnp.repeat(heights, dims[axis_at] // blocks).reshape([-1 if axis == axis_at else 1 for axis in range(len(dims))])
    return factor_of


def scatter_about(stream_key, dims, scale, limit, pieces=(), kind=jnp.bfloat16):
    factor_of = block_scale(stream_key, dims, pieces, -0.22, 0.18) if pieces else 1.0
    drawn = jax.random.normal(stream_key, dims, jnp.float32) * scale * factor_of
    return jnp.minimum(jnp.maximum(drawn, -limit), limit).astype(kind)


def setup_inputs(seed: int = 0) -> dict:
    key_list = jax.random.split(jax.random.key(seed), 16)
    tokens_in = scatter_about(key_list[0], (ROWS, L, D), 1.0, 6.0, ((0, 8), (1, 4)))
    seg_starts = draw_seg_starts(jax.random.fold_in(key_list[15], 71), 0)
    pad_mask = draw_pad_mask(jax.random.fold_in(key_list[15], 71), 0)
    w_qkv = scatter_about(key_list[3], (N_SECTION, D, 3 * D), D ** -0.5, 0.21875, ((0, 4),))
    b_qv = scatter_about(key_list[4], (N_SECTION, 2 * D), 0.5, 3.0, ((0, 4),), jnp.float32)
    w_attn_out = scatter_about(key_list[5], (N_SECTION, D, D), (D // 16) ** -0.5, 0.875, ((0, 4),))
    b_attn_out = scatter_about(key_list[6], (N_SECTION, D), 0.5, 3.0, ((0, 4),), jnp.float32)
    ln_gain = jnp.clip(1.0 + 0.1 * jax.random.normal(key_list[7], (N_SECTION, 2, D), jnp.float32), 0.5, 1.5)
    ln_bias = scatter_about(key_list[8], (N_SECTION, 2, D), 0.3, 2.0, ((0, 4),), jnp.float32)
    w_up = scatter_about(key_list[9], (N_SECTION, D, FF), D ** -0.5, 0.21875, ((0, 4),))
    b_up = scatter_about(key_list[10], (N_SECTION, FF), 0.5, 3.0, ((0, 4),), jnp.float32)
    w_down = scatter_about(key_list[11], (N_SECTION, FF, D), FF ** -0.5, 0.109375, ((0, 4),))
    b_down = scatter_about(key_list[12], (N_SECTION, D), 0.5, 3.0, ((0, 4),), jnp.float32)
    w_proj = scatter_about(key_list[13], (D, DIM), D ** -0.5, 0.21875, ((1, 4),))
    cotangent = scatter_about(key_list[14], (ROWS, L, DIM), 1.0, 6.0, ((0, 8), (2, 4)))
    return {"tokens_in": tokens_in, "seg_starts": seg_starts, "pad_mask": pad_mask, "w_qkv": w_qkv, "b_qv": b_qv, "w_attn_out": w_attn_out, "b_attn_out": b_attn_out, "ln_gain": ln_gain, "ln_bias": ln_bias, "w_up": w_up, "b_up": b_up, "w_down": w_down, "b_down": b_down, "w_proj": w_proj, "cotangent": cotangent}


@jax.custom_vjp
def low(v):
    return lax.optimization_barrier(v.astype(jnp.bfloat16)).astype(jnp.float32)

@jax.custom_vjp
def low_back(v):
    return v

def low_keep(v):
    return (low(v), None)

def low_pass(kept, grad):
    return (grad,)

def back_keep(v):
    return (v, None)

def back_low(kept, grad):
    return (low(grad),)
low.defvjp(low_keep, low_pass)
low_back.defvjp(back_keep, back_low)
EPS_NORM = 1e-05
EPS_PROJ = 1e-06
NEG_FILL = -1e+30
HIGHEST = lax.Precision.HIGHEST

def product(left_rows, right_rows):
    return jnp.dot(left_rows, right_rows, preferred_element_type=jnp.float32, precision=HIGHEST)

def norm_rows(values, gain_row, shift_by):
    centred = values - lax.optimization_barrier(jnp.mean(values, axis=-1, keepdims=True))
    spread = lax.optimization_barrier(jnp.mean(centred * centred, axis=-1, keepdims=True))
    return centred * lax.rsqrt(spread + EPS_NORM) * gain_row + shift_by

def row_allowed(starts, real_flags):
    places = jnp.arange(real_flags.shape[0], dtype=jnp.int32)
    segment = lax.optimization_barrier(jnp.sum((starts[None, :] <= places[:, None]).astype(jnp.int32), axis=1))
    same_segment = segment[:, None] == segment[None, :]
    usable = (real_flags[None, :] == 1) | (places[:, None] == places[None, :])
    return same_segment & usable

def attention(queries, key_rows, value_rows, allowed):
    length = queries.shape[0]
    block_rows = min(512, length)
    score_scale = HEAD ** (-0.5)
    query_blocks = queries.reshape(length // block_rows, block_rows, HEADS, HEAD)
    mask_blocks = allowed.reshape(length // block_rows, block_rows, length)
    keys_split = key_rows.reshape(length, HEADS, HEAD)
    values_split = value_rows.reshape(length, HEADS, HEAD)

    def one_block(block_piece):
        query_part, mask_part = block_piece
        scores = jnp.einsum('qhd,khd->hqk', query_part, keys_split, precision=HIGHEST) * score_scale
        scores = jnp.where(mask_part[None], low_back(scores), NEG_FILL)
        row_top = lax.optimization_barrier(jnp.max(scores, axis=-1, keepdims=True))
        expo_scores = jnp.exp(scores - row_top)
        soft_probs = low(expo_scores / lax.optimization_barrier(jnp.sum(expo_scores, axis=-1, keepdims=True)))
        return jnp.einsum('hqk,khd->qhd', soft_probs, values_split, precision=HIGHEST)
    context = lax.map(jax.checkpoint(one_block), (query_blocks, mask_blocks))
    return context.reshape(length, HEADS * HEAD)

def run_layer(inputs, weights, allowed, is_first):
    w_qkv, b_qv, w_out, b_out, norm_gains, shifts, w_up, b_up, w_down, b_down = weights
    if not is_first:
        inputs = low_back(low(inputs))
    mixed_rows = product(inputs, w_qkv)
    queries = low_back(low(mixed_rows[:, :D] + b_qv[:D]))
    key_rows = low_back(low(mixed_rows[:, D:2 * D]))
    value_rows = low_back(low(mixed_rows[:, 2 * D:] + b_qv[D:]))
    context = low_back(low(attention(queries, key_rows, value_rows, allowed)))
    summed = inputs + low_back(product(context, w_out) + b_out)
    hidden = norm_rows(summed, norm_gains[0], shifts[0])
    raised = low_back(product(low(hidden), w_up) + b_up)
    lowered = low_back(product(low(jax.nn.gelu(raised, approximate=False)), w_down) + b_down)
    return norm_rows(hidden + lowered, norm_gains[1], shifts[1])

def project_rows(final_rows, projection):
    columns = low_back(product(low(final_rows), projection))
    inverse = lax.rsqrt(lax.optimization_barrier(jnp.sum(columns * columns, axis=-1, keepdims=True)) + EPS_PROJ)
    return DIM ** 0.5 * columns * inverse

def reference(tokens_in, seg_starts, pad_mask, w_qkv, b_qv, w_attn_out, b_attn_out, ln_gain, ln_bias, w_up, b_up, w_down, b_down, w_proj, cotangent):
    weights = tuple((member.astype(jnp.float32) for member in (w_qkv, b_qv, w_attn_out, b_attn_out, ln_gain, ln_bias, w_up, b_up, w_down, b_down)))
    projection = w_proj.astype(jnp.float32)
    rows_in = tokens_in.astype(jnp.float32)

    def forward(rows_all, layer_weights, projection_now):

        def one_row(carried, block_piece):
            row_values, starts, real_flags = block_piece
            allowed = row_allowed(starts, real_flags)
            layer_state = row_values
            for section_at in range(N_SECTION):
                these = tuple((member[section_at] for member in layer_weights))
                layer_state = run_layer(layer_state, these, allowed, section_at == 0)
            return (carried, project_rows(layer_state, projection_now))
        _, embedded_rows = lax.scan(jax.checkpoint(one_row), jnp.zeros((), jnp.float32), (rows_all, seg_starts, pad_mask))
        return embedded_rows
    embedded, pull_back = jax.vjp(forward, rows_in, weights, projection)
    grad_rows, grad_weights, grad_projection = pull_back(cotangent.astype(jnp.float32))
    return (embedded.astype(jnp.bfloat16), grad_rows, grad_weights[0], grad_weights[1], grad_weights[2], grad_weights[3], grad_weights[4], grad_weights[5], grad_weights[6], grad_weights[7], grad_weights[8], grad_weights[9], grad_projection)
```

```python
from functools import partial
import math

import jax
import jax.numpy as jnp
from jax import lax
from jax.experimental import pallas as pl
from jax.experimental.pallas import tpu as pltpu
from jax.sharding import PartitionSpec as P

HEAD = 64
PAIR = 2 * HEAD
GROUPS = 2
QB = 128
KB = 256
EPS_NORM = 1e-05
EPS_PROJ = 1e-06
NEG_FILL = -1e30
VMEM = 56 * 1024 * 1024
BF = jnp.bfloat16
F32 = jnp.float32

NT = (((1,), (1,)), ((), ()))
TN = (((0,), (0,)), ((), ()))


def dot(a, b):
    return jnp.dot(a, b, preferred_element_type=F32)


def dot_nt(a, b):
    return lax.dot_general(a, b, NT, preferred_element_type=F32)


def dot_tn(a, b):
    return lax.dot_general(a, b, TN, preferred_element_type=F32)


def pack_small(b_qv, b_out, gains, shifts, b_up, b_down):
    return jnp.concatenate(
        [b_up, b_qv, b_out, gains[0], gains[1], shifts[0], shifts[1], b_down]
    )


def small_spec(layer, width):
    return pl.BlockSpec((1, 1, width), lambda *_: (layer, 0, 0))


def attention_plan(starts, real_flags):
    length = real_flags.shape[0]
    places = jnp.arange(length, dtype=jnp.int32)
    segment = jnp.sum((starts[None, :] <= places[:, None]).astype(jnp.int32), axis=1)
    key_code = jnp.where(real_flags == 1, segment, -1).astype(F32)
    key_code = jnp.broadcast_to(key_code[:, None], (length, PAIR))
    query_code = segment.astype(F32).reshape(length // QB, QB)
    first = jnp.arange(length // QB, dtype=jnp.int32) * QB
    low = jnp.max(jnp.where(starts[None, :] <= first[:, None], starts[None, :], 0), axis=1)
    high = jnp.min(
        jnp.where(starts[None, :] > first[:, None] + (QB - 1), starts[None, :], length), axis=1
    )
    begin = (low // QB) * QB
    count = (high - begin + KB - 1) // KB
    begin = jnp.minimum(begin, length - KB * count)
    return (begin, count, key_code, query_code)


def pair_mask(rows):
    return lax.broadcasted_iota(jnp.int32, (rows, PAIR), 1) < HEAD


def stacked_heads(block):
    first = pair_mask(block.shape[0])
    zero = jnp.zeros_like(block)
    return jnp.concatenate([jnp.where(first, block, zero), jnp.where(first, zero, block)], axis=0)


def block_bias(key_code, query_code, key_at, query_at):
    keys = lax.broadcasted_iota(jnp.int32, (KB, QB), 0) + (key_at - query_at)
    same = keys == lax.broadcasted_iota(jnp.int32, (KB, QB), 1)
    bias = jnp.where((key_code == query_code) | same, 0.0, NEG_FILL)
    return jnp.concatenate([bias, bias], axis=1)


def top_rows(values, op):
    folded = values.reshape(values.shape[0] // 8, 8, values.shape[1])
    return op(folded, axis=0)


def unstack_heads(flat):
    rows = lax.broadcasted_iota(jnp.int32, (PAIR, QB), 0)
    return jnp.where(rows < HEAD, flat[:PAIR, :QB], flat[:PAIR, QB:]).T


def attend_forward_kernel(
    begin_ref, count_ref, qkv_ref, key_code_ref, query_code_ref, out_ref, logsum_ref,
    value_scr, query_scr, score_scr, total_scr,
):
    length = qkv_ref.shape[1]
    pairs = qkv_ref.shape[2] // PAIR
    cols = [slice(p * PAIR, (p + 1) * PAIR) for p in range(pairs)]
    for p in range(pairs):
        value_scr[p, :PAIR, :] = qkv_ref[2, :, cols[p]].T
        value_scr[p, PAIR:, :] = jnp.ones((value_scr.shape[1] - PAIR, length), BF)

    def one_query_block(i, _):
        query_at = pl.multiple_of(i * QB, QB)
        begin, count = begin_ref[i], count_ref[i]
        query_code = query_code_ref[pl.ds(i, 1), :]
        for p in range(pairs):
            query_scr[p] = stacked_heads(qkv_ref[0, pl.ds(query_at, QB), cols[p]])

        def scores(j, tops):
            key_at = pl.multiple_of(begin + j * KB, QB)
            bias = block_bias(key_code_ref[pl.ds(key_at, KB), :], query_code, key_at, query_at)
            fresh = []
            for p in range(pairs):
                part = dot_nt(qkv_ref[1, pl.ds(key_at, KB), cols[p]], query_scr[p]) + bias
                score_scr[p, pl.ds(j * KB, KB), :] = part
                fresh.append(jnp.maximum(tops[p], top_rows(part, jnp.max)))
            return tuple(fresh)

        tops = lax.fori_loop(
            0, count, scores, tuple(jnp.full((8, 2 * QB), NEG_FILL, F32) for _ in range(pairs))
        )
        tops = [jnp.max(top, axis=0, keepdims=True) for top in tops]
        total_scr[...] = jnp.zeros_like(total_scr)

        def sums(j, _):
            key_at = pl.multiple_of(begin + j * KB, QB)
            for p in range(pairs):
                probs = jnp.exp(score_scr[p, pl.ds(j * KB, KB), :] - tops[p]).astype(BF)
                total_scr[p] += dot(value_scr[p, :, pl.ds(key_at, KB)], probs)
            return 0

        lax.fori_loop(0, count, sums, 0)
        for p in range(pairs):
            weight = total_scr[p, PAIR : PAIR + 1, :]
            logsum_ref[0, pl.ds(p * (length // QB) + i, 1), :] = tops[p] + jnp.log(weight)
            out_ref[pl.ds(query_at, QB), cols[p]] = unstack_heads(
                total_scr[p, :PAIR, :] / weight
            ).astype(BF)
        return 0

    lax.fori_loop(0, length // QB, one_query_block, 0)


def attend_forward(qkv, plan):
    _, length, width = qkv.shape
    begin, count, key_code, query_code = plan
    group = width // GROUPS
    pairs = group // PAIR
    blocks = length // QB
    return pl.pallas_call(
        attend_forward_kernel,
        name="attend_forward",
        grid_spec=pltpu.PrefetchScalarGridSpec(
            num_scalar_prefetch=2,
            grid=(GROUPS,),
            in_specs=[
                pl.BlockSpec((3, length, group), lambda g, *_: (0, 0, g)),
                pl.BlockSpec((length, PAIR), lambda g, *_: (0, 0)),
                pl.BlockSpec((blocks, QB), lambda g, *_: (0, 0)),
            ],
            out_specs=[
                pl.BlockSpec((length, group), lambda g, *_: (0, g)),
                pl.BlockSpec((1, pairs * blocks, 2 * QB), lambda g, *_: (g, 0, 0)),
            ],
            scratch_shapes=[
                pltpu.VMEM((pairs, PAIR + 16, length), BF),
                pltpu.VMEM((pairs, 2 * QB, PAIR), BF),
                pltpu.VMEM((pairs, length, 2 * QB), F32),
                pltpu.VMEM((pairs, PAIR + 16, 2 * QB), F32),
            ],
        ),
        out_shape=[
            jax.ShapeDtypeStruct((length, width), BF),
            jax.ShapeDtypeStruct((GROUPS, pairs * blocks, 2 * QB), F32),
        ],
        compiler_params=pltpu.CompilerParams(vmem_limit_bytes=VMEM),
        cost_estimate=pl.CostEstimate(
            flops=4 * length * length * width, bytes_accessed=8 * length * width, transcendentals=0
        ),
    )(begin, count, qkv, key_code, query_code)


def attend_backward_kernel(
    begin_ref, count_ref, qkv_ref, key_code_ref, query_code_ref, context_ref, logsum_ref, grad_ref,
    out_ref, sums_ref, key_scr, query_scr, given_scr, down_scr, grad_key_scr, grad_value_scr,
):
    length = qkv_ref.shape[1]
    pairs = qkv_ref.shape[2] // PAIR
    blocks = length // QB
    cols = [slice(p * PAIR, (p + 1) * PAIR) for p in range(pairs)]
    for p in range(pairs):
        key_scr[p] = qkv_ref[1, :, cols[p]].T
    grad_key_scr[...] = jnp.zeros_like(grad_key_scr)
    grad_value_scr[...] = jnp.zeros_like(grad_value_scr)
    sums_ref[...] = jnp.zeros_like(sums_ref)

    def one_query_block(i, _):
        query_at = pl.multiple_of(i * QB, QB)
        begin, count = begin_ref[i], count_ref[i]
        query_code = query_code_ref[pl.ds(i, 1), :]
        inner, logsum = [], []
        for p in range(pairs):
            query_scr[p] = stacked_heads(qkv_ref[0, pl.ds(query_at, QB), cols[p]])
            given = grad_ref[pl.ds(query_at, QB), cols[p]]
            given_scr[p] = stacked_heads(given)
            both = (given.astype(F32) * context_ref[pl.ds(query_at, QB), cols[p]].astype(F32)).T
            inner.append(
                jnp.concatenate(
                    [
                        jnp.sum(both[:HEAD], axis=0, keepdims=True),
                        jnp.sum(both[HEAD:], axis=0, keepdims=True),
                    ],
                    axis=1,
                )
            )
            logsum.append(logsum_ref[0, pl.ds(p * blocks + i, 1), :])
        down_scr[...] = jnp.zeros_like(down_scr)

        def one_key_block(j, _):
            key_at = pl.multiple_of(begin + j * KB, QB)
            rows = pl.ds(key_at, KB)
            bias = block_bias(key_code_ref[rows, :], query_code, key_at, query_at)
            for p in range(pairs):
                part = dot_nt(qkv_ref[1, rows, cols[p]], query_scr[p]) + bias
                probs = jnp.exp(part - logsum[p])
                grad_probs = dot_nt(qkv_ref[2, rows, cols[p]], given_scr[p])
                grad_scores = (probs * (grad_probs - inner[p])).astype(BF)
                grad_value_scr[rows, cols[p]] += dot(probs.astype(BF), given_scr[p])
                grad_key_scr[rows, cols[p]] += dot(grad_scores, query_scr[p])
                down_scr[p] += dot(key_scr[p, :, rows], grad_scores)
            return 0

        lax.fori_loop(0, count, one_key_block, 0)
        for p in range(pairs):
            grad_query = (unstack_heads(down_scr[p]) * (HEAD**-0.5)).astype(BF)
            out_ref[0, pl.ds(query_at, QB), cols[p]] = grad_query
            sums_ref[0, 0:1, cols[p]] += jnp.sum(grad_query.astype(F32), axis=0, keepdims=True)
        return 0

    lax.fori_loop(0, blocks, one_query_block, 0)
    out_ref[1] = grad_key_scr[...].astype(BF)
    grad_value = grad_value_scr[...].astype(BF)
    out_ref[2] = grad_value
    sums_ref[0, 1:2, :] = jnp.sum(grad_value.astype(F32), axis=0, keepdims=True)


def attend_backward(qkv, context, logsum, grad_context, plan):
    _, length, width = qkv.shape
    begin, count, key_code, query_code = plan
    group = width // GROUPS
    pairs = group // PAIR
    blocks = length // QB
    return pl.pallas_call(
        attend_backward_kernel,
        name="attend_backward",
        grid_spec=pltpu.PrefetchScalarGridSpec(
            num_scalar_prefetch=2,
            grid=(GROUPS,),
            in_specs=[
                pl.BlockSpec((3, length, group), lambda g, *_: (0, 0, g)),
                pl.BlockSpec((length, PAIR), lambda g, *_: (0, 0)),
                pl.BlockSpec((blocks, QB), lambda g, *_: (0, 0)),
                pl.BlockSpec((length, group), lambda g, *_: (0, g)),
                pl.BlockSpec((1, pairs * blocks, 2 * QB), lambda g, *_: (g, 0, 0)),
                pl.BlockSpec((length, group), lambda g, *_: (0, g)),
            ],
            out_specs=[
                pl.BlockSpec((3, length, group), lambda g, *_: (0, 0, g)),
                pl.BlockSpec((1, 2, group), lambda g, *_: (g, 0, 0)),
            ],
            scratch_shapes=[
                pltpu.VMEM((pairs, PAIR, length), BF),
                pltpu.VMEM((pairs, 2 * QB, PAIR), BF),
                pltpu.VMEM((pairs, 2 * QB, PAIR), BF),
                pltpu.VMEM((pairs, PAIR, 2 * QB), F32),
                pltpu.VMEM((length, group), F32),
                pltpu.VMEM((length, group), F32),
            ],
        ),
        out_shape=[
            jax.ShapeDtypeStruct((3, length, width), BF),
            jax.ShapeDtypeStruct((GROUPS, 2, group), F32),
        ],
        compiler_params=pltpu.CompilerParams(vmem_limit_bytes=VMEM),
        cost_estimate=pl.CostEstimate(
            flops=10 * length * length * width, bytes_accessed=16 * length * width, transcendentals=0
        ),
    )(begin, count, qkv, key_code, query_code, context, logsum, grad_context)


def mix_kernel(x_ref, w_ref, small_ref, out_ref):
    part = pl.program_id(0)
    width = x_ref.shape[1]
    ff_width = small_ref.shape[2] - 8 * width
    at = ff_width + width * jnp.where(part == 2, 1, 0)
    shift = small_ref[0, :, pl.ds(pl.multiple_of(at, 128), width)]
    shift = jnp.where(part == 1, jnp.zeros_like(shift), shift)
    scale = jnp.where(part == 0, HEAD**-0.5, 1.0)
    for r in range(0, x_ref.shape[0], 256):
        rows = slice(r, r + 256)
        out_ref[0, rows, :] = ((dot(x_ref[rows, :], w_ref[0]) + shift) * scale).astype(BF)


def mix(x, w_qkv, small, layer):
    length, width = x.shape
    return pl.pallas_call(
        mix_kernel,
        name="mix",
        grid=(3,),
        in_specs=[
            pl.BlockSpec((length, width), lambda c: (0, 0)),
            pl.BlockSpec((1, width, width), lambda c: (layer, 0, c)),
            small_spec(layer, small.shape[2]),
        ],
        out_specs=pl.BlockSpec((1, length, width), lambda c: (c, 0, 0)),
        out_shape=jax.ShapeDtypeStruct((3, length, width), BF),
        compiler_params=pltpu.CompilerParams(vmem_limit_bytes=VMEM),
        cost_estimate=pl.CostEstimate(
            flops=6 * length * width * width, bytes_accessed=14 * length * width, transcendentals=0
        ),
    )(x, w_qkv, small)


def unmix_kernel(grad_ref, w_ref, skip_ref, out_ref, total):
    part = pl.program_id(0)

    @pl.when(part == 0)
    def _():
        total[...] = skip_ref[...].astype(F32)

    for r in range(0, total.shape[0], 256):
        rows = slice(r, r + 256)
        total[rows, :] += dot_nt(grad_ref[0, rows, :], w_ref[0])

    @pl.when(part == 2)
    def _():
        out_ref[...] = total[...].astype(BF)


def unmix(grad_mixed, w_qkv, skip, layer):
    _, length, width = grad_mixed.shape
    return pl.pallas_call(
        unmix_kernel,
        name="unmix",
        grid=(3,),
        in_specs=[
            pl.BlockSpec((1, length, width), lambda c: (c, 0, 0)),
            pl.BlockSpec((1, width, width), lambda c: (layer, 0, c)),
            pl.BlockSpec((length, width), lambda c: (0, 0)),
        ],
        out_specs=pl.BlockSpec((length, width), lambda c: (0, 0)),
        out_shape=jax.ShapeDtypeStruct((length, width), BF),
        scratch_shapes=[pltpu.VMEM((length, width), F32)],
        compiler_params=pltpu.CompilerParams(vmem_limit_bytes=VMEM),
        cost_estimate=pl.CostEstimate(
            flops=6 * length * width * width, bytes_accessed=14 * length * width, transcendentals=0
        ),
    )(grad_mixed, w_qkv, skip)


def normalized(values):
    centred = values - jnp.mean(values, axis=-1, keepdims=True)
    inverse = lax.rsqrt(jnp.mean(centred * centred, axis=-1, keepdims=True) + EPS_NORM)
    return (centred * inverse, inverse)


def normalized_pull(grad_hat, hat, inverse):
    return inverse * (
        grad_hat
        - jnp.mean(grad_hat, axis=-1, keepdims=True)
        - hat * jnp.mean(grad_hat * hat, axis=-1, keepdims=True)
    )


ERF = (0.254829592, -0.284496736, 1.421413741, -1.453152027, 1.061405429)
ERF_SLOPE = 0.3275911


def gelu_parts(x):
    t = pl.reciprocal(1.0 + (ERF_SLOPE * math.sqrt(0.5)) * jnp.abs(x), approx=True)
    bell = jnp.exp(-0.5 * (x * x))
    tail = 0.5 * ERF[4]
    for term in ERF[3::-1]:
        tail = tail * t + 0.5 * term
    tail = tail * t * bell
    below = jnp.where(x >= 0, 1.0 - tail, tail)
    return (x * below, below + x * bell * (1.0 / math.sqrt(2.0 * math.pi)))


FB = 512
ROWS = 256


def small_slices(width, ff_width):
    names = ("b_q", "b_v", "b_out", "gain1", "gain2", "shift1", "shift2", "b_down")
    at = {"b_up": slice(0, ff_width)}
    for n, name in enumerate(names):
        at[name] = slice(ff_width + n * width, ff_width + (n + 1) * width)
    return at


def refine_kernel(
    x_ref, context_ref, w_out_ref, w_up_ref, w_down_ref, small_ref, b_up_ref,
    out_ref, hidden_ref, hat1_ref, hat2_ref, scale1_ref, scale2_ref, active_ref, slope_ref,
    total,
):
    step = pl.program_id(0)
    length, width = x_ref.shape
    at = small_slices(width, small_ref.shape[2] - 8 * width)

    def vector(name):
        return small_ref[0, :, at[name]]

    @pl.when(step == 0)
    def _():
        for r in range(0, length, ROWS):
            rows = slice(r, r + ROWS)
            summed = x_ref[rows, :].astype(F32) + dot(context_ref[rows, :], w_out_ref[0])
            hat, inverse = normalized(summed + vector("b_out"))
            hidden = hat * vector("gain1") + vector("shift1")
            hat1_ref[rows, :] = hat.astype(BF)
            scale1_ref[rows, :] = jnp.broadcast_to(inverse, (ROWS, 128))
            hidden_ref[rows, :] = hidden.astype(BF)
            total[rows, :] = hidden + vector("b_down")

    for r in range(0, length, ROWS):
        rows = slice(r, r + ROWS)
        raised = dot(hidden_ref[rows, :], w_up_ref[0]) + b_up_ref[0]
        active, slope = gelu_parts(raised)
        active = active.astype(BF)
        active_ref[rows, :] = active
        slope_ref[rows, :] = slope.astype(BF)
        total[rows, :] += dot(active, w_down_ref[0])

    @pl.when(step == pl.num_programs(0) - 1)
    def _():
        for r in range(0, length, ROWS):
            rows = slice(r, r + ROWS)
            hat, inverse = normalized(total[rows, :])
            hat2_ref[rows, :] = hat.astype(BF)
            scale2_ref[rows, :] = jnp.broadcast_to(inverse, (ROWS, 128))
            out_ref[rows, :] = (hat * vector("gain2") + vector("shift2")).astype(BF)


def refine(x, context, weights, layer):
    w_out, w_up, w_down, small = weights
    length, width = x.shape
    ff_width = w_up.shape[2]
    whole = pl.BlockSpec((length, width), lambda f: (0, 0))
    lanes = pl.BlockSpec((length, 128), lambda f: (0, 0))
    part = pl.BlockSpec((length, FB), lambda f: (0, f))
    row_shape = jax.ShapeDtypeStruct((length, width), BF)
    lane_shape = jax.ShapeDtypeStruct((length, 128), F32)
    ff_shape = jax.ShapeDtypeStruct((length, ff_width), BF)
    return pl.pallas_call(
        refine_kernel,
        name="refine",
        grid=(ff_width // FB,),
        in_specs=[
            whole,
            whole,
            pl.BlockSpec((1, width, width), lambda f: (layer, 0, 0)),
            pl.BlockSpec((1, width, FB), lambda f: (layer, 0, f)),
            pl.BlockSpec((1, FB, width), lambda f: (layer, f, 0)),
            small_spec(layer, small.shape[2]),
            pl.BlockSpec((1, 1, FB), lambda f: (layer, 0, f)),
        ],
        out_specs=[whole, whole, whole, whole, lanes, lanes, part, part],
        out_shape=[row_shape] * 4 + [lane_shape] * 2 + [ff_shape] * 2,
        scratch_shapes=[pltpu.VMEM((length, width), F32)],
        compiler_params=pltpu.CompilerParams(vmem_limit_bytes=VMEM),
        cost_estimate=pl.CostEstimate(
            flops=2 * length * width * (width + 2 * ff_width),
            bytes_accessed=2 * width * (width + 2 * ff_width) + 4 * length * ff_width,
            transcendentals=0,
        ),
    )(x, context, w_out, w_up, w_down, small, small)


def refine_back_kernel(
    grad_ref, hat1_ref, hat2_ref, scale1_ref, scale2_ref, slope_ref,
    w_out_ref, w_up_ref, w_down_ref, small_ref,
    grad_low_ref, grad_raised_ref, grad_attn_ref, grad_context_ref, sums_ref, up_sums_ref,
    total,
):
    step = pl.program_id(0)
    length, width = grad_ref.shape
    at = small_slices(width, small_ref.shape[2] - 8 * width)

    def vector(name):
        return small_ref[0, :, at[name]]

    def add(row, values, first):
        part = jnp.sum(values, axis=0, keepdims=True)
        sums_ref[row : row + 1, :] = part if first else sums_ref[row : row + 1, :] + part

    @pl.when(step == 0)
    def _():
        for r in range(0, length, ROWS):
            rows = slice(r, r + ROWS)
            grad = grad_ref[rows, :].astype(F32)
            hat = hat2_ref[rows, :].astype(F32)
            joined = normalized_pull(grad * vector("gain2"), hat, scale2_ref[rows, :1])
            low = joined.astype(BF)
            grad_low_ref[rows, :] = low
            total[rows, :] = joined
            add(2, grad * hat, r == 0)
            add(4, grad, r == 0)
            add(5, low.astype(F32), r == 0)

    for r in range(0, length, ROWS):
        rows = slice(r, r + ROWS)
        grad_active = dot_nt(grad_low_ref[rows, :], w_down_ref[0])
        raised = (grad_active * slope_ref[rows, :].astype(F32)).astype(BF)
        grad_raised_ref[rows, :] = raised
        part = jnp.sum(raised.astype(F32), axis=0, keepdims=True)
        up_sums_ref[...] = part if r == 0 else up_sums_ref[...] + part
        total[rows, :] += dot_nt(raised, w_up_ref[0])

    @pl.when(step == pl.num_programs(0) - 1)
    def _():
        for r in range(0, length, ROWS):
            rows = slice(r, r + ROWS)
            grad = total[rows, :]
            hat = hat1_ref[rows, :].astype(F32)
            summed = normalized_pull(grad * vector("gain1"), hat, scale1_ref[rows, :1])
            attn = summed.astype(BF)
            grad_attn_ref[rows, :] = attn
            grad_context_ref[rows, :] = dot_nt(attn, w_out_ref[0]).astype(BF)
            add(1, grad * hat, r == 0)
            add(3, grad, r == 0)
            add(0, attn.astype(F32), r == 0)


def refine_back(grad, kept, weights, layer):
    w_out, w_up, w_down, small = weights
    hat1, hat2, scale1, scale2, slope = kept
    length, width = grad.shape
    ff_width = w_up.shape[2]
    whole = pl.BlockSpec((length, width), lambda f: (0, 0))
    lanes = pl.BlockSpec((length, 128), lambda f: (0, 0))
    part = pl.BlockSpec((length, FB), lambda f: (0, f))
    row_shape = jax.ShapeDtypeStruct((length, width), BF)
    return pl.pallas_call(
        refine_back_kernel,
        name="refine_back",
        grid=(ff_width // FB,),
        in_specs=[
            whole, whole, whole, lanes, lanes, part,
            pl.BlockSpec((1, width, width), lambda f: (layer, 0, 0)),
            pl.BlockSpec((1, width, FB), lambda f: (layer, 0, f)),
            pl.BlockSpec((1, FB, width), lambda f: (layer, f, 0)),
            small_spec(layer, small.shape[2]),
        ],
        out_specs=[
            whole, part, whole, whole,
            pl.BlockSpec((6, width), lambda f: (0, 0)),
            pl.BlockSpec((1, FB), lambda f: (0, f)),
        ],
        out_shape=[
            row_shape,
            jax.ShapeDtypeStruct((length, ff_width), BF),
            row_shape,
            row_shape,
            jax.ShapeDtypeStruct((6, width), F32),
            jax.ShapeDtypeStruct((1, ff_width), F32),
        ],
        scratch_shapes=[pltpu.VMEM((length, width), F32)],
        compiler_params=pltpu.CompilerParams(vmem_limit_bytes=VMEM),
        cost_estimate=pl.CostEstimate(
            flops=2 * length * width * (width + 2 * ff_width),
            bytes_accessed=2 * width * (width + 2 * ff_width) + 4 * length * ff_width,
            transcendentals=0,
        ),
    )(grad, hat1, hat2, scale1, scale2, slope, w_out, w_up, w_down, small)


def layer_forward(x, weights, layer, plan):
    w_qkv, w_out, w_up, w_down, small = weights
    qkv = mix(x, w_qkv, small, layer)
    context, logsum = attend_forward(qkv, plan)
    out, hidden, hat1, hat2, scale1, scale2, active, slope = refine(
        x, context, (w_out, w_up, w_down, small), layer
    )
    return (out, (x, qkv, context, logsum, hidden, hat1, hat2, scale1, scale2, active, slope))


def layer_backward(grad, kept, weights, layer, plan):
    w_qkv, w_out, w_up, w_down, small = weights
    x, qkv, context, logsum, hidden, hat1, hat2, scale1, scale2, active, slope = kept
    grad_low, grad_raised, grad_attn, grad_context, sums, up_sums = refine_back(
        grad, (hat1, hat2, scale1, scale2, slope), (w_out, w_up, w_down, small), layer
    )
    grad_mixed, mix_sums = attend_backward(qkv, context, logsum, grad_context, plan)
    grad_x = unmix(grad_mixed, w_qkv, grad_attn, layer)
    return (grad_x, (grad_low, grad_raised, grad_attn, grad_mixed), (sums, up_sums, mix_sums))


CORE_PAIRS = ((0, 1), (1, 0), (2, 3), (3, 2))


def pair_gather(value):
    return lax.all_gather(value, "section", axis_index_groups=[[0, 1], [2, 3]])


def send(value, routes):
    return lax.ppermute(value, "section", routes)


def swap_cores(value):
    return send(value, CORE_PAIRS)


def keep_half(value, core, axis):
    width = value.shape[axis] // 2
    return lax.dynamic_slice_in_dim(value, core * width, width, axis)


def weight_parts(kept, grads, half):
    x, context, hidden, active = kept[0], kept[2], kept[4], kept[9]
    grad_low, grad_raised, grad_attn, grad_mixed = grads

    def product(rows, cols):
        return dot_tn(rows, keep_half(cols, half, cols.ndim - 1)).astype(BF)

    return (
        product(active, grad_low),
        product(hidden, grad_raised),
        product(context, grad_attn),
        jnp.concatenate([product(x, grad_mixed[c]) for c in range(3)], axis=1),
    )


def sum_shards(kept, grads, core):
    theirs = weight_parts(kept, grads, 1 - core)
    arrived = [swap_cores(part) for part in theirs]
    mine = weight_parts(kept, grads, core)
    both = [(a.astype(F32) + b.astype(F32)).astype(BF) for a, b in zip(mine, arrived)]
    return [lax.psum_scatter(part, "dp", scatter_dimension=0, tiled=True) for part in both]


def small_sums(sums):
    sums, up_sums, mix_sums = sums
    rows = [up_sums[0], mix_sums.transpose(1, 0, 2).reshape(-1)]
    rows += [sums[n] for n in range(6)]
    shards = lax.axis_size("dp")
    return jnp.concatenate([row.reshape(shards, -1) for row in rows], axis=1)


def body(
    tokens_in, seg_starts, pad_mask, w_qkv, b_qv, w_attn_out, b_attn_out, ln_gain, ln_bias,
    w_up, b_up, w_down, b_down, w_proj, cotangent,
):
    section_at = lax.axis_index("section")
    core = section_at % 2
    is_late = section_at >= 2
    quarter = tokens_in.shape[1]
    length, width = 4 * quarter, tokens_in.shape[2]
    ff_width = w_up.shape[2]

    own = tokens_in[core]
    other = tokens_in[1 - core]
    near = swap_cores(other)
    straight = send(own, [(2, 0), (3, 1)])
    crossed = send(other, [(2, 1), (3, 0)])
    flip = core == 1
    x = jnp.concatenate(
        [
            jnp.where(flip, near, own),
            jnp.where(flip, own, near),
            jnp.where(flip, crossed, straight),
            jnp.where(flip, straight, crossed),
        ],
        axis=0,
    )
    small = pack_small(b_qv[0], b_attn_out[0], ln_gain[0], ln_bias[0], b_up[0], b_down[0])
    small = pair_gather(small[None])
    weights = (
        pair_gather(w_qkv[0]),
        pair_gather(w_attn_out[0]),
        pair_gather(w_up[0]),
        pair_gather(w_down[0]),
        small,
    )
    projection = lax.all_gather(w_proj, "section", axis=1, tiled=True)
    target = lax.all_gather(cotangent, "section", axis=2, tiled=True)[core]
    plan = attention_plan(seg_starts[core], pad_mask[core])

    def both_forward(rows):
        middle, kept_even = layer_forward(rows, weights, 0, plan)
        last, kept_odd = layer_forward(middle, weights, 1, plan)
        return (last, kept_even, kept_odd)

    early = both_forward(x)
    hopped = send(early[0], [(0, 2), (1, 3)])
    last, kept_even, kept_odd = lax.cond(
        is_late, lambda rows, _: both_forward(rows), lambda _, state: state, hopped, early
    )

    def head(rows):
        factor = math.sqrt(projection.shape[1])
        columns = dot(rows, projection)
        given = target.astype(F32)
        inverse = lax.rsqrt(jnp.sum(columns * columns, axis=1, keepdims=True) + EPS_PROJ)
        cross = jnp.sum(columns * given, axis=1, keepdims=True)
        embedded = (factor * columns * inverse).astype(BF)
        grad_columns = (factor * (given * inverse - columns * cross * inverse**3)).astype(BF)
        return (embedded, dot_tn(rows, grad_columns), dot_nt(grad_columns, projection).astype(BF))

    def layer_zero():
        row = jnp.zeros((length, width), BF)
        return (
            row,
            (row, jnp.zeros((length, ff_width), BF), row, jnp.zeros((3, length, width), BF)),
            (
                jnp.zeros((6, width), F32),
                jnp.zeros((1, ff_width), F32),
                jnp.zeros((GROUPS, 2, width // GROUPS), F32),
            ),
        )

    def back_late(rows):
        embedded, grad_proj, grad_last = head(rows)
        grad, grads_odd, sums_odd = layer_backward(grad_last, kept_odd, weights, 1, plan)
        grad, grads_even, sums_even = layer_backward(grad, kept_even, weights, 0, plan)
        return (embedded, grad_proj, grad, grads_odd, sums_odd, grads_even, sums_even)

    def back_none(rows):
        embedded = jnp.zeros((length, projection.shape[1]), BF)
        grad_proj = jnp.zeros(projection.shape, F32)
        grad, grads_odd, sums_odd = layer_zero()
        _, grads_even, sums_even = layer_zero()
        return (embedded, grad_proj, grad, grads_odd, sums_odd, grads_even, sums_even)

    embedded, grad_proj, grad_mid, grads_odd, sums_odd, grads_even, sums_even = lax.cond(
        is_late, back_late, back_none, last
    )
    hopped = send(grad_mid, [(2, 0), (3, 1)])

    def back_one(kept, layer):
        return lambda grad, late: layer_backward(grad, kept, weights, layer, plan)

    grad, grads_odd, sums_odd = lax.cond(
        is_late, lambda _, late: late, back_one(kept_odd, 1), hopped, (hopped, grads_odd, sums_odd)
    )
    shards_odd = sum_shards(kept_odd, grads_odd, core)
    grad, grads_even, sums_even = lax.cond(
        is_late, lambda _, late: late, back_one(kept_even, 0), grad, (grad, grads_even, sums_even)
    )
    shards_even = sum_shards(kept_even, grads_even, core)

    def owned(even, odd):
        mine = jnp.where(flip, odd, even)
        arrived = swap_cores(jnp.where(flip, even, odd))
        parts = (mine, arrived)
        return (jnp.where(flip, parts[1], parts[0]), jnp.where(flip, parts[0], parts[1]))

    owned_parts = [owned(even, odd) for even, odd in zip(shards_even, shards_odd)]

    def joined(pair):
        return jnp.concatenate(pair, axis=1).astype(F32)[None]

    grad_w_down, grad_w_up, grad_w_out = [joined(pair) for pair in owned_parts[:3]]
    first, second = owned_parts[3]
    third = first.shape[1] // 3
    pieces = []
    for c in range(3):
        pieces += [first[:, c * third : (c + 1) * third], second[:, c * third : (c + 1) * third]]
    grad_w_qkv = jnp.concatenate(pieces, axis=1).astype(F32)[None]

    small_even, small_odd = small_sums(sums_even), small_sums(sums_odd)
    small_mine = jnp.where(flip, small_odd, small_even) + swap_cores(
        jnp.where(flip, small_even, small_odd)
    )
    small_mine = lax.psum_scatter(small_mine, "dp", scatter_dimension=0, tiled=True)[0]
    share = width // lax.axis_size("dp")
    at = ff_width // lax.axis_size("dp")
    grad_b_up = small_mine[None, :at]
    grad_b_qv = small_mine[None, at : at + 2 * share]
    rows = small_mine[at + 2 * share :].reshape(6, share)

    shards = lax.axis_size("dp")
    proj_cols = w_proj.shape[1]
    grad_proj = grad_proj.reshape(shards, share, 4, proj_cols).transpose(2, 0, 1, 3)
    grad_w_proj = lax.psum_scatter(
        grad_proj.reshape(4 * shards, share * proj_cols),
        ("section", "dp"),
        scatter_dimension=0,
        tiled=True,
    ).reshape(share, proj_cols)

    spread = lax.all_gather(embedded, "section")[2:]
    embedded_out = lax.dynamic_slice_in_dim(spread, section_at * proj_cols, proj_cols, 2)

    quarters = grad.reshape(4, quarter, width)
    own_grad = quarters[core]
    near_grad = swap_cores(quarters[1 - core])
    straight_grad = send(quarters[2 + core], [(0, 2), (1, 3)])
    crossed_grad = send(quarters[3 - core], [(0, 3), (1, 2)])
    mine = jnp.where(is_late, straight_grad, own_grad)
    others = jnp.where(is_late, crossed_grad, near_grad)
    grad_in = jnp.stack(
        [jnp.where(flip, others, mine), jnp.where(flip, mine, others)]
    ).astype(F32)

    return (
        embedded_out,
        grad_in,
        grad_w_qkv,
        grad_b_qv,
        grad_w_out,
        rows[0][None],
        rows[1:3][None],
        rows[3:5][None],
        grad_w_up,
        grad_b_up,
        grad_w_down,
        rows[5][None],
        grad_w_proj,
    )


def solution(mesh):
    in_specs = (
        P("dp", "section", None),
        P("dp", None),
        P("dp", None),
        P("section", None, None),
        P("section", None),
        P("section", None, None),
        P("section", None),
        P("section", None, None),
        P("section", None, None),
        P("section", None, None),
        P("section", None),
        P("section", None, None),
        P("section", None),
        P(None, "section"),
        P("dp", None, "section"),
    )
    out_specs = (
        P("dp", None, "section"),
        P("dp", "section", None),
        P("section", "dp", None),
        P("section", "dp"),
        P("section", "dp", None),
        P("section", "dp"),
        P("section", None, "dp"),
        P("section", None, "dp"),
        P("section", "dp", None),
        P("section", "dp"),
        P("section", "dp", None),
        P("section", "dp"),
        P("dp", "section"),
    )
    return jax.shard_map(body, mesh=mesh, in_specs=in_specs, out_specs=out_specs, check_vma=False)
```

```python
from functools import partial
import math

import jax
import jax.numpy as jnp
from jax import lax
from jax.experimental import pallas as pl
from jax.experimental.pallas import tpu as pltpu
from jax.sharding import PartitionSpec as P

HEAD = 64
PAIR = 2 * HEAD
GROUPS = 2
QB = 128
KB = 256
EPS_NORM = 1e-05
EPS_PROJ = 1e-06
NEG_FILL = -1e30
PARAMS = pltpu.CompilerParams(vmem_limit_bytes=56 * 1024 * 1024)
COST = pl.CostEstimate(flops=1, bytes_accessed=1, transcendentals=0)
BF = jnp.bfloat16
F32 = jnp.float32

NT = (((1,), (1,)), ((), ()))
TN = (((0,), (0,)), ((), ()))


def dot(a, b):
    return jnp.dot(a, b, preferred_element_type=F32)


def dot_nt(a, b):
    return lax.dot_general(a, b, NT, preferred_element_type=F32)


def dot_tn(a, b):
    return lax.dot_general(a, b, TN, preferred_element_type=F32)


def pack_small(b_qv, b_out, gains, shifts, b_up, b_down):
    return jnp.concatenate(
        [b_up, b_qv, b_out, gains[0], gains[1], shifts[0], shifts[1], b_down]
    )


def small_spec(layer, width):
    return pl.BlockSpec((1, 1, width), lambda *_: (layer, 0, 0))


def weight_specs(block, index, layer):
    def spec(wanted):
        def at(*grid):
            return tuple(jnp.where((grid[-1][0] == layer) == wanted, n, 0) for n in index(grid[0]))

        return pl.BlockSpec(block, at)

    return [spec(True), spec(False)]


def pick(sel_ref, layer, pair):
    return jnp.where(sel_ref[0] == layer, pair[0][...], pair[1][...])


def attention_plan(starts, real_flags):
    length = real_flags.shape[0]
    places = jnp.arange(length, dtype=jnp.int32)
    segment = jnp.sum((starts[None, :] <= places[:, None]).astype(jnp.int32), axis=1)
    key_code = jnp.where(real_flags == 1, segment, -1).astype(F32)
    key_code = jnp.broadcast_to(key_code[:, None], (length, PAIR))
    query_code = segment.astype(F32).reshape(length // QB, QB)
    first = jnp.arange(length // QB, dtype=jnp.int32) * QB
    low = jnp.max(jnp.where(starts[None, :] <= first[:, None], starts[None, :], 0), axis=1)
    high = jnp.min(
        jnp.where(starts[None, :] > first[:, None] + (QB - 1), starts[None, :], length), axis=1
    )
    begin = (low // QB) * QB
    count = (high - begin + KB - 1) // KB
    begin = jnp.minimum(begin, length - KB * count)
    return (begin, count, key_code, query_code)


def pair_mask(rows):
    return lax.broadcasted_iota(jnp.int32, (rows, PAIR), 1) < HEAD


def stacked_heads(block):
    first = pair_mask(block.shape[0])
    zero = jnp.zeros_like(block)
    return jnp.concatenate([jnp.where(first, block, zero), jnp.where(first, zero, block)], axis=0)


def block_bias(key_code, query_code, key_at, query_at):
    keys = lax.broadcasted_iota(jnp.int32, (KB, QB), 0) + (key_at - query_at)
    same = keys == lax.broadcasted_iota(jnp.int32, (KB, QB), 1)
    bias = jnp.where((key_code == query_code) | same, 0.0, NEG_FILL)
    return jnp.concatenate([bias, bias], axis=1)


def top_rows(values, op):
    folded = values.reshape(values.shape[0] // 8, 8, values.shape[1])
    return op(folded, axis=0)


def unstack_heads(flat):
    rows = lax.broadcasted_iota(jnp.int32, (PAIR, QB), 0)
    return jnp.where(rows < HEAD, flat[:PAIR, :QB], flat[:PAIR, QB:]).T


def attend_forward_kernel(
    begin_ref, count_ref, qkv_ref, key_code_ref, query_code_ref, out_ref, logsum_ref,
    value_scr, query_scr, score_scr, total_scr,
):
    length = qkv_ref.shape[1]
    pairs = qkv_ref.shape[2] // PAIR
    cols = [slice(p * PAIR, (p + 1) * PAIR) for p in range(pairs)]
    for p in range(pairs):
        value_scr[p, :PAIR, :] = qkv_ref[2, :, cols[p]].T
        value_scr[p, PAIR:, :] = jnp.ones((value_scr.shape[1] - PAIR, length), BF)

    def one_query_block(i, _):
        query_at = pl.multiple_of(i * QB, QB)
        begin, count = begin_ref[i], count_ref[i]
        query_code = query_code_ref[pl.ds(i, 1), :]
        for p in range(pairs):
            query_scr[p] = stacked_heads(qkv_ref[0, pl.ds(query_at, QB), cols[p]])

        def scores(j, tops):
            key_at = pl.multiple_of(begin + j * KB, QB)
            bias = block_bias(key_code_ref[pl.ds(key_at, KB), :], query_code, key_at, query_at)
            fresh = []
            for p in range(pairs):
                part = dot_nt(qkv_ref[1, pl.ds(key_at, KB), cols[p]], query_scr[p]) + bias
                score_scr[p, pl.ds(j * KB, KB), :] = part
                fresh.append(jnp.maximum(tops[p], top_rows(part, jnp.max)))
            return tuple(fresh)

        tops = lax.fori_loop(
            0, count, scores, tuple(jnp.full((8, 2 * QB), NEG_FILL, F32) for _ in range(pairs))
        )
        tops = [jnp.max(top, axis=0, keepdims=True) for top in tops]
        total_scr[...] = jnp.zeros_like(total_scr)

        def sums(j, _):
            key_at = pl.multiple_of(begin + j * KB, QB)
            for p in range(pairs):
                probs = jnp.exp(score_scr[p, pl.ds(j * KB, KB), :] - tops[p]).astype(BF)
                total_scr[p] += dot(value_scr[p, :, pl.ds(key_at, KB)], probs)
            return 0

        lax.fori_loop(0, count, sums, 0)
        for p in range(pairs):
            weight = total_scr[p, PAIR : PAIR + 1, :]
            logsum_ref[0, pl.ds(p * (length // QB) + i, 1), :] = tops[p] + jnp.log(weight)
            out_ref[pl.ds(query_at, QB), cols[p]] = unstack_heads(
                total_scr[p, :PAIR, :] / weight
            ).astype(BF)
        return 0

    lax.fori_loop(0, length // QB, one_query_block, 0)


def attend_forward(qkv, plan):
    _, length, width = qkv.shape
    begin, count, key_code, query_code = plan
    group = width // GROUPS
    pairs = group // PAIR
    blocks = length // QB
    return pl.pallas_call(
        attend_forward_kernel,
        name="attend_forward",
        grid_spec=pltpu.PrefetchScalarGridSpec(
            num_scalar_prefetch=2,
            grid=(GROUPS,),
            in_specs=[
                pl.BlockSpec((3, length, group), lambda g, *_: (0, 0, g)),
                pl.BlockSpec((length, PAIR), lambda g, *_: (0, 0)),
                pl.BlockSpec((blocks, QB), lambda g, *_: (0, 0)),
            ],
            out_specs=[
                pl.BlockSpec((length, group), lambda g, *_: (0, g)),
                pl.BlockSpec((1, pairs * blocks, 2 * QB), lambda g, *_: (g, 0, 0)),
            ],
            scratch_shapes=[
                pltpu.VMEM((pairs, PAIR + 16, length), BF),
                pltpu.VMEM((pairs, 2 * QB, PAIR), BF),
                pltpu.VMEM((pairs, length, 2 * QB), F32),
                pltpu.VMEM((pairs, PAIR + 16, 2 * QB), F32),
            ],
        ),
        out_shape=[
            jax.ShapeDtypeStruct((length, width), BF),
            jax.ShapeDtypeStruct((GROUPS, pairs * blocks, 2 * QB), F32),
        ],
        compiler_params=PARAMS,
        cost_estimate=COST,
    )(begin, count, qkv, key_code, query_code)


def attend_backward_kernel(
    begin_ref, count_ref, qkv_ref, key_code_ref, query_code_ref, context_ref, logsum_ref, grad_ref,
    out_ref, sums_ref, key_scr, query_scr, given_scr, down_scr, grad_key_scr, grad_value_scr,
):
    length = qkv_ref.shape[1]
    pairs = qkv_ref.shape[2] // PAIR
    blocks = length // QB
    cols = [slice(p * PAIR, (p + 1) * PAIR) for p in range(pairs)]
    for p in range(pairs):
        key_scr[p] = qkv_ref[1, :, cols[p]].T
    grad_key_scr[...] = jnp.zeros_like(grad_key_scr)
    grad_value_scr[...] = jnp.zeros_like(grad_value_scr)
    sums_ref[...] = jnp.zeros_like(sums_ref)

    def one_query_block(i, _):
        query_at = pl.multiple_of(i * QB, QB)
        begin, count = begin_ref[i], count_ref[i]
        query_code = query_code_ref[pl.ds(i, 1), :]
        inner, logsum = [], []
        for p in range(pairs):
            query_scr[p] = stacked_heads(qkv_ref[0, pl.ds(query_at, QB), cols[p]])
            given = grad_ref[pl.ds(query_at, QB), cols[p]]
            given_scr[p] = stacked_heads(given)
            both = (given.astype(F32) * context_ref[pl.ds(query_at, QB), cols[p]].astype(F32)).T
            inner.append(
                jnp.concatenate(
                    [
                        jnp.sum(both[:HEAD], axis=0, keepdims=True),
                        jnp.sum(both[HEAD:], axis=0, keepdims=True),
                    ],
                    axis=1,
                )
            )
            logsum.append(logsum_ref[0, pl.ds(p * blocks + i, 1), :])
        down_scr[...] = jnp.zeros_like(down_scr)

        def one_key_block(j, _):
            key_at = pl.multiple_of(begin + j * KB, QB)
            rows = pl.ds(key_at, KB)
            bias = block_bias(key_code_ref[rows, :], query_code, key_at, query_at)
            for p in range(pairs):
                part = dot_nt(qkv_ref[1, rows, cols[p]], query_scr[p]) + bias
                probs = jnp.exp(part - logsum[p])
                grad_probs = dot_nt(qkv_ref[2, rows, cols[p]], given_scr[p])
                grad_scores = (probs * (grad_probs - inner[p])).astype(BF)
                grad_value_scr[rows, cols[p]] += dot(probs.astype(BF), given_scr[p])
                grad_key_scr[rows, cols[p]] += dot(grad_scores, query_scr[p])
                down_scr[p] += dot(key_scr[p, :, rows], grad_scores)
            return 0

        lax.fori_loop(0, count, one_key_block, 0)
        for p in range(pairs):
            grad_query = (unstack_heads(down_scr[p]) * (HEAD**-0.5)).astype(BF)
            out_ref[0, pl.ds(query_at, QB), cols[p]] = grad_query
            sums_ref[0, 0:1, cols[p]] += jnp.sum(grad_query.astype(F32), axis=0, keepdims=True)
        return 0

    lax.fori_loop(0, blocks, one_query_block, 0)
    out_ref[1] = grad_key_scr[...].astype(BF)
    grad_value = grad_value_scr[...].astype(BF)
    out_ref[2] = grad_value
    sums_ref[0, 1:2, :] = jnp.sum(grad_value.astype(F32), axis=0, keepdims=True)


def attend_backward(qkv, context, logsum, grad_context, plan):
    _, length, width = qkv.shape
    begin, count, key_code, query_code = plan
    group = width // GROUPS
    pairs = group // PAIR
    blocks = length // QB
    return pl.pallas_call(
        attend_backward_kernel,
        name="attend_backward",
        grid_spec=pltpu.PrefetchScalarGridSpec(
            num_scalar_prefetch=2,
            grid=(GROUPS,),
            in_specs=[
                pl.BlockSpec((3, length, group), lambda g, *_: (0, 0, g)),
                pl.BlockSpec((length, PAIR), lambda g, *_: (0, 0)),
                pl.BlockSpec((blocks, QB), lambda g, *_: (0, 0)),
                pl.BlockSpec((length, group), lambda g, *_: (0, g)),
                pl.BlockSpec((1, pairs * blocks, 2 * QB), lambda g, *_: (g, 0, 0)),
                pl.BlockSpec((length, group), lambda g, *_: (0, g)),
            ],
            out_specs=[
                pl.BlockSpec((3, length, group), lambda g, *_: (0, 0, g)),
                pl.BlockSpec((1, 2, group), lambda g, *_: (g, 0, 0)),
            ],
            scratch_shapes=[
                pltpu.VMEM((pairs, PAIR, length), BF),
                pltpu.VMEM((pairs, 2 * QB, PAIR), BF),
                pltpu.VMEM((pairs, 2 * QB, PAIR), BF),
                pltpu.VMEM((pairs, PAIR, 2 * QB), F32),
                pltpu.VMEM((length, group), F32),
                pltpu.VMEM((length, group), F32),
            ],
        ),
        out_shape=[
            jax.ShapeDtypeStruct((3, length, width), BF),
            jax.ShapeDtypeStruct((GROUPS, 2, group), F32),
        ],
        compiler_params=PARAMS,
        cost_estimate=COST,
    )(begin, count, qkv, key_code, query_code, context, logsum, grad_context)


def mix_kernel(layer, sel_ref, x_ref, own_ref, other_ref, small_ref, out_ref):
    part = pl.program_id(0)
    width = x_ref.shape[1]
    ff_width = small_ref.shape[2] - 8 * width
    at = ff_width + width * jnp.where(part == 2, 1, 0)
    shift = small_ref[0, :, pl.ds(pl.multiple_of(at, 128), width)]
    shift = jnp.where(part == 1, jnp.zeros_like(shift), shift)
    scale = jnp.where(part == 0, HEAD**-0.5, 1.0)
    weight = pick(sel_ref, layer, (own_ref, other_ref))
    for r in range(0, x_ref.shape[0], 256):
        rows = slice(r, r + 256)
        out_ref[0, rows, :] = ((dot(x_ref[rows, :], weight) + shift) * scale).astype(BF)


def mix(sel, x, w_qkv, small, layer):
    length, width = x.shape
    return pl.pallas_call(
        partial(mix_kernel, layer),
        name="mix",
        grid_spec=pltpu.PrefetchScalarGridSpec(
            num_scalar_prefetch=1,
            grid=(3,),
            in_specs=[
                pl.BlockSpec((length, width), lambda c, _: (0, 0)),
                *weight_specs((width, width), lambda c: (0, c), layer),
                small_spec(layer, small.shape[2]),
            ],
            out_specs=pl.BlockSpec((1, length, width), lambda c, _: (c, 0, 0)),
        ),
        out_shape=jax.ShapeDtypeStruct((3, length, width), BF),
        compiler_params=PARAMS,
        cost_estimate=COST,
    )(sel, x, *w_qkv, small)


def unmix_kernel(layer, sel_ref, grad_ref, own_ref, other_ref, skip_ref, out_ref, total):
    part = pl.program_id(0)

    @pl.when(part == 0)
    def _():
        total[...] = skip_ref[...].astype(F32)

    weight = pick(sel_ref, layer, (own_ref, other_ref))
    for r in range(0, total.shape[0], 256):
        rows = slice(r, r + 256)
        total[rows, :] += dot_nt(grad_ref[0, rows, :], weight)

    @pl.when(part == 2)
    def _():
        out_ref[...] = total[...].astype(BF)


def unmix(sel, grad_mixed, w_qkv, skip, layer):
    _, length, width = grad_mixed.shape
    return pl.pallas_call(
        partial(unmix_kernel, layer),
        name="unmix",
        grid_spec=pltpu.PrefetchScalarGridSpec(
            num_scalar_prefetch=1,
            grid=(3,),
            in_specs=[
                pl.BlockSpec((1, length, width), lambda c, _: (c, 0, 0)),
                *weight_specs((width, width), lambda c: (0, c), layer),
                pl.BlockSpec((length, width), lambda c, _: (0, 0)),
            ],
            out_specs=pl.BlockSpec((length, width), lambda c, _: (0, 0)),
            scratch_shapes=[pltpu.VMEM((length, width), F32)],
        ),
        out_shape=jax.ShapeDtypeStruct((length, width), BF),
        compiler_params=PARAMS,
        cost_estimate=COST,
    )(sel, grad_mixed, *w_qkv, skip)


def normalized(values):
    centred = values - jnp.mean(values, axis=-1, keepdims=True)
    inverse = lax.rsqrt(jnp.mean(centred * centred, axis=-1, keepdims=True) + EPS_NORM)
    return (centred * inverse, inverse)


def normalized_pull(grad_hat, hat, inverse):
    return inverse * (
        grad_hat
        - jnp.mean(grad_hat, axis=-1, keepdims=True)
        - hat * jnp.mean(grad_hat * hat, axis=-1, keepdims=True)
    )


ERF = (0.254829592, -0.284496736, 1.421413741, -1.453152027, 1.061405429)
ERF_SLOPE = 0.3275911


def gelu_parts(x):
    t = pl.reciprocal(1.0 + (ERF_SLOPE * math.sqrt(0.5)) * jnp.abs(x), approx=True)
    bell = jnp.exp(-0.5 * (x * x))
    tail = 0.5 * ERF[4]
    for term in ERF[3::-1]:
        tail = tail * t + 0.5 * term
    tail = tail * t * bell
    below = jnp.where(x >= 0, 1.0 - tail, tail)
    return (x * below, below + x * bell * (1.0 / math.sqrt(2.0 * math.pi)))


FB = 512
ROWS = 256


def small_slices(width, ff_width):
    names = ("b_q", "b_v", "b_out", "gain1", "gain2", "shift1", "shift2", "b_down")
    at = {"b_up": slice(0, ff_width)}
    for n, name in enumerate(names):
        at[name] = slice(ff_width + n * width, ff_width + (n + 1) * width)
    return at


def refine_kernel(
    layer, sel_ref, x_ref, context_ref,
    out_own_ref, out_other_ref, up_own_ref, up_other_ref, down_own_ref, down_other_ref,
    small_ref, b_up_ref,
    out_ref, hidden_ref, hat1_ref, hat2_ref, scale1_ref, scale2_ref, active_ref, slope_ref,
    total,
):
    step = pl.program_id(0)
    length, width = x_ref.shape
    at = small_slices(width, small_ref.shape[2] - 8 * width)

    def vector(name):
        return small_ref[0, :, at[name]]

    @pl.when(step == 0)
    def _():
        w_out = pick(sel_ref, layer, (out_own_ref, out_other_ref))
        for r in range(0, length, ROWS):
            rows = slice(r, r + ROWS)
            summed = x_ref[rows, :].astype(F32) + dot(context_ref[rows, :], w_out)
            hat, inverse = normalized(summed + vector("b_out"))
            hidden = hat * vector("gain1") + vector("shift1")
            hat1_ref[rows, :] = hat.astype(BF)
            scale1_ref[rows, :] = jnp.broadcast_to(inverse, (ROWS, 128))
            hidden_ref[rows, :] = hidden.astype(BF)
            total[rows, :] = hidden + vector("b_down")

    w_up = pick(sel_ref, layer, (up_own_ref, up_other_ref))
    w_down = pick(sel_ref, layer, (down_own_ref, down_other_ref))
    for r in range(0, length, ROWS):
        rows = slice(r, r + ROWS)
        raised = dot(hidden_ref[rows, :], w_up) + b_up_ref[0]
        active, slope = gelu_parts(raised)
        active = active.astype(BF)
        active_ref[rows, :] = active
        slope_ref[rows, :] = slope.astype(BF)
        total[rows, :] += dot(active, w_down)

    @pl.when(step == pl.num_programs(0) - 1)
    def _():
        for r in range(0, length, ROWS):
            rows = slice(r, r + ROWS)
            hat, inverse = normalized(total[rows, :])
            hat2_ref[rows, :] = hat.astype(BF)
            scale2_ref[rows, :] = jnp.broadcast_to(inverse, (ROWS, 128))
            out_ref[rows, :] = (hat * vector("gain2") + vector("shift2")).astype(BF)


def weights_specs(width, layer):
    return [
        *weight_specs((width, width), lambda f: (0, 0), layer),
        *weight_specs((width, FB), lambda f: (0, f), layer),
        *weight_specs((FB, width), lambda f: (f, 0), layer),
    ]


def refine(sel, x, context, weights, layer):
    w_out, w_up, w_down, small = weights
    length, width = x.shape
    ff_width = w_up[0].shape[1]
    whole = pl.BlockSpec((length, width), lambda f, _: (0, 0))
    lanes = pl.BlockSpec((length, 128), lambda f, _: (0, 0))
    part = pl.BlockSpec((length, FB), lambda f, _: (0, f))
    row_shape = jax.ShapeDtypeStruct((length, width), BF)
    lane_shape = jax.ShapeDtypeStruct((length, 128), F32)
    ff_shape = jax.ShapeDtypeStruct((length, ff_width), BF)
    return pl.pallas_call(
        partial(refine_kernel, layer),
        name="refine",
        grid_spec=pltpu.PrefetchScalarGridSpec(
            num_scalar_prefetch=1,
            grid=(ff_width // FB,),
            in_specs=[
                whole,
                whole,
                *weights_specs(width, layer),
                small_spec(layer, small.shape[2]),
                pl.BlockSpec((1, 1, FB), lambda f, _: (layer, 0, f)),
            ],
            out_specs=[whole, whole, whole, whole, lanes, lanes, part, part],
            scratch_shapes=[pltpu.VMEM((length, width), F32)],
        ),
        out_shape=[row_shape] * 4 + [lane_shape] * 2 + [ff_shape] * 2,
        compiler_params=PARAMS,
        cost_estimate=COST,
    )(sel, x, context, *w_out, *w_up, *w_down, small, small)


def refine_back_kernel(
    layer, sel_ref, grad_ref, hat1_ref, hat2_ref, scale1_ref, scale2_ref, slope_ref,
    out_own_ref, out_other_ref, up_own_ref, up_other_ref, down_own_ref, down_other_ref, small_ref,
    grad_low_ref, grad_raised_ref, grad_attn_ref, grad_context_ref, sums_ref, up_sums_ref,
    total,
):
    step = pl.program_id(0)
    length, width = grad_ref.shape
    at = small_slices(width, small_ref.shape[2] - 8 * width)

    def vector(name):
        return small_ref[0, :, at[name]]

    def add(row, values, first):
        part = jnp.sum(values, axis=0, keepdims=True)
        sums_ref[row : row + 1, :] = part if first else sums_ref[row : row + 1, :] + part

    @pl.when(step == 0)
    def _():
        for r in range(0, length, ROWS):
            rows = slice(r, r + ROWS)
            grad = grad_ref[rows, :].astype(F32)
            hat = hat2_ref[rows, :].astype(F32)
            joined = normalized_pull(grad * vector("gain2"), hat, scale2_ref[rows, :1])
            low = joined.astype(BF)
            grad_low_ref[rows, :] = low
            total[rows, :] = joined
            add(2, grad * hat, r == 0)
            add(4, grad, r == 0)
            add(5, low.astype(F32), r == 0)

    w_up = pick(sel_ref, layer, (up_own_ref, up_other_ref))
    w_down = pick(sel_ref, layer, (down_own_ref, down_other_ref))
    for r in range(0, length, ROWS):
        rows = slice(r, r + ROWS)
        grad_active = dot_nt(grad_low_ref[rows, :], w_down)
        raised = (grad_active * slope_ref[rows, :].astype(F32)).astype(BF)
        grad_raised_ref[rows, :] = raised
        part = jnp.sum(raised.astype(F32), axis=0, keepdims=True)
        up_sums_ref[...] = part if r == 0 else up_sums_ref[...] + part
        total[rows, :] += dot_nt(raised, w_up)

    @pl.when(step == pl.num_programs(0) - 1)
    def _():
        w_out = pick(sel_ref, layer, (out_own_ref, out_other_ref))
        for r in range(0, length, ROWS):
            rows = slice(r, r + ROWS)
            grad = total[rows, :]
            hat = hat1_ref[rows, :].astype(F32)
            summed = normalized_pull(grad * vector("gain1"), hat, scale1_ref[rows, :1])
            attn = summed.astype(BF)
            grad_attn_ref[rows, :] = attn
            grad_context_ref[rows, :] = dot_nt(attn, w_out).astype(BF)
            add(1, grad * hat, r == 0)
            add(3, grad, r == 0)
            add(0, attn.astype(F32), r == 0)


def refine_back(sel, grad, kept, weights, layer):
    w_out, w_up, w_down, small = weights
    hat1, hat2, scale1, scale2, slope = kept
    length, width = grad.shape
    ff_width = w_up[0].shape[1]
    whole = pl.BlockSpec((length, width), lambda f, _: (0, 0))
    lanes = pl.BlockSpec((length, 128), lambda f, _: (0, 0))
    part = pl.BlockSpec((length, FB), lambda f, _: (0, f))
    row_shape = jax.ShapeDtypeStruct((length, width), BF)
    return pl.pallas_call(
        partial(refine_back_kernel, layer),
        name="refine_back",
        grid_spec=pltpu.PrefetchScalarGridSpec(
            num_scalar_prefetch=1,
            grid=(ff_width // FB,),
            in_specs=[
                whole, whole, whole, lanes, lanes, part,
                *weights_specs(width, layer),
                small_spec(layer, small.shape[2]),
            ],
            out_specs=[
                whole, part, whole, whole,
                pl.BlockSpec((6, width), lambda f, _: (0, 0)),
                pl.BlockSpec((1, FB), lambda f, _: (0, f)),
            ],
            scratch_shapes=[pltpu.VMEM((length, width), F32)],
        ),
        out_shape=[
            row_shape,
            jax.ShapeDtypeStruct((length, ff_width), BF),
            row_shape,
            row_shape,
            jax.ShapeDtypeStruct((6, width), F32),
            jax.ShapeDtypeStruct((1, ff_width), F32),
        ],
        compiler_params=PARAMS,
        cost_estimate=COST,
    )(sel, grad, hat1, hat2, scale1, scale2, slope, *w_out, *w_up, *w_down, small)


HALF = 384
SHARDS = 8


def feed_grads_kernel(
    sel_ref, hidden_ref, raised_late_ref, raised_ref, active_ref, low_late_ref, low_ref, out_ref,
    hidden_scr, low_scr, raised_scr,
):
    step = pl.program_id(0)
    blocks = raised_ref.shape[1] // HALF
    share = hidden_ref.shape[1] // SHARDS
    late = sel_ref[1] == 1

    @pl.when(step == 0)
    def _():
        hidden_scr[...] = hidden_ref[...].T
        low_scr[...] = jnp.where(late, low_late_ref[...], low_ref[...]).T
        raised_scr[...] = jnp.where(late, raised_late_ref[...], raised_ref[...])

    @pl.when(step < 4)
    def _():
        at = pl.multiple_of(step * (2 * share), 2 * share)
        part = dot(hidden_scr[pl.ds(at, 2 * share), :], raised_scr[...]).astype(BF)
        for m in range(2):
            for n in range(blocks):
                out_ref[m, n * share : (n + 1) * share, :] = part[
                    m * share : (m + 1) * share, n * HALF : (n + 1) * HALF
                ]

    @pl.when(step >= 4)
    def _():
        rows = out_ref.shape[1]
        for m in range(2):
            part = dot(low_scr[...], active_ref[:, m * rows : (m + 1) * rows])
            out_ref[m] = part.T.astype(BF)


def feed_grads(sel, hidden, raised_late, raised, active, low_late, low):
    length, width = hidden.shape
    ff_width = active.shape[1]
    half_ff = ff_width // 2

    def late_spec(shape, wanted):
        return pl.BlockSpec(shape, lambda n, sel: (0, jnp.where(sel[1] == wanted, sel[2], 0)))

    return pl.pallas_call(
        feed_grads_kernel,
        name="feed_grads",
        grid_spec=pltpu.PrefetchScalarGridSpec(
            num_scalar_prefetch=1,
            grid=(8,),
            in_specs=[
                pl.BlockSpec((length, width), lambda n, _: (0, 0)),
                late_spec((length, half_ff), 1),
                late_spec((length, half_ff), 0),
                pl.BlockSpec((length, ff_width // 4), lambda n, _: (0, jnp.maximum(n - 4, 0))),
                late_spec((length, width // 2), 1),
                late_spec((length, width // 2), 0),
            ],
            out_specs=pl.BlockSpec(
                (2, ff_width // SHARDS, HALF), lambda n, _: (lax.rem(n, 4), n // 4, 0)
            ),
            scratch_shapes=[
                pltpu.VMEM((width, length), BF),
                pltpu.VMEM((width // 2, length), BF),
                pltpu.VMEM((length, half_ff), BF),
            ],
        ),
        out_shape=jax.ShapeDtypeStruct((SHARDS, 2 * (ff_width // SHARDS), HALF), BF),
        compiler_params=PARAMS,
        cost_estimate=COST,
    )(sel, hidden, raised_late, raised, active, low_late, low)


def attend_grads_kernel(
    sel_ref, context_ref, x_ref, attn_late_ref, attn_ref, mixed_late_ref, mixed_ref, out_ref, turned
):
    step = pl.program_id(0)
    late = sel_ref[1] == 1

    def store(cols):
        out_ref[...] = dot(turned[...], cols).astype(BF).reshape(out_ref.shape)

    @pl.when(step == 0)
    def _():
        turned[...] = context_ref[...].T
        store(jnp.where(late, attn_late_ref[...], attn_ref[...]))

    @pl.when(step == 1)
    def _():
        turned[...] = x_ref[...].T

    @pl.when(step > 0)
    def _():
        store(jnp.where(late, mixed_late_ref[0], mixed_ref[0]))


def attend_grads(sel, context, x, attn_late, attn, mixed_late, mixed):
    length, width = x.shape

    def late_spec(wanted):
        return pl.BlockSpec(
            (length, HALF), lambda n, sel: (0, jnp.where(sel[1] == wanted, sel[2], 0))
        )

    def mixed_spec(wanted):
        def at(n, sel):
            return (
                jnp.where(sel[1] == wanted, jnp.maximum(n - 1, 0), 0),
                0,
                jnp.where(sel[1] == wanted, sel[2], 0),
            )

        return pl.BlockSpec((1, length, HALF), at)

    whole = pl.BlockSpec((length, width), lambda n, _: (0, 0))
    share = width // SHARDS
    return pl.pallas_call(
        attend_grads_kernel,
        name="attend_grads",
        grid_spec=pltpu.PrefetchScalarGridSpec(
            num_scalar_prefetch=1,
            grid=(4,),
            in_specs=[whole, whole, late_spec(1), late_spec(0), mixed_spec(1), mixed_spec(0)],
            out_specs=pl.BlockSpec((SHARDS, share, HALF), lambda n, _: (0, n, 0)),
            scratch_shapes=[pltpu.VMEM((width, length), BF)],
        ),
        out_shape=jax.ShapeDtypeStruct((SHARDS, 4 * share, HALF), BF),
        compiler_params=PARAMS,
        cost_estimate=COST,
    )(sel, context, x, attn_late, attn, mixed_late, mixed)


def layer_forward(sel, x, weights, layer, plan):
    w_qkv, w_out, w_up, w_down, small = weights
    qkv = mix(sel, x, w_qkv, small, layer)
    context, logsum = attend_forward(qkv, plan)
    out, hidden, hat1, hat2, scale1, scale2, active, slope = refine(
        sel, x, context, (w_out, w_up, w_down, small), layer
    )
    return (out, (x, qkv, context, logsum, hidden, hat1, hat2, scale1, scale2, active, slope))


def feed_backward(sel, grad, kept, weights, layer):
    _, w_out, w_up, w_down, small = weights
    hat1, hat2, scale1, scale2 = kept[5:9]
    grad_low, grad_raised, grad_attn, grad_context, sums, up_sums = refine_back(
        sel, grad, (hat1, hat2, scale1, scale2, kept[10]), (w_out, w_up, w_down, small), layer
    )
    return (grad_context, (grad_low, grad_raised, grad_attn), (sums, up_sums))


def mixed_backward(grad_context, kept, plan):
    return attend_backward(kept[1], kept[2], kept[3], grad_context, plan)


def layer_backward(sel, grad, kept, weights, layer, plan):
    grad_context, grads, sums = feed_backward(sel, grad, kept, weights, layer)
    grad_mixed, mix_sums = mixed_backward(grad_context, kept, plan)
    grad_x = unmix(sel, grad_mixed, weights[0], grads[2], layer)
    return (grad_x, grads + (grad_mixed,), sums + (mix_sums,))


def swap_cores(value):
    return send(value, ((0, 1), (1, 0), (2, 3), (3, 2)))


def send(value, routes):
    return lax.ppermute(value, "section", routes)


def pick_row(value, at, axis=0):
    return lax.dynamic_index_in_dim(value, at, axis, keepdims=False)


def plus(*values):
    return sum(value.astype(F32) for value in values).astype(BF)


class RowSum:
    def __init__(self, value, x_first):
        at = lax.axis_index("dp")
        self.z, self.x, self.x_first = at // 2, at % 2, x_first
        self.value = value.reshape(4, 2, *value.shape[1:])
        self.travelling = None
        self.steps = [self.cross, self.line, self.line, self.line]
        if not x_first:
            self.steps = self.steps[1:] + self.steps[:1]
        self.line_at = 0

    def cross(self):
        axis = 1 if self.x_first else 0
        other = pick_row(self.value, 1 - self.x, axis)
        arrived = lax.ppermute(other, "dp", [(n, n ^ 1) for n in range(8)])
        self.value = plus(pick_row(self.value, self.x, axis), arrived)

    def line(self):
        self.line_at += 1
        far = 4 - self.line_at
        right = pick_row(self.value, jnp.minimum(self.z + far, 3))
        left = pick_row(self.value, jnp.maximum(self.z - far, 0))
        if self.travelling is not None:
            right, left = plus(right, self.travelling[0]), plus(left, self.travelling[1])
        self.travelling = (
            lax.ppermute(right, "dp", [(n, n + 2) for n in range(6)]),
            lax.ppermute(left, "dp", [(n + 2, n) for n in range(6)]),
        )
        if self.line_at == 3:
            self.value = plus(pick_row(self.value, self.z), *self.travelling)

    def step(self):
        if self.steps:
            self.steps.pop(0)()

    def result(self):
        while self.steps:
            self.step()
        return self.value


class PlainSum:
    def __init__(self, value, blocks):
        shards = lax.axis_size("dp")
        parts, at = [], 0
        for rows in blocks:
            part = value[:, at : at + rows].reshape(shards, -1, value.shape[2])
            parts, at = parts + [part], at + rows
        whole = jnp.concatenate(parts, axis=1)
        self.value = lax.psum_scatter(whole, "dp", scatter_dimension=0, tiled=True)[0]
        self.travelling = None

    def step(self):
        pass

    def result(self):
        return self.value


def body(
    tokens_in, seg_starts, pad_mask, w_qkv, b_qv, w_attn_out, b_attn_out, ln_gain, ln_bias,
    w_up, b_up, w_down, b_down, w_proj, cotangent,
):
    section_at = lax.axis_index("section")
    core = section_at % 2
    is_late = section_at >= 2
    flip = core == 1
    quarter = tokens_in.shape[1]
    length, width = 4 * quarter, tokens_in.shape[2]
    ff_width = w_up.shape[2]
    proj_cols = w_proj.shape[1]
    shards = lax.axis_size("dp")
    share = width // shards

    def sel_for(half):
        return jnp.stack([core, section_at // 2, half]).astype(jnp.int32)

    sel_mine, sel_theirs = sel_for(core), sel_for(1 - core)

    own = pick_row(tokens_in, core)
    other = pick_row(tokens_in, 1 - core)
    straight = send(own, [(2, 0), (3, 1)])
    crossed = send(other, [(2, 1), (3, 0)])
    near = swap_cores(other)
    small = pack_small(b_qv[0], b_attn_out[0], ln_gain[0], ln_bias[0], b_up[0], b_down[0])[None]
    small_other = swap_cores(small)
    small = jnp.stack([jnp.where(flip, small_other, small), jnp.where(flip, small, small_other)])
    weights = tuple((w[0], swap_cores(w[0])) for w in (w_qkv, w_attn_out, w_up, w_down)) + (small,)
    x = jnp.concatenate(
        [
            jnp.where(flip, near, own),
            jnp.where(flip, own, near),
            jnp.where(flip, crossed, straight),
            jnp.where(flip, straight, crossed),
        ],
        axis=0,
    )

    head_own = jnp.concatenate([w_proj, pick_row(cotangent, core)], axis=0)
    head_other = jnp.concatenate([w_proj, pick_row(cotangent, 1 - core)], axis=0)
    head_own = head_own.reshape(-1, 4 * proj_cols)
    head_other = head_other.reshape(-1, 4 * proj_cols)
    head_parts = (
        head_own,
        send(head_other, [(2, 3), (3, 2)]),
        send(head_own, [(0, 2), (1, 3)]),
        send(head_other, [(0, 3), (1, 2)]),
    )
    plan = attention_plan(pick_row(seg_starts, core), pick_row(pad_mask, core))

    def both_forward(rows):
        middle, kept_even = layer_forward(sel_mine, rows, weights, 0, plan)
        last, kept_odd = layer_forward(sel_mine, middle, weights, 1, plan)
        return (last, kept_even, kept_odd)

    def head(rows):
        mine, late, straight, crossed = [part.reshape(-1, proj_cols) for part in head_parts]
        joined_parts = jnp.concatenate(
            [
                jnp.where(flip, crossed, straight),
                jnp.where(flip, straight, crossed),
                jnp.where(flip, late, mine),
                jnp.where(flip, mine, late),
            ],
            axis=1,
        )
        projection, target = joined_parts[:width], joined_parts[width:]
        factor = math.sqrt(projection.shape[1])
        columns = dot(rows, projection)
        given = target.astype(F32)
        inverse = lax.rsqrt(jnp.sum(columns * columns, axis=1, keepdims=True) + EPS_PROJ)
        cross = jnp.sum(columns * given, axis=1, keepdims=True)
        embedded = (factor * columns * inverse).astype(BF)
        grad_columns = (factor * (given * inverse - columns * cross * inverse**3)).astype(BF)
        return (
            embedded,
            dot_tn(rows, grad_columns).astype(BF),
            dot_nt(grad_columns, projection).astype(BF),
        )

    early, kept_even, kept_odd = both_forward(x)
    hopped = send(early, [(0, 2), (1, 3)])
    hopped, head_parts = lax.optimization_barrier((hopped, head_parts))

    def late_turn(rows, *_):
        last, kept_even, kept_odd = both_forward(rows)
        embedded, grad_proj, grad = head(last)
        grad, grads_odd, sums_odd = layer_backward(sel_mine, grad, kept_odd, weights, 1, plan)
        grad, grads_even, sums_even = layer_backward(sel_mine, grad, kept_even, weights, 0, plan)
        return (
            kept_even, kept_odd, embedded, grad_proj, grad,
            grads_odd, sums_odd, grads_even, sums_even,
        )

    def early_turn(rows, kept_even, kept_odd):
        row, ff = jnp.zeros((length, width), BF), jnp.zeros((length, ff_width), BF)
        grads = (row, ff, row, jnp.zeros((3, length, width), BF))
        sums = (
            jnp.zeros((6, width), F32),
            jnp.zeros((1, ff_width), F32),
            jnp.zeros((GROUPS, 2, width // GROUPS), F32),
        )
        return (
            kept_even, kept_odd, jnp.zeros((length, 4 * proj_cols), BF),
            jnp.zeros((width, 4 * proj_cols), BF), row, grads, sums, grads, sums,
        )

    (
        kept_even, kept_odd, embedded, grad_proj, grad_mid,
        late_odd, late_sums_odd, late_even, late_sums_even,
    ) = lax.cond(is_late, late_turn, early_turn, hopped, kept_even, kept_odd)

    grad = send(grad_mid, [(2, 0), (3, 1)])
    embedded_cols = embedded.reshape(length, 4, proj_cols).transpose(1, 0, 2)

    rows_of_one = width // SHARDS
    attend_blocks = (rows_of_one,) * 4
    feed_blocks = (rows_of_one,) * (ff_width // (2 * HALF)) + (ff_width // SHARDS,)

    def row_sum(value, blocks):
        return RowSum(value, True) if shards == SHARDS else PlainSum(value, blocks)

    def feed_sum(kept, late, now):
        args = (kept[4], late[1], now[1], kept[9], late[0], now[0])
        arrived = swap_cores(feed_grads(sel_theirs, *args))
        return row_sum(plus(feed_grads(sel_mine, *args), arrived), feed_blocks)

    def attend_parts(kept, late, now, mixed):
        args = (kept[2], kept[0], late[2], now[2], late[3], mixed)
        return (attend_grads(sel_theirs, *args), attend_grads(sel_mine, *args))

    def merged(late_sums, sums):
        return tuple(jnp.where(is_late, a, b) for a, b in zip(late_sums, sums))

    def tie(*values):
        return lax.optimization_barrier(values)

    grad_context, grads_odd, sums_odd = feed_backward(sel_mine, grad, kept_odd, weights, 1)
    feed_odd = feed_sum(kept_odd, late_odd, grads_odd)
    grad_context, feed_odd.value = tie(grad_context, feed_odd.value)
    feed_odd.step()
    mixed_odd, mix_sums = mixed_backward(grad_context, kept_odd, plan)
    sums_odd = merged(late_sums_odd, sums_odd + (mix_sums,))
    grad = unmix(sel_mine, mixed_odd, weights[0], grads_odd[2], 1)
    theirs, mine = attend_parts(kept_odd, late_odd, grads_odd, mixed_odd)
    attend_odd = row_sum(plus(mine, swap_cores(theirs)), attend_blocks)
    grad, attend_odd.value, feed_odd.value = tie(grad, attend_odd.value, feed_odd.value)
    feed_odd.step()
    attend_odd.step()

    grad_context, grads_even, sums_even = feed_backward(sel_mine, grad, kept_even, weights, 0)
    feed_even = feed_sum(kept_even, late_even, grads_even)
    grad_context, feed_even.value, feed_odd.travelling, attend_odd.value = tie(
        grad_context, feed_even.value, feed_odd.travelling, attend_odd.value
    )
    feed_odd.step()
    feed_even.step()
    attend_odd.step()
    mixed_even, mix_sums = mixed_backward(grad_context, kept_even, plan)
    sums_even = merged(late_sums_even, sums_even + (mix_sums,))
    mixed_even, feed_odd.travelling, attend_odd.travelling = tie(
        mixed_even, feed_odd.travelling, attend_odd.travelling
    )
    feed_odd.step()
    attend_odd.step()
    theirs, mine = attend_parts(kept_even, late_even, grads_even, mixed_even)
    arrived = swap_cores(theirs)
    grad = unmix(sel_mine, mixed_even, weights[0], grads_even[2], 0)

    def small_rows(sums):
        sums, up_sums, mix_sums = sums
        rows = [up_sums[0], mix_sums.transpose(1, 0, 2).reshape(-1)]
        rows += [sums[n] for n in range(6)]
        return jnp.concatenate([row.reshape(shards, -1) for row in rows], axis=1)

    extras = jnp.concatenate(
        [small_rows(sums_even), small_rows(sums_odd), grad_proj.reshape(shards, -1).astype(F32)],
        axis=1,
    )
    small_width = 12 * share
    lines = -(-extras.shape[1] // HALF)
    lines = -(-lines // 16) * 16
    extras = jnp.pad(extras, ((0, 0), (0, lines * HALF - extras.shape[1])))
    extras = extras.reshape(shards, lines, HALF).astype(BF)
    extras = plus(extras, swap_cores(extras))
    attend_even = plus(mine, arrived)
    if shards == SHARDS:
        tail = RowSum(jnp.concatenate([attend_even, extras], axis=1), True)
        feed_odd, attend_odd = feed_odd.result(), attend_odd.result()
        tail.step()
        feed_even = feed_even.result()
        tail = tail.result()
        attend_even, extras = tail[: 4 * share], tail[4 * share :]
    else:
        feed_odd, attend_odd, feed_even = [
            part.result() for part in (feed_odd, attend_odd, feed_even)
        ]
        attend_even = PlainSum(attend_even, attend_blocks).result()
        extras = lax.psum_scatter(extras, "dp", scatter_dimension=0, tiled=True)[0]

    routes_odd, routes_even = ((0, 1), (2, 3)), ((1, 0), (3, 2))

    def halves(even, odd):
        arrived = jnp.where(flip, send(odd, routes_odd), send(even, routes_even))
        mine = jnp.where(flip, odd, even)
        return (jnp.where(flip, arrived, mine), jnp.where(flip, mine, arrived))

    blocks = ff_width // (2 * HALF)
    feed_halves = halves(feed_even, feed_odd)
    attend_halves = halves(attend_even, attend_odd)

    def columns(pair, first, count):
        parts = [part[n * share : (n + 1) * share] for part in pair for n in range(first, first + count)]
        return jnp.concatenate(parts, axis=1).astype(F32)

    grad_w_up = columns(feed_halves, 0, blocks)[None]
    grad_w_down = jnp.concatenate([part[blocks * share :] for part in feed_halves], axis=1)
    grad_w_down = grad_w_down.astype(F32)[None]
    grad_w_out = columns(attend_halves, 0, 1)[None]
    grad_w_qkv = jnp.concatenate([columns(attend_halves, 1 + c, 1) for c in range(3)], axis=1)[None]

    extras = extras.reshape(-1).astype(F32)
    small_mine = jnp.where(flip, extras[small_width : 2 * small_width], extras[:small_width])
    at = ff_width // shards
    grad_b_up = small_mine[None, :at]
    grad_b_qv = small_mine[None, at : at + 2 * share]
    rows = small_mine[at + 2 * share :].reshape(6, share)
    grad_proj = extras[2 * small_width : 2 * small_width + share * 4 * proj_cols]
    grad_proj = grad_proj.reshape(share, 4 * proj_cols).astype(BF)
    grad_proj = jnp.where(is_late, grad_proj, send(grad_proj, [(2, 0), (3, 1)])).astype(F32)
    grad_w_proj = lax.dynamic_slice_in_dim(grad_proj, section_at * proj_cols, proj_cols, 1)

    straight_cols = send(pick_row(embedded_cols, core), [(2, 0), (3, 1)])
    crossed_cols = send(pick_row(embedded_cols, 1 - core), [(2, 1), (3, 0)])
    near_cols = swap_cores(pick_row(embedded_cols, 3 - core))
    own_cols = jnp.where(is_late, pick_row(embedded_cols, section_at), straight_cols)
    other_cols = jnp.where(is_late, near_cols, crossed_cols)
    embedded_out = jnp.stack(
        [jnp.where(flip, other_cols, own_cols), jnp.where(flip, own_cols, other_cols)]
    )

    quarters = grad.reshape(4, quarter, width)
    straight_grad = send(pick_row(quarters, 2 + core), [(0, 2), (1, 3)])
    crossed_grad = send(pick_row(quarters, 3 - core), [(0, 3), (1, 2)])
    near_grad = swap_cores(pick_row(quarters, 1 - core))
    mine = jnp.where(is_late, straight_grad, pick_row(quarters, core))
    others = jnp.where(is_late, crossed_grad, near_grad)
    grad_in = jnp.stack(
        [jnp.where(flip, others, mine), jnp.where(flip, mine, others)]
    ).astype(F32)

    return (
        embedded_out,
        grad_in,
        grad_w_qkv,
        grad_b_qv,
        grad_w_out,
        rows[0][None],
        rows[1:3][None],
        rows[3:5][None],
        grad_w_up,
        grad_b_up,
        grad_w_down,
        rows[5][None],
        grad_w_proj,
    )


def solution(mesh):
    in_specs = (
        P("dp", "section", None),
        P("dp", None),
        P("dp", None),
        P("section", None, None),
        P("section", None),
        P("section", None, None),
        P("section", None),
        P("section", None, None),
        P("section", None, None),
        P("section", None, None),
        P("section", None),
        P("section", None, None),
        P("section", None),
        P(None, "section"),
        P("dp", None, "section"),
    )
    out_specs = (
        P("dp", None, "section"),
        P("dp", "section", None),
        P("section", "dp", None),
        P("section", "dp"),
        P("section", "dp", None),
        P("section", "dp"),
        P("section", None, "dp"),
        P("section", None, "dp"),
        P("section", "dp", None),
        P("section", "dp"),
        P("section", "dp", None),
        P("section", "dp"),
        P("dp", "section"),
    )
    return jax.shard_map(body, mesh=mesh, in_specs=in_specs, out_specs=out_specs, check_vma=False)
```

```python
from functools import partial
import math

import jax
import jax.numpy as jnp
from jax import lax
from jax.experimental import pallas as pl
from jax.experimental.pallas import tpu as pltpu
from jax.sharding import PartitionSpec as P

HEAD = 64
PAIR = 2 * HEAD
QB = 128
KB = 512
EPS_NORM = 1e-05
EPS_PROJ = 1e-06
NEG_FILL = -1e30
PARAMS = pltpu.CompilerParams(vmem_limit_bytes=60 * 1024 * 1024)
COST = pl.CostEstimate(flops=1, bytes_accessed=1, transcendentals=0)
BF = jnp.bfloat16
F32 = jnp.float32

NT = (((1,), (1,)), ((), ()))
TN = (((0,), (0,)), ((), ()))


def dot(a, b):
    return jnp.dot(a, b, preferred_element_type=F32)


def dot_nt(a, b):
    return lax.dot_general(a, b, NT, preferred_element_type=F32)


def dot_tn(a, b):
    return lax.dot_general(a, b, TN, preferred_element_type=F32)


def pack_small(b_qv, b_out, gains, shifts, b_up, b_down):
    return jnp.concatenate(
        [b_up, b_qv, b_out, gains[0], gains[1], shifts[0], shifts[1], b_down]
    )


def small_spec(layer, width):
    return pl.BlockSpec((1, 1, width), lambda *_: (layer, 0, 0))


def attention_plan(starts, real_flags):
    length = real_flags.shape[0]
    places = jnp.arange(length, dtype=jnp.int32)
    segment = jnp.sum((starts[None, :] <= places[:, None]).astype(jnp.int32), axis=1)
    key_code = jnp.where(real_flags == 1, segment, -1).astype(F32)
    key_code = jnp.broadcast_to(key_code[:, None], (length, PAIR))
    query_code = segment.astype(F32).reshape(length // QB, QB)
    first = jnp.arange(length // QB, dtype=jnp.int32) * QB
    low = jnp.max(jnp.where(starts[None, :] <= first[:, None], starts[None, :], 0), axis=1)
    high = jnp.min(
        jnp.where(starts[None, :] > first[:, None] + (QB - 1), starts[None, :], length), axis=1
    )
    begin = (low // QB) * QB
    count = (high - begin + KB - 1) // KB
    begin = jnp.minimum(begin, length - KB * count)
    return (begin, count, key_code, query_code)


def pair_mask(rows):
    return lax.broadcasted_iota(jnp.int32, (rows, PAIR), 1) < HEAD


def stacked_heads(block):
    first = pair_mask(block.shape[0])
    zero = jnp.zeros_like(block)
    return jnp.concatenate([jnp.where(first, block, zero), jnp.where(first, zero, block)], axis=0)


def block_bias(key_code, query_code, key_at, query_at):
    keys = lax.broadcasted_iota(jnp.int32, (KB, QB), 0) + (key_at - query_at)
    same = keys == lax.broadcasted_iota(jnp.int32, (KB, QB), 1)
    bias = jnp.where((key_code == query_code) | same, 0.0, NEG_FILL)
    return jnp.concatenate([bias, bias], axis=1)


def top_rows(values, op):
    folded = values.reshape(values.shape[0] // 8, 8, values.shape[1])
    return op(folded, axis=0)


def unstack_heads(flat):
    rows = lax.broadcasted_iota(jnp.int32, (PAIR, QB), 0)
    return jnp.where(rows < HEAD, flat[:PAIR, :QB], flat[:PAIR, QB:]).T


def attend_forward(
    begin_ref, count_ref, qkv_ref, key_code_ref, query_code_ref, out_ref, logsum_ref,
    value_scr, query_scr, total_scr,
):
    length = qkv_ref.shape[1]
    pairs = qkv_ref.shape[2] // PAIR
    every = range(pairs)
    cols = [slice(p * PAIR, (p + 1) * PAIR) for p in every]
    for p in every:
        value_scr[p, :PAIR, :] = qkv_ref[2, :, cols[p]].T
        value_scr[p, PAIR:, :] = jnp.ones((value_scr.shape[1] - PAIR, length), BF)

    def one_query_block(i, _):
        query_at = pl.multiple_of(i * QB, QB)
        begin, count = begin_ref[i], count_ref[i]
        query_code = query_code_ref[pl.ds(i, 1), :]
        for p in every:
            query_scr[p] = stacked_heads(qkv_ref[0, pl.ds(query_at, QB), cols[p]])
        total_scr[...] = jnp.zeros_like(total_scr)

        def one_key_block(j, tops):
            key_at = pl.multiple_of(begin + j * KB, QB)
            rows = pl.ds(key_at, KB)
            bias = block_bias(key_code_ref[rows, :], query_code, key_at, query_at)
            scores = [dot_nt(qkv_ref[1, rows, cols[p]], query_scr[p]) + bias for p in every]
            fresh = [
                jnp.maximum(tops[p], jnp.max(scores[p], axis=0, keepdims=True)) for p in every
            ]
            probs = [jnp.exp(scores[p] - fresh[p]).astype(BF) for p in every]
            for p in every:
                total_scr[p] = total_scr[p] * jnp.exp(tops[p] - fresh[p]) + dot(
                    value_scr[p, :, rows], probs[p]
                )
            return tuple(fresh)

        tops = lax.fori_loop(
            0, count, one_key_block, tuple(jnp.full((1, 2 * QB), 2 * NEG_FILL, F32) for _ in every)
        )
        for p in every:
            weight = total_scr[p, PAIR : PAIR + 1, :]
            logsum_ref[pl.ds(p * (length // QB) + i, 1), :] = tops[p] + jnp.log(weight)
            out_ref[pl.ds(query_at, QB), cols[p]] = unstack_heads(
                total_scr[p, :PAIR, :] * (1.0 / weight)
            ).astype(BF)
        return 0

    lax.fori_loop(0, length // QB, one_query_block, 0)


def attend_backward(
    begin_ref, count_ref, qkv, key_code_ref, query_code_ref, context, logsum_ref, grad, sums_ref,
    key_scr, query_scr, given_scr, down_scr, grad_key_scr, grad_value_scr,
):
    length = qkv.shape[1]
    pairs = qkv.shape[2] // PAIR
    every = range(pairs)
    blocks = length // QB
    cols = [slice(p * PAIR, (p + 1) * PAIR) for p in every]
    for p in every:
        key_scr[p] = qkv[1, :, cols[p]].T
    grad_key_scr[...] = jnp.zeros_like(grad_key_scr)
    grad_value_scr[...] = jnp.zeros_like(grad_value_scr)
    sums_ref[...] = jnp.zeros_like(sums_ref)

    def one_query_block(i, _):
        query_at = pl.multiple_of(i * QB, QB)
        queries = pl.ds(query_at, QB)
        begin, count = begin_ref[i], count_ref[i]
        query_code = query_code_ref[pl.ds(i, 1), :]
        inner, logsum = [], []
        for p in every:
            query_scr[p] = stacked_heads(qkv[0, queries, cols[p]])
            given = grad[queries, cols[p]]
            given_scr[p] = stacked_heads(given)
            both = (given.astype(F32) * context[queries, cols[p]].astype(F32)).T
            inner.append(
                jnp.concatenate(
                    [
                        jnp.sum(both[:HEAD], axis=0, keepdims=True),
                        jnp.sum(both[HEAD:], axis=0, keepdims=True),
                    ],
                    axis=1,
                )
            )
            logsum.append(logsum_ref[pl.ds(p * blocks + i, 1), :])
        down_scr[...] = jnp.zeros_like(down_scr)

        def one_key_block(j, _):
            key_at = pl.multiple_of(begin + j * KB, QB)
            rows = pl.ds(key_at, KB)
            bias = block_bias(key_code_ref[rows, :], query_code, key_at, query_at)
            parts = [dot_nt(qkv[1, rows, cols[p]], query_scr[p]) + bias for p in every]
            grads = [dot_nt(qkv[2, rows, cols[p]], given_scr[p]) - inner[p] for p in every]
            probs = [jnp.exp(parts[p] - logsum[p]) for p in every]
            scores = [(probs[p] * grads[p]).astype(BF) for p in every]
            probs = [probs[p].astype(BF) for p in every]
            for p in every:
                grad_value_scr[rows, cols[p]] += dot(probs[p], given_scr[p])
            for p in every:
                grad_key_scr[rows, cols[p]] += dot(scores[p], query_scr[p])
            for p in every:
                down_scr[p] += dot(key_scr[p, :, rows], scores[p])
            return 0

        lax.fori_loop(0, count, one_key_block, 0)
        for p in every:
            grad_query = (unstack_heads(down_scr[p]) * (HEAD**-0.5)).astype(BF)
            qkv[0, queries, cols[p]] = grad_query
            sums_ref[0:1, cols[p]] += jnp.sum(grad_query.astype(F32), axis=0, keepdims=True)
        return 0

    lax.fori_loop(0, blocks, one_query_block, 0)
    qkv[1] = grad_key_scr[...].astype(BF)
    grad_value = grad_value_scr[...].astype(BF)
    qkv[2] = grad_value
    sums_ref[1:2, :] = jnp.sum(grad_value.astype(F32), axis=0, keepdims=True)


ANY = pl.BlockSpec(memory_space=pl.ANY)
ROWS = 256


class Held:
    def __init__(self, sel_ref, layer, pairs, held, sems, first=None):
        self.own = sel_ref[0] == layer
        self.items = list(zip(pairs, held, range(len(held))))
        self.sems = sems
        self.first = pl.program_id(0) == 0 if first is None else first

    def start(self):
        for pair, held, n in self.items:
            for wanted, source in zip((self.own, jnp.logical_not(self.own)), pair):

                @pl.when(self.first & wanted)
                def _():
                    pltpu.make_async_copy(source, held, self.sems.at[n]).start()

    def wait(self, n):
        pair, held, _ = self.items[n]

        @pl.when(self.first)
        def _():
            pltpu.make_async_copy(pair[0], held, self.sems.at[n]).wait()


def held_shapes(*weights):
    return [pltpu.VMEM(own.shape, own.dtype) for own, _ in weights]


def normalized(values):
    centred = values - jnp.mean(values, axis=-1, keepdims=True)
    inverse = lax.rsqrt(jnp.mean(centred * centred, axis=-1, keepdims=True) + EPS_NORM)
    return (centred * inverse, inverse)


def normalized_pull(grad_hat, hat, inverse):
    return inverse * (
        grad_hat
        - jnp.mean(grad_hat, axis=-1, keepdims=True)
        - hat * jnp.mean(grad_hat * hat, axis=-1, keepdims=True)
    )


ERF = (0.254829592, -0.284496736, 1.421413741, -1.453152027, 1.061405429)
ERF_SLOPE = 0.3275911


def gelu_parts(x):
    t = pl.reciprocal(1.0 + (ERF_SLOPE * math.sqrt(0.5)) * jnp.abs(x), approx=True)
    bell = jnp.exp(-0.5 * (x * x))
    tail = 0.5 * ERF[4]
    for term in ERF[3::-1]:
        tail = tail * t + 0.5 * term
    tail = tail * t * bell
    below = jnp.where(x >= 0, 1.0 - tail, tail)
    return (x * below, below + x * bell * (1.0 / math.sqrt(2.0 * math.pi)))


FB = 1024


def small_slices(width, ff_width):
    names = ("b_q", "b_v", "b_out", "gain1", "gain2", "shift1", "shift2", "b_down")
    at = {"b_up": slice(0, ff_width)}
    for n, name in enumerate(names):
        at[name] = slice(ff_width + n * width, ff_width + (n + 1) * width)
    return at


def refine_back_kernel(
    layer, sel_ref, grad_ref, hidden_ref, out_ref, scale1_ref, scale2_ref, slope_ref,
    out_own_ref, out_other_ref, up_own_ref, up_other_ref, down_own_ref, down_other_ref, small_ref,
    grad_low_ref, grad_raised_ref, grad_attn_ref, grad_context_ref, sums_ref, up_sums_ref,
    w_out, w_up, w_down, sems,
):
    pairs = [(out_own_ref, out_other_ref), (up_own_ref, up_other_ref), (down_own_ref, down_other_ref)]
    weights = Held(sel_ref, layer, pairs, [w_out, w_up, w_down], sems)
    weights.start()
    rows, width = grad_ref.shape
    ff_width = slope_ref.shape[1]
    at = small_slices(width, ff_width)

    @pl.when(pl.program_id(0) == 0)
    def _():
        sums_ref[...] = jnp.zeros_like(sums_ref)
        up_sums_ref[...] = jnp.zeros_like(up_sums_ref)

    def vector(name):
        return small_ref[0, :, at[name]]

    def add(row, values):
        sums_ref[row : row + 1, :] += jnp.sum(values, axis=0, keepdims=True)

    grad = grad_ref[...].astype(F32)
    hat = (out_ref[...].astype(F32) - vector("shift2")) * (1.0 / vector("gain2"))
    joined = normalized_pull(grad * vector("gain2"), hat, scale2_ref[:, :1])
    low = joined.astype(BF)
    grad_low_ref[...] = low
    add(2, grad * hat)
    add(4, grad)
    add(5, low.astype(F32))
    weights.wait(2)
    weights.wait(1)
    total = joined
    parts = [slice(f, f + FB) for f in range(0, ff_width, FB)]
    active = dot_nt(low, w_down[parts[0], :])
    for n, part in enumerate(parts):
        following = dot_nt(low, w_down[parts[n + 1], :]) if n + 1 < len(parts) else None
        raised = active * slope_ref[:, part].astype(F32)
        up_sums_ref[:, part] += jnp.sum(raised, axis=0, keepdims=True)
        raised = raised.astype(BF)
        grad_raised_ref[:, part] = raised
        total += dot_nt(raised, w_up[:, part])
        active = following
    hat = (hidden_ref[...].astype(F32) - vector("shift1")) * (1.0 / vector("gain1"))
    summed = normalized_pull(total * vector("gain1"), hat, scale1_ref[:, :1])
    attn = summed.astype(BF)
    grad_attn_ref[...] = attn
    weights.wait(0)
    grad_context_ref[...] = dot_nt(attn, w_out[...]).astype(BF)
    add(1, total * hat)
    add(3, total)
    add(0, attn.astype(F32))


def refine_back(sel, grad, kept, weights, layer):
    w_out, w_up, w_down, small = weights
    hidden, out, scale1, scale2, slope = kept
    length, width = grad.shape
    ff_width = w_up[0].shape[1]
    rows = pl.BlockSpec((ROWS, width), lambda n, _: (n, 0))
    lanes = pl.BlockSpec((ROWS, 128), lambda n, _: (n, 0))
    part = pl.BlockSpec((ROWS, ff_width), lambda n, _: (n, 0))
    row_shape = jax.ShapeDtypeStruct((length, width), BF)
    return pl.pallas_call(
        partial(refine_back_kernel, layer),
        name="refine_back",
        grid_spec=pltpu.PrefetchScalarGridSpec(
            num_scalar_prefetch=1,
            grid=(length // ROWS,),
            in_specs=[rows, rows, rows, lanes, lanes, part]
            + [ANY] * 6
            + [small_spec(layer, small.shape[2])],
            out_specs=[
                rows, part, rows, rows,
                pl.BlockSpec((6, width), lambda n, _: (0, 0)),
                pl.BlockSpec((1, ff_width), lambda n, _: (0, 0)),
            ],
            scratch_shapes=[
                *held_shapes(w_out, w_up, w_down),
                pltpu.SemaphoreType.DMA((3,)),
            ],
        ),
        out_shape=[
            row_shape,
            jax.ShapeDtypeStruct((length, ff_width), BF),
            row_shape,
            row_shape,
            jax.ShapeDtypeStruct((6, width), F32),
            jax.ShapeDtypeStruct((1, ff_width), F32),
        ],
        compiler_params=PARAMS,
        cost_estimate=COST,
    )(sel, grad, hidden, out, scale1, scale2, slope, *w_out, *w_up, *w_down, small)


def head_kernel(rows_ref, proj_ref, given_ref, embedded_ref, grad_proj_ref, grad_rows_ref):
    factor = math.sqrt(proj_ref.shape[0])
    columns = dot_nt(proj_ref[...], rows_ref[...])
    given = given_ref[...].astype(F32)
    inverse = lax.rsqrt(jnp.sum(columns * columns, axis=0, keepdims=True) + EPS_PROJ)
    cross = jnp.sum(columns * given, axis=0, keepdims=True)
    embedded_ref[...] = (factor * columns * inverse).astype(BF)
    grad = (factor * (given * inverse - columns * (cross * inverse * inverse * inverse))).astype(BF)
    grad_proj_ref[...] = dot(grad, rows_ref[...]).T.astype(BF)
    grad_rows_ref[...] = dot_tn(grad, proj_ref[...]).astype(BF)


def head(rows, proj, given):
    length, width = rows.shape
    cols = proj.shape[0]
    return pl.pallas_call(
        head_kernel,
        name="head",
        out_shape=[
            jax.ShapeDtypeStruct((cols, length), BF),
            jax.ShapeDtypeStruct((width, cols), BF),
            jax.ShapeDtypeStruct((length, width), BF),
        ],
        compiler_params=PARAMS,
        cost_estimate=COST,
    )(rows, proj, given)


HALF = 384
SHARDS = 8


def feed_grads_kernel(
    sel_ref, hidden_ref, raised_late_ref, raised_ref, active_ref, low_late_ref, low_ref, out_ref,
    hidden_scr, low_scr, raised_scr,
):
    step = pl.program_id(0)
    blocks = raised_ref.shape[1] // HALF
    share = hidden_ref.shape[1] // SHARDS
    late = sel_ref[1] == 1

    @pl.when(step == 0)
    def _():
        hidden_scr[...] = hidden_ref[...].T
        low_scr[...] = jnp.where(late, low_late_ref[...], low_ref[...]).T
        raised_scr[...] = jnp.where(late, raised_late_ref[...], raised_ref[...])

    @pl.when(step < 4)
    def _():
        at = pl.multiple_of(step * (2 * share), 2 * share)
        part = dot(hidden_scr[pl.ds(at, 2 * share), :], raised_scr[...]).astype(BF)
        for m in range(2):
            for n in range(blocks):
                out_ref[m, n * share : (n + 1) * share, :] = part[
                    m * share : (m + 1) * share, n * HALF : (n + 1) * HALF
                ]

    @pl.when(step >= 4)
    def _():
        rows = out_ref.shape[1]
        for m in range(2):
            part = dot(low_scr[...], active_ref[:, m * rows : (m + 1) * rows])
            out_ref[m] = part.T.astype(BF)


def feed_grads(sel, hidden, raised_late, raised, active, low_late, low):
    length, width = hidden.shape
    ff_width = active.shape[1]
    half_ff = ff_width // 2

    def late_spec(shape, wanted):
        return pl.BlockSpec(shape, lambda n, sel: (0, jnp.where(sel[1] == wanted, sel[2], 0)))

    return pl.pallas_call(
        feed_grads_kernel,
        name="feed_grads",
        grid_spec=pltpu.PrefetchScalarGridSpec(
            num_scalar_prefetch=1,
            grid=(8,),
            in_specs=[
                pl.BlockSpec((length, width), lambda n, _: (0, 0)),
                late_spec((length, half_ff), 1),
                late_spec((length, half_ff), 0),
                pl.BlockSpec((length, ff_width // 4), lambda n, _: (0, jnp.maximum(n - 4, 0))),
                late_spec((length, width // 2), 1),
                late_spec((length, width // 2), 0),
            ],
            out_specs=pl.BlockSpec(
                (2, ff_width // SHARDS, HALF), lambda n, _: (lax.rem(n, 4), n // 4, 0)
            ),
            scratch_shapes=[
                pltpu.VMEM((width, length), BF),
                pltpu.VMEM((width // 2, length), BF),
                pltpu.VMEM((length, half_ff), BF),
            ],
        ),
        out_shape=jax.ShapeDtypeStruct((SHARDS, 2 * (ff_width // SHARDS), HALF), BF),
        compiler_params=PARAMS,
        cost_estimate=COST,
    )(sel, hidden, raised_late, raised, active, low_late, low)


def attend_grads_kernel(
    sel_ref, context_ref, x_ref, attn_late_ref, attn_ref, mixed_late_ref, mixed_ref, out_ref, turned
):
    step = pl.program_id(0)
    late = sel_ref[1] == 1

    def store(cols):
        out_ref[...] = dot(turned[...], cols).astype(BF).reshape(out_ref.shape)

    @pl.when(step == 0)
    def _():
        turned[...] = context_ref[...].T
        store(jnp.where(late, attn_late_ref[...], attn_ref[...]))

    @pl.when(step == 1)
    def _():
        turned[...] = x_ref[...].T

    @pl.when(step > 0)
    def _():
        store(jnp.where(late, mixed_late_ref[0], mixed_ref[0]))


def attend_grads(sel, context, x, attn_late, attn, mixed_late, mixed):
    length, width = x.shape

    def late_spec(wanted):
        return pl.BlockSpec(
            (length, HALF), lambda n, sel: (0, jnp.where(sel[1] == wanted, sel[2], 0))
        )

    def mixed_spec(wanted):
        def at(n, sel):
            return (
                jnp.where(sel[1] == wanted, jnp.maximum(n - 1, 0), 0),
                0,
                jnp.where(sel[1] == wanted, sel[2], 0),
            )

        return pl.BlockSpec((1, length, HALF), at)

    whole = pl.BlockSpec((length, width), lambda n, _: (0, 0))
    share = width // SHARDS
    return pl.pallas_call(
        attend_grads_kernel,
        name="attend_grads",
        grid_spec=pltpu.PrefetchScalarGridSpec(
            num_scalar_prefetch=1,
            grid=(4,),
            in_specs=[whole, whole, late_spec(1), late_spec(0), mixed_spec(1), mixed_spec(0)],
            out_specs=pl.BlockSpec((SHARDS, share, HALF), lambda n, _: (0, n, 0)),
            scratch_shapes=[pltpu.VMEM((width, length), BF)],
        ),
        out_shape=jax.ShapeDtypeStruct((SHARDS, 4 * share, HALF), BF),
        compiler_params=PARAMS,
        cost_estimate=COST,
    )(sel, context, x, attn_late, attn, mixed_late, mixed)


def forward_kernel(
    layer, begin_ref, count_ref, sel_ref, x_hbm, key_code_ref, query_code_ref,
    mix_own_ref, mix_other_ref, out_own_ref, out_other_ref,
    up_own_ref, up_other_ref, down_own_ref, down_other_ref, small_ref,
    qkv_hbm, context_hbm, logsum_ref, out_hbm, hidden_hbm, scale1_ref, scale2_ref,
    active_hbm, slope_hbm,
    w_mix, w_out, w_up, w_down, x, qkv, context, hidden_rows, out_rows, active_rows, slope_rows,
    value_scr, query_scr, total_scr, weight_sems, in_sems, qkv_sems, row_sems, context_sem,
):
    pairs = [
        (mix_own_ref, mix_other_ref), (out_own_ref, out_other_ref),
        (up_own_ref, up_other_ref), (down_own_ref, down_other_ref),
    ]
    length, width = x.shape
    ff_width = w_up.shape[1]
    blocks = length // ROWS
    at = small_slices(width, ff_width)

    def vector(name):
        return small_ref[0, :, at[name]]

    def rows_of(n):
        return pl.ds(pl.multiple_of(n * ROWS, ROWS), ROWS)

    def x_copy(n):
        return pltpu.make_async_copy(x_hbm.at[rows_of(n)], x.at[rows_of(n)], in_sems.at[n])

    def qkv_copy(n):
        return pltpu.make_async_copy(
            qkv.at[:, rows_of(n)], qkv_hbm.at[:, rows_of(n)], qkv_sems.at[n]
        )

    saved = [
        (hidden_rows, hidden_hbm), (out_rows, out_hbm),
        (active_rows, active_hbm), (slope_rows, slope_hbm),
    ]

    def row_copies(n):
        return [
            pltpu.make_async_copy(rows.at[rows_of(n)], whole.at[rows_of(n)], row_sems.at[k, n])
            for k, (rows, whole) in enumerate(saved)
        ]

    weights = Held(sel_ref, layer, pairs, [w_mix, w_out, w_up, w_down], weight_sems, True)
    for n in range(blocks):
        x_copy(n).start()
    weights.start()
    weights.wait(0)

    def mix_rows(n, _):
        x_copy(n).wait()
        rows = rows_of(n)
        part = dot(x[rows, :], w_mix[...])
        qkv[0, rows, :] = ((part[:, :width] + vector("b_q")) * HEAD**-0.5).astype(BF)
        qkv[1, rows, :] = part[:, width : 2 * width].astype(BF)
        qkv[2, rows, :] = (part[:, 2 * width :] + vector("b_v")).astype(BF)
        qkv_copy(n).start()
        return 0

    lax.fori_loop(0, blocks, mix_rows, 0)
    attend_forward(
        begin_ref, count_ref, qkv, key_code_ref, query_code_ref, context, logsum_ref,
        value_scr, query_scr, total_scr,
    )
    context_copy = pltpu.make_async_copy(context, context_hbm, context_sem)
    context_copy.start()
    for n in (1, 2, 3):
        weights.wait(n)

    def refine_rows(n, _):
        rows = rows_of(n)
        summed = x[rows, :].astype(F32) + dot(context[rows, :], w_out[...]) + vector("b_out")
        hat, inverse = normalized(summed)
        hidden = hat * vector("gain1") + vector("shift1")
        scale1_ref[rows, :] = jnp.broadcast_to(inverse, (ROWS, 128))
        hidden_low = hidden.astype(BF)
        hidden_rows[rows, :] = hidden_low
        total = hidden + vector("b_down")
        parts = [slice(f, f + FB) for f in range(0, ff_width, FB)]
        raised = dot(hidden_low, w_up[:, parts[0]])
        for m, part in enumerate(parts):
            following = dot(hidden_low, w_up[:, parts[m + 1]]) if m + 1 < len(parts) else None
            active, slope = gelu_parts(raised + small_ref[0, :, part])
            active = active.astype(BF)
            active_rows[rows, part] = active
            slope_rows[rows, part] = slope.astype(BF)
            total += dot(active, w_down[part, :])
            raised = following
        hat, inverse = normalized(total)
        scale2_ref[rows, :] = jnp.broadcast_to(inverse, (ROWS, 128))
        out_rows[rows, :] = (hat * vector("gain2") + vector("shift2")).astype(BF)
        for copy in row_copies(n):
            copy.start()
        return 0

    lax.fori_loop(0, blocks, refine_rows, 0)
    context_copy.wait()
    for n in range(blocks):
        qkv_copy(n).wait()
        for copy in row_copies(n):
            copy.wait()


def layer_forward(sel, x, weights, layer, plan):
    w_qkv, w_out, w_up, w_down, small = weights
    begin, count, key_code, query_code = plan
    length, width = x.shape
    ff_width = w_up[0].shape[1]
    pairs = width // PAIR
    blocks = length // ROWS

    def whole(shape):
        return pl.BlockSpec(shape, lambda *_: (0,) * len(shape))

    row = jax.ShapeDtypeStruct((length, width), BF)
    lanes = jax.ShapeDtypeStruct((length, 128), F32)
    wide = jax.ShapeDtypeStruct((length, ff_width), BF)
    logsum_shape = (pairs * (length // QB), 2 * QB)
    qkv, context, logsum, out, hidden, scale1, scale2, active, slope = pl.pallas_call(
        partial(forward_kernel, layer),
        name="layer_forward",
        grid_spec=pltpu.PrefetchScalarGridSpec(
            num_scalar_prefetch=3,
            grid=(1,),
            in_specs=[ANY, whole(key_code.shape), whole(query_code.shape)]
            + [ANY] * 8
            + [small_spec(layer, small.shape[2])],
            out_specs=[
                ANY, ANY, whole(logsum_shape), ANY, ANY,
                whole((length, 128)), whole((length, 128)), ANY, ANY,
            ],
            scratch_shapes=[
                *held_shapes(w_qkv, w_out, w_up, w_down),
                pltpu.VMEM((length, width), BF),
                pltpu.VMEM((3, length, width), BF),
                pltpu.VMEM((length, width), BF),
                pltpu.VMEM((length, width), BF),
                pltpu.VMEM((length, width), BF),
                pltpu.VMEM((length, ff_width), BF),
                pltpu.VMEM((length, ff_width), BF),
                pltpu.VMEM((pairs, PAIR + 16, length), BF),
                pltpu.VMEM((pairs, 2 * QB, PAIR), BF),
                pltpu.VMEM((pairs, PAIR + 16, 2 * QB), F32),
                pltpu.SemaphoreType.DMA((4,)),
                pltpu.SemaphoreType.DMA((blocks,)),
                pltpu.SemaphoreType.DMA((blocks,)),
                pltpu.SemaphoreType.DMA((4, blocks)),
                pltpu.SemaphoreType.DMA,
            ],
        ),
        out_shape=[
            jax.ShapeDtypeStruct((3, length, width), BF), row,
            jax.ShapeDtypeStruct(logsum_shape, F32), row, row, lanes, lanes, wide, wide,
        ],
        compiler_params=PARAMS,
        cost_estimate=COST,
    )(begin, count, sel, x, key_code, query_code, *w_qkv, *w_out, *w_up, *w_down, small)
    return (out, (x, qkv, context, logsum, hidden, out, scale1, scale2, slope, active))


def feed_backward(sel, grad, kept, weights, layer):
    grad_low, grad_raised, grad_attn, grad_context, sums, up_sums = refine_back(
        sel, grad, kept[4:9], weights[1:], layer
    )
    return (grad_context, (grad_low, grad_raised, grad_attn), (sums, up_sums))


def mixed_backward_kernel(
    layer, begin_ref, count_ref, sel_ref, qkv_hbm, key_code_ref, query_code_ref, context_hbm,
    logsum_ref, grad_hbm, skip_hbm, mix_own_ref, mix_other_ref,
    mixed_hbm, grad_x_hbm, sums_ref,
    w_mix, qkv, context, grad, skip, key_scr, query_scr, given_scr, down_scr,
    grad_key_scr, grad_value_scr, weight_sems, in_sems, mixed_sems, row_sems,
):
    length, width = skip.shape
    blocks = length // ROWS
    weights = Held(sel_ref, layer, [(mix_own_ref, mix_other_ref)], [w_mix], weight_sems, True)
    arrays = [(qkv_hbm, qkv), (context_hbm, context), (grad_hbm, grad), (skip_hbm, skip)]
    loads = [
        pltpu.make_async_copy(whole, held, in_sems.at[n]) for n, (whole, held) in enumerate(arrays)
    ]
    for load in loads:
        load.start()
    weights.start()
    for load in loads:
        load.wait()
    attend_backward(
        begin_ref, count_ref, qkv, key_code_ref, query_code_ref, context, logsum_ref, grad,
        sums_ref, key_scr, query_scr, given_scr, down_scr, grad_key_scr, grad_value_scr,
    )
    store = pltpu.make_async_copy(qkv, mixed_hbm, mixed_sems.at[0])
    store.start()
    weights.wait(0)

    def rows_of(n):
        return pl.ds(pl.multiple_of(n * ROWS, ROWS), ROWS)

    def row_copy(n):
        return pltpu.make_async_copy(skip.at[rows_of(n)], grad_x_hbm.at[rows_of(n)], row_sems.at[n])

    def unmix_rows(n, _):
        rows = rows_of(n)
        total = skip[rows, :].astype(F32)
        for c in range(3):
            total += dot_nt(qkv[c, rows, :], w_mix[:, c * width : (c + 1) * width])
        skip[rows, :] = total.astype(BF)
        row_copy(n).start()
        return 0

    lax.fori_loop(0, blocks, unmix_rows, 0)
    store.wait()
    for n in range(blocks):
        row_copy(n).wait()


def mixed_backward(sel, grad_context, skip, kept, weights, layer, plan):
    _, qkv, context, logsum = kept[:4]
    begin, count, key_code, query_code = plan
    _, length, width = qkv.shape
    pairs = width // PAIR
    blocks = length // ROWS
    w_qkv = weights[0]

    def whole(shape):
        return pl.BlockSpec(shape, lambda *_: (0,) * len(shape))

    row = pltpu.VMEM((length, width), BF)
    return pl.pallas_call(
        partial(mixed_backward_kernel, layer),
        name="mixed_backward",
        grid_spec=pltpu.PrefetchScalarGridSpec(
            num_scalar_prefetch=3,
            grid=(1,),
            in_specs=[ANY, whole(key_code.shape), whole(query_code.shape), ANY, whole(logsum.shape)]
            + [ANY] * 4,
            out_specs=[ANY, ANY, whole((2, width))],
            scratch_shapes=[
                *held_shapes(w_qkv),
                pltpu.VMEM((3, length, width), BF),
                row, row, row,
                pltpu.VMEM((pairs, PAIR, length), BF),
                pltpu.VMEM((pairs, 2 * QB, PAIR), BF),
                pltpu.VMEM((pairs, 2 * QB, PAIR), BF),
                pltpu.VMEM((pairs, PAIR, 2 * QB), F32),
                pltpu.VMEM((length, width), F32),
                pltpu.VMEM((length, width), F32),
                pltpu.SemaphoreType.DMA((1,)),
                pltpu.SemaphoreType.DMA((4,)),
                pltpu.SemaphoreType.DMA((1,)),
                pltpu.SemaphoreType.DMA((blocks,)),
            ],
        ),
        out_shape=[
            jax.ShapeDtypeStruct((3, length, width), BF),
            jax.ShapeDtypeStruct((length, width), BF),
            jax.ShapeDtypeStruct((2, width), F32),
        ],
        compiler_params=PARAMS,
        cost_estimate=COST,
    )(begin, count, sel, qkv, key_code, query_code, context, logsum, grad_context, skip, *w_qkv)


def layer_backward(sel, grad, kept, weights, layer, plan):
    grad_context, grads, sums = feed_backward(sel, grad, kept, weights, layer)
    grad_mixed, grad_x, mix_sums = mixed_backward(
        sel, grad_context, grads[2], kept, weights, layer, plan
    )
    return (grad_x, grads + (grad_mixed,), sums + (mix_sums,))


def swap_cores(value):
    return send(value, ((0, 1), (1, 0), (2, 3), (3, 2)))


def send(value, routes):
    return lax.ppermute(value, "section", routes)


def pick_row(value, at, axis=0):
    return lax.dynamic_index_in_dim(value, at, axis, keepdims=False)


def plus(*values):
    return sum(value.astype(F32) for value in values).astype(BF)


class RowSum:
    def __init__(self, value, x_first):
        at = lax.axis_index("dp")
        self.z, self.x, self.x_first = at // 2, at % 2, x_first
        self.value = value.reshape(4, 2, *value.shape[1:])
        self.travelling = None
        self.steps = [self.cross, self.line, self.line, self.line]
        if not x_first:
            self.steps = self.steps[1:] + self.steps[:1]
        self.line_at = 0

    def cross(self):
        axis = 1 if self.x_first else 0
        other = pick_row(self.value, 1 - self.x, axis)
        arrived = lax.ppermute(other, "dp", [(n, n ^ 1) for n in range(8)])
        self.value = plus(pick_row(self.value, self.x, axis), arrived)

    def line(self):
        self.line_at += 1
        far = 4 - self.line_at
        right = pick_row(self.value, jnp.minimum(self.z + far, 3))
        left = pick_row(self.value, jnp.maximum(self.z - far, 0))
        if self.travelling is not None:
            right, left = plus(right, self.travelling[0]), plus(left, self.travelling[1])
        self.travelling = (
            lax.ppermute(right, "dp", [(n, n + 2) for n in range(6)]),
            lax.ppermute(left, "dp", [(n + 2, n) for n in range(6)]),
        )
        if self.line_at == 3:
            self.value = plus(pick_row(self.value, self.z), *self.travelling)

    def step(self):
        if self.steps:
            self.steps.pop(0)()

    def result(self):
        while self.steps:
            self.step()
        return self.value


class PlainSum:
    def __init__(self, value, blocks):
        shards = lax.axis_size("dp")
        parts, at = [], 0
        for rows in blocks:
            part = value[:, at : at + rows].reshape(shards, -1, value.shape[2])
            parts, at = parts + [part], at + rows
        whole = jnp.concatenate(parts, axis=1)
        self.value = lax.psum_scatter(whole, "dp", scatter_dimension=0, tiled=True)[0]
        self.travelling = None

    def step(self):
        pass

    def result(self):
        return self.value


def body(
    tokens_in, seg_starts, pad_mask, w_qkv, b_qv, w_attn_out, b_attn_out, ln_gain, ln_bias,
    w_up, b_up, w_down, b_down, w_proj, cotangent,
):
    section_at = lax.axis_index("section")
    core = section_at % 2
    is_late = section_at >= 2
    flip = core == 1
    quarter = tokens_in.shape[1]
    length, width = 4 * quarter, tokens_in.shape[2]
    ff_width = w_up.shape[2]
    proj_cols = w_proj.shape[1]
    shards = lax.axis_size("dp")
    share = width // shards

    def sel_for(half):
        return jnp.stack([core, section_at // 2, half]).astype(jnp.int32)

    sel_mine, sel_theirs = sel_for(core), sel_for(1 - core)

    own = pick_row(tokens_in, core)
    other = pick_row(tokens_in, 1 - core)
    straight = send(own, [(2, 0), (3, 1)])
    crossed = send(other, [(2, 1), (3, 0)])
    near = swap_cores(other)
    small = pack_small(b_qv[0], b_attn_out[0], ln_gain[0], ln_bias[0], b_up[0], b_down[0])[None]
    small_other = swap_cores(small)
    small = jnp.stack([jnp.where(flip, small_other, small), jnp.where(flip, small, small_other)])
    weights = tuple((w[0], swap_cores(w[0])) for w in (w_qkv, w_attn_out, w_up, w_down)) + (small,)
    x = jnp.concatenate(
        [
            jnp.where(flip, near, own),
            jnp.where(flip, own, near),
            jnp.where(flip, crossed, straight),
            jnp.where(flip, straight, crossed),
        ],
        axis=0,
    )

    head_own = jnp.concatenate([w_proj.T, pick_row(cotangent, core).T], axis=1)
    head_other = jnp.concatenate([w_proj.T, pick_row(cotangent, 1 - core).T], axis=1)
    head_late = send(head_other, [(2, 3), (3, 2)])
    head_straight = send(head_own, [(0, 2), (1, 3)])
    head_crossed = send(head_other, [(0, 3), (1, 2)])
    head_cols = jnp.concatenate(
        [
            jnp.where(flip, head_crossed, head_straight),
            jnp.where(flip, head_straight, head_crossed),
            jnp.where(flip, head_late, head_own),
            jnp.where(flip, head_own, head_late),
        ],
        axis=0,
    )
    proj_rows, given_rows = head_cols[:, :width], head_cols[:, width:]
    plan = attention_plan(pick_row(seg_starts, core), pick_row(pad_mask, core))

    def both_forward(rows):
        middle, kept_even = layer_forward(sel_mine, rows, weights, 0, plan)
        last, kept_odd = layer_forward(sel_mine, middle, weights, 1, plan)
        return (last, kept_even, kept_odd)

    early, kept_even, kept_odd = both_forward(x)
    hopped = send(early, [(0, 2), (1, 3)])
    hopped, proj_rows, given_rows = lax.optimization_barrier((hopped, proj_rows, given_rows))

    def late_turn(rows, *_):
        last, kept_even, kept_odd = both_forward(rows)
        embedded, grad_proj, grad = head(last, proj_rows, given_rows)
        grad, grads_odd, sums_odd = layer_backward(sel_mine, grad, kept_odd, weights, 1, plan)
        grad, grads_even, sums_even = layer_backward(sel_mine, grad, kept_even, weights, 0, plan)
        return (
            kept_even, kept_odd, embedded, grad_proj, grad,
            grads_odd, sums_odd, grads_even, sums_even,
        )

    def early_turn(rows, kept_even, kept_odd):
        row, ff = jnp.zeros((length, width), BF), jnp.zeros((length, ff_width), BF)
        grads = (row, ff, row, jnp.zeros((3, length, width), BF))
        sums = (
            jnp.zeros((6, width), F32),
            jnp.zeros((1, ff_width), F32),
            jnp.zeros((2, width), F32),
        )
        return (
            kept_even, kept_odd, jnp.zeros((4 * proj_cols, length), BF),
            jnp.zeros((width, 4 * proj_cols), BF), row, grads, sums, grads, sums,
        )

    (
        kept_even, kept_odd, embedded, grad_proj, grad_mid,
        late_odd, late_sums_odd, late_even, late_sums_even,
    ) = lax.cond(is_late, late_turn, early_turn, hopped, kept_even, kept_odd)

    grad = send(grad_mid, [(2, 0), (3, 1)])
    embedded_cols = embedded.reshape(4, proj_cols, length)

    rows_of_one = width // SHARDS
    attend_blocks = (rows_of_one,) * 4
    feed_blocks = (rows_of_one,) * (ff_width // (2 * HALF)) + (ff_width // SHARDS,)

    def row_sum(value, blocks):
        return RowSum(value, True) if shards == SHARDS else PlainSum(value, blocks)

    def feed_sum(kept, late, now):
        args = (kept[4], late[1], now[1], kept[9], late[0], now[0])
        arrived = swap_cores(feed_grads(sel_theirs, *args))
        return row_sum(plus(feed_grads(sel_mine, *args), arrived), feed_blocks)

    def attend_parts(kept, late, now, mixed):
        args = (kept[2], kept[0], late[2], now[2], late[3], mixed)
        return (attend_grads(sel_theirs, *args), attend_grads(sel_mine, *args))

    def merged(late_sums, sums):
        return tuple(jnp.where(is_late, a, b) for a, b in zip(late_sums, sums))

    def tie(*values):
        return lax.optimization_barrier(values)

    grad_context, grads_odd, sums_odd = feed_backward(sel_mine, grad, kept_odd, weights, 1)
    feed_odd = feed_sum(kept_odd, late_odd, grads_odd)
    grad_context, feed_odd.value = tie(grad_context, feed_odd.value)
    feed_odd.step()
    mixed_odd, grad, mix_sums = mixed_backward(
        sel_mine, grad_context, grads_odd[2], kept_odd, weights, 1, plan
    )
    sums_odd = merged(late_sums_odd, sums_odd + (mix_sums,))
    theirs, mine = attend_parts(kept_odd, late_odd, grads_odd, mixed_odd)
    attend_odd = row_sum(plus(mine, swap_cores(theirs)), attend_blocks)
    grad, attend_odd.value, feed_odd.value = tie(grad, attend_odd.value, feed_odd.value)
    feed_odd.step()
    attend_odd.step()

    grad_context, grads_even, sums_even = feed_backward(sel_mine, grad, kept_even, weights, 0)
    args = (kept_even[4], late_even[1], grads_even[1], kept_even[9], late_even[0], grads_even[0])
    args, feed_odd.travelling, attend_odd.value = tie(
        args, feed_odd.travelling, attend_odd.value
    )
    feed_odd.step()
    attend_odd.step()
    theirs = feed_grads(sel_theirs, *args)
    arrived = swap_cores(theirs)
    args, theirs, feed_odd.travelling = tie(args, theirs, feed_odd.travelling)
    feed_odd.step()
    feed_even = row_sum(plus(feed_grads(sel_mine, *args), arrived), feed_blocks)
    grad_context, feed_even.value, feed_odd.value, attend_odd.travelling = tie(
        grad_context, feed_even.value, feed_odd.value, attend_odd.travelling
    )
    feed_even.step()
    attend_odd.step()
    mixed_even, grad, mix_sums = mixed_backward(
        sel_mine, grad_context, grads_even[2], kept_even, weights, 0, plan
    )
    sums_even = merged(late_sums_even, sums_even + (mix_sums,))
    args = (kept_even[2], kept_even[0], late_even[2], grads_even[2], late_even[3], mixed_even)
    args, attend_odd.travelling, feed_even.value = tie(
        args, attend_odd.travelling, feed_even.value
    )
    feed_even.step()
    attend_odd.step()
    theirs = attend_grads(sel_theirs, *args)
    arrived = swap_cores(theirs)
    args, theirs, feed_even.travelling = tie(args, theirs, feed_even.travelling)
    feed_even.step()
    mine = attend_grads(sel_mine, *args)

    def small_rows(sums):
        sums, up_sums, mix_sums = sums
        rows = [up_sums[0], mix_sums.reshape(-1)]
        rows += [sums[n] for n in range(6)]
        return jnp.concatenate([row.reshape(shards, -1) for row in rows], axis=1)

    extras = jnp.concatenate(
        [small_rows(sums_even), small_rows(sums_odd), grad_proj.reshape(shards, -1).astype(F32)],
        axis=1,
    )
    small_width = 12 * share
    lines = -(-extras.shape[1] // HALF)
    lines = -(-lines // 16) * 16
    extras = jnp.pad(extras, ((0, 0), (0, lines * HALF - extras.shape[1])))
    extras = extras.reshape(shards, lines, HALF).astype(BF)
    extras = plus(extras, swap_cores(extras))
    attend_even = plus(mine, arrived)
    if shards == SHARDS:
        tail = jnp.concatenate([attend_even, extras], axis=1)
        cut = tail.shape[1] // 32 * 16
        tails = [RowSum(tail[:, :cut], True), RowSum(tail[:, cut:], False)]
        for n in range(4):
            for part in tails:
                part.step()
            feed_even.step()
        feed_odd, attend_odd, feed_even = [
            part.result() for part in (feed_odd, attend_odd, feed_even)
        ]
        tail = jnp.concatenate([part.result() for part in tails], axis=0)
        attend_even, extras = tail[: 4 * share], tail[4 * share :]
    else:
        feed_odd, attend_odd, feed_even = [
            part.result() for part in (feed_odd, attend_odd, feed_even)
        ]
        attend_even = PlainSum(attend_even, attend_blocks).result()
        extras = lax.psum_scatter(extras, "dp", scatter_dimension=0, tiled=True)[0]

    routes_odd, routes_even = ((0, 1), (2, 3)), ((1, 0), (3, 2))

    def halves(even, odd):
        arrived = jnp.where(flip, send(odd, routes_odd), send(even, routes_even))
        mine = jnp.where(flip, odd, even)
        return (jnp.where(flip, arrived, mine), jnp.where(flip, mine, arrived))

    blocks = ff_width // (2 * HALF)
    feed_halves = halves(feed_even, feed_odd)
    attend_halves = halves(attend_even, attend_odd)

    def columns(pair, first, count):
        parts = [part[n * share : (n + 1) * share] for part in pair for n in range(first, first + count)]
        return jnp.concatenate(parts, axis=1).astype(F32)

    grad_w_up = columns(feed_halves, 0, blocks)[None]
    grad_w_down = jnp.concatenate([part[blocks * share :] for part in feed_halves], axis=1)
    grad_w_down = grad_w_down.astype(F32)[None]
    grad_w_out = columns(attend_halves, 0, 1)[None]
    grad_w_qkv = jnp.concatenate([columns(attend_halves, 1 + c, 1) for c in range(3)], axis=1)[None]

    extras = extras.reshape(-1).astype(F32)
    small_mine = jnp.where(flip, extras[small_width : 2 * small_width], extras[:small_width])
    at = ff_width // shards
    grad_b_up = small_mine[None, :at]
    grad_b_qv = small_mine[None, at : at + 2 * share]
    rows = small_mine[at + 2 * share :].reshape(6, share)
    grad_proj = extras[2 * small_width : 2 * small_width + share * 4 * proj_cols]
    grad_proj = grad_proj.reshape(share, 4 * proj_cols).astype(BF)
    grad_proj = jnp.where(is_late, grad_proj, send(grad_proj, [(2, 0), (3, 1)])).astype(F32)
    grad_w_proj = lax.dynamic_slice_in_dim(grad_proj, section_at * proj_cols, proj_cols, 1)

    straight_cols = send(pick_row(embedded_cols, core), [(2, 0), (3, 1)])
    crossed_cols = send(pick_row(embedded_cols, 1 - core), [(2, 1), (3, 0)])
    near_cols = swap_cores(pick_row(embedded_cols, 3 - core))
    own_cols = jnp.where(is_late, pick_row(embedded_cols, section_at), straight_cols)
    other_cols = jnp.where(is_late, near_cols, crossed_cols)
    embedded_out = jnp.stack(
        [jnp.where(flip, other_cols, own_cols).T, jnp.where(flip, own_cols, other_cols).T]
    )

    quarters = grad.reshape(4, quarter, width)
    straight_grad = send(pick_row(quarters, 2 + core), [(0, 2), (1, 3)])
    crossed_grad = send(pick_row(quarters, 3 - core), [(0, 3), (1, 2)])
    near_grad = swap_cores(pick_row(quarters, 1 - core))
    mine = jnp.where(is_late, straight_grad, pick_row(quarters, core))
    others = jnp.where(is_late, crossed_grad, near_grad)
    grad_in = jnp.stack(
        [jnp.where(flip, others, mine), jnp.where(flip, mine, others)]
    ).astype(F32)

    return (
        embedded_out,
        grad_in,
        grad_w_qkv,
        grad_b_qv,
        grad_w_out,
        rows[0][None],
        rows[1:3][None],
        rows[3:5][None],
        grad_w_up,
        grad_b_up,
        grad_w_down,
        rows[5][None],
        grad_w_proj,
    )


def solution(mesh):
    in_specs = (
        P("dp", "section", None),
        P("dp", None),
        P("dp", None),
        P("section", None, None),
        P("section", None),
        P("section", None, None),
        P("section", None),
        P("section", None, None),
        P("section", None, None),
        P("section", None, None),
        P("section", None),
        P("section", None, None),
        P("section", None),
        P(None, "section"),
        P("dp", None, "section"),
    )
    out_specs = (
        P("dp", None, "section"),
        P("dp", "section", None),
        P("section", "dp", None),
        P("section", "dp"),
        P("section", "dp", None),
        P("section", "dp"),
        P("section", None, "dp"),
        P("section", None, "dp"),
        P("section", "dp", None),
        P("section", "dp"),
        P("section", "dp", None),
        P("section", "dp"),
        P("dp", "section"),
    )
    return jax.shard_map(body, mesh=mesh, in_specs=in_specs, out_specs=out_specs, check_vma=False)
```

```python
from functools import partial
import math

import jax
import jax.numpy as jnp
from jax import lax
from jax.experimental import pallas as pl
from jax.experimental.pallas import tpu as pltpu
from jax.sharding import PartitionSpec as P

HEAD = 64
PAIR = 2 * HEAD
QB = 128
KB = 512
EPS_NORM = 1e-05
EPS_PROJ = 1e-06
NEG_FILL = -1e30
PARAMS = pltpu.CompilerParams(vmem_limit_bytes=60 * 1024 * 1024)


def cost(micros):
    return pl.CostEstimate(flops=int(micros * 1e9), bytes_accessed=1024, transcendentals=0)


BF = jnp.bfloat16
F32 = jnp.float32

NT = (((1,), (1,)), ((), ()))
TN = (((0,), (0,)), ((), ()))


def dot(a, b):
    return jnp.dot(a, b, preferred_element_type=F32)


def dot_nt(a, b):
    return lax.dot_general(a, b, NT, preferred_element_type=F32)


def dot_tn(a, b):
    return lax.dot_general(a, b, TN, preferred_element_type=F32)


def pack_small(b_qv, b_out, gains, shifts, b_up, b_down):
    return jnp.concatenate(
        [b_up, b_qv, b_out, gains[0], gains[1], shifts[0], shifts[1], b_down]
    )


def small_spec(layer, width):
    return pl.BlockSpec((1, 1, width), lambda *_: (layer, 0, 0))


def attention_plan(starts, real_flags):
    length = real_flags.shape[0]
    places = jnp.arange(length, dtype=jnp.int32)
    segment = jnp.sum((starts[None, :] <= places[:, None]).astype(jnp.int32), axis=1)
    key_code = jnp.where(real_flags == 1, segment, -1).astype(F32)
    key_code = jnp.broadcast_to(key_code[:, None], (length, PAIR))
    query_code = segment.astype(F32).reshape(length // QB, QB)
    first = jnp.arange(length // QB, dtype=jnp.int32) * QB
    low = jnp.max(jnp.where(starts[None, :] <= first[:, None], starts[None, :], 0), axis=1)
    high = jnp.min(
        jnp.where(starts[None, :] > first[:, None] + (QB - 1), starts[None, :], length), axis=1
    )
    begin = (low // QB) * QB
    count = (high - begin + KB - 1) // KB
    begin = jnp.minimum(begin, length - KB * count)
    return (begin, count, key_code, query_code)


def pair_mask(rows):
    return lax.broadcasted_iota(jnp.int32, (rows, PAIR), 1) < HEAD


def stacked_heads(block):
    first = pair_mask(block.shape[0])
    zero = jnp.zeros_like(block)
    return jnp.concatenate([jnp.where(first, block, zero), jnp.where(first, zero, block)], axis=0)


def block_bias(key_code, query_code, key_at, query_at):
    keys = lax.broadcasted_iota(jnp.int32, (KB, QB), 0) + (key_at - query_at)
    same = keys == lax.broadcasted_iota(jnp.int32, (KB, QB), 1)
    bias = jnp.where((key_code == query_code) | same, 0.0, NEG_FILL)
    return jnp.concatenate([bias, bias], axis=1)


def top_rows(values, op):
    folded = values.reshape(values.shape[0] // 8, 8, values.shape[1])
    return op(folded, axis=0)


def unstack_heads(flat):
    rows = lax.broadcasted_iota(jnp.int32, (PAIR, QB), 0)
    return jnp.where(rows < HEAD, flat[:PAIR, :QB], flat[:PAIR, QB:]).T


def attend_forward(
    begin_ref, count_ref, qkv_ref, key_code_ref, query_code_ref, out_ref, logsum_ref,
    value_scr, query_scr, total_scr,
):
    length = qkv_ref.shape[1]
    pairs = qkv_ref.shape[2] // PAIR
    every = range(pairs)
    cols = [slice(p * PAIR, (p + 1) * PAIR) for p in every]
    for p in every:
        value_scr[p, :PAIR, :] = qkv_ref[2, :, cols[p]].T
        value_scr[p, PAIR:, :] = jnp.ones((value_scr.shape[1] - PAIR, length), BF)

    def one_query_block(i, _):
        query_at = pl.multiple_of(i * QB, QB)
        begin, count = begin_ref[i], count_ref[i]
        query_code = query_code_ref[pl.ds(i, 1), :]
        for p in every:
            query_scr[p] = stacked_heads(qkv_ref[0, pl.ds(query_at, QB), cols[p]])
        total_scr[...] = jnp.zeros_like(total_scr)

        def one_key_block(j, tops):
            key_at = pl.multiple_of(begin + j * KB, QB)
            rows = pl.ds(key_at, KB)
            bias = block_bias(key_code_ref[rows, :], query_code, key_at, query_at)
            scores = [dot_nt(qkv_ref[1, rows, cols[p]], query_scr[p]) + bias for p in every]
            fresh = [
                jnp.maximum(tops[p], jnp.max(scores[p], axis=0, keepdims=True)) for p in every
            ]
            probs = [jnp.exp(scores[p] - fresh[p]).astype(BF) for p in every]
            for p in every:
                total_scr[p] = total_scr[p] * jnp.exp(tops[p] - fresh[p]) + dot(
                    value_scr[p, :, rows], probs[p]
                )
            return tuple(fresh)

        tops = lax.fori_loop(
            0, count, one_key_block, tuple(jnp.full((1, 2 * QB), 2 * NEG_FILL, F32) for _ in every)
        )
        for p in every:
            weight = total_scr[p, PAIR : PAIR + 1, :]
            logsum_ref[pl.ds(p * (length // QB) + i, 1), :] = tops[p] + jnp.log(weight)
            out_ref[pl.ds(query_at, QB), cols[p]] = unstack_heads(
                total_scr[p, :PAIR, :] * (1.0 / weight)
            ).astype(BF)
        return 0

    lax.fori_loop(0, length // QB, one_query_block, 0)


def attend_backward(
    begin_ref, count_ref, qkv, key_code_ref, query_code_ref, context, logsum_ref, grad, sums_ref,
    key_scr, query_scr, given_scr, down_scr, grad_key_scr, grad_value_scr,
):
    length = qkv.shape[1]
    pairs = qkv.shape[2] // PAIR
    every = range(pairs)
    blocks = length // QB
    cols = [slice(p * PAIR, (p + 1) * PAIR) for p in every]
    for p in every:
        key_scr[p] = qkv[1, :, cols[p]].T
    grad_key_scr[...] = jnp.zeros_like(grad_key_scr)
    grad_value_scr[...] = jnp.zeros_like(grad_value_scr)
    sums_ref[...] = jnp.zeros_like(sums_ref)

    def one_query_block(i, _):
        query_at = pl.multiple_of(i * QB, QB)
        queries = pl.ds(query_at, QB)
        begin, count = begin_ref[i], count_ref[i]
        query_code = query_code_ref[pl.ds(i, 1), :]
        inner, logsum = [], []
        for p in every:
            query_scr[p] = stacked_heads(qkv[0, queries, cols[p]])
            given = grad[queries, cols[p]]
            given_scr[p] = stacked_heads(given)
            both = (given.astype(F32) * context[queries, cols[p]].astype(F32)).T
            inner.append(
                jnp.concatenate(
                    [
                        jnp.sum(both[:HEAD], axis=0, keepdims=True),
                        jnp.sum(both[HEAD:], axis=0, keepdims=True),
                    ],
                    axis=1,
                )
            )
            logsum.append(logsum_ref[pl.ds(p * blocks + i, 1), :])
        down_scr[...] = jnp.zeros_like(down_scr)

        def one_key_block(j, _):
            key_at = pl.multiple_of(begin + j * KB, QB)
            rows = pl.ds(key_at, KB)
            bias = block_bias(key_code_ref[rows, :], query_code, key_at, query_at)
            parts = [dot_nt(qkv[1, rows, cols[p]], query_scr[p]) + bias for p in every]
            grads = [dot_nt(qkv[2, rows, cols[p]], given_scr[p]) - inner[p] for p in every]
            probs = [jnp.exp(parts[p] - logsum[p]) for p in every]
            scores = [(probs[p] * grads[p]).astype(BF) for p in every]
            probs = [probs[p].astype(BF) for p in every]
            for p in every:
                grad_value_scr[rows, cols[p]] += dot(probs[p], given_scr[p])
            for p in every:
                grad_key_scr[rows, cols[p]] += dot(scores[p], query_scr[p])
            for p in every:
                down_scr[p] += dot(key_scr[p, :, rows], scores[p])
            return 0

        lax.fori_loop(0, count, one_key_block, 0)
        for p in every:
            grad_query = (unstack_heads(down_scr[p]) * (HEAD**-0.5)).astype(BF)
            qkv[0, queries, cols[p]] = grad_query
            sums_ref[0:1, cols[p]] += jnp.sum(grad_query.astype(F32), axis=0, keepdims=True)
        return 0

    lax.fori_loop(0, blocks, one_query_block, 0)
    qkv[1] = grad_key_scr[...].astype(BF)
    grad_value = grad_value_scr[...].astype(BF)
    qkv[2] = grad_value
    sums_ref[1:2, :] = jnp.sum(grad_value.astype(F32), axis=0, keepdims=True)


ANY = pl.BlockSpec(memory_space=pl.ANY)
ROWS = 256


class Held:
    def __init__(self, sel_ref, layer, pairs, held, sems, first=None):
        self.own = sel_ref[0] == layer
        self.items = list(zip(pairs, held, range(len(held))))
        self.sems = sems
        self.first = pl.program_id(0) == 0 if first is None else first

    def start(self):
        for pair, held, n in self.items:
            for wanted, source in zip((self.own, jnp.logical_not(self.own)), pair):

                @pl.when(self.first & wanted)
                def _():
                    pltpu.make_async_copy(source, held, self.sems.at[n]).start()

    def wait(self, n):
        pair, held, _ = self.items[n]

        @pl.when(self.first)
        def _():
            pltpu.make_async_copy(pair[0], held, self.sems.at[n]).wait()


def held_shapes(*weights):
    return [pltpu.VMEM(own.shape, own.dtype) for own, _ in weights]


def normalized(values):
    centred = values - jnp.mean(values, axis=-1, keepdims=True)
    inverse = lax.rsqrt(jnp.mean(centred * centred, axis=-1, keepdims=True) + EPS_NORM)
    return (centred * inverse, inverse)


def normalized_pull(grad_hat, hat, inverse):
    return inverse * (
        grad_hat
        - jnp.mean(grad_hat, axis=-1, keepdims=True)
        - hat * jnp.mean(grad_hat * hat, axis=-1, keepdims=True)
    )


ERF = (0.254829592, -0.284496736, 1.421413741, -1.453152027, 1.061405429)
ERF_SLOPE = 0.3275911


def gelu_parts(x):
    t = pl.reciprocal(1.0 + (ERF_SLOPE * math.sqrt(0.5)) * jnp.abs(x), approx=True)
    bell = jnp.exp(-0.5 * (x * x))
    tail = 0.5 * ERF[4]
    for term in ERF[3::-1]:
        tail = tail * t + 0.5 * term
    tail = tail * t * bell
    below = jnp.where(x >= 0, 1.0 - tail, tail)
    return (x * below, below + x * bell * (1.0 / math.sqrt(2.0 * math.pi)))


FB = 1024


def small_slices(width, ff_width):
    names = ("b_q", "b_v", "b_out", "gain1", "gain2", "shift1", "shift2", "b_down")
    at = {"b_up": slice(0, ff_width)}
    for n, name in enumerate(names):
        at[name] = slice(ff_width + n * width, ff_width + (n + 1) * width)
    return at


def refine_back_kernel(
    layer, sel_ref, grad_ref, hidden_ref, out_ref, scale1_ref, scale2_ref, slope_ref,
    out_own_ref, out_other_ref, up_own_ref, up_other_ref, down_own_ref, down_other_ref, small_ref,
    grad_low_ref, grad_raised_ref, grad_attn_ref, grad_context_ref, sums_ref, up_sums_ref,
    w_out, w_up, w_down, sems,
):
    pairs = [(out_own_ref, out_other_ref), (up_own_ref, up_other_ref), (down_own_ref, down_other_ref)]
    weights = Held(sel_ref, layer, pairs, [w_out, w_up, w_down], sems)
    weights.start()
    rows, width = grad_ref.shape
    ff_width = slope_ref.shape[1]
    at = small_slices(width, ff_width)

    @pl.when(pl.program_id(0) == 0)
    def _():
        sums_ref[...] = jnp.zeros_like(sums_ref)
        up_sums_ref[...] = jnp.zeros_like(up_sums_ref)

    def vector(name):
        return small_ref[0, :, at[name]]

    def add(row, values):
        sums_ref[row : row + 1, :] += jnp.sum(values, axis=0, keepdims=True)

    grad = grad_ref[...].astype(F32)
    hat = (out_ref[...].astype(F32) - vector("shift2")) * (1.0 / vector("gain2"))
    joined = normalized_pull(grad * vector("gain2"), hat, scale2_ref[:, :1])
    low = joined.astype(BF)
    grad_low_ref[...] = low
    add(2, grad * hat)
    add(4, grad)
    add(5, low.astype(F32))
    weights.wait(2)
    weights.wait(1)
    total = joined
    parts = [slice(f, f + FB) for f in range(0, ff_width, FB)]
    active = dot_nt(low, w_down[parts[0], :])
    for n, part in enumerate(parts):
        following = dot_nt(low, w_down[parts[n + 1], :]) if n + 1 < len(parts) else None
        raised = active * slope_ref[:, part].astype(F32)
        up_sums_ref[:, part] += jnp.sum(raised, axis=0, keepdims=True)
        raised = raised.astype(BF)
        grad_raised_ref[:, part] = raised
        total += dot_nt(raised, w_up[:, part])
        active = following
    hat = (hidden_ref[...].astype(F32) - vector("shift1")) * (1.0 / vector("gain1"))
    summed = normalized_pull(total * vector("gain1"), hat, scale1_ref[:, :1])
    attn = summed.astype(BF)
    grad_attn_ref[...] = attn
    weights.wait(0)
    grad_context_ref[...] = dot_nt(attn, w_out[...]).astype(BF)
    add(1, total * hat)
    add(3, total)
    add(0, attn.astype(F32))


def refine_back(sel, grad, kept, weights, layer):
    w_out, w_up, w_down, small = weights
    hidden, out, scale1, scale2, slope = kept
    length, width = grad.shape
    ff_width = w_up[0].shape[1]
    rows = pl.BlockSpec((ROWS, width), lambda n, _: (n, 0))
    lanes = pl.BlockSpec((ROWS, 128), lambda n, _: (n, 0))
    part = pl.BlockSpec((ROWS, ff_width), lambda n, _: (n, 0))
    row_shape = jax.ShapeDtypeStruct((length, width), BF)
    return pl.pallas_call(
        partial(refine_back_kernel, layer),
        name="refine_back",
        grid_spec=pltpu.PrefetchScalarGridSpec(
            num_scalar_prefetch=1,
            grid=(length // ROWS,),
            in_specs=[rows, rows, rows, lanes, lanes, part]
            + [ANY] * 6
            + [small_spec(layer, small.shape[2])],
            out_specs=[
                rows, part, rows, rows,
                pl.BlockSpec((6, width), lambda n, _: (0, 0)),
                pl.BlockSpec((1, ff_width), lambda n, _: (0, 0)),
            ],
            scratch_shapes=[
                *held_shapes(w_out, w_up, w_down),
                pltpu.SemaphoreType.DMA((3,)),
            ],
        ),
        out_shape=[
            row_shape,
            jax.ShapeDtypeStruct((length, ff_width), BF),
            row_shape,
            row_shape,
            jax.ShapeDtypeStruct((6, width), F32),
            jax.ShapeDtypeStruct((1, ff_width), F32),
        ],
        compiler_params=PARAMS,
        cost_estimate=cost(24),
    )(sel, grad, hidden, out, scale1, scale2, slope, *w_out, *w_up, *w_down, small)


def head_kernel(rows_ref, proj_ref, given_ref, embedded_ref, grad_proj_ref, grad_rows_ref):
    factor = math.sqrt(proj_ref.shape[0])
    columns = dot_nt(proj_ref[...], rows_ref[...])
    given = given_ref[...].astype(F32)
    inverse = lax.rsqrt(jnp.sum(columns * columns, axis=0, keepdims=True) + EPS_PROJ)
    cross = jnp.sum(columns * given, axis=0, keepdims=True)
    embedded_ref[...] = (factor * columns * inverse).astype(BF)
    grad = (factor * (given * inverse - columns * (cross * inverse * inverse * inverse))).astype(BF)
    grad_proj_ref[...] = dot(grad, rows_ref[...]).T.astype(BF)
    grad_rows_ref[...] = dot_tn(grad, proj_ref[...]).astype(BF)


def head(rows, proj, given):
    length, width = rows.shape
    cols = proj.shape[0]
    return pl.pallas_call(
        head_kernel,
        name="head",
        out_shape=[
            jax.ShapeDtypeStruct((cols, length), BF),
            jax.ShapeDtypeStruct((width, cols), BF),
            jax.ShapeDtypeStruct((length, width), BF),
        ],
        compiler_params=PARAMS,
        cost_estimate=cost(6),
    )(rows, proj, given)


HALF = 384
SHARDS = 8


def feed_grads_kernel(
    sel_ref, hidden_ref, raised_late_ref, raised_ref, active_ref, low_late_ref, low_ref, out_ref
):
    step = pl.program_id(0)
    shards, rows, _ = out_ref.shape
    blocks = raised_ref.shape[1] // HALF
    share = rows // blocks
    late = sel_ref[1] == 1

    def up(raised):
        part = dot_tn(hidden_ref[...], raised).astype(BF)
        for m in range(shards):
            for n in range(blocks):
                out_ref[m, n * share : (n + 1) * share, :] = part[
                    m * share : (m + 1) * share, n * HALF : (n + 1) * HALF
                ]

    def down(low):
        for m in range(shards):
            out_ref[m] = dot_tn(active_ref[:, m * rows : (m + 1) * rows], low).astype(BF)

    for wanted, raised_now, low_now in (
        (late, raised_late_ref, low_late_ref),
        (jnp.logical_not(late), raised_ref, low_ref),
    ):

        @pl.when(wanted & (step < 2))
        def _():
            up(raised_now[...])

        @pl.when(wanted & (step >= 2))
        def _():
            down(low_now[...])


def feed_grads(sel, hidden, raised_late, raised, active, low_late, low):
    length, width = hidden.shape
    ff_width = active.shape[1]
    half_ff = ff_width // 2

    def late_spec(shape, wanted):
        return pl.BlockSpec(shape, lambda n, sel: (0, jnp.where(sel[1] == wanted, sel[2], 0)))

    return pl.pallas_call(
        feed_grads_kernel,
        name="feed_grads",
        grid_spec=pltpu.PrefetchScalarGridSpec(
            num_scalar_prefetch=1,
            grid=(4,),
            in_specs=[
                pl.BlockSpec((length, width // 2), lambda n, _: (0, jnp.minimum(n, 1))),
                late_spec((length, half_ff), 1),
                late_spec((length, half_ff), 0),
                pl.BlockSpec((length, ff_width // 2), lambda n, _: (0, jnp.maximum(n - 2, 0))),
                late_spec((length, width // 2), 1),
                late_spec((length, width // 2), 0),
            ],
            out_specs=pl.BlockSpec(
                (SHARDS // 2, ff_width // SHARDS, HALF), lambda n, _: (lax.rem(n, 2), n // 2, 0)
            ),
        ),
        out_shape=jax.ShapeDtypeStruct((SHARDS, 2 * (ff_width // SHARDS), HALF), BF),
        compiler_params=PARAMS,
        cost_estimate=cost(12),
    )(sel, hidden, raised_late, raised, active, low_late, low)


def attend_grads_kernel(
    sel_ref, context_ref, x_ref, attn_late_ref, attn_ref, mixed_late_ref, mixed_ref, out_ref
):
    step = pl.program_id(0)
    late = sel_ref[1] == 1

    for wanted, attn_now, mixed_now in (
        (late, attn_late_ref, mixed_late_ref),
        (jnp.logical_not(late), attn_ref, mixed_ref),
    ):

        @pl.when(wanted & (step == 0))
        def _():
            part = dot_tn(context_ref[...], attn_now[...]).astype(BF)
            out_ref[...] = part.reshape(out_ref.shape)

        @pl.when(wanted & (step > 0))
        def _():
            part = dot_tn(x_ref[...], mixed_now[0]).astype(BF)
            out_ref[...] = part.reshape(out_ref.shape)


def attend_grads(sel, context, x, attn_late, attn, mixed_late, mixed):
    length, width = x.shape

    def late_spec(wanted):
        return pl.BlockSpec(
            (length, HALF), lambda n, sel: (0, jnp.where(sel[1] == wanted, sel[2], 0))
        )

    def mixed_spec(wanted):
        def at(n, sel):
            return (
                jnp.where(sel[1] == wanted, jnp.maximum(n - 1, 0), 0),
                0,
                jnp.where(sel[1] == wanted, sel[2], 0),
            )

        return pl.BlockSpec((1, length, HALF), at)

    whole = pl.BlockSpec((length, width), lambda n, _: (0, 0))
    share = width // SHARDS
    return pl.pallas_call(
        attend_grads_kernel,
        name="attend_grads",
        grid_spec=pltpu.PrefetchScalarGridSpec(
            num_scalar_prefetch=1,
            grid=(4,),
            in_specs=[whole, whole, late_spec(1), late_spec(0), mixed_spec(1), mixed_spec(0)],
            out_specs=pl.BlockSpec((SHARDS, share, HALF), lambda n, _: (0, n, 0)),
        ),
        out_shape=jax.ShapeDtypeStruct((SHARDS, 4 * share, HALF), BF),
        compiler_params=PARAMS,
        cost_estimate=cost(8),
    )(sel, context, x, attn_late, attn, mixed_late, mixed)


def forward_kernel(
    layer, begin_ref, count_ref, sel_ref, x_hbm, key_code_ref, query_code_ref,
    mix_own_ref, mix_other_ref, out_own_ref, out_other_ref,
    up_own_ref, up_other_ref, down_own_ref, down_other_ref, small_ref,
    qkv_hbm, context_hbm, logsum_ref, out_hbm, hidden_hbm, scale1_ref, scale2_ref,
    active_hbm, slope_hbm,
    w_mix, w_out, w_up, w_down, x, qkv, context, hidden_rows, out_rows, active_rows, slope_rows,
    value_scr, query_scr, total_scr, weight_sems, in_sems, qkv_sems, row_sems, context_sem,
):
    pairs = [
        (mix_own_ref, mix_other_ref), (out_own_ref, out_other_ref),
        (up_own_ref, up_other_ref), (down_own_ref, down_other_ref),
    ]
    length, width = x.shape
    ff_width = w_up.shape[1]
    blocks = length // ROWS
    at = small_slices(width, ff_width)

    def vector(name):
        return small_ref[0, :, at[name]]

    def rows_of(n):
        return pl.ds(pl.multiple_of(n * ROWS, ROWS), ROWS)

    def x_copy(n):
        return pltpu.make_async_copy(x_hbm.at[rows_of(n)], x.at[rows_of(n)], in_sems.at[n])

    def qkv_copy(n):
        return pltpu.make_async_copy(
            qkv.at[:, rows_of(n)], qkv_hbm.at[:, rows_of(n)], qkv_sems.at[n]
        )

    saved = [
        (hidden_rows, hidden_hbm), (out_rows, out_hbm),
        (active_rows, active_hbm), (slope_rows, slope_hbm),
    ]

    def row_copies(n):
        return [
            pltpu.make_async_copy(rows.at[rows_of(n)], whole.at[rows_of(n)], row_sems.at[k, n])
            for k, (rows, whole) in enumerate(saved)
        ]

    weights = Held(sel_ref, layer, pairs, [w_mix, w_out, w_up, w_down], weight_sems, True)
    for n in range(blocks):
        x_copy(n).start()
    weights.start()
    weights.wait(0)

    def mix_rows(n, _):
        x_copy(n).wait()
        rows = rows_of(n)
        part = dot(x[rows, :], w_mix[...])
        qkv[0, rows, :] = ((part[:, :width] + vector("b_q")) * HEAD**-0.5).astype(BF)
        qkv[1, rows, :] = part[:, width : 2 * width].astype(BF)
        qkv[2, rows, :] = (part[:, 2 * width :] + vector("b_v")).astype(BF)
        qkv_copy(n).start()
        return 0

    lax.fori_loop(0, blocks, mix_rows, 0)
    attend_forward(
        begin_ref, count_ref, qkv, key_code_ref, query_code_ref, context, logsum_ref,
        value_scr, query_scr, total_scr,
    )
    context_copy = pltpu.make_async_copy(context, context_hbm, context_sem)
    context_copy.start()
    for n in (1, 2, 3):
        weights.wait(n)

    def refine_rows(n, _):
        rows = rows_of(n)
        summed = x[rows, :].astype(F32) + dot(context[rows, :], w_out[...]) + vector("b_out")
        hat, inverse = normalized(summed)
        hidden = hat * vector("gain1") + vector("shift1")
        scale1_ref[rows, :] = jnp.broadcast_to(inverse, (ROWS, 128))
        hidden_low = hidden.astype(BF)
        hidden_rows[rows, :] = hidden_low
        total = hidden + vector("b_down")
        parts = [slice(f, f + FB) for f in range(0, ff_width, FB)]
        raised = dot(hidden_low, w_up[:, parts[0]])
        for m, part in enumerate(parts):
            following = dot(hidden_low, w_up[:, parts[m + 1]]) if m + 1 < len(parts) else None
            active, slope = gelu_parts(raised + small_ref[0, :, part])
            active = active.astype(BF)
            active_rows[rows, part] = active
            slope_rows[rows, part] = slope.astype(BF)
            total += dot(active, w_down[part, :])
            raised = following
        hat, inverse = normalized(total)
        scale2_ref[rows, :] = jnp.broadcast_to(inverse, (ROWS, 128))
        out_rows[rows, :] = (hat * vector("gain2") + vector("shift2")).astype(BF)
        for copy in row_copies(n):
            copy.start()
        return 0

    lax.fori_loop(0, blocks, refine_rows, 0)
    context_copy.wait()
    for n in range(blocks):
        qkv_copy(n).wait()
        for copy in row_copies(n):
            copy.wait()


def layer_forward(sel, x, weights, layer, plan):
    w_qkv, w_out, w_up, w_down, small = weights
    begin, count, key_code, query_code = plan
    length, width = x.shape
    ff_width = w_up[0].shape[1]
    pairs = width // PAIR
    blocks = length // ROWS

    def whole(shape):
        return pl.BlockSpec(shape, lambda *_: (0,) * len(shape))

    row = jax.ShapeDtypeStruct((length, width), BF)
    lanes = jax.ShapeDtypeStruct((length, 128), F32)
    wide = jax.ShapeDtypeStruct((length, ff_width), BF)
    logsum_shape = (pairs * (length // QB), 2 * QB)
    qkv, context, logsum, out, hidden, scale1, scale2, active, slope = pl.pallas_call(
        partial(forward_kernel, layer),
        name="layer_forward",
        grid_spec=pltpu.PrefetchScalarGridSpec(
            num_scalar_prefetch=3,
            grid=(1,),
            in_specs=[ANY, whole(key_code.shape), whole(query_code.shape)]
            + [ANY] * 8
            + [small_spec(layer, small.shape[2])],
            out_specs=[
                ANY, ANY, whole(logsum_shape), ANY, ANY,
                whole((length, 128)), whole((length, 128)), ANY, ANY,
            ],
            scratch_shapes=[
                *held_shapes(w_qkv, w_out, w_up, w_down),
                pltpu.VMEM((length, width), BF),
                pltpu.VMEM((3, length, width), BF),
                pltpu.VMEM((length, width), BF),
                pltpu.VMEM((length, width), BF),
                pltpu.VMEM((length, width), BF),
                pltpu.VMEM((length, ff_width), BF),
                pltpu.VMEM((length, ff_width), BF),
                pltpu.VMEM((pairs, PAIR + 16, length), BF),
                pltpu.VMEM((pairs, 2 * QB, PAIR), BF),
                pltpu.VMEM((pairs, PAIR + 16, 2 * QB), F32),
                pltpu.SemaphoreType.DMA((4,)),
                pltpu.SemaphoreType.DMA((blocks,)),
                pltpu.SemaphoreType.DMA((blocks,)),
                pltpu.SemaphoreType.DMA((4, blocks)),
                pltpu.SemaphoreType.DMA,
            ],
        ),
        out_shape=[
            jax.ShapeDtypeStruct((3, length, width), BF), row,
            jax.ShapeDtypeStruct(logsum_shape, F32), row, row, lanes, lanes, wide, wide,
        ],
        compiler_params=PARAMS,
        cost_estimate=cost(48),
    )(begin, count, sel, x, key_code, query_code, *w_qkv, *w_out, *w_up, *w_down, small)
    return (out, (x, qkv, context, logsum, hidden, out, scale1, scale2, slope, active))


def feed_backward(sel, grad, kept, weights, layer):
    grad_low, grad_raised, grad_attn, grad_context, sums, up_sums = refine_back(
        sel, grad, kept[4:9], weights[1:], layer
    )
    return (grad_context, (grad_low, grad_raised, grad_attn), (sums, up_sums))


def mixed_backward_kernel(
    layer, begin_ref, count_ref, sel_ref, qkv_hbm, key_code_ref, query_code_ref, context_hbm,
    logsum_ref, grad_hbm, skip_hbm, mix_own_ref, mix_other_ref,
    mixed_hbm, grad_x_hbm, sums_ref,
    w_mix, qkv, context, grad, skip, key_scr, query_scr, given_scr, down_scr,
    grad_key_scr, grad_value_scr, weight_sems, in_sems, mixed_sems, row_sems,
):
    length, width = skip.shape
    blocks = length // ROWS
    weights = Held(sel_ref, layer, [(mix_own_ref, mix_other_ref)], [w_mix], weight_sems, True)
    arrays = [(qkv_hbm, qkv), (context_hbm, context), (grad_hbm, grad), (skip_hbm, skip)]
    loads = [
        pltpu.make_async_copy(whole, held, in_sems.at[n]) for n, (whole, held) in enumerate(arrays)
    ]
    for load in loads:
        load.start()
    weights.start()
    for load in loads:
        load.wait()
    attend_backward(
        begin_ref, count_ref, qkv, key_code_ref, query_code_ref, context, logsum_ref, grad,
        sums_ref, key_scr, query_scr, given_scr, down_scr, grad_key_scr, grad_value_scr,
    )
    store = pltpu.make_async_copy(qkv, mixed_hbm, mixed_sems.at[0])
    store.start()
    weights.wait(0)

    def rows_of(n):
        return pl.ds(pl.multiple_of(n * ROWS, ROWS), ROWS)

    def row_copy(n):
        return pltpu.make_async_copy(skip.at[rows_of(n)], grad_x_hbm.at[rows_of(n)], row_sems.at[n])

    def unmix_rows(n, _):
        rows = rows_of(n)
        total = skip[rows, :].astype(F32)
        for c in range(3):
            total += dot_nt(qkv[c, rows, :], w_mix[:, c * width : (c + 1) * width])
        skip[rows, :] = total.astype(BF)
        row_copy(n).start()
        return 0

    lax.fori_loop(0, blocks, unmix_rows, 0)
    store.wait()
    for n in range(blocks):
        row_copy(n).wait()


def mixed_backward(sel, grad_context, skip, kept, weights, layer, plan):
    _, qkv, context, logsum = kept[:4]
    begin, count, key_code, query_code = plan
    _, length, width = qkv.shape
    pairs = width // PAIR
    blocks = length // ROWS
    w_qkv = weights[0]

    def whole(shape):
        return pl.BlockSpec(shape, lambda *_: (0,) * len(shape))

    row = pltpu.VMEM((length, width), BF)
    return pl.pallas_call(
        partial(mixed_backward_kernel, layer),
        name="mixed_backward",
        grid_spec=pltpu.PrefetchScalarGridSpec(
            num_scalar_prefetch=3,
            grid=(1,),
            in_specs=[ANY, whole(key_code.shape), whole(query_code.shape), ANY, whole(logsum.shape)]
            + [ANY] * 4,
            out_specs=[ANY, ANY, whole((2, width))],
            scratch_shapes=[
                *held_shapes(w_qkv),
                pltpu.VMEM((3, length, width), BF),
                row, row, row,
                pltpu.VMEM((pairs, PAIR, length), BF),
                pltpu.VMEM((pairs, 2 * QB, PAIR), BF),
                pltpu.VMEM((pairs, 2 * QB, PAIR), BF),
                pltpu.VMEM((pairs, PAIR, 2 * QB), F32),
                pltpu.VMEM((length, width), F32),
                pltpu.VMEM((length, width), F32),
                pltpu.SemaphoreType.DMA((1,)),
                pltpu.SemaphoreType.DMA((4,)),
                pltpu.SemaphoreType.DMA((1,)),
                pltpu.SemaphoreType.DMA((blocks,)),
            ],
        ),
        out_shape=[
            jax.ShapeDtypeStruct((3, length, width), BF),
            jax.ShapeDtypeStruct((length, width), BF),
            jax.ShapeDtypeStruct((2, width), F32),
        ],
        compiler_params=PARAMS,
        cost_estimate=cost(38),
    )(begin, count, sel, qkv, key_code, query_code, context, logsum, grad_context, skip, *w_qkv)


def layer_backward(sel, grad, kept, weights, layer, plan):
    grad_context, grads, sums = feed_backward(sel, grad, kept, weights, layer)
    grad_mixed, grad_x, mix_sums = mixed_backward(
        sel, grad_context, grads[2], kept, weights, layer, plan
    )
    return (grad_x, grads + (grad_mixed,), sums + (mix_sums,))


def swap_cores(value):
    return send(value, ((0, 1), (1, 0), (2, 3), (3, 2)))


def send(value, routes):
    return lax.ppermute(value, "section", routes)


def pick_row(value, at, axis=0):
    return lax.dynamic_index_in_dim(value, at, axis, keepdims=False)


def plus(*values):
    return sum(value.astype(F32) for value in values).astype(BF)


class RowSum:
    def __init__(self, value, blocks):
        self.value, self.blocks, self.travelling = value, blocks, None
        self.plain = lax.axis_size("dp") != SHARDS
        if not self.plain:
            at = lax.axis_index("dp")
            self.z, self.x, self.line_at = at // 2, at % 2, 0

    def state(self):
        return (self.value, self.travelling)

    def set(self, state):
        self.value, self.travelling = state

    def cross(self):
        if self.plain:
            return
        value = self.value.reshape(4, 2, *self.value.shape[1:])
        other = pick_row(value, 1 - self.x, 1)
        arrived = lax.ppermute(other, "dp", [(n, n ^ 1) for n in range(8)])
        self.value = plus(pick_row(value, self.x, 1), arrived)

    def line(self):
        if self.plain:
            return
        self.line_at += 1
        far = 4 - self.line_at
        right = pick_row(self.value, jnp.minimum(self.z + far, 3))
        left = pick_row(self.value, jnp.maximum(self.z - far, 0))
        if self.travelling is not None:
            right, left = plus(right, self.travelling[0]), plus(left, self.travelling[1])
        self.travelling = (
            lax.ppermute(right, "dp", [(n, n + 2) for n in range(6)]),
            lax.ppermute(left, "dp", [(n + 2, n) for n in range(6)]),
        )

    def direct(self):
        if self.plain:
            return
        arrived = []
        for far in (3, 2, 1):
            for way in (far, -far):
                part = pick_row(self.value, jnp.clip(self.z + way, 0, 3))
                routes = [(n, n + 2 * way) for n in range(8) if 0 <= n + 2 * way < 8]
                arrived.append(lax.ppermute(part, "dp", routes))
        self.travelling = tuple(arrived)

    def result(self):
        if not self.plain:
            return plus(pick_row(self.value, self.z), *self.travelling)
        shards = lax.axis_size("dp")
        parts, at = [], 0
        for rows in self.blocks:
            part = self.value[:, at : at + rows].reshape(shards, -1, self.value.shape[2])
            parts, at = parts + [part], at + rows
        whole = jnp.concatenate(parts, axis=1)
        return lax.psum_scatter(whole, "dp", scatter_dimension=0, tiled=True)[0]


def body(
    tokens_in, seg_starts, pad_mask, w_qkv, b_qv, w_attn_out, b_attn_out, ln_gain, ln_bias,
    w_up, b_up, w_down, b_down, w_proj, cotangent,
):
    section_at = lax.axis_index("section")
    core = section_at % 2
    is_late = section_at >= 2
    flip = core == 1
    quarter = tokens_in.shape[1]
    length, width = 4 * quarter, tokens_in.shape[2]
    ff_width = w_up.shape[2]
    proj_cols = w_proj.shape[1]
    shards = lax.axis_size("dp")
    share = width // shards

    def sel_for(half):
        return jnp.stack([core, section_at // 2, half]).astype(jnp.int32)

    sel_mine, sel_theirs = sel_for(core), sel_for(1 - core)

    own = pick_row(tokens_in, core)
    other = pick_row(tokens_in, 1 - core)
    straight = send(own, [(2, 0), (3, 1)])
    crossed = send(other, [(2, 1), (3, 0)])
    near = swap_cores(other)
    small = pack_small(b_qv[0], b_attn_out[0], ln_gain[0], ln_bias[0], b_up[0], b_down[0])[None]
    small_other = swap_cores(small)
    small = jnp.stack([jnp.where(flip, small_other, small), jnp.where(flip, small, small_other)])
    weights = tuple((w[0], swap_cores(w[0])) for w in (w_qkv, w_attn_out, w_up, w_down)) + (small,)
    x = jnp.concatenate(
        [
            jnp.where(flip, near, own),
            jnp.where(flip, own, near),
            jnp.where(flip, crossed, straight),
            jnp.where(flip, straight, crossed),
        ],
        axis=0,
    )

    head_own = jnp.concatenate([w_proj.T, pick_row(cotangent, core).T], axis=1)
    head_other = jnp.concatenate([w_proj.T, pick_row(cotangent, 1 - core).T], axis=1)
    head_late = send(head_other, [(2, 3), (3, 2)])
    head_straight = send(head_own, [(0, 2), (1, 3)])
    head_crossed = send(head_other, [(0, 3), (1, 2)])
    head_cols = jnp.concatenate(
        [
            jnp.where(flip, head_crossed, head_straight),
            jnp.where(flip, head_straight, head_crossed),
            jnp.where(flip, head_late, head_own),
            jnp.where(flip, head_own, head_late),
        ],
        axis=0,
    )
    proj_rows, given_rows = head_cols[:, :width], head_cols[:, width:]
    plan = attention_plan(pick_row(seg_starts, core), pick_row(pad_mask, core))

    def both_forward(rows):
        middle, kept_even = layer_forward(sel_mine, rows, weights, 0, plan)
        last, kept_odd = layer_forward(sel_mine, middle, weights, 1, plan)
        return (last, kept_even, kept_odd)

    early, kept_even, kept_odd = both_forward(x)
    hopped = send(early, [(0, 2), (1, 3)])
    hopped, proj_rows, given_rows = lax.optimization_barrier((hopped, proj_rows, given_rows))

    def late_turn(rows, *_):
        last, kept_even, kept_odd = both_forward(rows)
        embedded, grad_proj, grad = head(last, proj_rows, given_rows)
        grad, grads_odd, sums_odd = layer_backward(sel_mine, grad, kept_odd, weights, 1, plan)
        grad, grads_even, sums_even = layer_backward(sel_mine, grad, kept_even, weights, 0, plan)
        return (
            kept_even, kept_odd, embedded, grad_proj, grad,
            grads_odd, sums_odd, grads_even, sums_even,
        )

    def early_turn(rows, kept_even, kept_odd):
        row, ff = jnp.zeros((length, width), BF), jnp.zeros((length, ff_width), BF)
        grads = (row, ff, row, jnp.zeros((3, length, width), BF))
        sums = (
            jnp.zeros((6, width), F32),
            jnp.zeros((1, ff_width), F32),
            jnp.zeros((2, width), F32),
        )
        return (
            kept_even, kept_odd, jnp.zeros((4 * proj_cols, length), BF),
            jnp.zeros((width, 4 * proj_cols), BF), row, grads, sums, grads, sums,
        )

    (
        kept_even, kept_odd, embedded, grad_proj, grad_mid,
        late_odd, late_sums_odd, late_even, late_sums_even,
    ) = lax.cond(is_late, late_turn, early_turn, hopped, kept_even, kept_odd)

    grad = send(grad_mid, [(2, 0), (3, 1)])
    embedded_cols = embedded.reshape(4, proj_cols, length)

    rows_of_one = width // SHARDS
    attend_blocks = (rows_of_one,) * 4
    feed_blocks = (rows_of_one,) * (ff_width // (2 * HALF)) + (ff_width // SHARDS,)

    def merged(late_sums, sums):
        return tuple(jnp.where(is_late, a, b) for a, b in zip(late_sums, sums))

    def tie(*values):
        return lax.optimization_barrier(values)

    def feed_args(kept, late, now):
        return (kept[4], late[1], now[1], kept[9], late[0], now[0])

    def attend_args(kept, late, now, mixed):
        return (kept[2], kept[0], late[2], now[2], late[3], mixed)

    def tie_sums(values, *sums):
        values, states = tie(values, [part.state() for part in sums])
        for part, state in zip(sums, states):
            part.set(state)
        return values

    grad_context, grads_odd, sums_odd = feed_backward(sel_mine, grad, kept_odd, weights, 1)
    args = feed_args(kept_odd, late_odd, grads_odd)
    arrived = swap_cores(feed_grads(sel_theirs, *args))
    feed_odd = RowSum(plus(feed_grads(sel_mine, *args), arrived), feed_blocks)
    grad_context = tie_sums(grad_context, feed_odd)
    feed_odd.cross()
    mixed_odd, grad, mix_sums = mixed_backward(
        sel_mine, grad_context, grads_odd[2], kept_odd, weights, 1, plan
    )
    sums_odd = merged(late_sums_odd, sums_odd + (mix_sums,))
    args = tie_sums(attend_args(kept_odd, late_odd, grads_odd, mixed_odd), feed_odd)
    feed_odd.line()
    theirs = attend_grads(sel_theirs, *args)
    args, theirs = tie_sums((args, theirs), feed_odd)
    arrived = swap_cores(theirs)
    attend_odd = RowSum(plus(attend_grads(sel_mine, *args), arrived), attend_blocks)
    grad = tie_sums(grad, feed_odd, attend_odd)
    feed_odd.line()
    attend_odd.cross()

    grad_context, grads_even, sums_even = feed_backward(sel_mine, grad, kept_even, weights, 0)
    args = tie_sums(feed_args(kept_even, late_even, grads_even), feed_odd, attend_odd)
    feed_odd.line()
    theirs = feed_grads(sel_theirs, *args)
    args, theirs = tie_sums((args, theirs), feed_odd)
    arrived = swap_cores(theirs)
    feed_even = RowSum(plus(feed_grads(sel_mine, *args), arrived), feed_blocks)
    grad_context = tie_sums(grad_context, feed_even, attend_odd)
    feed_even.cross()
    attend_odd.direct()
    mixed_even, grad, mix_sums = mixed_backward(
        sel_mine, grad_context, grads_even[2], kept_even, weights, 0, plan
    )
    sums_even = merged(late_sums_even, sums_even + (mix_sums,))
    args = attend_args(kept_even, late_even, grads_even, mixed_even)
    args = tie_sums(args, feed_even, attend_odd)
    feed_even.line()
    theirs = attend_grads(sel_theirs, *args)
    args, theirs = tie_sums((args, theirs), feed_even)
    arrived = swap_cores(theirs)
    feed_even.line()
    attend_even = plus(attend_grads(sel_mine, *args), arrived)

    def small_rows(sums):
        sums, up_sums, mix_sums = sums
        rows = [up_sums[0], mix_sums.reshape(-1)]
        rows += [sums[n] for n in range(6)]
        return jnp.concatenate([row.reshape(shards, -1) for row in rows], axis=1)

    extras = jnp.concatenate(
        [small_rows(sums_even), small_rows(sums_odd), grad_proj.reshape(shards, -1).astype(F32)],
        axis=1,
    )
    small_width = 12 * share
    lines = -(-extras.shape[1] // HALF)
    lines = -(-lines // 16) * 16
    extras = jnp.pad(extras, ((0, 0), (0, lines * HALF - extras.shape[1])))
    extras = extras.reshape(shards, lines, HALF).astype(BF)
    extras = plus(extras, swap_cores(extras))
    attend_even = tie_sums(attend_even, feed_even)
    feed_even.line()
    if shards == SHARDS:
        tail = RowSum(jnp.concatenate([attend_even, extras], axis=1), None)
        tail.cross()
        tail.direct()
        tail = tail.result()
        attend_even, extras = tail[: 4 * share], tail[4 * share :]
    else:
        attend_even = RowSum(attend_even, attend_blocks).result()
        extras = lax.psum_scatter(extras, "dp", scatter_dimension=0, tiled=True)[0]
    feed_odd, attend_odd, feed_even = [
        part.result() for part in (feed_odd, attend_odd, feed_even)
    ]

    routes_odd, routes_even = ((0, 1), (2, 3)), ((1, 0), (3, 2))

    def halves(even, odd):
        arrived = jnp.where(flip, send(odd, routes_odd), send(even, routes_even))
        mine = jnp.where(flip, odd, even)
        return (jnp.where(flip, arrived, mine), jnp.where(flip, mine, arrived))

    blocks = ff_width // (2 * HALF)
    feed_halves = halves(feed_even, feed_odd)
    attend_halves = halves(attend_even, attend_odd)

    def columns(pair, first, count):
        parts = [part[n * share : (n + 1) * share] for part in pair for n in range(first, first + count)]
        return jnp.concatenate(parts, axis=1).astype(F32)

    grad_w_up = columns(feed_halves, 0, blocks)[None]
    grad_w_down = jnp.concatenate([part[blocks * share :] for part in feed_halves], axis=1)
    grad_w_down = grad_w_down.astype(F32)[None]
    grad_w_out = columns(attend_halves, 0, 1)[None]
    grad_w_qkv = jnp.concatenate([columns(attend_halves, 1 + c, 1) for c in range(3)], axis=1)[None]

    extras = extras.reshape(-1).astype(F32)
    small_mine = jnp.where(flip, extras[small_width : 2 * small_width], extras[:small_width])
    at = ff_width // shards
    grad_b_up = small_mine[None, :at]
    grad_b_qv = small_mine[None, at : at + 2 * share]
    rows = small_mine[at + 2 * share :].reshape(6, share)
    grad_proj = extras[2 * small_width : 2 * small_width + share * 4 * proj_cols]
    grad_proj = grad_proj.reshape(share, 4 * proj_cols).astype(BF)
    grad_proj = jnp.where(is_late, grad_proj, send(grad_proj, [(2, 0), (3, 1)])).astype(F32)
    grad_w_proj = lax.dynamic_slice_in_dim(grad_proj, section_at * proj_cols, proj_cols, 1)

    straight_cols = send(pick_row(embedded_cols, core), [(2, 0), (3, 1)])
    crossed_cols = send(pick_row(embedded_cols, 1 - core), [(2, 1), (3, 0)])
    near_cols = swap_cores(pick_row(embedded_cols, 3 - core))
    own_cols = jnp.where(is_late, pick_row(embedded_cols, section_at), straight_cols)
    other_cols = jnp.where(is_late, near_cols, crossed_cols)
    embedded_out = jnp.stack(
        [jnp.where(flip, other_cols, own_cols).T, jnp.where(flip, own_cols, other_cols).T]
    )

    quarters = grad.reshape(4, quarter, width)
    straight_grad = send(pick_row(quarters, 2 + core), [(0, 2), (1, 3)])
    crossed_grad = send(pick_row(quarters, 3 - core), [(0, 3), (1, 2)])
    near_grad = swap_cores(pick_row(quarters, 1 - core))
    mine = jnp.where(is_late, straight_grad, pick_row(quarters, core))
    others = jnp.where(is_late, crossed_grad, near_grad)
    grad_in = jnp.stack(
        [jnp.where(flip, others, mine), jnp.where(flip, mine, others)]
    ).astype(F32)

    return (
        embedded_out,
        grad_in,
        grad_w_qkv,
        grad_b_qv,
        grad_w_out,
        rows[0][None],
        rows[1:3][None],
        rows[3:5][None],
        grad_w_up,
        grad_b_up,
        grad_w_down,
        rows[5][None],
        grad_w_proj,
    )


def solution(mesh):
    in_specs = (
        P("dp", "section", None),
        P("dp", None),
        P("dp", None),
        P("section", None, None),
        P("section", None),
        P("section", None, None),
        P("section", None),
        P("section", None, None),
        P("section", None, None),
        P("section", None, None),
        P("section", None),
        P("section", None, None),
        P("section", None),
        P(None, "section"),
        P("dp", None, "section"),
    )
    out_specs = (
        P("dp", None, "section"),
        P("dp", "section", None),
        P("section", "dp", None),
        P("section", "dp"),
        P("section", "dp", None),
        P("section", "dp"),
        P("section", None, "dp"),
        P("section", None, "dp"),
        P("section", "dp", None),
        P("section", "dp"),
        P("section", "dp", None),
        P("section", "dp"),
        P("dp", "section"),
    )
    return jax.shard_map(body, mesh=mesh, in_specs=in_specs, out_specs=out_specs, check_vma=False)
```

```python
from functools import partial
import math

import jax
import jax.numpy as jnp
from jax import lax
from jax.experimental import pallas as pl
from jax.experimental.pallas import tpu as pltpu
from jax.sharding import PartitionSpec as P

HEAD = 64
PAIR = 2 * HEAD
QB = 128
KB = 512
EPS_NORM = 1e-05
EPS_PROJ = 1e-06
NEG_FILL = -1e30
PARAMS = pltpu.CompilerParams(vmem_limit_bytes=60 * 1024 * 1024)


def cost(micros):
    return pl.CostEstimate(flops=int(micros * 1e9), bytes_accessed=1024, transcendentals=0)


BF = jnp.bfloat16
F32 = jnp.float32

NT = (((1,), (1,)), ((), ()))
TN = (((0,), (0,)), ((), ()))


def dot(a, b):
    return jnp.dot(a, b, preferred_element_type=F32)


def dot_nt(a, b):
    return lax.dot_general(a, b, NT, preferred_element_type=F32)


def dot_tn(a, b):
    return lax.dot_general(a, b, TN, preferred_element_type=F32)


def pack_small(b_qv, b_out, gains, shifts, b_up, b_down):
    return jnp.concatenate(
        [b_up, b_qv, b_out, gains[0], gains[1], shifts[0], shifts[1], b_down]
    )


def small_spec(layer, width):
    return pl.BlockSpec((1, 1, width), lambda *_: (layer, 0, 0))


def attention_plan(starts, real_flags):
    length = real_flags.shape[0]
    places = jnp.arange(length, dtype=jnp.int32)
    segment = jnp.sum((starts[None, :] <= places[:, None]).astype(jnp.int32), axis=1)
    key_code = jnp.where(real_flags == 1, segment, -1).astype(F32)
    key_code = jnp.broadcast_to(key_code[:, None], (length, PAIR))
    query_code = segment.astype(F32).reshape(length // QB, QB)
    first = jnp.arange(length // QB, dtype=jnp.int32) * QB
    low = jnp.max(jnp.where(starts[None, :] <= first[:, None], starts[None, :], 0), axis=1)
    high = jnp.min(
        jnp.where(starts[None, :] > first[:, None] + (QB - 1), starts[None, :], length), axis=1
    )
    begin = (low // QB) * QB
    count = (high - begin + KB - 1) // KB
    begin = jnp.minimum(begin, length - KB * count)
    return (begin, count, key_code, query_code)


def pair_mask(rows):
    return lax.broadcasted_iota(jnp.int32, (rows, PAIR), 1) < HEAD


def stacked_heads(block):
    first = pair_mask(block.shape[0])
    zero = jnp.zeros_like(block)
    return jnp.concatenate([jnp.where(first, block, zero), jnp.where(first, zero, block)], axis=0)


def block_bias(key_code, query_code, key_at, query_at):
    keys = lax.broadcasted_iota(jnp.int32, (KB, QB), 0) + (key_at - query_at)
    same = keys == lax.broadcasted_iota(jnp.int32, (KB, QB), 1)
    bias = jnp.where((key_code == query_code) | same, 0.0, NEG_FILL)
    return jnp.concatenate([bias, bias], axis=1)


def top_rows(values, op):
    folded = values.reshape(values.shape[0] // 8, 8, values.shape[1])
    return op(folded, axis=0)


def unstack_heads(flat):
    rows = lax.broadcasted_iota(jnp.int32, (PAIR, QB), 0)
    return jnp.where(rows < HEAD, flat[:PAIR, :QB], flat[:PAIR, QB:]).T


def attend_forward(
    begin_ref, count_ref, qkv_ref, key_code_ref, query_code_ref, out_ref, logsum_ref,
    value_scr, query_scr, total_scr,
):
    length = qkv_ref.shape[1]
    pairs = qkv_ref.shape[2] // PAIR
    every = range(pairs)
    cols = [slice(p * PAIR, (p + 1) * PAIR) for p in every]
    for p in every:
        value_scr[p, :PAIR, :] = qkv_ref[2, :, cols[p]].T
        value_scr[p, PAIR:, :] = jnp.ones((value_scr.shape[1] - PAIR, length), BF)

    def one_query_block(i, _):
        query_at = pl.multiple_of(i * QB, QB)
        begin, count = begin_ref[i], count_ref[i]
        query_code = query_code_ref[pl.ds(i, 1), :]
        for p in every:
            query_scr[p] = stacked_heads(qkv_ref[0, pl.ds(query_at, QB), cols[p]])
        total_scr[...] = jnp.zeros_like(total_scr)

        def one_key_block(j, tops):
            key_at = pl.multiple_of(begin + j * KB, QB)
            rows = pl.ds(key_at, KB)
            bias = block_bias(key_code_ref[rows, :], query_code, key_at, query_at)
            scores = [dot_nt(qkv_ref[1, rows, cols[p]], query_scr[p]) + bias for p in every]
            fresh = [
                jnp.maximum(tops[p], jnp.max(scores[p], axis=0, keepdims=True)) for p in every
            ]
            probs = [jnp.exp(scores[p] - fresh[p]).astype(BF) for p in every]
            for p in every:
                total_scr[p] = total_scr[p] * jnp.exp(tops[p] - fresh[p]) + dot(
                    value_scr[p, :, rows], probs[p]
                )
            return tuple(fresh)

        tops = lax.fori_loop(
            0, count, one_key_block, tuple(jnp.full((1, 2 * QB), 2 * NEG_FILL, F32) for _ in every)
        )
        for p in every:
            weight = total_scr[p, PAIR : PAIR + 1, :]
            logsum_ref[pl.ds(p * (length // QB) + i, 1), :] = tops[p] + jnp.log(weight)
            out_ref[pl.ds(query_at, QB), cols[p]] = unstack_heads(
                total_scr[p, :PAIR, :] * (1.0 / weight)
            ).astype(BF)
        return 0

    lax.fori_loop(0, length // QB, one_query_block, 0)


def attend_backward(
    begin_ref, count_ref, qkv, key_code_ref, query_code_ref, context, logsum_ref, grad, sums_ref,
    key_scr, query_scr, given_scr, down_scr, grad_key_scr, grad_value_scr,
):
    length = qkv.shape[1]
    pairs = qkv.shape[2] // PAIR
    every = range(pairs)
    blocks = length // QB
    cols = [slice(p * PAIR, (p + 1) * PAIR) for p in every]
    for p in every:
        key_scr[p] = qkv[1, :, cols[p]].T
    grad_key_scr[...] = jnp.zeros_like(grad_key_scr)
    grad_value_scr[...] = jnp.zeros_like(grad_value_scr)
    sums_ref[...] = jnp.zeros_like(sums_ref)

    def one_query_block(i, _):
        query_at = pl.multiple_of(i * QB, QB)
        queries = pl.ds(query_at, QB)
        begin, count = begin_ref[i], count_ref[i]
        query_code = query_code_ref[pl.ds(i, 1), :]
        inner, logsum = [], []
        for p in every:
            query_scr[p] = stacked_heads(qkv[0, queries, cols[p]])
            given = grad[queries, cols[p]]
            given_scr[p] = stacked_heads(given)
            both = (given.astype(F32) * context[queries, cols[p]].astype(F32)).T
            inner.append(
                jnp.concatenate(
                    [
                        jnp.sum(both[:HEAD], axis=0, keepdims=True),
                        jnp.sum(both[HEAD:], axis=0, keepdims=True),
                    ],
                    axis=1,
                )
            )
            logsum.append(logsum_ref[pl.ds(p * blocks + i, 1), :])
        down_scr[...] = jnp.zeros_like(down_scr)

        def one_key_block(j, _):
            key_at = pl.multiple_of(begin + j * KB, QB)
            rows = pl.ds(key_at, KB)
            bias = block_bias(key_code_ref[rows, :], query_code, key_at, query_at)
            parts = [dot_nt(qkv[1, rows, cols[p]], query_scr[p]) + bias for p in every]
            grads = [dot_nt(qkv[2, rows, cols[p]], given_scr[p]) - inner[p] for p in every]
            probs = [jnp.exp(parts[p] - logsum[p]) for p in every]
            scores = [(probs[p] * grads[p]).astype(BF) for p in every]
            probs = [probs[p].astype(BF) for p in every]
            for p in every:
                grad_value_scr[rows, cols[p]] += dot(probs[p], given_scr[p])
            for p in every:
                grad_key_scr[rows, cols[p]] += dot(scores[p], query_scr[p])
            for p in every:
                down_scr[p] += dot(key_scr[p, :, rows], scores[p])
            return 0

        lax.fori_loop(0, count, one_key_block, 0)
        for p in every:
            grad_query = (unstack_heads(down_scr[p]) * (HEAD**-0.5)).astype(BF)
            qkv[0, queries, cols[p]] = grad_query
            sums_ref[0:1, cols[p]] += jnp.sum(grad_query.astype(F32), axis=0, keepdims=True)
        return 0

    lax.fori_loop(0, blocks, one_query_block, 0)
    qkv[1] = grad_key_scr[...].astype(BF)
    grad_value = grad_value_scr[...].astype(BF)
    qkv[2] = grad_value
    sums_ref[1:2, :] = jnp.sum(grad_value.astype(F32), axis=0, keepdims=True)


ANY = pl.BlockSpec(memory_space=pl.ANY)
ROWS = 256


class Held:
    def __init__(self, sel_ref, layer, pairs, held, sems, first=None):
        self.own = sel_ref[0] == layer
        self.items = list(zip(pairs, held, range(len(held))))
        self.sems = sems
        self.first = pl.program_id(0) == 0 if first is None else first

    def start(self):
        for pair, held, n in self.items:
            for wanted, source in zip((self.own, jnp.logical_not(self.own)), pair):

                @pl.when(self.first & wanted)
                def _():
                    pltpu.make_async_copy(source, held, self.sems.at[n]).start()

    def wait(self, n):
        pair, held, _ = self.items[n]

        @pl.when(self.first)
        def _():
            pltpu.make_async_copy(pair[0], held, self.sems.at[n]).wait()


def held_shapes(*weights):
    return [pltpu.VMEM(own.shape, own.dtype) for own, _ in weights]


def normalized(values):
    centred = values - jnp.mean(values, axis=-1, keepdims=True)
    inverse = lax.rsqrt(jnp.mean(centred * centred, axis=-1, keepdims=True) + EPS_NORM)
    return (centred * inverse, inverse)


def normalized_pull(grad_hat, hat, inverse):
    return inverse * (
        grad_hat
        - jnp.mean(grad_hat, axis=-1, keepdims=True)
        - hat * jnp.mean(grad_hat * hat, axis=-1, keepdims=True)
    )


ERF = (0.254829592, -0.284496736, 1.421413741, -1.453152027, 1.061405429)
ERF_SLOPE = 0.3275911


def gelu_parts(x):
    t = pl.reciprocal(1.0 + (ERF_SLOPE * math.sqrt(0.5)) * jnp.abs(x), approx=True)
    bell = jnp.exp(-0.5 * (x * x))
    tail = 0.5 * ERF[4]
    for term in ERF[3::-1]:
        tail = tail * t + 0.5 * term
    tail = tail * t * bell
    below = jnp.where(x >= 0, 1.0 - tail, tail)
    return (x * below, below + x * bell * (1.0 / math.sqrt(2.0 * math.pi)))


FB = 1024


def small_slices(width, ff_width):
    names = ("b_q", "b_v", "b_out", "gain1", "gain2", "shift1", "shift2", "b_down")
    at = {"b_up": slice(0, ff_width)}
    for n, name in enumerate(names):
        at[name] = slice(ff_width + n * width, ff_width + (n + 1) * width)
    return at


def refine_back_kernel(
    layer, sel_ref, grad_ref, hidden_ref, out_ref, scale1_ref, scale2_ref, slope_ref,
    out_own_ref, out_other_ref, up_own_ref, up_other_ref, down_own_ref, down_other_ref, small_ref,
    grad_low_ref, grad_raised_ref, grad_attn_ref, grad_context_ref, sums_ref, up_sums_ref,
    w_out, w_up, w_down, sems,
):
    pairs = [(out_own_ref, out_other_ref), (up_own_ref, up_other_ref), (down_own_ref, down_other_ref)]
    weights = Held(sel_ref, layer, pairs, [w_out, w_up, w_down], sems)
    weights.start()
    rows, width = grad_ref.shape
    ff_width = slope_ref.shape[1]
    at = small_slices(width, ff_width)

    @pl.when(pl.program_id(0) == 0)
    def _():
        sums_ref[...] = jnp.zeros_like(sums_ref)
        up_sums_ref[...] = jnp.zeros_like(up_sums_ref)

    def vector(name):
        return small_ref[0, :, at[name]]

    def add(row, values):
        sums_ref[row : row + 1, :] += jnp.sum(values, axis=0, keepdims=True)

    grad = grad_ref[...].astype(F32)
    hat = (out_ref[...].astype(F32) - vector("shift2")) * (1.0 / vector("gain2"))
    joined = normalized_pull(grad * vector("gain2"), hat, scale2_ref[:, :1])
    low = joined.astype(BF)
    grad_low_ref[...] = low
    add(2, grad * hat)
    add(4, grad)
    add(5, low.astype(F32))
    weights.wait(2)
    weights.wait(1)
    total = joined
    parts = [slice(f, f + FB) for f in range(0, ff_width, FB)]
    active = dot_nt(low, w_down[parts[0], :])
    for n, part in enumerate(parts):
        following = dot_nt(low, w_down[parts[n + 1], :]) if n + 1 < len(parts) else None
        raised = active * slope_ref[:, part].astype(F32)
        up_sums_ref[:, part] += jnp.sum(raised, axis=0, keepdims=True)
        raised = raised.astype(BF)
        grad_raised_ref[:, part] = raised
        total += dot_nt(raised, w_up[:, part])
        active = following
    hat = (hidden_ref[...].astype(F32) - vector("shift1")) * (1.0 / vector("gain1"))
    summed = normalized_pull(total * vector("gain1"), hat, scale1_ref[:, :1])
    attn = summed.astype(BF)
    grad_attn_ref[...] = attn
    weights.wait(0)
    grad_context_ref[...] = dot_nt(attn, w_out[...]).astype(BF)
    add(1, total * hat)
    add(3, total)
    add(0, attn.astype(F32))


def refine_back(sel, grad, kept, weights, layer):
    w_out, w_up, w_down, small = weights
    hidden, out, scale1, scale2, slope = kept
    length, width = grad.shape
    ff_width = w_up[0].shape[1]
    rows = pl.BlockSpec((ROWS, width), lambda n, _: (n, 0))
    lanes = pl.BlockSpec((ROWS, 128), lambda n, _: (n, 0))
    part = pl.BlockSpec((ROWS, ff_width), lambda n, _: (n, 0))
    row_shape = jax.ShapeDtypeStruct((length, width), BF)
    return pl.pallas_call(
        partial(refine_back_kernel, layer),
        name="refine_back",
        grid_spec=pltpu.PrefetchScalarGridSpec(
            num_scalar_prefetch=1,
            grid=(length // ROWS,),
            in_specs=[rows, rows, rows, lanes, lanes, part]
            + [ANY] * 6
            + [small_spec(layer, small.shape[2])],
            out_specs=[
                rows, part, rows, rows,
                pl.BlockSpec((6, width), lambda n, _: (0, 0)),
                pl.BlockSpec((1, ff_width), lambda n, _: (0, 0)),
            ],
            scratch_shapes=[
                *held_shapes(w_out, w_up, w_down),
                pltpu.SemaphoreType.DMA((3,)),
            ],
        ),
        out_shape=[
            row_shape,
            jax.ShapeDtypeStruct((length, ff_width), BF),
            row_shape,
            row_shape,
            jax.ShapeDtypeStruct((6, width), F32),
            jax.ShapeDtypeStruct((1, ff_width), F32),
        ],
        compiler_params=PARAMS,
        cost_estimate=cost(24),
    )(sel, grad, hidden, out, scale1, scale2, slope, *w_out, *w_up, *w_down, small)


def head_kernel(rows_ref, proj_ref, given_ref, embedded_ref, grad_proj_ref, grad_rows_ref):
    factor = math.sqrt(proj_ref.shape[0])
    columns = dot_nt(proj_ref[...], rows_ref[...])
    given = given_ref[...].astype(F32)
    inverse = lax.rsqrt(jnp.sum(columns * columns, axis=0, keepdims=True) + EPS_PROJ)
    cross = jnp.sum(columns * given, axis=0, keepdims=True)
    embedded_ref[...] = (factor * columns * inverse).astype(BF)
    grad = (factor * (given * inverse - columns * (cross * inverse * inverse * inverse))).astype(BF)
    grad_proj_ref[...] = dot(grad, rows_ref[...]).T.astype(BF)
    grad_rows_ref[...] = dot_tn(grad, proj_ref[...]).astype(BF)


def head(rows, proj, given):
    length, width = rows.shape
    cols = proj.shape[0]
    return pl.pallas_call(
        head_kernel,
        name="head",
        out_shape=[
            jax.ShapeDtypeStruct((cols, length), BF),
            jax.ShapeDtypeStruct((width, cols), BF),
            jax.ShapeDtypeStruct((length, width), BF),
        ],
        compiler_params=PARAMS,
        cost_estimate=cost(6),
    )(rows, proj, given)


HALF = 384
SHARDS = 8


def feed_grads_kernel(
    sel_ref, hidden_ref, raised_late_ref, raised_ref, active_ref, low_late_ref, low_ref, out_ref
):
    step = pl.program_id(0)
    shards, rows, _ = out_ref.shape
    blocks = raised_ref.shape[1] // HALF
    share = rows // blocks
    late = sel_ref[1] == 1

    def up(raised):
        part = dot_tn(hidden_ref[...], raised).astype(BF)
        for m in range(shards):
            for n in range(blocks):
                out_ref[m, n * share : (n + 1) * share, :] = part[
                    m * share : (m + 1) * share, n * HALF : (n + 1) * HALF
                ]

    def down(low):
        for m in range(shards):
            out_ref[m] = dot_tn(active_ref[:, m * rows : (m + 1) * rows], low).astype(BF)

    for wanted, raised_now, low_now in (
        (late, raised_late_ref, low_late_ref),
        (jnp.logical_not(late), raised_ref, low_ref),
    ):

        @pl.when(wanted & (step < 2))
        def _():
            up(raised_now[...])

        @pl.when(wanted & (step >= 2))
        def _():
            down(low_now[...])


def feed_grads(sel, hidden, raised_late, raised, active, low_late, low):
    length, width = hidden.shape
    ff_width = active.shape[1]
    half_ff = ff_width // 2

    def late_spec(shape, wanted):
        return pl.BlockSpec(shape, lambda n, sel: (0, jnp.where(sel[1] == wanted, sel[2], 0)))

    return pl.pallas_call(
        feed_grads_kernel,
        name="feed_grads",
        grid_spec=pltpu.PrefetchScalarGridSpec(
            num_scalar_prefetch=1,
            grid=(4,),
            in_specs=[
                pl.BlockSpec((length, width // 2), lambda n, _: (0, jnp.minimum(n, 1))),
                late_spec((length, half_ff), 1),
                late_spec((length, half_ff), 0),
                pl.BlockSpec((length, ff_width // 2), lambda n, _: (0, jnp.maximum(n - 2, 0))),
                late_spec((length, width // 2), 1),
                late_spec((length, width // 2), 0),
            ],
            out_specs=pl.BlockSpec(
                (SHARDS // 2, ff_width // SHARDS, HALF), lambda n, _: (lax.rem(n, 2), n // 2, 0)
            ),
        ),
        out_shape=jax.ShapeDtypeStruct((SHARDS, 2 * (ff_width // SHARDS), HALF), BF),
        compiler_params=PARAMS,
        cost_estimate=cost(12),
    )(sel, hidden, raised_late, raised, active, low_late, low)


def attend_grads_kernel(
    sel_ref, context_ref, x_ref, attn_late_ref, attn_ref, mixed_late_ref, mixed_ref, out_ref
):
    step = pl.program_id(0)
    late = sel_ref[1] == 1

    for wanted, attn_now, mixed_now in (
        (late, attn_late_ref, mixed_late_ref),
        (jnp.logical_not(late), attn_ref, mixed_ref),
    ):

        @pl.when(wanted & (step == 0))
        def _():
            part = dot_tn(context_ref[...], attn_now[...]).astype(BF)
            out_ref[...] = part.reshape(out_ref.shape)

        @pl.when(wanted & (step > 0))
        def _():
            part = dot_tn(x_ref[...], mixed_now[0]).astype(BF)
            out_ref[...] = part.reshape(out_ref.shape)


def attend_grads(sel, context, x, attn_late, attn, mixed_late, mixed):
    length, width = x.shape

    def late_spec(wanted):
        return pl.BlockSpec(
            (length, HALF), lambda n, sel: (0, jnp.where(sel[1] == wanted, sel[2], 0))
        )

    def mixed_spec(wanted):
        def at(n, sel):
            return (
                jnp.where(sel[1] == wanted, jnp.maximum(n - 1, 0), 0),
                0,
                jnp.where(sel[1] == wanted, sel[2], 0),
            )

        return pl.BlockSpec((1, length, HALF), at)

    whole = pl.BlockSpec((length, width), lambda n, _: (0, 0))
    share = width // SHARDS
    return pl.pallas_call(
        attend_grads_kernel,
        name="attend_grads",
        grid_spec=pltpu.PrefetchScalarGridSpec(
            num_scalar_prefetch=1,
            grid=(4,),
            in_specs=[whole, whole, late_spec(1), late_spec(0), mixed_spec(1), mixed_spec(0)],
            out_specs=pl.BlockSpec((SHARDS, share, HALF), lambda n, _: (0, n, 0)),
        ),
        out_shape=jax.ShapeDtypeStruct((SHARDS, 4 * share, HALF), BF),
        compiler_params=PARAMS,
        cost_estimate=cost(8),
    )(sel, context, x, attn_late, attn, mixed_late, mixed)


EXTRA_ROWS = 48


def pack_extras_kernel(
    sel_ref, proj_ref,
    late_sums_0, late_up_0, late_mix_0, late_sums_1, late_up_1, late_mix_1,
    sums_0, up_0, mix_0, sums_1, up_1, mix_1, out_ref,
):
    shards = out_ref.shape[0]
    width = sums_0.shape[1]
    share = width // shards
    third = share // 3
    cols = proj_ref.shape[1]
    out_ref[...] = jnp.zeros_like(out_ref)

    def layer(first, sums, up, mix):
        up_share = up.shape[1] // shards
        both = jnp.concatenate([mix[0:1, :], mix[1:2, :]], axis=1)
        for m in range(shards):
            rows = [up[0:1, m * up_share : (m + 1) * up_share]]
            rows += [both[:, 2 * m * share : 2 * (m + 1) * share]]
            rows += [sums[n : n + 1, m * share : (m + 1) * share] for n in range(6)]
            for n, row in enumerate(rows):
                out_ref[m, first + n : first + n + 1, : row.shape[1]] = row

    late = sel_ref[1] == 1
    for wanted, even, odd in (
        (late, (late_sums_0, late_up_0, late_mix_0), (late_sums_1, late_up_1, late_mix_1)),
        (jnp.logical_not(late), (sums_0, up_0, mix_0), (sums_1, up_1, mix_1)),
    ):

        @pl.when(wanted)
        def _():
            layer(0, *even)
            layer(8, *odd)

    for m in range(shards):
        for n in range(3):
            at = m * share + n * third
            out_ref[m, 16:, n * cols : (n + 1) * cols] = proj_ref[at : at + third, :].astype(F32)


def pack_extras(sel, proj, late_even, late_odd, even, odd):
    vmem = pl.BlockSpec(memory_space=pltpu.VMEM)
    return pl.pallas_call(
        pack_extras_kernel,
        name="pack_extras",
        in_specs=[pl.BlockSpec(memory_space=pltpu.SMEM)] + [vmem] * 13,
        out_specs=vmem,
        out_shape=jax.ShapeDtypeStruct((SHARDS, EXTRA_ROWS, HALF), F32),
        compiler_params=PARAMS,
        cost_estimate=cost(3),
    )(sel, proj, *late_even, *late_odd, *even, *odd)


def forward_kernel(
    layer, begin_ref, count_ref, sel_ref, x_hbm, key_code_ref, query_code_ref,
    mix_own_ref, mix_other_ref, out_own_ref, out_other_ref,
    up_own_ref, up_other_ref, down_own_ref, down_other_ref, small_ref,
    qkv_hbm, context_hbm, logsum_ref, out_hbm, hidden_hbm, scale1_ref, scale2_ref,
    active_hbm, slope_hbm,
    w_mix, w_out, w_up, w_down, x, qkv, context, hidden_rows, out_rows, active_rows, slope_rows,
    value_scr, query_scr, total_scr, weight_sems, in_sems, qkv_sems, row_sems, context_sem,
):
    pairs = [
        (mix_own_ref, mix_other_ref), (out_own_ref, out_other_ref),
        (up_own_ref, up_other_ref), (down_own_ref, down_other_ref),
    ]
    length, width = x.shape
    ff_width = w_up.shape[1]
    blocks = length // ROWS
    at = small_slices(width, ff_width)

    def vector(name):
        return small_ref[0, :, at[name]]

    def rows_of(n):
        return pl.ds(pl.multiple_of(n * ROWS, ROWS), ROWS)

    def x_copy(n):
        return pltpu.make_async_copy(x_hbm.at[rows_of(n)], x.at[rows_of(n)], in_sems.at[n])

    def qkv_copy(n):
        return pltpu.make_async_copy(
            qkv.at[:, rows_of(n)], qkv_hbm.at[:, rows_of(n)], qkv_sems.at[n]
        )

    saved = [
        (hidden_rows, hidden_hbm), (out_rows, out_hbm),
        (active_rows, active_hbm), (slope_rows, slope_hbm),
    ]

    def row_copies(n):
        return [
            pltpu.make_async_copy(rows.at[rows_of(n)], whole.at[rows_of(n)], row_sems.at[k, n])
            for k, (rows, whole) in enumerate(saved)
        ]

    weights = Held(sel_ref, layer, pairs, [w_mix, w_out, w_up, w_down], weight_sems, True)
    for n in range(blocks):
        x_copy(n).start()
    weights.start()
    weights.wait(0)

    def mix_rows(n, _):
        x_copy(n).wait()
        rows = rows_of(n)
        part = dot(x[rows, :], w_mix[...])
        qkv[0, rows, :] = ((part[:, :width] + vector("b_q")) * HEAD**-0.5).astype(BF)
        qkv[1, rows, :] = part[:, width : 2 * width].astype(BF)
        qkv[2, rows, :] = (part[:, 2 * width :] + vector("b_v")).astype(BF)
        qkv_copy(n).start()
        return 0

    lax.fori_loop(0, blocks, mix_rows, 0)
    attend_forward(
        begin_ref, count_ref, qkv, key_code_ref, query_code_ref, context, logsum_ref,
        value_scr, query_scr, total_scr,
    )
    context_copy = pltpu.make_async_copy(context, context_hbm, context_sem)
    context_copy.start()
    for n in (1, 2, 3):
        weights.wait(n)

    def refine_rows(n, _):
        rows = rows_of(n)
        summed = x[rows, :].astype(F32) + dot(context[rows, :], w_out[...]) + vector("b_out")
        hat, inverse = normalized(summed)
        hidden = hat * vector("gain1") + vector("shift1")
        scale1_ref[rows, :] = jnp.broadcast_to(inverse, (ROWS, 128))
        hidden_low = hidden.astype(BF)
        hidden_rows[rows, :] = hidden_low
        total = hidden + vector("b_down")
        parts = [slice(f, f + FB) for f in range(0, ff_width, FB)]
        raised = dot(hidden_low, w_up[:, parts[0]])
        for m, part in enumerate(parts):
            following = dot(hidden_low, w_up[:, parts[m + 1]]) if m + 1 < len(parts) else None
            active, slope = gelu_parts(raised + small_ref[0, :, part])
            active = active.astype(BF)
            active_rows[rows, part] = active
            slope_rows[rows, part] = slope.astype(BF)
            total += dot(active, w_down[part, :])
            raised = following
        hat, inverse = normalized(total)
        scale2_ref[rows, :] = jnp.broadcast_to(inverse, (ROWS, 128))
        out_rows[rows, :] = (hat * vector("gain2") + vector("shift2")).astype(BF)
        for copy in row_copies(n):
            copy.start()
        return 0

    lax.fori_loop(0, blocks, refine_rows, 0)
    context_copy.wait()
    for n in range(blocks):
        qkv_copy(n).wait()
        for copy in row_copies(n):
            copy.wait()


def layer_forward(sel, x, weights, layer, plan):
    w_qkv, w_out, w_up, w_down, small = weights
    begin, count, key_code, query_code = plan
    length, width = x.shape
    ff_width = w_up[0].shape[1]
    pairs = width // PAIR
    blocks = length // ROWS

    def whole(shape):
        return pl.BlockSpec(shape, lambda *_: (0,) * len(shape))

    row = jax.ShapeDtypeStruct((length, width), BF)
    lanes = jax.ShapeDtypeStruct((length, 128), F32)
    wide = jax.ShapeDtypeStruct((length, ff_width), BF)
    logsum_shape = (pairs * (length // QB), 2 * QB)
    qkv, context, logsum, out, hidden, scale1, scale2, active, slope = pl.pallas_call(
        partial(forward_kernel, layer),
        name="layer_forward",
        grid_spec=pltpu.PrefetchScalarGridSpec(
            num_scalar_prefetch=3,
            grid=(1,),
            in_specs=[ANY, whole(key_code.shape), whole(query_code.shape)]
            + [ANY] * 8
            + [small_spec(layer, small.shape[2])],
            out_specs=[
                ANY, ANY, whole(logsum_shape), ANY, ANY,
                whole((length, 128)), whole((length, 128)), ANY, ANY,
            ],
            scratch_shapes=[
                *held_shapes(w_qkv, w_out, w_up, w_down),
                pltpu.VMEM((length, width), BF),
                pltpu.VMEM((3, length, width), BF),
                pltpu.VMEM((length, width), BF),
                pltpu.VMEM((length, width), BF),
                pltpu.VMEM((length, width), BF),
                pltpu.VMEM((length, ff_width), BF),
                pltpu.VMEM((length, ff_width), BF),
                pltpu.VMEM((pairs, PAIR + 16, length), BF),
                pltpu.VMEM((pairs, 2 * QB, PAIR), BF),
                pltpu.VMEM((pairs, PAIR + 16, 2 * QB), F32),
                pltpu.SemaphoreType.DMA((4,)),
                pltpu.SemaphoreType.DMA((blocks,)),
                pltpu.SemaphoreType.DMA((blocks,)),
                pltpu.SemaphoreType.DMA((4, blocks)),
                pltpu.SemaphoreType.DMA,
            ],
        ),
        out_shape=[
            jax.ShapeDtypeStruct((3, length, width), BF), row,
            jax.ShapeDtypeStruct(logsum_shape, F32), row, row, lanes, lanes, wide, wide,
        ],
        compiler_params=PARAMS,
        cost_estimate=cost(48),
    )(begin, count, sel, x, key_code, query_code, *w_qkv, *w_out, *w_up, *w_down, small)
    return (out, (x, qkv, context, logsum, hidden, out, scale1, scale2, slope, active))


def feed_backward(sel, grad, kept, weights, layer):
    grad_low, grad_raised, grad_attn, grad_context, sums, up_sums = refine_back(
        sel, grad, kept[4:9], weights[1:], layer
    )
    return (grad_context, (grad_low, grad_raised, grad_attn), (sums, up_sums))


def mixed_backward_kernel(
    layer, begin_ref, count_ref, sel_ref, qkv_hbm, key_code_ref, query_code_ref, context_hbm,
    logsum_ref, grad_hbm, skip_hbm, mix_own_ref, mix_other_ref,
    mixed_hbm, grad_x_hbm, sums_ref,
    w_mix, qkv, context, grad, skip, key_scr, query_scr, given_scr, down_scr,
    grad_key_scr, grad_value_scr, weight_sems, in_sems, mixed_sems, row_sems,
):
    length, width = skip.shape
    blocks = length // ROWS
    weights = Held(sel_ref, layer, [(mix_own_ref, mix_other_ref)], [w_mix], weight_sems, True)
    arrays = [(qkv_hbm, qkv), (context_hbm, context), (grad_hbm, grad), (skip_hbm, skip)]
    loads = [
        pltpu.make_async_copy(whole, held, in_sems.at[n]) for n, (whole, held) in enumerate(arrays)
    ]
    for load in loads:
        load.start()
    weights.start()
    for load in loads:
        load.wait()
    attend_backward(
        begin_ref, count_ref, qkv, key_code_ref, query_code_ref, context, logsum_ref, grad,
        sums_ref, key_scr, query_scr, given_scr, down_scr, grad_key_scr, grad_value_scr,
    )
    store = pltpu.make_async_copy(qkv, mixed_hbm, mixed_sems.at[0])
    store.start()
    weights.wait(0)

    def rows_of(n):
        return pl.ds(pl.multiple_of(n * ROWS, ROWS), ROWS)

    def row_copy(n):
        return pltpu.make_async_copy(skip.at[rows_of(n)], grad_x_hbm.at[rows_of(n)], row_sems.at[n])

    def unmix_rows(n, _):
        rows = rows_of(n)
        total = skip[rows, :].astype(F32)
        for c in range(3):
            total += dot_nt(qkv[c, rows, :], w_mix[:, c * width : (c + 1) * width])
        skip[rows, :] = total.astype(BF)
        row_copy(n).start()
        return 0

    lax.fori_loop(0, blocks, unmix_rows, 0)
    store.wait()
    for n in range(blocks):
        row_copy(n).wait()


def mixed_backward(sel, grad_context, skip, kept, weights, layer, plan):
    _, qkv, context, logsum = kept[:4]
    begin, count, key_code, query_code = plan
    _, length, width = qkv.shape
    pairs = width // PAIR
    blocks = length // ROWS
    w_qkv = weights[0]

    def whole(shape):
        return pl.BlockSpec(shape, lambda *_: (0,) * len(shape))

    row = pltpu.VMEM((length, width), BF)
    return pl.pallas_call(
        partial(mixed_backward_kernel, layer),
        name="mixed_backward",
        grid_spec=pltpu.PrefetchScalarGridSpec(
            num_scalar_prefetch=3,
            grid=(1,),
            in_specs=[ANY, whole(key_code.shape), whole(query_code.shape), ANY, whole(logsum.shape)]
            + [ANY] * 4,
            out_specs=[ANY, ANY, whole((2, width))],
            scratch_shapes=[
                *held_shapes(w_qkv),
                pltpu.VMEM((3, length, width), BF),
                row, row, row,
                pltpu.VMEM((pairs, PAIR, length), BF),
                pltpu.VMEM((pairs, 2 * QB, PAIR), BF),
                pltpu.VMEM((pairs, 2 * QB, PAIR), BF),
                pltpu.VMEM((pairs, PAIR, 2 * QB), F32),
                pltpu.VMEM((length, width), F32),
                pltpu.VMEM((length, width), F32),
                pltpu.SemaphoreType.DMA((1,)),
                pltpu.SemaphoreType.DMA((4,)),
                pltpu.SemaphoreType.DMA((1,)),
                pltpu.SemaphoreType.DMA((blocks,)),
            ],
        ),
        out_shape=[
            jax.ShapeDtypeStruct((3, length, width), BF),
            jax.ShapeDtypeStruct((length, width), BF),
            jax.ShapeDtypeStruct((2, width), F32),
        ],
        compiler_params=PARAMS,
        cost_estimate=cost(38),
    )(begin, count, sel, qkv, key_code, query_code, context, logsum, grad_context, skip, *w_qkv)


def layer_backward(sel, grad, kept, weights, layer, plan):
    grad_context, grads, sums = feed_backward(sel, grad, kept, weights, layer)
    grad_mixed, grad_x, mix_sums = mixed_backward(
        sel, grad_context, grads[2], kept, weights, layer, plan
    )
    return (grad_x, grads + (grad_mixed,), sums + (mix_sums,))


def swap_cores(value):
    return send(value, ((0, 1), (1, 0), (2, 3), (3, 2)))


def send(value, routes):
    return lax.ppermute(value, "section", routes)


def pick_row(value, at, axis=0):
    return lax.dynamic_index_in_dim(value, at, axis, keepdims=False)


def plus(*values):
    return sum(value.astype(F32) for value in values).astype(BF)


class RowSum:
    def __init__(self, mine, arrived, blocks):
        self.value, self.blocks, self.travelling = (mine, arrived), blocks, None
        self.plain = lax.axis_size("dp") != SHARDS
        if not self.plain:
            at = lax.axis_index("dp")
            self.z, self.x, self.line_at = at // 2, at % 2, 0

    def state(self):
        return (self.value, self.travelling)

    def set(self, state):
        self.value, self.travelling = state

    def cross(self):
        if self.plain:
            return
        values = [part.reshape(4, 2, *part.shape[1:]) for part in self.value]
        other = plus(*[pick_row(part, 1 - self.x, 1) for part in values])
        arrived = lax.ppermute(other, "dp", [(n, n ^ 1) for n in range(8)])
        self.value = plus(*[pick_row(part, self.x, 1) for part in values], arrived)

    def line(self):
        if self.plain:
            return
        self.line_at += 1
        far = 4 - self.line_at
        right = pick_row(self.value, jnp.minimum(self.z + far, 3))
        left = pick_row(self.value, jnp.maximum(self.z - far, 0))
        if self.travelling is not None:
            right, left = plus(right, self.travelling[0]), plus(left, self.travelling[1])
        self.travelling = (
            lax.ppermute(right, "dp", [(n, n + 2) for n in range(6)]),
            lax.ppermute(left, "dp", [(n + 2, n) for n in range(6)]),
        )

    def direct(self):
        if self.plain:
            return
        arrived = []
        for far in (3, 2, 1):
            for way in (far, -far):
                part = pick_row(self.value, jnp.clip(self.z + way, 0, 3))
                routes = [(n, n + 2 * way) for n in range(8) if 0 <= n + 2 * way < 8]
                arrived.append(lax.ppermute(part, "dp", routes))
        self.travelling = tuple(arrived)

    def result(self):
        if not self.plain:
            return plus(pick_row(self.value, self.z), *self.travelling)
        shards = lax.axis_size("dp")
        parts, at, value = [], 0, plus(*self.value)
        for rows in self.blocks:
            part = value[:, at : at + rows].reshape(shards, -1, value.shape[2])
            parts, at = parts + [part], at + rows
        whole = jnp.concatenate(parts, axis=1)
        return lax.psum_scatter(whole, "dp", scatter_dimension=0, tiled=True)[0]


def body(
    tokens_in, seg_starts, pad_mask, w_qkv, b_qv, w_attn_out, b_attn_out, ln_gain, ln_bias,
    w_up, b_up, w_down, b_down, w_proj, cotangent,
):
    section_at = lax.axis_index("section")
    core = section_at % 2
    is_late = section_at >= 2
    flip = core == 1
    quarter = tokens_in.shape[1]
    length, width = 4 * quarter, tokens_in.shape[2]
    ff_width = w_up.shape[2]
    proj_cols = w_proj.shape[1]
    shards = lax.axis_size("dp")
    share = width // shards

    def sel_for(half):
        return jnp.stack([core, section_at // 2, half]).astype(jnp.int32)

    sel_mine, sel_theirs = sel_for(core), sel_for(1 - core)

    own = pick_row(tokens_in, core)
    other = pick_row(tokens_in, 1 - core)
    straight = send(own, [(2, 0), (3, 1)])
    crossed = send(other, [(2, 1), (3, 0)])
    near = swap_cores(other)
    small = pack_small(b_qv[0], b_attn_out[0], ln_gain[0], ln_bias[0], b_up[0], b_down[0])[None]
    small_other = swap_cores(small)
    small = jnp.stack([jnp.where(flip, small_other, small), jnp.where(flip, small, small_other)])
    weights = tuple((w[0], swap_cores(w[0])) for w in (w_qkv, w_attn_out, w_up, w_down)) + (small,)
    x = jnp.concatenate(
        [
            jnp.where(flip, near, own),
            jnp.where(flip, own, near),
            jnp.where(flip, crossed, straight),
            jnp.where(flip, straight, crossed),
        ],
        axis=0,
    )

    head_own = jnp.concatenate([w_proj.T, pick_row(cotangent, core).T], axis=1)
    head_other = jnp.concatenate([w_proj.T, pick_row(cotangent, 1 - core).T], axis=1)
    head_late = send(head_other, [(2, 3), (3, 2)])
    head_straight = send(head_own, [(0, 2), (1, 3)])
    head_crossed = send(head_other, [(0, 3), (1, 2)])
    head_cols = jnp.concatenate(
        [
            jnp.where(flip, head_crossed, head_straight),
            jnp.where(flip, head_straight, head_crossed),
            jnp.where(flip, head_late, head_own),
            jnp.where(flip, head_own, head_late),
        ],
        axis=0,
    )
    proj_rows, given_rows = head_cols[:, :width], head_cols[:, width:]
    plan = attention_plan(pick_row(seg_starts, core), pick_row(pad_mask, core))

    def both_forward(rows):
        middle, kept_even = layer_forward(sel_mine, rows, weights, 0, plan)
        last, kept_odd = layer_forward(sel_mine, middle, weights, 1, plan)
        return (last, kept_even, kept_odd)

    early, kept_even, kept_odd = both_forward(x)
    hopped = send(early, [(0, 2), (1, 3)])
    hopped, proj_rows, given_rows = lax.optimization_barrier((hopped, proj_rows, given_rows))

    def late_turn(rows, *_):
        last, kept_even, kept_odd = both_forward(rows)
        embedded, grad_proj, grad = head(last, proj_rows, given_rows)
        grad, grads_odd, sums_odd = layer_backward(sel_mine, grad, kept_odd, weights, 1, plan)
        grad, grads_even, sums_even = layer_backward(sel_mine, grad, kept_even, weights, 0, plan)
        return (
            kept_even, kept_odd, embedded, grad_proj, grad,
            grads_odd, sums_odd, grads_even, sums_even,
        )

    def early_turn(rows, kept_even, kept_odd):
        row, ff = jnp.zeros((length, width), BF), jnp.zeros((length, ff_width), BF)
        grads = (row, ff, row, jnp.zeros((3, length, width), BF))
        sums = (
            jnp.zeros((6, width), F32),
            jnp.zeros((1, ff_width), F32),
            jnp.zeros((2, width), F32),
        )
        return (
            kept_even, kept_odd, jnp.zeros((4 * proj_cols, length), BF),
            jnp.zeros((width, 4 * proj_cols), BF), row, grads, sums, grads, sums,
        )

    (
        kept_even, kept_odd, embedded, grad_proj, grad_mid,
        late_odd, late_sums_odd, late_even, late_sums_even,
    ) = lax.cond(is_late, late_turn, early_turn, hopped, kept_even, kept_odd)

    grad = send(grad_mid, [(2, 0), (3, 1)])
    embedded_cols = embedded.reshape(4, proj_cols, length)

    rows_of_one = width // SHARDS
    attend_blocks = (rows_of_one,) * 4
    feed_blocks = (rows_of_one,) * (ff_width // (2 * HALF)) + (ff_width // SHARDS,)

    def tie(*values):
        return lax.optimization_barrier(values)

    def feed_args(kept, late, now):
        return (kept[4], late[1], now[1], kept[9], late[0], now[0])

    def attend_args(kept, late, now, mixed):
        return (kept[2], kept[0], late[2], now[2], late[3], mixed)

    def tie_sums(values, *sums):
        values, states = tie(values, [part.state() for part in sums])
        for part, state in zip(sums, states):
            part.set(state)
        return values

    grad_context, grads_odd, sums_odd = feed_backward(sel_mine, grad, kept_odd, weights, 1)
    args = feed_args(kept_odd, late_odd, grads_odd)
    arrived = swap_cores(feed_grads(sel_theirs, *args))
    feed_odd = RowSum(feed_grads(sel_mine, *args), arrived, feed_blocks)
    grad_context = tie_sums(grad_context, feed_odd)
    feed_odd.cross()
    straight_cols = send(pick_row(embedded_cols, core), [(2, 0), (3, 1)])
    crossed_cols = send(pick_row(embedded_cols, 1 - core), [(2, 1), (3, 0)])
    near_cols = swap_cores(pick_row(embedded_cols, 3 - core))
    mixed_odd, grad, mix_sums = mixed_backward(
        sel_mine, grad_context, grads_odd[2], kept_odd, weights, 1, plan
    )
    sums_odd = sums_odd + (mix_sums,)
    args = attend_args(kept_odd, late_odd, grads_odd, mixed_odd)
    args, straight_cols, crossed_cols, near_cols = tie_sums(
        (args, straight_cols, crossed_cols, near_cols), feed_odd
    )
    feed_odd.line()
    theirs = attend_grads(sel_theirs, *args)
    args, theirs = tie_sums((args, theirs), feed_odd)
    arrived = swap_cores(theirs)
    attend_odd = RowSum(attend_grads(sel_mine, *args), arrived, attend_blocks)
    grad = tie_sums(grad, feed_odd, attend_odd)
    feed_odd.line()
    attend_odd.cross()

    grad_context, grads_even, sums_even = feed_backward(sel_mine, grad, kept_even, weights, 0)
    args = tie_sums(feed_args(kept_even, late_even, grads_even), feed_odd, attend_odd)
    feed_odd.line()
    theirs = feed_grads(sel_theirs, *args)
    args, theirs = tie_sums((args, theirs), feed_odd)
    arrived = swap_cores(theirs)
    feed_even = RowSum(feed_grads(sel_mine, *args), arrived, feed_blocks)
    grad_context = tie_sums(grad_context, feed_even, attend_odd)
    feed_even.cross()
    attend_odd.direct()
    mixed_even, grad, mix_sums = mixed_backward(
        sel_mine, grad_context, grads_even[2], kept_even, weights, 0, plan
    )
    sums_even = sums_even + (mix_sums,)
    args = attend_args(kept_even, late_even, grads_even, mixed_even)
    args = tie_sums(args, feed_even, attend_odd)
    feed_even.line()
    theirs = attend_grads(sel_theirs, *args)
    extras = pack_extras(sel_mine, grad_proj, late_sums_even, late_sums_odd, sums_even, sums_odd)
    theirs = jnp.concatenate([theirs, extras.astype(BF)], axis=1)
    args, theirs, extras = tie_sums((args, theirs, extras), feed_even)
    arrived = swap_cores(theirs)
    feed_even.line()
    quarters = grad.reshape(4, quarter, width)
    near_grad = swap_cores(pick_row(quarters, 1 - core))
    mine = jnp.concatenate([attend_grads(sel_mine, *args), extras.astype(BF)], axis=1)
    mine, quarters, near_grad = tie_sums((mine, quarters, near_grad), feed_even)
    attend_even = RowSum(mine, arrived, attend_blocks)
    attend_even.cross()
    feed_even.line()
    straight_grad = send(pick_row(quarters, 2 + core), [(0, 2), (1, 3)])
    crossed_grad = send(pick_row(quarters, 3 - core), [(0, 3), (1, 2)])
    feed_odd, attend_odd = feed_odd.result(), attend_odd.result()
    straight_grad, crossed_grad = tie_sums((straight_grad, crossed_grad), feed_even, attend_even)
    attend_even.direct()
    feed_even = feed_even.result()
    if shards == SHARDS:
        tail = attend_even.result()
        attend_even, extras = tail[: 4 * share], tail[4 * share :].astype(F32)
    else:
        attend_even = attend_even.result()
        extras = plus(mine[:, -EXTRA_ROWS:], arrived[:, -EXTRA_ROWS:])
        extras = lax.psum(extras.astype(F32), "dp")

    routes_odd, routes_even = ((0, 1), (2, 3)), ((1, 0), (3, 2))

    def halves(even, odd):
        arrived = jnp.where(flip, send(odd, routes_odd), send(even, routes_even))
        mine = jnp.where(flip, odd, even)
        return (jnp.where(flip, arrived, mine), jnp.where(flip, mine, arrived))

    blocks = ff_width // (2 * HALF)
    feed_halves = halves(feed_even, feed_odd)
    attend_halves = halves(attend_even, attend_odd)

    def columns(pair, first, count):
        parts = [part[n * share : (n + 1) * share] for part in pair for n in range(first, first + count)]
        return jnp.concatenate(parts, axis=1).astype(F32)

    grad_w_up = columns(feed_halves, 0, blocks)[None]
    grad_w_down = jnp.concatenate([part[blocks * share :] for part in feed_halves], axis=1)
    grad_w_down = grad_w_down.astype(F32)[None]
    grad_w_out = columns(attend_halves, 0, 1)[None]
    grad_w_qkv = jnp.concatenate([columns(attend_halves, 1 + c, 1) for c in range(3)], axis=1)[None]

    if shards == SHARDS:
        at, pick = 0, lambda values: values
    else:
        at = lax.axis_index("dp") % (shards // SHARDS)
        extras = pick_row(extras, lax.axis_index("dp") // (shards // SHARDS))

        def pick(values):
            size = values.shape[-1] * SHARDS // shards
            return lax.dynamic_slice_in_dim(values, at * size, size, values.ndim - 1)

    one = width // SHARDS
    small_mine = jnp.where(flip, extras[8:16], extras[:8])
    grad_b_up = pick(small_mine[0:1, : ff_width // SHARDS])
    grad_b_qv = pick(small_mine[1:2, : 2 * one])
    rows = pick(small_mine[2:8, :one])
    grad_proj = extras[16:].reshape(-1, 3, 4 * proj_cols).transpose(1, 0, 2)
    grad_proj = grad_proj.reshape(one, 4 * proj_cols)
    grad_proj = lax.dynamic_slice_in_dim(grad_proj, at * share, share, 0).astype(BF)
    grad_proj = jnp.where(is_late, grad_proj, send(grad_proj, [(2, 0), (3, 1)])).astype(F32)
    grad_w_proj = lax.dynamic_slice_in_dim(grad_proj, section_at * proj_cols, proj_cols, 1)

    own_cols = jnp.where(is_late, pick_row(embedded_cols, section_at), straight_cols)
    other_cols = jnp.where(is_late, near_cols, crossed_cols)
    embedded_out = jnp.stack(
        [jnp.where(flip, other_cols, own_cols).T, jnp.where(flip, own_cols, other_cols).T]
    )

    mine = jnp.where(is_late, straight_grad, pick_row(quarters, core))
    others = jnp.where(is_late, crossed_grad, near_grad)
    grad_in = jnp.stack(
        [jnp.where(flip, others, mine), jnp.where(flip, mine, others)]
    ).astype(F32)

    return (
        embedded_out,
        grad_in,
        grad_w_qkv,
        grad_b_qv,
        grad_w_out,
        rows[0][None],
        rows[1:3][None],
        rows[3:5][None],
        grad_w_up,
        grad_b_up,
        grad_w_down,
        rows[5][None],
        grad_w_proj,
    )


def solution(mesh):
    in_specs = (
        P("dp", "section", None),
        P("dp", None),
        P("dp", None),
        P("section", None, None),
        P("section", None),
        P("section", None, None),
        P("section", None),
        P("section", None, None),
        P("section", None, None),
        P("section", None, None),
        P("section", None),
        P("section", None, None),
        P("section", None),
        P(None, "section"),
        P("dp", None, "section"),
    )
    out_specs = (
        P("dp", None, "section"),
        P("dp", "section", None),
        P("section", "dp", None),
        P("section", "dp"),
        P("section", "dp", None),
        P("section", "dp"),
        P("section", None, "dp"),
        P("section", None, "dp"),
        P("section", "dp", None),
        P("section", "dp"),
        P("section", "dp", None),
        P("section", "dp"),
        P("dp", "section"),
    )
    return jax.shard_map(body, mesh=mesh, in_specs=in_specs, out_specs=out_specs, check_vma=False)
```

```python
from functools import partial
import math

import jax
import jax.numpy as jnp
from jax import lax
from jax.experimental import pallas as pl
from jax.experimental.pallas import tpu as pltpu
from jax.sharding import PartitionSpec as P

HEAD = 64
PAIR = 2 * HEAD
QB = 128
KB = 512
KEYS = 256
EPS_NORM = 1e-05
EPS_PROJ = 1e-06
NEG_FILL = -1e30
PARAMS = pltpu.CompilerParams(vmem_limit_bytes=60 * 1024 * 1024)


def cost(micros):
    return pl.CostEstimate(flops=int(micros * 1e9), bytes_accessed=1024, transcendentals=0)


BF = jnp.bfloat16
F32 = jnp.float32

NT = (((1,), (1,)), ((), ()))
TN = (((0,), (0,)), ((), ()))


def dot(a, b):
    return jnp.dot(a, b, preferred_element_type=F32)


def dot_nt(a, b):
    return lax.dot_general(a, b, NT, preferred_element_type=F32)


def dot_tn(a, b):
    return lax.dot_general(a, b, TN, preferred_element_type=F32)


def pack_small(b_qv, b_out, gains, shifts, b_up, b_down):
    return jnp.concatenate(
        [b_up, b_qv, b_out, gains[0], gains[1], shifts[0], shifts[1], b_down]
    )


def small_spec(layer, width):
    return pl.BlockSpec((1, 1, width), lambda *_: (layer, 0, 0))


def attention_plan(starts, real_flags):
    length = real_flags.shape[0]
    places = jnp.arange(length, dtype=jnp.int32)
    segment = jnp.sum((starts[None, :] <= places[:, None]).astype(jnp.int32), axis=1)
    key_code = jnp.where(real_flags == 1, segment, -1).astype(F32)
    key_code = jnp.broadcast_to(key_code[:, None], (length, PAIR))
    query_code = segment.astype(F32).reshape(length // QB, QB)
    first = jnp.arange(length // QB, dtype=jnp.int32) * QB
    low = jnp.max(jnp.where(starts[None, :] <= first[:, None], starts[None, :], 0), axis=1)
    high = jnp.min(
        jnp.where(starts[None, :] > first[:, None] + (QB - 1), starts[None, :], length), axis=1
    )
    begin = (low // QB) * QB
    count = (high - begin + KEYS - 1) // KEYS
    begin = jnp.minimum(begin, length - KEYS * count)
    return (begin, count, key_code, query_code)


def pair_mask(rows):
    return lax.broadcasted_iota(jnp.int32, (rows, PAIR), 1) < HEAD


def stacked_heads(block):
    first = pair_mask(block.shape[0])
    zero = jnp.zeros_like(block)
    return jnp.concatenate([jnp.where(first, block, zero), jnp.where(first, zero, block)], axis=0)


def block_bias(key_code, query_code, key_at, query_at):
    shape = key_code.shape
    keys = lax.broadcasted_iota(jnp.int32, shape, 0) + (key_at - query_at)
    same = keys == lax.broadcasted_iota(jnp.int32, shape, 1)
    bias = jnp.where((key_code == query_code) | same, 0.0, NEG_FILL)
    return jnp.concatenate([bias, bias], axis=1)


def over_keys(begin, count, step, state):
    state = lax.fori_loop(
        0,
        lax.shift_right_logical(count, 1),
        lambda j, now: step(pl.multiple_of(begin + j * KB, QB), KB, now),
        state,
    )
    last = pl.multiple_of(begin + (count - 1) * KEYS, QB)
    return lax.fori_loop(
        0, jnp.bitwise_and(count, 1), lambda _, now: step(last, KEYS, now), state
    )


def unstack_heads(flat):
    rows = lax.broadcasted_iota(jnp.int32, (PAIR, QB), 0)
    return jnp.where(rows < HEAD, flat[:PAIR, :QB], flat[:PAIR, QB:]).T


def attend_forward(
    begin_ref, count_ref, qkv_ref, key_code_ref, query_code_ref, out_ref, logsum_ref,
    value_scr, query_scr, total_scr,
):
    length = qkv_ref.shape[1]
    pairs = qkv_ref.shape[2] // PAIR
    every = range(pairs)
    cols = [slice(p * PAIR, (p + 1) * PAIR) for p in every]
    for p in every:
        value_scr[p, :PAIR, :] = qkv_ref[2, :, cols[p]].T
        value_scr[p, PAIR:, :] = jnp.ones((value_scr.shape[1] - PAIR, length), BF)

    def one_query_block(i, _):
        query_at = pl.multiple_of(i * QB, QB)
        begin, count = begin_ref[i], count_ref[i]
        query_code = query_code_ref[pl.ds(i, 1), :]
        for p in every:
            query_scr[p] = stacked_heads(qkv_ref[0, pl.ds(query_at, QB), cols[p]])
        total_scr[...] = jnp.zeros_like(total_scr)

        def one_key_block(key_at, size, tops):
            rows = pl.ds(key_at, size)
            bias = block_bias(key_code_ref[rows, :], query_code, key_at, query_at)
            scores = [dot_nt(qkv_ref[1, rows, cols[p]], query_scr[p]) + bias for p in every]
            fresh = [
                jnp.maximum(tops[p], jnp.max(scores[p], axis=0, keepdims=True)) for p in every
            ]
            probs = [jnp.exp(scores[p] - fresh[p]).astype(BF) for p in every]
            for p in every:
                total_scr[p] = total_scr[p] * jnp.exp(tops[p] - fresh[p]) + dot(
                    value_scr[p, :, rows], probs[p]
                )
            return tuple(fresh)

        tops = tuple(jnp.full((1, 2 * QB), 2 * NEG_FILL, F32) for _ in every)
        tops = over_keys(begin, count, one_key_block, tops)
        for p in every:
            weight = total_scr[p, PAIR : PAIR + 1, :]
            logsum_ref[pl.ds(p * (length // QB) + i, 1), :] = tops[p] + jnp.log(weight)
            out_ref[pl.ds(query_at, QB), cols[p]] = unstack_heads(
                total_scr[p, :PAIR, :] * (1.0 / weight)
            ).astype(BF)
        return 0

    lax.fori_loop(0, length // QB, one_query_block, 0)


def attend_backward(
    begin_ref, count_ref, qkv, key_code_ref, query_code_ref, context, logsum_ref, grad, sums_ref,
    key_scr, query_scr, given_scr, down_scr, grad_key_scr, grad_value_scr,
):
    length = qkv.shape[1]
    pairs = qkv.shape[2] // PAIR
    every = range(pairs)
    blocks = length // QB
    cols = [slice(p * PAIR, (p + 1) * PAIR) for p in every]
    for p in every:
        key_scr[p] = qkv[1, :, cols[p]].T

    def one_query_block(i, _):
        query_at = pl.multiple_of(i * QB, QB)
        queries = pl.ds(query_at, QB)
        begin, count = begin_ref[i], count_ref[i]
        query_code = query_code_ref[pl.ds(i, 1), :]
        inner, logsum = [], []
        for p in every:
            query_scr[p] = stacked_heads(qkv[0, queries, cols[p]])
            given = grad[queries, cols[p]]
            given_scr[p] = stacked_heads(given)
            both = (given.astype(F32) * context[queries, cols[p]].astype(F32)).T
            inner.append(
                jnp.concatenate(
                    [
                        jnp.sum(both[:HEAD], axis=0, keepdims=True),
                        jnp.sum(both[HEAD:], axis=0, keepdims=True),
                    ],
                    axis=1,
                )
            )
            logsum.append(logsum_ref[pl.ds(p * blocks + i, 1), :])
        down_scr[...] = jnp.zeros_like(down_scr)

        def one_key_block(key_at, size, state):
            rows = pl.ds(key_at, size)
            bias = block_bias(key_code_ref[rows, :], query_code, key_at, query_at)
            grads = [
                (dot_nt(qkv[2, rows, cols[p]], given_scr[p]) - inner[p]).astype(BF) for p in every
            ]
            parts = [dot_nt(qkv[1, rows, cols[p]], query_scr[p]) + bias for p in every]
            probs = [jnp.exp(parts[p] - logsum[p]).astype(BF) for p in every]
            scores = [probs[p] * grads[p] for p in every]
            for p in every:
                grad_value_scr[rows, cols[p]] += dot(probs[p], given_scr[p])
            for p in every:
                grad_key_scr[rows, cols[p]] += dot(scores[p], query_scr[p])
            for p in every:
                down_scr[p] += dot(key_scr[p, :, rows], scores[p])
            return state

        over_keys(begin, count, one_key_block, 0)
        for p in every:
            grad_query = (unstack_heads(down_scr[p]) * (HEAD**-0.5)).astype(BF)
            qkv[0, queries, cols[p]] = grad_query
            sums_ref[0:1, cols[p]] += jnp.sum(grad_query.astype(F32), axis=0, keepdims=True)
        return 0

    lax.fori_loop(0, blocks, one_query_block, 0)
    qkv[1] = grad_key_scr[...].astype(BF)
    grad_value = grad_value_scr[...].astype(BF)
    qkv[2] = grad_value
    sums_ref[1:2, :] = jnp.sum(grad_value.astype(F32), axis=0, keepdims=True)


ANY = pl.BlockSpec(memory_space=pl.ANY)
ROWS = 256


class Held:
    def __init__(self, sel_ref, layer, pairs, held, sems, first=None):
        self.own = sel_ref[0] == layer
        self.items = list(zip(pairs, held, range(len(held))))
        self.sems = sems
        self.first = pl.program_id(0) == 0 if first is None else first

    def start(self):
        for pair, held, n in self.items:
            for wanted, source in zip((self.own, jnp.logical_not(self.own)), pair):

                @pl.when(self.first & wanted)
                def _():
                    pltpu.make_async_copy(source, held, self.sems.at[n]).start()

    def wait(self, n):
        pair, held, _ = self.items[n]

        @pl.when(self.first)
        def _():
            pltpu.make_async_copy(pair[0], held, self.sems.at[n]).wait()


def held_shapes(*weights):
    return [pltpu.VMEM(own.shape, own.dtype) for own, _ in weights]


def normalized(values):
    centred = values - jnp.mean(values, axis=-1, keepdims=True)
    inverse = lax.rsqrt(jnp.mean(centred * centred, axis=-1, keepdims=True) + EPS_NORM)
    return (centred * inverse, inverse)


def normalized_pull(grad_hat, hat, inverse):
    return inverse * (
        grad_hat
        - jnp.mean(grad_hat, axis=-1, keepdims=True)
        - hat * jnp.mean(grad_hat * hat, axis=-1, keepdims=True)
    )


ERF = (0.254829592, -0.284496736, 1.421413741, -1.453152027, 1.061405429)
ERF_SLOPE = 0.3275911


def gelu_parts(x):
    t = pl.reciprocal(1.0 + (ERF_SLOPE * math.sqrt(0.5)) * jnp.abs(x), approx=True)
    bell = jnp.exp(-0.5 * (x * x))
    tail = 0.5 * ERF[4]
    for term in ERF[3::-1]:
        tail = tail * t + 0.5 * term
    tail = tail * t * bell
    below = jnp.where(x >= 0, 1.0 - tail, tail)
    return (x * below, below + x * bell * (1.0 / math.sqrt(2.0 * math.pi)))


FB = 1024


def small_slices(width, ff_width):
    names = ("b_q", "b_v", "b_out", "gain1", "gain2", "shift1", "shift2", "b_down")
    at = {"b_up": slice(0, ff_width)}
    for n, name in enumerate(names):
        at[name] = slice(ff_width + n * width, ff_width + (n + 1) * width)
    return at


def refine_back_kernel(
    layer, sel_ref, grad_ref, hidden_ref, out_ref, scale1_ref, scale2_ref, slope_ref,
    out_own_ref, out_other_ref, up_own_ref, up_other_ref, down_own_ref, down_other_ref, small_ref,
    grad_low_ref, grad_raised_ref, grad_attn_ref, grad_context_ref, sums_ref, up_sums_ref,
    w_out, w_up, w_down, sems,
):
    pairs = [(out_own_ref, out_other_ref), (up_own_ref, up_other_ref), (down_own_ref, down_other_ref)]
    weights = Held(sel_ref, layer, pairs, [w_out, w_up, w_down], sems)
    weights.start()
    rows, width = grad_ref.shape
    ff_width = slope_ref.shape[1]
    at = small_slices(width, ff_width)

    @pl.when(pl.program_id(0) == 0)
    def _():
        sums_ref[...] = jnp.zeros_like(sums_ref)
        up_sums_ref[...] = jnp.zeros_like(up_sums_ref)

    def vector(name):
        return small_ref[0, :, at[name]]

    def add(row, values):
        sums_ref[row : row + 1, :] += jnp.sum(values, axis=0, keepdims=True)

    grad = grad_ref[...].astype(F32)
    hat = (out_ref[...].astype(F32) - vector("shift2")) * (1.0 / vector("gain2"))
    joined = normalized_pull(grad * vector("gain2"), hat, scale2_ref[:, :1])
    low = joined.astype(BF)
    grad_low_ref[...] = low
    add(2, grad * hat)
    add(4, grad)
    add(5, low.astype(F32))
    weights.wait(2)
    weights.wait(1)
    total = joined
    parts = [slice(f, f + FB) for f in range(0, ff_width, FB)]
    active = dot_nt(low, w_down[parts[0], :])
    for n, part in enumerate(parts):
        following = dot_nt(low, w_down[parts[n + 1], :]) if n + 1 < len(parts) else None
        raised = active * slope_ref[:, part].astype(F32)
        up_sums_ref[:, part] += jnp.sum(raised, axis=0, keepdims=True)
        raised = raised.astype(BF)
        grad_raised_ref[:, part] = raised
        total += dot_nt(raised, w_up[:, part])
        active = following
    hat = (hidden_ref[...].astype(F32) - vector("shift1")) * (1.0 / vector("gain1"))
    summed = normalized_pull(total * vector("gain1"), hat, scale1_ref[:, :1])
    attn = summed.astype(BF)
    grad_attn_ref[...] = attn
    weights.wait(0)
    grad_context_ref[...] = dot_nt(attn, w_out[...]).astype(BF)
    add(1, total * hat)
    add(3, total)
    add(0, attn.astype(F32))


def refine_back_second_kernel(layer, *refs):
    refine_back_kernel(layer, *refs[:14], *refs[18:])


def refine_back(sel, grad, kept, weights, layer, first=0, begun=()):
    w_out, w_up, w_down, small = weights
    hidden, out, scale1, scale2, slope = kept
    length, width = hidden.shape
    ff_width = w_up[0].shape[1]
    at = first // ROWS
    rows = pl.BlockSpec((ROWS, width), lambda n, _: (n + at, 0))
    lanes = pl.BlockSpec((ROWS, 128), lambda n, _: (n + at, 0))
    part = pl.BlockSpec((ROWS, ff_width), lambda n, _: (n + at, 0))
    row_shape = jax.ShapeDtypeStruct((length, width), BF)
    return pl.pallas_call(
        partial(refine_back_second_kernel if begun else refine_back_kernel, layer),
        name="refine_back",
        grid_spec=pltpu.PrefetchScalarGridSpec(
            num_scalar_prefetch=1,
            grid=(grad.shape[0] // ROWS,),
            in_specs=[
                pl.BlockSpec((ROWS, width), lambda n, _: (n, 0)),
                rows, rows, lanes, lanes, part,
            ]
            + [ANY] * 6
            + [small_spec(layer, small.shape[2])]
            + [ANY] * len(begun),
            out_specs=[
                rows, part, rows, rows,
                pl.BlockSpec((6, width), lambda n, _: (0, 0)),
                pl.BlockSpec((1, ff_width), lambda n, _: (0, 0)),
            ],
            scratch_shapes=[
                *held_shapes(w_out, w_up, w_down),
                pltpu.SemaphoreType.DMA((3,)),
            ],
        ),
        out_shape=[
            row_shape,
            jax.ShapeDtypeStruct((length, ff_width), BF),
            row_shape,
            row_shape,
            jax.ShapeDtypeStruct((6, width), F32),
            jax.ShapeDtypeStruct((1, ff_width), F32),
        ],
        input_output_aliases={14 + n: n for n in range(len(begun))},
        compiler_params=PARAMS,
        cost_estimate=cost(24),
    )(sel, grad, hidden, out, scale1, scale2, slope, *w_out, *w_up, *w_down, small, *begun)


def head_kernel(rows_ref, proj_ref, given_ref, embedded_ref, grad_proj_ref, grad_rows_ref):
    factor = math.sqrt(proj_ref.shape[0])
    columns = dot_nt(proj_ref[...], rows_ref[...])
    given = given_ref[...].astype(F32)
    inverse = lax.rsqrt(jnp.sum(columns * columns, axis=0, keepdims=True) + EPS_PROJ)
    cross = jnp.sum(columns * given, axis=0, keepdims=True)
    embedded_ref[...] = (factor * columns * inverse).astype(BF)
    grad = (factor * (given * inverse - columns * (cross * inverse * inverse * inverse))).astype(BF)
    grad_proj_ref[...] = dot(grad, rows_ref[...]).T.astype(BF)
    grad_rows_ref[...] = dot_tn(grad, proj_ref[...]).astype(BF)


def head(rows, proj, given):
    length, width = rows.shape
    cols = proj.shape[0]
    return pl.pallas_call(
        head_kernel,
        name="head",
        out_shape=[
            jax.ShapeDtypeStruct((cols, length), BF),
            jax.ShapeDtypeStruct((width, cols), BF),
            jax.ShapeDtypeStruct((length, width), BF),
        ],
        compiler_params=PARAMS,
        cost_estimate=cost(6),
    )(rows, proj, given)


HALF = 384
SHARDS = 8


def feed_grads_kernel(
    sel_ref, hidden_ref, raised_late_ref, raised_ref, active_ref, low_late_ref, low_ref, out_ref
):
    step = pl.program_id(0)
    shards, rows, _ = out_ref.shape
    blocks = raised_ref.shape[1] // HALF
    share = rows // blocks
    late = sel_ref[1] == 1

    def up(raised):
        part = dot_tn(hidden_ref[...], raised).astype(BF)
        for m in range(shards):
            for n in range(blocks):
                out_ref[m, n * share : (n + 1) * share, :] = part[
                    m * share : (m + 1) * share, n * HALF : (n + 1) * HALF
                ]

    def down(low):
        for m in range(shards):
            out_ref[m] = dot_tn(active_ref[:, m * rows : (m + 1) * rows], low).astype(BF)

    for wanted, raised_now, low_now in (
        (late, raised_late_ref, low_late_ref),
        (jnp.logical_not(late), raised_ref, low_ref),
    ):

        @pl.when(wanted & (step < 2))
        def _():
            up(raised_now[...])

        @pl.when(wanted & (step >= 2))
        def _():
            down(low_now[...])


def feed_grads(sel, hidden, raised_late, raised, active, low_late, low):
    length, width = hidden.shape
    ff_width = active.shape[1]
    half_ff = ff_width // 2

    def late_spec(shape, wanted):
        return pl.BlockSpec(shape, lambda n, sel: (0, jnp.where(sel[1] == wanted, sel[2], 0)))

    return pl.pallas_call(
        feed_grads_kernel,
        name="feed_grads",
        grid_spec=pltpu.PrefetchScalarGridSpec(
            num_scalar_prefetch=1,
            grid=(4,),
            in_specs=[
                pl.BlockSpec((length, width // 2), lambda n, _: (0, jnp.minimum(n, 1))),
                late_spec((length, half_ff), 1),
                late_spec((length, half_ff), 0),
                pl.BlockSpec((length, ff_width // 2), lambda n, _: (0, jnp.maximum(n - 2, 0))),
                late_spec((length, width // 2), 1),
                late_spec((length, width // 2), 0),
            ],
            out_specs=pl.BlockSpec(
                (SHARDS // 2, ff_width // SHARDS, HALF), lambda n, _: (lax.rem(n, 2), n // 2, 0)
            ),
        ),
        out_shape=jax.ShapeDtypeStruct((SHARDS, 2 * (ff_width // SHARDS), HALF), BF),
        compiler_params=PARAMS,
        cost_estimate=cost(12),
    )(sel, hidden, raised_late, raised, active, low_late, low)


def attend_grads_kernel(
    sel_ref, context_ref, x_ref, attn_late_ref, attn_ref, mixed_late_ref, mixed_ref, out_ref
):
    step = pl.program_id(0)
    late = sel_ref[1] == 1

    for wanted, attn_now, mixed_now in (
        (late, attn_late_ref, mixed_late_ref),
        (jnp.logical_not(late), attn_ref, mixed_ref),
    ):

        @pl.when(wanted & (step == 0))
        def _():
            part = dot_tn(context_ref[...], attn_now[...]).astype(BF)
            out_ref[...] = part.reshape(out_ref.shape)

        @pl.when(wanted & (step > 0))
        def _():
            part = dot_tn(x_ref[...], mixed_now[0]).astype(BF)
            out_ref[...] = part.reshape(out_ref.shape)


def attend_grads(sel, context, x, attn_late, attn, mixed_late, mixed):
    length, width = x.shape

    def late_spec(wanted):
        return pl.BlockSpec(
            (length, HALF), lambda n, sel: (0, jnp.where(sel[1] == wanted, sel[2], 0))
        )

    def mixed_spec(wanted):
        def at(n, sel):
            return (
                jnp.where(sel[1] == wanted, jnp.maximum(n - 1, 0), 0),
                0,
                jnp.where(sel[1] == wanted, sel[2], 0),
            )

        return pl.BlockSpec((1, length, HALF), at)

    whole = pl.BlockSpec((length, width), lambda n, _: (0, 0))
    share = width // SHARDS
    return pl.pallas_call(
        attend_grads_kernel,
        name="attend_grads",
        grid_spec=pltpu.PrefetchScalarGridSpec(
            num_scalar_prefetch=1,
            grid=(4,),
            in_specs=[whole, whole, late_spec(1), late_spec(0), mixed_spec(1), mixed_spec(0)],
            out_specs=pl.BlockSpec((SHARDS, share, HALF), lambda n, _: (0, n, 0)),
        ),
        out_shape=jax.ShapeDtypeStruct((SHARDS, 4 * share, HALF), BF),
        compiler_params=PARAMS,
        cost_estimate=cost(8),
    )(sel, context, x, attn_late, attn, mixed_late, mixed)


EXTRA_ROWS = 48


def pack_extras_kernel(
    sel_ref, proj_ref,
    late_sums_0, late_up_0, late_mix_0, late_sums_1, late_up_1, late_mix_1,
    sums_0, up_0, mix_0, sums_1, up_1, mix_1, out_ref,
):
    shards = out_ref.shape[0]
    width = sums_0.shape[1]
    share = width // shards
    third = share // 3
    cols = proj_ref.shape[1]
    out_ref[...] = jnp.zeros_like(out_ref)

    def layer(first, sums, up, mix):
        up_share = up.shape[1] // shards
        both = jnp.concatenate([mix[0:1, :], mix[1:2, :]], axis=1)
        for m in range(shards):
            rows = [up[0:1, m * up_share : (m + 1) * up_share]]
            rows += [both[:, 2 * m * share : 2 * (m + 1) * share]]
            rows += [sums[n : n + 1, m * share : (m + 1) * share] for n in range(6)]
            for n, row in enumerate(rows):
                out_ref[m, first + n : first + n + 1, : row.shape[1]] = row

    late = sel_ref[1] == 1
    for wanted, even, odd in (
        (late, (late_sums_0, late_up_0, late_mix_0), (late_sums_1, late_up_1, late_mix_1)),
        (jnp.logical_not(late), (sums_0, up_0, mix_0), (sums_1, up_1, mix_1)),
    ):

        @pl.when(wanted)
        def _():
            layer(0, *even)
            layer(8, *odd)

    for m in range(shards):
        for n in range(3):
            at = m * share + n * third
            out_ref[m, 16:, n * cols : (n + 1) * cols] = proj_ref[at : at + third, :].astype(F32)


def pack_extras(sel, proj, late_even, late_odd, even, odd):
    vmem = pl.BlockSpec(memory_space=pltpu.VMEM)
    return pl.pallas_call(
        pack_extras_kernel,
        name="pack_extras",
        in_specs=[pl.BlockSpec(memory_space=pltpu.SMEM)] + [vmem] * 13,
        out_specs=vmem,
        out_shape=jax.ShapeDtypeStruct((SHARDS, EXTRA_ROWS, HALF), F32),
        compiler_params=PARAMS,
        cost_estimate=cost(3),
    )(sel, proj, *late_even, *late_odd, *even, *odd)


def forward_kernel(
    layer, begin_ref, count_ref, sel_ref, x_hbm, key_code_ref, query_code_ref,
    mix_own_ref, mix_other_ref, out_own_ref, out_other_ref,
    up_own_ref, up_other_ref, down_own_ref, down_other_ref, small_ref,
    qkv_hbm, context_hbm, logsum_ref, out_hbm, hidden_hbm, scale1_ref, scale2_ref,
    active_hbm, slope_hbm,
    w_mix, w_out, w_up, w_down, x, qkv, context, hidden_rows, out_rows, active_rows, slope_rows,
    value_scr, query_scr, total_scr, weight_sems, in_sems, qkv_sems, row_sems, context_sem,
):
    pairs = [
        (mix_own_ref, mix_other_ref), (out_own_ref, out_other_ref),
        (up_own_ref, up_other_ref), (down_own_ref, down_other_ref),
    ]
    length, width = x.shape
    ff_width = w_up.shape[1]
    blocks = length // ROWS
    at = small_slices(width, ff_width)

    def vector(name):
        return small_ref[0, :, at[name]]

    def rows_of(n):
        return pl.ds(pl.multiple_of(n * ROWS, ROWS), ROWS)

    def x_copy(n):
        return pltpu.make_async_copy(x_hbm.at[rows_of(n)], x.at[rows_of(n)], in_sems.at[n])

    def qkv_copy(n):
        return pltpu.make_async_copy(
            qkv.at[:, rows_of(n)], qkv_hbm.at[:, rows_of(n)], qkv_sems.at[n]
        )

    saved = [
        (hidden_rows, hidden_hbm), (out_rows, out_hbm),
        (active_rows, active_hbm), (slope_rows, slope_hbm),
    ]

    def row_copies(n):
        return [
            pltpu.make_async_copy(rows.at[rows_of(n)], whole.at[rows_of(n)], row_sems.at[k, n])
            for k, (rows, whole) in enumerate(saved)
        ]

    weights = Held(sel_ref, layer, pairs, [w_mix, w_out, w_up, w_down], weight_sems, True)
    for n in range(blocks):
        x_copy(n).start()
    weights.start()
    weights.wait(0)

    def mix_rows(n, _):
        x_copy(n).wait()
        rows = rows_of(n)
        part = dot(x[rows, :], w_mix[...])
        qkv[0, rows, :] = ((part[:, :width] + vector("b_q")) * HEAD**-0.5).astype(BF)
        qkv[1, rows, :] = part[:, width : 2 * width].astype(BF)
        qkv[2, rows, :] = (part[:, 2 * width :] + vector("b_v")).astype(BF)
        qkv_copy(n).start()
        return 0

    lax.fori_loop(0, blocks, mix_rows, 0)
    attend_forward(
        begin_ref, count_ref, qkv, key_code_ref, query_code_ref, context, logsum_ref,
        value_scr, query_scr, total_scr,
    )
    context_copy = pltpu.make_async_copy(context, context_hbm, context_sem)
    context_copy.start()
    for n in (1, 2, 3):
        weights.wait(n)

    def refine_rows(n, _):
        rows = rows_of(n)
        summed = x[rows, :].astype(F32) + dot(context[rows, :], w_out[...]) + vector("b_out")
        hat, inverse = normalized(summed)
        hidden = hat * vector("gain1") + vector("shift1")
        scale1_ref[rows, :] = jnp.broadcast_to(inverse, (ROWS, 128))
        hidden_low = hidden.astype(BF)
        hidden_rows[rows, :] = hidden_low
        total = hidden + vector("b_down")
        parts = [slice(f, f + FB) for f in range(0, ff_width, FB)]
        raised = dot(hidden_low, w_up[:, parts[0]])
        for m, part in enumerate(parts):
            following = dot(hidden_low, w_up[:, parts[m + 1]]) if m + 1 < len(parts) else None
            active, slope = gelu_parts(raised + small_ref[0, :, part])
            active = active.astype(BF)
            active_rows[rows, part] = active
            slope_rows[rows, part] = slope.astype(BF)
            total += dot(active, w_down[part, :])
            raised = following
        hat, inverse = normalized(total)
        scale2_ref[rows, :] = jnp.broadcast_to(inverse, (ROWS, 128))
        out_rows[rows, :] = (hat * vector("gain2") + vector("shift2")).astype(BF)
        for copy in row_copies(n):
            copy.start()
        return 0

    lax.fori_loop(0, blocks, refine_rows, 0)
    context_copy.wait()
    for n in range(blocks):
        qkv_copy(n).wait()
        for copy in row_copies(n):
            copy.wait()


def layer_forward(sel, x, weights, layer, plan):
    w_qkv, w_out, w_up, w_down, small = weights
    begin, count, key_code, query_code = plan
    length, width = x.shape
    ff_width = w_up[0].shape[1]
    pairs = width // PAIR
    blocks = length // ROWS

    def whole(shape):
        return pl.BlockSpec(shape, lambda *_: (0,) * len(shape))

    row = jax.ShapeDtypeStruct((length, width), BF)
    lanes = jax.ShapeDtypeStruct((length, 128), F32)
    wide = jax.ShapeDtypeStruct((length, ff_width), BF)
    logsum_shape = (pairs * (length // QB), 2 * QB)
    qkv, context, logsum, out, hidden, scale1, scale2, active, slope = pl.pallas_call(
        partial(forward_kernel, layer),
        name="layer_forward",
        grid_spec=pltpu.PrefetchScalarGridSpec(
            num_scalar_prefetch=3,
            grid=(1,),
            in_specs=[ANY, whole(key_code.shape), whole(query_code.shape)]
            + [ANY] * 8
            + [small_spec(layer, small.shape[2])],
            out_specs=[
                ANY, ANY, whole(logsum_shape), ANY, ANY,
                whole((length, 128)), whole((length, 128)), ANY, ANY,
            ],
            scratch_shapes=[
                *held_shapes(w_qkv, w_out, w_up, w_down),
                pltpu.VMEM((length, width), BF),
                pltpu.VMEM((3, length, width), BF),
                pltpu.VMEM((length, width), BF),
                pltpu.VMEM((length, width), BF),
                pltpu.VMEM((length, width), BF),
                pltpu.VMEM((length, ff_width), BF),
                pltpu.VMEM((length, ff_width), BF),
                pltpu.VMEM((pairs, PAIR + 16, length), BF),
                pltpu.VMEM((pairs, 2 * QB, PAIR), BF),
                pltpu.VMEM((pairs, PAIR + 16, 2 * QB), F32),
                pltpu.SemaphoreType.DMA((4,)),
                pltpu.SemaphoreType.DMA((blocks,)),
                pltpu.SemaphoreType.DMA((blocks,)),
                pltpu.SemaphoreType.DMA((4, blocks)),
                pltpu.SemaphoreType.DMA,
            ],
        ),
        out_shape=[
            jax.ShapeDtypeStruct((3, length, width), BF), row,
            jax.ShapeDtypeStruct(logsum_shape, F32), row, row, lanes, lanes, wide, wide,
        ],
        compiler_params=PARAMS,
        cost_estimate=cost(48),
    )(begin, count, sel, x, key_code, query_code, *w_qkv, *w_out, *w_up, *w_down, small)
    return (out, (x, qkv, context, logsum, hidden, out, scale1, scale2, slope, active))


def feed_backward(sel, grads, kept, weights, layer):
    first, begun, totals = 0, (), []
    for grad in grads:
        *begun, sums, up_sums = refine_back(
            sel, grad, kept[4:9], weights[1:], layer, first, tuple(begun)
        )
        first += grad.shape[0]
        totals.append((sums, up_sums))
    grad_low, grad_raised, grad_attn, grad_context = begun
    sums = tuple(sum(parts) for parts in zip(*totals))
    return (grad_context, (grad_low, grad_raised, grad_attn), sums)


def mixed_backward_kernel(
    layer, begin_ref, count_ref, sel_ref, qkv_hbm, key_code_ref, query_code_ref, context_hbm,
    logsum_ref, grad_hbm, skip_hbm, mix_own_ref, mix_other_ref,
    mixed_hbm, grad_x_hbm, sums_ref,
    w_mix, qkv, context, grad, skip, key_scr, query_scr, given_scr, down_scr,
    grad_key_scr, grad_value_scr, weight_sems, in_sems, mixed_sems, row_sems,
):
    length, width = skip.shape
    blocks = length // ROWS
    weights = Held(sel_ref, layer, [(mix_own_ref, mix_other_ref)], [w_mix], weight_sems, True)
    arrays = [(qkv_hbm, qkv), (context_hbm, context), (grad_hbm, grad), (skip_hbm, skip)]
    loads = [
        pltpu.make_async_copy(whole, held, in_sems.at[n]) for n, (whole, held) in enumerate(arrays)
    ]
    for load in loads:
        load.start()
    weights.start()
    grad_key_scr[...] = jnp.zeros_like(grad_key_scr)
    grad_value_scr[...] = jnp.zeros_like(grad_value_scr)
    sums_ref[...] = jnp.zeros_like(sums_ref)
    for load in loads:
        load.wait()
    attend_backward(
        begin_ref, count_ref, qkv, key_code_ref, query_code_ref, context, logsum_ref, grad,
        sums_ref, key_scr, query_scr, given_scr, down_scr, grad_key_scr, grad_value_scr,
    )
    store = pltpu.make_async_copy(qkv, mixed_hbm, mixed_sems.at[0])
    store.start()
    weights.wait(0)

    def rows_of(n):
        return pl.ds(pl.multiple_of(n * ROWS, ROWS), ROWS)

    def row_copy(n):
        return pltpu.make_async_copy(skip.at[rows_of(n)], grad_x_hbm.at[rows_of(n)], row_sems.at[n])

    def unmix_rows(n, _):
        rows = rows_of(n)
        total = skip[rows, :].astype(F32)
        for c in range(3):
            total += dot_nt(qkv[c, rows, :], w_mix[:, c * width : (c + 1) * width])
        skip[rows, :] = total.astype(BF)
        row_copy(n).start()
        return 0

    lax.fori_loop(0, blocks, unmix_rows, 0)
    store.wait()
    for n in range(blocks):
        row_copy(n).wait()


def mixed_backward(sel, grad_context, skip, kept, weights, layer, plan):
    _, qkv, context, logsum = kept[:4]
    begin, count, key_code, query_code = plan
    _, length, width = qkv.shape
    pairs = width // PAIR
    blocks = length // ROWS
    w_qkv = weights[0]

    def whole(shape):
        return pl.BlockSpec(shape, lambda *_: (0,) * len(shape))

    row = pltpu.VMEM((length, width), BF)
    return pl.pallas_call(
        partial(mixed_backward_kernel, layer),
        name="mixed_backward",
        grid_spec=pltpu.PrefetchScalarGridSpec(
            num_scalar_prefetch=3,
            grid=(1,),
            in_specs=[ANY, whole(key_code.shape), whole(query_code.shape), ANY, whole(logsum.shape)]
            + [ANY] * 4,
            out_specs=[ANY, ANY, whole((2, width))],
            scratch_shapes=[
                *held_shapes(w_qkv),
                pltpu.VMEM((3, length, width), BF),
                row, row, row,
                pltpu.VMEM((pairs, PAIR, length), BF),
                pltpu.VMEM((pairs, 2 * QB, PAIR), BF),
                pltpu.VMEM((pairs, 2 * QB, PAIR), BF),
                pltpu.VMEM((pairs, PAIR, 2 * QB), F32),
                pltpu.VMEM((length, width), F32),
                pltpu.VMEM((length, width), F32),
                pltpu.SemaphoreType.DMA((1,)),
                pltpu.SemaphoreType.DMA((4,)),
                pltpu.SemaphoreType.DMA((1,)),
                pltpu.SemaphoreType.DMA((blocks,)),
            ],
        ),
        out_shape=[
            jax.ShapeDtypeStruct((3, length, width), BF),
            jax.ShapeDtypeStruct((length, width), BF),
            jax.ShapeDtypeStruct((2, width), F32),
        ],
        compiler_params=PARAMS,
        cost_estimate=cost(38),
    )(begin, count, sel, qkv, key_code, query_code, context, logsum, grad_context, skip, *w_qkv)


def layer_backward(sel, grad, kept, weights, layer, plan):
    grad_context, grads, sums = feed_backward(sel, (grad,), kept, weights, layer)
    grad_mixed, grad_x, mix_sums = mixed_backward(
        sel, grad_context, grads[2], kept, weights, layer, plan
    )
    return (grad_x, grads + (grad_mixed,), sums + (mix_sums,))


def swap_cores(value):
    return send(value, ((0, 1), (1, 0), (2, 3), (3, 2)))


def send(value, routes):
    return lax.ppermute(value, "section", routes)


def pick_row(value, at, axis=0):
    return lax.dynamic_index_in_dim(value, at, axis, keepdims=False)


def plus(*values):
    return sum(value.astype(F32) for value in values).astype(BF)


class RowSum:
    def __init__(self, mine, arrived, blocks):
        self.value, self.blocks, self.travelling = (mine, arrived), blocks, None
        self.plain = lax.axis_size("dp") != SHARDS
        if not self.plain:
            at = lax.axis_index("dp")
            self.z, self.x, self.line_at = at // 2, at % 2, 0

    def state(self):
        return (self.value, self.travelling)

    def set(self, state):
        self.value, self.travelling = state

    def cross(self):
        if self.plain:
            return
        values = [part.reshape(4, 2, *part.shape[1:]) for part in self.value]
        other = plus(*[pick_row(part, 1 - self.x, 1) for part in values])
        arrived = lax.ppermute(other, "dp", [(n, n ^ 1) for n in range(8)])
        self.value = plus(*[pick_row(part, self.x, 1) for part in values], arrived)

    def line(self):
        if self.plain:
            return
        self.line_at += 1
        far = 4 - self.line_at
        right = pick_row(self.value, jnp.minimum(self.z + far, 3))
        left = pick_row(self.value, jnp.maximum(self.z - far, 0))
        if self.travelling is not None:
            right, left = plus(right, self.travelling[0]), plus(left, self.travelling[1])
        self.travelling = (
            lax.ppermute(right, "dp", [(n, n + 2) for n in range(6)]),
            lax.ppermute(left, "dp", [(n + 2, n) for n in range(6)]),
        )

    def direct(self):
        if self.plain:
            return
        arrived = []
        for far in (3, 2, 1):
            for way in (far, -far):
                part = pick_row(self.value, jnp.clip(self.z + way, 0, 3))
                routes = [(n, n + 2 * way) for n in range(8) if 0 <= n + 2 * way < 8]
                arrived.append(lax.ppermute(part, "dp", routes))
        self.travelling = tuple(arrived)

    def result(self):
        if not self.plain:
            return plus(pick_row(self.value, self.z), *self.travelling)
        shards = lax.axis_size("dp")
        parts, at, value = [], 0, plus(*self.value)
        for rows in self.blocks:
            part = value[:, at : at + rows].reshape(shards, -1, value.shape[2])
            parts, at = parts + [part], at + rows
        whole = jnp.concatenate(parts, axis=1)
        return lax.psum_scatter(whole, "dp", scatter_dimension=0, tiled=True)[0]


def body(
    tokens_in, seg_starts, pad_mask, w_qkv, b_qv, w_attn_out, b_attn_out, ln_gain, ln_bias,
    w_up, b_up, w_down, b_down, w_proj, cotangent,
):
    section_at = lax.axis_index("section")
    core = section_at % 2
    is_late = section_at >= 2
    flip = core == 1
    quarter = tokens_in.shape[1]
    length, width = 4 * quarter, tokens_in.shape[2]
    ff_width = w_up.shape[2]
    proj_cols = w_proj.shape[1]
    shards = lax.axis_size("dp")
    share = width // shards

    def sel_for(half):
        return jnp.stack([core, section_at // 2, half]).astype(jnp.int32)

    sel_mine, sel_theirs = sel_for(core), sel_for(1 - core)

    own = pick_row(tokens_in, core)
    other = pick_row(tokens_in, 1 - core)
    straight = send(own, [(2, 0), (3, 1)])
    crossed = send(other, [(2, 1), (3, 0)])
    near = swap_cores(other)
    small = pack_small(b_qv[0], b_attn_out[0], ln_gain[0], ln_bias[0], b_up[0], b_down[0])[None]
    small_other = swap_cores(small)
    small = jnp.stack([jnp.where(flip, small_other, small), jnp.where(flip, small, small_other)])
    weights = tuple((w[0], swap_cores(w[0])) for w in (w_qkv, w_attn_out, w_up, w_down)) + (small,)
    x = jnp.concatenate(
        [
            jnp.where(flip, near, own),
            jnp.where(flip, own, near),
            jnp.where(flip, crossed, straight),
            jnp.where(flip, straight, crossed),
        ],
        axis=0,
    )

    head_own = jnp.concatenate([w_proj.T, pick_row(cotangent, core).T], axis=1)
    head_other = jnp.concatenate([w_proj.T, pick_row(cotangent, 1 - core).T], axis=1)
    head_late = send(head_other, [(2, 3), (3, 2)])
    head_straight = send(head_own, [(0, 2), (1, 3)])
    head_crossed = send(head_other, [(0, 3), (1, 2)])
    head_cols = jnp.concatenate(
        [
            jnp.where(flip, head_crossed, head_straight),
            jnp.where(flip, head_straight, head_crossed),
            jnp.where(flip, head_late, head_own),
            jnp.where(flip, head_own, head_late),
        ],
        axis=0,
    )
    proj_rows, given_rows = head_cols[:, :width], head_cols[:, width:]
    plan = attention_plan(pick_row(seg_starts, core), pick_row(pad_mask, core))

    def both_forward(rows):
        middle, kept_even = layer_forward(sel_mine, rows, weights, 0, plan)
        last, kept_odd = layer_forward(sel_mine, middle, weights, 1, plan)
        return (last, kept_even, kept_odd)

    early, kept_even, kept_odd = both_forward(x)
    hopped = send(early, [(0, 2), (1, 3)])
    hopped, proj_rows, given_rows = lax.optimization_barrier((hopped, proj_rows, given_rows))

    def late_turn(rows, *_):
        last, kept_even, kept_odd = both_forward(rows)
        embedded, grad_proj, grad = head(last, proj_rows, given_rows)
        grad, grads_odd, sums_odd = layer_backward(sel_mine, grad, kept_odd, weights, 1, plan)
        grad, grads_even, sums_even = layer_backward(sel_mine, grad, kept_even, weights, 0, plan)
        return (
            kept_even, kept_odd, embedded, grad_proj, grad,
            grads_odd, sums_odd, grads_even, sums_even,
        )

    def early_turn(rows, kept_even, kept_odd):
        row, ff = jnp.zeros((length, width), BF), jnp.zeros((length, ff_width), BF)
        grads = (row, ff, row, jnp.zeros((3, length, width), BF))
        sums = (
            jnp.zeros((6, width), F32),
            jnp.zeros((1, ff_width), F32),
            jnp.zeros((2, width), F32),
        )
        return (
            kept_even, kept_odd, jnp.zeros((4 * proj_cols, length), BF),
            jnp.zeros((width, 4 * proj_cols), BF), row, grads, sums, grads, sums,
        )

    (
        kept_even, kept_odd, embedded, grad_proj, grad_mid,
        late_odd, late_sums_odd, late_even, late_sums_even,
    ) = lax.cond(is_late, late_turn, early_turn, hopped, kept_even, kept_odd)

    halfway = length // 2
    arriving = [
        send(grad_mid[at : at + halfway], [(2, 0), (3, 1)]) for at in (0, halfway)
    ]
    embedded_cols = embedded.reshape(4, proj_cols, length)

    rows_of_one = width // SHARDS
    attend_blocks = (rows_of_one,) * 4
    feed_blocks = (rows_of_one,) * (ff_width // (2 * HALF)) + (ff_width // SHARDS,)

    def tie(*values):
        return lax.optimization_barrier(values)

    def feed_args(kept, late, now):
        return (kept[4], late[1], now[1], kept[9], late[0], now[0])

    def attend_args(kept, late, now, mixed):
        return (kept[2], kept[0], late[2], now[2], late[3], mixed)

    def tie_sums(values, *sums):
        values, states = tie(values, [part.state() for part in sums])
        for part, state in zip(sums, states):
            part.set(state)
        return values

    grad_context, grads_odd, sums_odd = feed_backward(sel_mine, arriving, kept_odd, weights, 1)
    args = feed_args(kept_odd, late_odd, grads_odd)
    arrived = swap_cores(feed_grads(sel_theirs, *args))
    feed_odd = RowSum(feed_grads(sel_mine, *args), arrived, feed_blocks)
    grad_context = tie_sums(grad_context, feed_odd)
    feed_odd.cross()
    straight_cols = send(pick_row(embedded_cols, core), [(2, 0), (3, 1)])
    crossed_cols = send(pick_row(embedded_cols, 1 - core), [(2, 1), (3, 0)])
    near_cols = swap_cores(pick_row(embedded_cols, 3 - core))
    mixed_odd, grad, mix_sums = mixed_backward(
        sel_mine, grad_context, grads_odd[2], kept_odd, weights, 1, plan
    )
    sums_odd = sums_odd + (mix_sums,)
    args = attend_args(kept_odd, late_odd, grads_odd, mixed_odd)
    args, straight_cols, crossed_cols, near_cols = tie_sums(
        (args, straight_cols, crossed_cols, near_cols), feed_odd
    )
    feed_odd.line()
    theirs = attend_grads(sel_theirs, *args)
    args, theirs = tie_sums((args, theirs), feed_odd)
    arrived = swap_cores(theirs)
    attend_odd = RowSum(attend_grads(sel_mine, *args), arrived, attend_blocks)
    grad = tie_sums(grad, feed_odd, attend_odd)
    feed_odd.line()
    attend_odd.cross()

    grad_context, grads_even, sums_even = feed_backward(sel_mine, (grad,), kept_even, weights, 0)
    args = tie_sums(feed_args(kept_even, late_even, grads_even), feed_odd, attend_odd)
    feed_odd.line()
    theirs = feed_grads(sel_theirs, *args)
    args, theirs = tie_sums((args, theirs), feed_odd)
    arrived = swap_cores(theirs)
    feed_even = RowSum(feed_grads(sel_mine, *args), arrived, feed_blocks)
    grad_context = tie_sums(grad_context, feed_even, attend_odd)
    feed_even.cross()
    attend_odd.direct()
    mixed_even, grad, mix_sums = mixed_backward(
        sel_mine, grad_context, grads_even[2], kept_even, weights, 0, plan
    )
    sums_even = sums_even + (mix_sums,)
    args = attend_args(kept_even, late_even, grads_even, mixed_even)
    args = tie_sums(args, feed_even, attend_odd)
    feed_even.line()
    routes_odd, routes_even = ((0, 1), (2, 3)), ((1, 0), (3, 2))
    feed_odd, attend_odd = feed_odd.result(), attend_odd.result()
    theirs = attend_grads(sel_theirs, *args)
    extras = pack_extras(sel_mine, grad_proj, late_sums_even, late_sums_odd, sums_even, sums_odd)
    theirs = jnp.concatenate([theirs, extras.astype(BF)], axis=1)
    args, theirs, extras = tie_sums((args, theirs, extras), feed_even)
    arrived = swap_cores(theirs)
    feed_even.line()
    quarters = grad.reshape(4, quarter, width)
    near_grad = swap_cores(pick_row(quarters, 1 - core))
    sent_odd = [send(part, routes_odd) for part in (feed_odd, attend_odd)]
    mine = jnp.concatenate([attend_grads(sel_mine, *args), extras.astype(BF)], axis=1)
    mine, quarters, near_grad, sent_odd = tie_sums(
        (mine, quarters, near_grad, sent_odd), feed_even
    )
    attend_even = RowSum(mine, arrived, attend_blocks)
    attend_even.cross()
    feed_even.line()
    straight_grad = send(pick_row(quarters, 2 + core), [(0, 2), (1, 3)])
    crossed_grad = send(pick_row(quarters, 3 - core), [(0, 3), (1, 2)])
    straight_grad, crossed_grad = tie_sums((straight_grad, crossed_grad), feed_even, attend_even)
    attend_even.direct()
    feed_even = feed_even.result()
    if shards == SHARDS:
        tail = attend_even.result()
        attend_even, extras = tail[: 4 * share], tail[4 * share :].astype(F32)
    else:
        attend_even = attend_even.result()
        extras = plus(mine[:, -EXTRA_ROWS:], arrived[:, -EXTRA_ROWS:])
        extras = lax.psum(extras.astype(F32), "dp")

    def halves(even, odd, sent):
        arrived = jnp.where(flip, sent, send(even, routes_even))
        mine = jnp.where(flip, odd, even)
        return (jnp.where(flip, arrived, mine), jnp.where(flip, mine, arrived))

    blocks = ff_width // (2 * HALF)
    feed_halves = halves(feed_even, feed_odd, sent_odd[0])
    attend_halves = halves(attend_even, attend_odd, sent_odd[1])

    def columns(pair, first, count):
        parts = [part[n * share : (n + 1) * share] for part in pair for n in range(first, first + count)]
        return jnp.concatenate(parts, axis=1).astype(F32)

    grad_w_up = columns(feed_halves, 0, blocks)[None]
    grad_w_down = jnp.concatenate([part[blocks * share :] for part in feed_halves], axis=1)
    grad_w_down = grad_w_down.astype(F32)[None]
    grad_w_out = columns(attend_halves, 0, 1)[None]
    grad_w_qkv = jnp.concatenate([columns(attend_halves, 1 + c, 1) for c in range(3)], axis=1)[None]

    if shards == SHARDS:
        at, pick = 0, lambda values: values
    else:
        at = lax.axis_index("dp") % (shards // SHARDS)
        extras = pick_row(extras, lax.axis_index("dp") // (shards // SHARDS))

        def pick(values):
            size = values.shape[-1] * SHARDS // shards
            return lax.dynamic_slice_in_dim(values, at * size, size, values.ndim - 1)

    one = width // SHARDS
    small_mine = jnp.where(flip, extras[8:16], extras[:8])
    grad_b_up = pick(small_mine[0:1, : ff_width // SHARDS])
    grad_b_qv = pick(small_mine[1:2, : 2 * one])
    rows = pick(small_mine[2:8, :one])
    grad_proj = extras[16:].reshape(-1, 3, 4 * proj_cols).transpose(1, 0, 2)
    grad_proj = grad_proj.reshape(one, 4 * proj_cols)
    grad_proj = lax.dynamic_slice_in_dim(grad_proj, at * share, share, 0).astype(BF)
    grad_proj = jnp.where(is_late, grad_proj, send(grad_proj, [(2, 0), (3, 1)])).astype(F32)
    grad_w_proj = lax.dynamic_slice_in_dim(grad_proj, section_at * proj_cols, proj_cols, 1)

    own_cols = jnp.where(is_late, pick_row(embedded_cols, section_at), straight_cols)
    other_cols = jnp.where(is_late, near_cols, crossed_cols)
    embedded_out = jnp.stack(
        [jnp.where(flip, other_cols, own_cols).T, jnp.where(flip, own_cols, other_cols).T]
    )

    mine = jnp.where(is_late, straight_grad, pick_row(quarters, core))
    others = jnp.where(is_late, crossed_grad, near_grad)
    grad_in = jnp.stack(
        [jnp.where(flip, others, mine), jnp.where(flip, mine, others)]
    ).astype(F32)

    return (
        embedded_out,
        grad_in,
        grad_w_qkv,
        grad_b_qv,
        grad_w_out,
        rows[0][None],
        rows[1:3][None],
        rows[3:5][None],
        grad_w_up,
        grad_b_up,
        grad_w_down,
        rows[5][None],
        grad_w_proj,
    )


def solution(mesh):
    in_specs = (
        P("dp", "section", None),
        P("dp", None),
        P("dp", None),
        P("section", None, None),
        P("section", None),
        P("section", None, None),
        P("section", None),
        P("section", None, None),
        P("section", None, None),
        P("section", None, None),
        P("section", None),
        P("section", None, None),
        P("section", None),
        P(None, "section"),
        P("dp", None, "section"),
    )
    out_specs = (
        P("dp", None, "section"),
        P("dp", "section", None),
        P("section", "dp", None),
        P("section", "dp"),
        P("section", "dp", None),
        P("section", "dp"),
        P("section", None, "dp"),
        P("section", None, "dp"),
        P("section", "dp", None),
        P("section", "dp"),
        P("section", "dp", None),
        P("section", "dp"),
        P("dp", "section"),
    )
    return jax.shard_map(body, mesh=mesh, in_specs=in_specs, out_specs=out_specs, check_vma=False)
```

```python
from functools import partial
import math

import jax
import jax.numpy as jnp
from jax import lax
from jax.experimental import pallas as pl
from jax.experimental.pallas import tpu as pltpu
from jax.sharding import PartitionSpec as P

HEAD = 64
PAIR = 2 * HEAD
QB = 128
KB = 512
KEYS = 256
EPS_NORM = 1e-05
EPS_PROJ = 1e-06
NEG_FILL = -1e30
PARAMS = pltpu.CompilerParams(vmem_limit_bytes=60 * 1024 * 1024)


def cost(micros):
    return pl.CostEstimate(flops=int(micros * 1e9), bytes_accessed=1024, transcendentals=0)


BF = jnp.bfloat16
F32 = jnp.float32

NT = (((1,), (1,)), ((), ()))
TN = (((0,), (0,)), ((), ()))


def dot(a, b):
    return jnp.dot(a, b, preferred_element_type=F32)


def dot_nt(a, b):
    return lax.dot_general(a, b, NT, preferred_element_type=F32)


def dot_tn(a, b):
    return lax.dot_general(a, b, TN, preferred_element_type=F32)


def pack_small(b_qv, b_out, gains, shifts, b_up, b_down):
    return jnp.concatenate(
        [b_up, b_qv, b_out, gains[0], gains[1], shifts[0], shifts[1], b_down]
    )


def small_spec(layer, width):
    return pl.BlockSpec((1, 1, width), lambda *_: (layer, 0, 0))


def attention_plan(starts, real_flags):
    length = real_flags.shape[0]
    places = jnp.arange(length, dtype=jnp.int32)
    segment = jnp.sum((starts[None, :] <= places[:, None]).astype(jnp.int32), axis=1)
    key_code = jnp.where(real_flags == 1, segment, -1).astype(F32)
    key_code = jnp.broadcast_to(key_code[:, None], (length, PAIR))
    query_code = segment.astype(F32).reshape(length // QB, QB)
    first = jnp.arange(length // QB, dtype=jnp.int32) * QB
    low = jnp.max(jnp.where(starts[None, :] <= first[:, None], starts[None, :], 0), axis=1)
    high = jnp.min(
        jnp.where(starts[None, :] > first[:, None] + (QB - 1), starts[None, :], length), axis=1
    )
    begin = (low // QB) * QB
    count = (high - begin + KEYS - 1) // KEYS
    begin = jnp.minimum(begin, length - KEYS * count)
    return (begin, count, key_code, query_code)


def pair_mask(rows):
    return lax.broadcasted_iota(jnp.int32, (rows, PAIR), 1) < HEAD


def stacked_heads(block):
    first = pair_mask(block.shape[0])
    zero = jnp.zeros_like(block)
    return jnp.concatenate([jnp.where(first, block, zero), jnp.where(first, zero, block)], axis=0)


def block_bias(key_code, query_code, key_at, query_at):
    shape = key_code.shape
    keys = lax.broadcasted_iota(jnp.int32, shape, 0) + (key_at - query_at)
    same = keys == lax.broadcasted_iota(jnp.int32, shape, 1)
    bias = jnp.where((key_code == query_code) | same, 0.0, NEG_FILL)
    return jnp.concatenate([bias, bias], axis=1)


def over_keys(begin, count, step, state):
    state = lax.fori_loop(
        0,
        lax.shift_right_logical(count, 1),
        lambda j, now: step(pl.multiple_of(begin + j * KB, QB), KB, now),
        state,
    )
    last = pl.multiple_of(begin + (count - 1) * KEYS, QB)
    return lax.fori_loop(
        0, jnp.bitwise_and(count, 1), lambda _, now: step(last, KEYS, now), state
    )


def unstack_heads(flat):
    rows = lax.broadcasted_iota(jnp.int32, (PAIR, QB), 0)
    return jnp.where(rows < HEAD, flat[:PAIR, :QB], flat[:PAIR, QB:]).T


def attend_forward(
    begin_ref, count_ref, qkv_ref, key_code_ref, query_code_ref, out_ref, logsum_ref,
    value_scr, query_scr, total_scr,
):
    length = qkv_ref.shape[1]
    pairs = qkv_ref.shape[2] // PAIR
    every = range(pairs)
    cols = [slice(p * PAIR, (p + 1) * PAIR) for p in every]
    for p in every:
        value_scr[p, :PAIR, :] = qkv_ref[2, :, cols[p]].T
        value_scr[p, PAIR:, :] = jnp.ones((value_scr.shape[1] - PAIR, length), BF)

    def one_query_block(i, _):
        query_at = pl.multiple_of(i * QB, QB)
        begin, count = begin_ref[i], count_ref[i]
        query_code = query_code_ref[pl.ds(i, 1), :]
        for p in every:
            query_scr[p] = stacked_heads(qkv_ref[0, pl.ds(query_at, QB), cols[p]])
        total_scr[...] = jnp.zeros_like(total_scr)

        def one_key_block(key_at, size, tops):
            rows = pl.ds(key_at, size)
            bias = block_bias(key_code_ref[rows, :], query_code, key_at, query_at)
            scores = [dot_nt(qkv_ref[1, rows, cols[p]], query_scr[p]) + bias for p in every]
            fresh = [
                jnp.maximum(tops[p], jnp.max(scores[p], axis=0, keepdims=True)) for p in every
            ]
            probs = [jnp.exp(scores[p] - fresh[p]).astype(BF) for p in every]
            for p in every:
                total_scr[p] = total_scr[p] * jnp.exp(tops[p] - fresh[p]) + dot(
                    value_scr[p, :, rows], probs[p]
                )
            return tuple(fresh)

        tops = tuple(jnp.full((1, 2 * QB), 2 * NEG_FILL, F32) for _ in every)
        tops = over_keys(begin, count, one_key_block, tops)
        for p in every:
            weight = total_scr[p, PAIR : PAIR + 1, :]
            logsum_ref[pl.ds(p * (length // QB) + i, 1), :] = tops[p] + jnp.log(weight)
            out_ref[pl.ds(query_at, QB), cols[p]] = unstack_heads(
                total_scr[p, :PAIR, :] * (1.0 / weight)
            ).astype(BF)
        return 0

    lax.fori_loop(0, length // QB, one_query_block, 0)


def attend_backward(
    begin_ref, count_ref, qkv, key_code_ref, query_code_ref, context, logsum_ref, grad, sums_ref,
    key_scr, query_scr, given_scr, down_scr, grad_key_scr, grad_value_scr,
):
    length = qkv.shape[1]
    pairs = qkv.shape[2] // PAIR
    every = range(pairs)
    blocks = length // QB
    cols = [slice(p * PAIR, (p + 1) * PAIR) for p in every]
    for p in every:
        key_scr[p] = qkv[1, :, cols[p]].T

    def one_query_block(i, _):
        query_at = pl.multiple_of(i * QB, QB)
        queries = pl.ds(query_at, QB)
        begin, count = begin_ref[i], count_ref[i]
        query_code = query_code_ref[pl.ds(i, 1), :]
        inner, logsum = [], []
        for p in every:
            query_scr[p] = stacked_heads(qkv[0, queries, cols[p]])
            given = grad[queries, cols[p]]
            given_scr[p] = stacked_heads(given)
            both = (given.astype(F32) * context[queries, cols[p]].astype(F32)).T
            inner.append(
                jnp.concatenate(
                    [
                        jnp.sum(both[:HEAD], axis=0, keepdims=True),
                        jnp.sum(both[HEAD:], axis=0, keepdims=True),
                    ],
                    axis=1,
                )
            )
            logsum.append(logsum_ref[pl.ds(p * blocks + i, 1), :])
        down_scr[...] = jnp.zeros_like(down_scr)

        def one_key_block(key_at, size, state):
            rows = pl.ds(key_at, size)
            bias = block_bias(key_code_ref[rows, :], query_code, key_at, query_at)
            grads = [
                (dot_nt(qkv[2, rows, cols[p]], given_scr[p]) - inner[p]).astype(BF) for p in every
            ]
            parts = [dot_nt(qkv[1, rows, cols[p]], query_scr[p]) + bias for p in every]
            probs = [jnp.exp(parts[p] - logsum[p]).astype(BF) for p in every]
            scores = [probs[p] * grads[p] for p in every]
            for p in every:
                grad_value_scr[rows, cols[p]] += dot(probs[p], given_scr[p])
            for p in every:
                grad_key_scr[rows, cols[p]] += dot(scores[p], query_scr[p])
            for p in every:
                down_scr[p] += dot(key_scr[p, :, rows], scores[p])
            return state

        over_keys(begin, count, one_key_block, 0)
        for p in every:
            grad_query = (unstack_heads(down_scr[p]) * (HEAD**-0.5)).astype(BF)
            qkv[0, queries, cols[p]] = grad_query
            sums_ref[0:1, cols[p]] += jnp.sum(grad_query.astype(F32), axis=0, keepdims=True)
        return 0

    lax.fori_loop(0, blocks, one_query_block, 0)
    qkv[1] = grad_key_scr[...].astype(BF)
    grad_value = grad_value_scr[...].astype(BF)
    qkv[2] = grad_value
    sums_ref[1:2, :] = jnp.sum(grad_value.astype(F32), axis=0, keepdims=True)


ANY = pl.BlockSpec(memory_space=pl.ANY)
ROWS = 256


class Held:
    def __init__(self, sel_ref, layer, pairs, held, sems, first=None):
        self.own = sel_ref[0] == layer
        self.items = list(zip(pairs, held, range(len(held))))
        self.sems = sems
        self.first = pl.program_id(0) == 0 if first is None else first

    def start(self):
        for pair, held, n in self.items:
            for wanted, source in zip((self.own, jnp.logical_not(self.own)), pair):

                @pl.when(self.first & wanted)
                def _():
                    pltpu.make_async_copy(source, held, self.sems.at[n]).start()

    def wait(self, n):
        pair, held, _ = self.items[n]

        @pl.when(self.first)
        def _():
            pltpu.make_async_copy(pair[0], held, self.sems.at[n]).wait()


def held_shapes(*weights):
    return [pltpu.VMEM(own.shape, own.dtype) for own, _ in weights]


def normalized(values):
    centred = values - jnp.mean(values, axis=-1, keepdims=True)
    inverse = lax.rsqrt(jnp.mean(centred * centred, axis=-1, keepdims=True) + EPS_NORM)
    return (centred * inverse, inverse)


def normalized_pull(grad_hat, hat, inverse):
    return inverse * (
        grad_hat
        - jnp.mean(grad_hat, axis=-1, keepdims=True)
        - hat * jnp.mean(grad_hat * hat, axis=-1, keepdims=True)
    )


ERF = (0.254829592, -0.284496736, 1.421413741, -1.453152027, 1.061405429)
ERF_SLOPE = 0.3275911


def gelu_parts(x):
    t = pl.reciprocal(1.0 + (ERF_SLOPE * math.sqrt(0.5)) * jnp.abs(x), approx=True)
    bell = jnp.exp(-0.5 * (x * x))
    tail = 0.5 * ERF[4]
    for term in ERF[3::-1]:
        tail = tail * t + 0.5 * term
    tail = tail * t * bell
    below = jnp.where(x >= 0, 1.0 - tail, tail)
    return (x * below, below + x * bell * (1.0 / math.sqrt(2.0 * math.pi)))


FB = 1024


def small_slices(width, ff_width):
    names = ("b_q", "b_v", "b_out", "gain1", "gain2", "shift1", "shift2", "b_down")
    at = {"b_up": slice(0, ff_width)}
    for n, name in enumerate(names):
        at[name] = slice(ff_width + n * width, ff_width + (n + 1) * width)
    return at


def refine_back_kernel(
    layer, sel_ref, grad_ref, hidden_ref, out_ref, scale1_ref, scale2_ref, slope_ref,
    out_own_ref, out_other_ref, up_own_ref, up_other_ref, down_own_ref, down_other_ref, small_ref,
    grad_low_ref, grad_raised_ref, grad_attn_ref, grad_context_ref, sums_ref, up_sums_ref,
    w_out, w_up, w_down, sems,
):
    pairs = [(out_own_ref, out_other_ref), (up_own_ref, up_other_ref), (down_own_ref, down_other_ref)]
    weights = Held(sel_ref, layer, pairs, [w_out, w_up, w_down], sems)
    weights.start()
    rows, width = grad_ref.shape
    ff_width = slope_ref.shape[1]
    at = small_slices(width, ff_width)

    @pl.when(pl.program_id(0) == 0)
    def _():
        sums_ref[...] = jnp.zeros_like(sums_ref)
        up_sums_ref[...] = jnp.zeros_like(up_sums_ref)

    def vector(name):
        return small_ref[0, :, at[name]]

    def add(row, values):
        sums_ref[row : row + 1, :] += jnp.sum(values, axis=0, keepdims=True)

    grad = grad_ref[...].astype(F32)
    hat = (out_ref[...].astype(F32) - vector("shift2")) * (1.0 / vector("gain2"))
    joined = normalized_pull(grad * vector("gain2"), hat, scale2_ref[:, :1])
    low = joined.astype(BF)
    grad_low_ref[...] = low
    add(2, grad * hat)
    add(4, grad)
    add(5, low.astype(F32))
    weights.wait(2)
    weights.wait(1)
    total = joined
    parts = [slice(f, f + FB) for f in range(0, ff_width, FB)]
    active = dot_nt(low, w_down[parts[0], :])
    for n, part in enumerate(parts):
        following = dot_nt(low, w_down[parts[n + 1], :]) if n + 1 < len(parts) else None
        raised = active * slope_ref[:, part].astype(F32)
        up_sums_ref[:, part] += jnp.sum(raised, axis=0, keepdims=True)
        raised = raised.astype(BF)
        grad_raised_ref[:, part] = raised
        total += dot_nt(raised, w_up[:, part])
        active = following
    hat = (hidden_ref[...].astype(F32) - vector("shift1")) * (1.0 / vector("gain1"))
    summed = normalized_pull(total * vector("gain1"), hat, scale1_ref[:, :1])
    attn = summed.astype(BF)
    grad_attn_ref[...] = attn
    weights.wait(0)
    grad_context_ref[...] = dot_nt(attn, w_out[...]).astype(BF)
    add(1, total * hat)
    add(3, total)
    add(0, attn.astype(F32))


def refine_back_second_kernel(layer, *refs):
    refine_back_kernel(layer, *refs[:14], *refs[18:])


def refine_back(sel, grad, kept, weights, layer, first=0, begun=()):
    w_out, w_up, w_down, small = weights
    hidden, out, scale1, scale2, slope = kept
    length, width = hidden.shape
    ff_width = w_up[0].shape[1]
    at = first // ROWS
    rows = pl.BlockSpec((ROWS, width), lambda n, _: (n + at, 0))
    lanes = pl.BlockSpec((ROWS, 128), lambda n, _: (n + at, 0))
    part = pl.BlockSpec((ROWS, ff_width), lambda n, _: (n + at, 0))
    row_shape = jax.ShapeDtypeStruct((length, width), BF)
    return pl.pallas_call(
        partial(refine_back_second_kernel if begun else refine_back_kernel, layer),
        name="refine_back",
        grid_spec=pltpu.PrefetchScalarGridSpec(
            num_scalar_prefetch=1,
            grid=(grad.shape[0] // ROWS,),
            in_specs=[
                pl.BlockSpec((ROWS, width), lambda n, _: (n, 0)),
                rows, rows, lanes, lanes, part,
            ]
            + [ANY] * 6
            + [small_spec(layer, small.shape[2])]
            + [ANY] * len(begun),
            out_specs=[
                rows, part, rows, rows,
                pl.BlockSpec((6, width), lambda n, _: (0, 0)),
                pl.BlockSpec((1, ff_width), lambda n, _: (0, 0)),
            ],
            scratch_shapes=[
                *held_shapes(w_out, w_up, w_down),
                pltpu.SemaphoreType.DMA((3,)),
            ],
        ),
        out_shape=[
            row_shape,
            jax.ShapeDtypeStruct((length, ff_width), BF),
            row_shape,
            row_shape,
            jax.ShapeDtypeStruct((6, width), F32),
            jax.ShapeDtypeStruct((1, ff_width), F32),
        ],
        input_output_aliases={14 + n: n for n in range(len(begun))},
        compiler_params=PARAMS,
        cost_estimate=cost(24),
    )(sel, grad, hidden, out, scale1, scale2, slope, *w_out, *w_up, *w_down, small, *begun)


def head_kernel(rows_ref, proj_ref, given_ref, embedded_ref, grad_proj_ref, grad_rows_ref):
    factor = math.sqrt(proj_ref.shape[0])
    columns = dot_nt(proj_ref[...], rows_ref[...])
    given = given_ref[...].astype(F32)
    inverse = lax.rsqrt(jnp.sum(columns * columns, axis=0, keepdims=True) + EPS_PROJ)
    cross = jnp.sum(columns * given, axis=0, keepdims=True)
    embedded_ref[...] = (factor * columns * inverse).astype(BF)
    grad = (factor * (given * inverse - columns * (cross * inverse * inverse * inverse))).astype(BF)
    grad_proj_ref[...] = dot(grad, rows_ref[...]).T.astype(BF)
    grad_rows_ref[...] = dot_tn(grad, proj_ref[...]).astype(BF)


def head(rows, proj, given):
    length, width = rows.shape
    cols = proj.shape[0]
    return pl.pallas_call(
        head_kernel,
        name="head",
        out_shape=[
            jax.ShapeDtypeStruct((cols, length), BF),
            jax.ShapeDtypeStruct((width, cols), BF),
            jax.ShapeDtypeStruct((length, width), BF),
        ],
        compiler_params=PARAMS,
        cost_estimate=cost(6),
    )(rows, proj, given)


HALF = 384
SHARDS = 8


def feed_grads_kernel(
    sel_ref, hidden_ref, raised_late_ref, raised_ref, active_ref, low_late_ref, low_ref, out_ref
):
    step = pl.program_id(0)
    shards, rows, _ = out_ref.shape
    blocks = raised_ref.shape[1] // HALF
    share = rows // blocks
    late = sel_ref[1] == 1

    def up(raised):
        part = dot_tn(hidden_ref[...], raised).astype(BF)
        for m in range(shards):
            for n in range(blocks):
                out_ref[m, n * share : (n + 1) * share, :] = part[
                    m * share : (m + 1) * share, n * HALF : (n + 1) * HALF
                ]

    def down(low):
        for m in range(shards):
            out_ref[m] = dot_tn(active_ref[:, m * rows : (m + 1) * rows], low).astype(BF)

    for wanted, raised_now, low_now in (
        (late, raised_late_ref, low_late_ref),
        (jnp.logical_not(late), raised_ref, low_ref),
    ):

        @pl.when(wanted & (step < 2))
        def _():
            up(raised_now[...])

        @pl.when(wanted & (step >= 2))
        def _():
            down(low_now[...])


def feed_grads(sel, hidden, raised_late, raised, active, low_late, low):
    length, width = hidden.shape
    ff_width = active.shape[1]
    half_ff = ff_width // 2

    def late_spec(shape, wanted):
        return pl.BlockSpec(shape, lambda n, sel: (0, jnp.where(sel[1] == wanted, sel[2], 0)))

    return pl.pallas_call(
        feed_grads_kernel,
        name="feed_grads",
        grid_spec=pltpu.PrefetchScalarGridSpec(
            num_scalar_prefetch=1,
            grid=(4,),
            in_specs=[
                pl.BlockSpec((length, width // 2), lambda n, _: (0, jnp.minimum(n, 1))),
                late_spec((length, half_ff), 1),
                late_spec((length, half_ff), 0),
                pl.BlockSpec((length, ff_width // 2), lambda n, _: (0, jnp.maximum(n - 2, 0))),
                late_spec((length, width // 2), 1),
                late_spec((length, width // 2), 0),
            ],
            out_specs=pl.BlockSpec(
                (SHARDS // 2, ff_width // SHARDS, HALF), lambda n, _: (lax.rem(n, 2), n // 2, 0)
            ),
        ),
        out_shape=jax.ShapeDtypeStruct((SHARDS, 2 * (ff_width // SHARDS), HALF), BF),
        compiler_params=PARAMS,
        cost_estimate=cost(12),
    )(sel, hidden, raised_late, raised, active, low_late, low)


def attend_grads_kernel(
    sel_ref, context_ref, x_ref, attn_late_ref, attn_ref, mixed_late_ref, mixed_ref, out_ref
):
    step = pl.program_id(0)
    late = sel_ref[1] == 1

    for wanted, attn_now, mixed_now in (
        (late, attn_late_ref, mixed_late_ref),
        (jnp.logical_not(late), attn_ref, mixed_ref),
    ):

        @pl.when(wanted & (step == 0))
        def _():
            part = dot_tn(context_ref[...], attn_now[...]).astype(BF)
            out_ref[...] = part.reshape(out_ref.shape)

        @pl.when(wanted & (step > 0))
        def _():
            part = dot_tn(x_ref[...], mixed_now[0]).astype(BF)
            out_ref[...] = part.reshape(out_ref.shape)


def attend_grads(sel, context, x, attn_late, attn, mixed_late, mixed):
    length, width = x.shape

    def late_spec(wanted):
        return pl.BlockSpec(
            (length, HALF), lambda n, sel: (0, jnp.where(sel[1] == wanted, sel[2], 0))
        )

    def mixed_spec(wanted):
        def at(n, sel):
            return (
                jnp.where(sel[1] == wanted, jnp.maximum(n - 1, 0), 0),
                0,
                jnp.where(sel[1] == wanted, sel[2], 0),
            )

        return pl.BlockSpec((1, length, HALF), at)

    whole = pl.BlockSpec((length, width), lambda n, _: (0, 0))
    share = width // SHARDS
    return pl.pallas_call(
        attend_grads_kernel,
        name="attend_grads",
        grid_spec=pltpu.PrefetchScalarGridSpec(
            num_scalar_prefetch=1,
            grid=(4,),
            in_specs=[whole, whole, late_spec(1), late_spec(0), mixed_spec(1), mixed_spec(0)],
            out_specs=pl.BlockSpec((SHARDS, share, HALF), lambda n, _: (0, n, 0)),
        ),
        out_shape=jax.ShapeDtypeStruct((SHARDS, 4 * share, HALF), BF),
        compiler_params=PARAMS,
        cost_estimate=cost(8),
    )(sel, context, x, attn_late, attn, mixed_late, mixed)


EXTRA_ROWS = 48


def pack_extras_kernel(
    sel_ref, proj_ref,
    late_sums_0, late_up_0, late_mix_0, late_sums_1, late_up_1, late_mix_1,
    sums_0, up_0, mix_0, sums_1, up_1, mix_1, out_ref,
):
    shards = out_ref.shape[0]
    width = sums_0.shape[1]
    share = width // shards
    third = share // 3
    cols = proj_ref.shape[1]
    out_ref[...] = jnp.zeros_like(out_ref)

    def layer(first, sums, up, mix):
        up_share = up.shape[1] // shards
        both = jnp.concatenate([mix[0:1, :], mix[1:2, :]], axis=1)
        for m in range(shards):
            rows = [up[0:1, m * up_share : (m + 1) * up_share]]
            rows += [both[:, 2 * m * share : 2 * (m + 1) * share]]
            rows += [sums[n : n + 1, m * share : (m + 1) * share] for n in range(6)]
            for n, row in enumerate(rows):
                out_ref[m, first + n : first + n + 1, : row.shape[1]] = row

    late = sel_ref[1] == 1
    for wanted, even, odd in (
        (late, (late_sums_0, late_up_0, late_mix_0), (late_sums_1, late_up_1, late_mix_1)),
        (jnp.logical_not(late), (sums_0, up_0, mix_0), (sums_1, up_1, mix_1)),
    ):

        @pl.when(wanted)
        def _():
            layer(0, *even)
            layer(8, *odd)

    for m in range(shards):
        for n in range(3):
            at = m * share + n * third
            out_ref[m, 16:, n * cols : (n + 1) * cols] = proj_ref[at : at + third, :].astype(F32)


def pack_extras(sel, proj, late_even, late_odd, even, odd):
    vmem = pl.BlockSpec(memory_space=pltpu.VMEM)
    return pl.pallas_call(
        pack_extras_kernel,
        name="pack_extras",
        in_specs=[pl.BlockSpec(memory_space=pltpu.SMEM)] + [vmem] * 13,
        out_specs=vmem,
        out_shape=jax.ShapeDtypeStruct((SHARDS, EXTRA_ROWS, HALF), F32),
        compiler_params=PARAMS,
        cost_estimate=cost(3),
    )(sel, proj, *late_even, *late_odd, *even, *odd)


def forward_kernel(
    layer, begin_ref, count_ref, sel_ref, x_hbm, key_code_ref, query_code_ref,
    mix_own_ref, mix_other_ref, out_own_ref, out_other_ref,
    up_own_ref, up_other_ref, down_own_ref, down_other_ref, small_ref,
    qkv_hbm, context_hbm, logsum_ref, out_hbm, hidden_hbm, scale1_ref, scale2_ref,
    active_hbm, slope_hbm,
    w_mix, w_out, w_up, w_down, x, qkv, context, hidden_rows, out_rows, active_rows, slope_rows,
    value_scr, query_scr, total_scr, weight_sems, in_sems, qkv_sems, row_sems, context_sem,
):
    pairs = [
        (mix_own_ref, mix_other_ref), (out_own_ref, out_other_ref),
        (up_own_ref, up_other_ref), (down_own_ref, down_other_ref),
    ]
    length, width = x.shape
    ff_width = w_up.shape[1]
    blocks = length // ROWS
    at = small_slices(width, ff_width)

    def vector(name):
        return small_ref[0, :, at[name]]

    def rows_of(n):
        return pl.ds(pl.multiple_of(n * ROWS, ROWS), ROWS)

    def x_copy(n):
        return pltpu.make_async_copy(x_hbm.at[rows_of(n)], x.at[rows_of(n)], in_sems.at[n])

    def qkv_copy(n):
        return pltpu.make_async_copy(
            qkv.at[:, rows_of(n)], qkv_hbm.at[:, rows_of(n)], qkv_sems.at[n]
        )

    saved = [
        (hidden_rows, hidden_hbm), (out_rows, out_hbm),
        (active_rows, active_hbm), (slope_rows, slope_hbm),
    ]

    def row_copies(n):
        return [
            pltpu.make_async_copy(rows.at[rows_of(n)], whole.at[rows_of(n)], row_sems.at[k, n])
            for k, (rows, whole) in enumerate(saved)
        ]

    weights = Held(sel_ref, layer, pairs, [w_mix, w_out, w_up, w_down], weight_sems, True)
    for n in range(blocks):
        x_copy(n).start()
    weights.start()
    weights.wait(0)

    def mix_rows(n, _):
        x_copy(n).wait()
        rows = rows_of(n)
        part = dot(x[rows, :], w_mix[...])
        qkv[0, rows, :] = ((part[:, :width] + vector("b_q")) * HEAD**-0.5).astype(BF)
        qkv[1, rows, :] = part[:, width : 2 * width].astype(BF)
        qkv[2, rows, :] = (part[:, 2 * width :] + vector("b_v")).astype(BF)
        qkv_copy(n).start()
        return 0

    lax.fori_loop(0, blocks, mix_rows, 0)
    attend_forward(
        begin_ref, count_ref, qkv, key_code_ref, query_code_ref, context, logsum_ref,
        value_scr, query_scr, total_scr,
    )
    context_copy = pltpu.make_async_copy(context, context_hbm, context_sem)
    context_copy.start()
    for n in (1, 2, 3):
        weights.wait(n)

    def refine_rows(n, _):
        rows = rows_of(n)
        summed = x[rows, :].astype(F32) + dot(context[rows, :], w_out[...]) + vector("b_out")
        hat, inverse = normalized(summed)
        hidden = hat * vector("gain1") + vector("shift1")
        scale1_ref[rows, :] = jnp.broadcast_to(inverse, (ROWS, 128))
        hidden_low = hidden.astype(BF)
        hidden_rows[rows, :] = hidden_low
        total = hidden + vector("b_down")
        parts = [slice(f, f + FB) for f in range(0, ff_width, FB)]
        raised = dot(hidden_low, w_up[:, parts[0]])
        for m, part in enumerate(parts):
            following = dot(hidden_low, w_up[:, parts[m + 1]]) if m + 1 < len(parts) else None
            active, slope = gelu_parts(raised + small_ref[0, :, part])
            active = active.astype(BF)
            active_rows[rows, part] = active
            slope_rows[rows, part] = slope.astype(BF)
            total += dot(active, w_down[part, :])
            raised = following
        hat, inverse = normalized(total)
        scale2_ref[rows, :] = jnp.broadcast_to(inverse, (ROWS, 128))
        out_rows[rows, :] = (hat * vector("gain2") + vector("shift2")).astype(BF)
        for copy in row_copies(n):
            copy.start()
        return 0

    lax.fori_loop(0, blocks, refine_rows, 0)
    context_copy.wait()
    for n in range(blocks):
        qkv_copy(n).wait()
        for copy in row_copies(n):
            copy.wait()


def layer_forward(sel, x, weights, layer, plan):
    w_qkv, w_out, w_up, w_down, small = weights
    begin, count, key_code, query_code = plan
    length, width = x.shape
    ff_width = w_up[0].shape[1]
    pairs = width // PAIR
    blocks = length // ROWS

    def whole(shape):
        return pl.BlockSpec(shape, lambda *_: (0,) * len(shape))

    row = jax.ShapeDtypeStruct((length, width), BF)
    lanes = jax.ShapeDtypeStruct((length, 128), F32)
    wide = jax.ShapeDtypeStruct((length, ff_width), BF)
    logsum_shape = (pairs * (length // QB), 2 * QB)
    qkv, context, logsum, out, hidden, scale1, scale2, active, slope = pl.pallas_call(
        partial(forward_kernel, layer),
        name="layer_forward",
        grid_spec=pltpu.PrefetchScalarGridSpec(
            num_scalar_prefetch=3,
            grid=(1,),
            in_specs=[ANY, whole(key_code.shape), whole(query_code.shape)]
            + [ANY] * 8
            + [small_spec(layer, small.shape[2])],
            out_specs=[
                ANY, ANY, whole(logsum_shape), ANY, ANY,
                whole((length, 128)), whole((length, 128)), ANY, ANY,
            ],
            scratch_shapes=[
                *held_shapes(w_qkv, w_out, w_up, w_down),
                pltpu.VMEM((length, width), BF),
                pltpu.VMEM((3, length, width), BF),
                pltpu.VMEM((length, width), BF),
                pltpu.VMEM((length, width), BF),
                pltpu.VMEM((length, width), BF),
                pltpu.VMEM((length, ff_width), BF),
                pltpu.VMEM((length, ff_width), BF),
                pltpu.VMEM((pairs, PAIR + 16, length), BF),
                pltpu.VMEM((pairs, 2 * QB, PAIR), BF),
                pltpu.VMEM((pairs, PAIR + 16, 2 * QB), F32),
                pltpu.SemaphoreType.DMA((4,)),
                pltpu.SemaphoreType.DMA((blocks,)),
                pltpu.SemaphoreType.DMA((blocks,)),
                pltpu.SemaphoreType.DMA((4, blocks)),
                pltpu.SemaphoreType.DMA,
            ],
        ),
        out_shape=[
            jax.ShapeDtypeStruct((3, length, width), BF), row,
            jax.ShapeDtypeStruct(logsum_shape, F32), row, row, lanes, lanes, wide, wide,
        ],
        compiler_params=PARAMS,
        cost_estimate=cost(48),
    )(begin, count, sel, x, key_code, query_code, *w_qkv, *w_out, *w_up, *w_down, small)
    return (out, (x, qkv, context, logsum, hidden, out, scale1, scale2, slope, active))


def feed_backward(sel, grads, kept, weights, layer):
    first, begun, totals = 0, (), []
    for grad in grads:
        *begun, sums, up_sums = refine_back(
            sel, grad, kept[4:9], weights[1:], layer, first, tuple(begun)
        )
        first += grad.shape[0]
        totals.append((sums, up_sums))
    grad_low, grad_raised, grad_attn, grad_context = begun
    sums = tuple(sum(parts) for parts in zip(*totals))
    return (grad_context, (grad_low, grad_raised, grad_attn), sums)


def mixed_backward_kernel(
    layer, begin_ref, count_ref, sel_ref, qkv_hbm, key_code_ref, query_code_ref, context_hbm,
    logsum_ref, grad_hbm, skip_hbm, mix_own_ref, mix_other_ref,
    mixed_hbm, grad_x_hbm, sums_ref,
    w_mix, qkv, context, grad, skip, key_scr, query_scr, given_scr, down_scr,
    grad_key_scr, grad_value_scr, weight_sems, in_sems, mixed_sems, row_sems,
):
    length, width = skip.shape
    blocks = length // ROWS
    weights = Held(sel_ref, layer, [(mix_own_ref, mix_other_ref)], [w_mix], weight_sems, True)
    arrays = [(qkv_hbm, qkv), (context_hbm, context), (grad_hbm, grad), (skip_hbm, skip)]
    loads = [
        pltpu.make_async_copy(whole, held, in_sems.at[n]) for n, (whole, held) in enumerate(arrays)
    ]
    for load in loads:
        load.start()
    weights.start()
    grad_key_scr[...] = jnp.zeros_like(grad_key_scr)
    grad_value_scr[...] = jnp.zeros_like(grad_value_scr)
    sums_ref[...] = jnp.zeros_like(sums_ref)
    for load in loads:
        load.wait()
    attend_backward(
        begin_ref, count_ref, qkv, key_code_ref, query_code_ref, context, logsum_ref, grad,
        sums_ref, key_scr, query_scr, given_scr, down_scr, grad_key_scr, grad_value_scr,
    )
    store = pltpu.make_async_copy(qkv, mixed_hbm, mixed_sems.at[0])
    store.start()
    weights.wait(0)

    def rows_of(n):
        return pl.ds(pl.multiple_of(n * ROWS, ROWS), ROWS)

    def row_copy(n):
        return pltpu.make_async_copy(skip.at[rows_of(n)], grad_x_hbm.at[rows_of(n)], row_sems.at[n])

    def unmix_rows(n, _):
        rows = rows_of(n)
        total = skip[rows, :].astype(F32)
        for c in range(3):
            total += dot_nt(qkv[c, rows, :], w_mix[:, c * width : (c + 1) * width])
        skip[rows, :] = total.astype(BF)
        row_copy(n).start()
        return 0

    lax.fori_loop(0, blocks, unmix_rows, 0)
    store.wait()
    for n in range(blocks):
        row_copy(n).wait()


def mixed_backward(sel, grad_context, skip, kept, weights, layer, plan):
    _, qkv, context, logsum = kept[:4]
    begin, count, key_code, query_code = plan
    _, length, width = qkv.shape
    pairs = width // PAIR
    blocks = length // ROWS
    w_qkv = weights[0]

    def whole(shape):
        return pl.BlockSpec(shape, lambda *_: (0,) * len(shape))

    row = pltpu.VMEM((length, width), BF)
    return pl.pallas_call(
        partial(mixed_backward_kernel, layer),
        name="mixed_backward",
        grid_spec=pltpu.PrefetchScalarGridSpec(
            num_scalar_prefetch=3,
            grid=(1,),
            in_specs=[ANY, whole(key_code.shape), whole(query_code.shape), ANY, whole(logsum.shape)]
            + [ANY] * 4,
            out_specs=[ANY, ANY, whole((2, width))],
            scratch_shapes=[
                *held_shapes(w_qkv),
                pltpu.VMEM((3, length, width), BF),
                row, row, row,
                pltpu.VMEM((pairs, PAIR, length), BF),
                pltpu.VMEM((pairs, 2 * QB, PAIR), BF),
                pltpu.VMEM((pairs, 2 * QB, PAIR), BF),
                pltpu.VMEM((pairs, PAIR, 2 * QB), F32),
                pltpu.VMEM((length, width), F32),
                pltpu.VMEM((length, width), F32),
                pltpu.SemaphoreType.DMA((1,)),
                pltpu.SemaphoreType.DMA((4,)),
                pltpu.SemaphoreType.DMA((1,)),
                pltpu.SemaphoreType.DMA((blocks,)),
            ],
        ),
        out_shape=[
            jax.ShapeDtypeStruct((3, length, width), BF),
            jax.ShapeDtypeStruct((length, width), BF),
            jax.ShapeDtypeStruct((2, width), F32),
        ],
        compiler_params=PARAMS,
        cost_estimate=cost(38),
    )(begin, count, sel, qkv, key_code, query_code, context, logsum, grad_context, skip, *w_qkv)


def layer_backward(sel, grad, kept, weights, layer, plan):
    grad_context, grads, sums = feed_backward(sel, (grad,), kept, weights, layer)
    grad_mixed, grad_x, mix_sums = mixed_backward(
        sel, grad_context, grads[2], kept, weights, layer, plan
    )
    return (grad_x, grads + (grad_mixed,), sums + (mix_sums,))


def swap_cores(value):
    return send(value, ((0, 1), (1, 0), (2, 3), (3, 2)))


def send(value, routes):
    return lax.ppermute(value, "section", routes)


def pick_row(value, at, axis=0):
    return lax.dynamic_index_in_dim(value, at, axis, keepdims=False)


def plus(*values):
    return sum(value.astype(F32) for value in values).astype(BF)


class RowSum:
    def __init__(self, mine, arrived, blocks):
        self.terms, self.blocks, self.crossed, self.travelling = (mine, arrived), blocks, (), ()
        self.plain = lax.axis_size("dp") != SHARDS
        self.crossed_rows, self.ring_at = 0, 0
        if not self.plain:
            at = lax.axis_index("dp")
            self.z, self.x = at // 2, at % 2

    def state(self):
        return (self.terms, self.crossed, self.travelling)

    def set(self, state):
        self.terms, self.crossed, self.travelling = state

    def cross(self, rows=None):
        if self.plain:
            return
        first, last = self.crossed_rows, rows or self.terms[0].shape[1]
        self.crossed_rows = last
        others = []
        for term in self.terms:
            cut = term.reshape(4, 2, *term.shape[1:])[:, :, first:last]
            others.append(pick_row(cut, 1 - self.x, 1))
        pairs = [(n, n ^ 1) for n in range(8)]
        self.crossed += (lax.ppermute(plus(*others), "dp", pairs),)

    def part(self, z, *more):
        values = []
        for term in self.terms:
            _, rows, cols = term.shape
            cut = lax.dynamic_slice(
                term.reshape(4, 2, rows, cols), (z, self.x, 0, 0), (1, 1, rows, cols)
            )
            values.append(cut[0, 0])
        values.append(jnp.concatenate([pick_row(part, z) for part in self.crossed], axis=0))
        return plus(*values, *more)

    def ring(self):
        if self.plain:
            return
        self.ring_at += 1
        passing = self.part(lax.rem(self.z + 4 - self.ring_at, 4), *self.travelling)
        self.travelling = (lax.ppermute(passing, "dp", [(n, (n + 2) % 8) for n in range(8)]),)

    def direct(self):
        if self.plain:
            return
        arrived = []
        for far in (3, 2, 1):
            for way in (far, -far):
                part = self.part(jnp.clip(self.z + way, 0, 3))
                routes = [(n, n + 2 * way) for n in range(8) if 0 <= n + 2 * way < 8]
                arrived.append(lax.ppermute(part, "dp", routes))
        self.travelling = tuple(arrived)

    def result(self):
        if not self.plain:
            return self.part(self.z, *self.travelling)
        shards = lax.axis_size("dp")
        parts, at, value = [], 0, plus(*self.terms)
        for rows in self.blocks:
            part = value[:, at : at + rows].reshape(shards, -1, value.shape[2])
            parts, at = parts + [part], at + rows
        whole = jnp.concatenate(parts, axis=1)
        return lax.psum_scatter(whole, "dp", scatter_dimension=0, tiled=True)[0]


def body(
    tokens_in, seg_starts, pad_mask, w_qkv, b_qv, w_attn_out, b_attn_out, ln_gain, ln_bias,
    w_up, b_up, w_down, b_down, w_proj, cotangent,
):
    section_at = lax.axis_index("section")
    core = section_at % 2
    is_late = section_at >= 2
    flip = core == 1
    quarter = tokens_in.shape[1]
    length, width = 4 * quarter, tokens_in.shape[2]
    ff_width = w_up.shape[2]
    proj_cols = w_proj.shape[1]
    shards = lax.axis_size("dp")
    share = width // shards

    def sel_for(half):
        return jnp.stack([core, section_at // 2, half]).astype(jnp.int32)

    sel_mine, sel_theirs = sel_for(core), sel_for(1 - core)

    own = pick_row(tokens_in, core)
    other = pick_row(tokens_in, 1 - core)
    straight = send(own, [(2, 0), (3, 1)])
    crossed = send(other, [(2, 1), (3, 0)])
    near = swap_cores(other)
    small = pack_small(b_qv[0], b_attn_out[0], ln_gain[0], ln_bias[0], b_up[0], b_down[0])[None]
    small_other = swap_cores(small)
    small = jnp.stack([jnp.where(flip, small_other, small), jnp.where(flip, small, small_other)])
    weights = tuple((w[0], swap_cores(w[0])) for w in (w_qkv, w_attn_out, w_up, w_down)) + (small,)
    x = jnp.concatenate(
        [
            jnp.where(flip, near, own),
            jnp.where(flip, own, near),
            jnp.where(flip, crossed, straight),
            jnp.where(flip, straight, crossed),
        ],
        axis=0,
    )

    head_own = jnp.concatenate([w_proj.T, pick_row(cotangent, core).T], axis=1)
    head_other = jnp.concatenate([w_proj.T, pick_row(cotangent, 1 - core).T], axis=1)
    head_late = send(head_other, [(2, 3), (3, 2)])
    head_straight = send(head_own, [(0, 2), (1, 3)])
    head_crossed = send(head_other, [(0, 3), (1, 2)])
    head_cols = jnp.concatenate(
        [
            jnp.where(flip, head_crossed, head_straight),
            jnp.where(flip, head_straight, head_crossed),
            jnp.where(flip, head_late, head_own),
            jnp.where(flip, head_own, head_late),
        ],
        axis=0,
    )
    proj_rows, given_rows = head_cols[:, :width], head_cols[:, width:]
    plan = attention_plan(pick_row(seg_starts, core), pick_row(pad_mask, core))

    def both_forward(rows):
        middle, kept_even = layer_forward(sel_mine, rows, weights, 0, plan)
        last, kept_odd = layer_forward(sel_mine, middle, weights, 1, plan)
        return (last, kept_even, kept_odd)

    early, kept_even, kept_odd = both_forward(x)
    hopped = send(early, [(0, 2), (1, 3)])
    hopped, proj_rows, given_rows = lax.optimization_barrier((hopped, proj_rows, given_rows))

    def late_turn(rows, *_):
        last, kept_even, kept_odd = both_forward(rows)
        embedded, grad_proj, grad = head(last, proj_rows, given_rows)
        grad, grads_odd, sums_odd = layer_backward(sel_mine, grad, kept_odd, weights, 1, plan)
        grad, grads_even, sums_even = layer_backward(sel_mine, grad, kept_even, weights, 0, plan)
        return (
            kept_even, kept_odd, embedded, grad_proj, grad,
            grads_odd, sums_odd, grads_even, sums_even,
        )

    def early_turn(rows, kept_even, kept_odd):
        row, ff = jnp.zeros((length, width), BF), jnp.zeros((length, ff_width), BF)
        grads = (row, ff, row, jnp.zeros((3, length, width), BF))
        sums = (
            jnp.zeros((6, width), F32),
            jnp.zeros((1, ff_width), F32),
            jnp.zeros((2, width), F32),
        )
        return (
            kept_even, kept_odd, jnp.zeros((4 * proj_cols, length), BF),
            jnp.zeros((width, 4 * proj_cols), BF), row, grads, sums, grads, sums,
        )

    (
        kept_even, kept_odd, embedded, grad_proj, grad_mid,
        late_odd, late_sums_odd, late_even, late_sums_even,
    ) = lax.cond(is_late, late_turn, early_turn, hopped, kept_even, kept_odd)

    halfway = length // 2
    arriving = [
        send(grad_mid[at : at + halfway], [(2, 0), (3, 1)]) for at in (0, halfway)
    ]
    embedded_cols = embedded.reshape(4, proj_cols, length)

    rows_of_one = width // SHARDS
    attend_blocks = (rows_of_one,) * 4
    feed_blocks = (rows_of_one,) * (ff_width // (2 * HALF)) + (ff_width // SHARDS,)

    def tie(*values):
        return lax.optimization_barrier(values)

    def feed_args(kept, late, now):
        return (kept[4], late[1], now[1], kept[9], late[0], now[0])

    def attend_args(kept, late, now, mixed):
        return (kept[2], kept[0], late[2], now[2], late[3], mixed)

    def tie_sums(values, *sums):
        values, states = tie(values, [part.state() for part in sums])
        for part, state in zip(sums, states):
            part.set(state)
        return values

    grad_context, grads_odd, sums_odd = feed_backward(sel_mine, arriving, kept_odd, weights, 1)
    args = feed_args(kept_odd, late_odd, grads_odd)
    arrived = swap_cores(feed_grads(sel_theirs, *args))
    feed_odd = RowSum(feed_grads(sel_mine, *args), arrived, feed_blocks)
    grad_context = tie_sums(grad_context, feed_odd)
    feed_odd.cross(rows_of_one * 6)
    straight_cols = send(pick_row(embedded_cols, core), [(2, 0), (3, 1)])
    crossed_cols = send(pick_row(embedded_cols, 1 - core), [(2, 1), (3, 0)])
    near_cols = swap_cores(pick_row(embedded_cols, 3 - core))
    mixed_odd, grad, mix_sums = mixed_backward(
        sel_mine, grad_context, grads_odd[2], kept_odd, weights, 1, plan
    )
    sums_odd = sums_odd + (mix_sums,)
    args = attend_args(kept_odd, late_odd, grads_odd, mixed_odd)
    args, straight_cols, crossed_cols, near_cols = tie_sums(
        (args, straight_cols, crossed_cols, near_cols), feed_odd
    )
    feed_odd.cross()
    theirs = attend_grads(sel_theirs, *args)
    args, theirs = tie_sums((args, theirs), feed_odd)
    feed_odd.ring()
    arrived = swap_cores(theirs)
    attend_odd = RowSum(attend_grads(sel_mine, *args), arrived, attend_blocks)
    grad = tie_sums(grad, feed_odd, attend_odd)
    feed_odd.ring()
    attend_odd.cross()

    grad_context, grads_even, sums_even = feed_backward(sel_mine, (grad,), kept_even, weights, 0)
    args = tie_sums(feed_args(kept_even, late_even, grads_even), feed_odd, attend_odd)
    feed_odd.ring()
    theirs = feed_grads(sel_theirs, *args)
    args, theirs = tie_sums((args, theirs), feed_odd)
    attend_odd.ring()
    arrived = swap_cores(theirs)
    feed_even = RowSum(feed_grads(sel_mine, *args), arrived, feed_blocks)
    grad_context = tie_sums(grad_context, feed_even, attend_odd)
    feed_even.cross()
    attend_odd.ring()
    mixed_even, grad, mix_sums = mixed_backward(
        sel_mine, grad_context, grads_even[2], kept_even, weights, 0, plan
    )
    sums_even = sums_even + (mix_sums,)
    args = attend_args(kept_even, late_even, grads_even, mixed_even)
    args = tie_sums(args, feed_even, attend_odd)
    feed_even.ring()
    routes_odd, routes_even = ((0, 1), (2, 3)), ((1, 0), (3, 2))
    feed_odd = feed_odd.result()
    theirs = attend_grads(sel_theirs, *args)
    extras = pack_extras(sel_mine, grad_proj, late_sums_even, late_sums_odd, sums_even, sums_odd)
    theirs = jnp.concatenate([theirs, extras.astype(BF)], axis=1)
    args, theirs, extras = tie_sums((args, theirs, extras), feed_even)
    arrived = swap_cores(theirs)
    feed_even.ring()
    attend_odd.ring()
    quarters = grad.reshape(4, quarter, width)
    near_grad = swap_cores(pick_row(quarters, 1 - core))
    mine = jnp.concatenate([attend_grads(sel_mine, *args), extras.astype(BF)], axis=1)
    mine, quarters, near_grad = tie_sums((mine, quarters, near_grad), feed_even, attend_odd)
    attend_even = RowSum(mine, arrived, attend_blocks)
    attend_even.cross()
    feed_even.ring()
    attend_odd = attend_odd.result()
    sent_odd = [send(part, routes_odd) for part in (feed_odd, attend_odd)]
    straight_grad = send(pick_row(quarters, 2 + core), [(0, 2), (1, 3)])
    crossed_grad = send(pick_row(quarters, 3 - core), [(0, 3), (1, 2)])
    straight_grad, crossed_grad, sent_odd = tie_sums(
        (straight_grad, crossed_grad, sent_odd), feed_even, attend_even
    )
    attend_even.direct()
    feed_even = feed_even.result()
    if shards == SHARDS:
        tail = attend_even.result()
        attend_even, extras = tail[: 4 * share], tail[4 * share :].astype(F32)
    else:
        attend_even = attend_even.result()
        extras = plus(mine[:, -EXTRA_ROWS:], arrived[:, -EXTRA_ROWS:])
        extras = lax.psum(extras.astype(F32), "dp")

    def halves(even, odd, sent):
        arrived = jnp.where(flip, sent, send(even, routes_even))
        mine = jnp.where(flip, odd, even)
        return (jnp.where(flip, arrived, mine), jnp.where(flip, mine, arrived))

    blocks = ff_width // (2 * HALF)
    feed_halves = halves(feed_even, feed_odd, sent_odd[0])
    attend_halves = halves(attend_even, attend_odd, sent_odd[1])

    def columns(pair, first, count):
        parts = [part[n * share : (n + 1) * share] for part in pair for n in range(first, first + count)]
        return jnp.concatenate(parts, axis=1).astype(F32)

    grad_w_up = columns(feed_halves, 0, blocks)[None]
    grad_w_down = jnp.concatenate([part[blocks * share :] for part in feed_halves], axis=1)
    grad_w_down = grad_w_down.astype(F32)[None]
    grad_w_out = columns(attend_halves, 0, 1)[None]
    grad_w_qkv = jnp.concatenate([columns(attend_halves, 1 + c, 1) for c in range(3)], axis=1)[None]

    if shards == SHARDS:
        at, pick = 0, lambda values: values
    else:
        at = lax.axis_index("dp") % (shards // SHARDS)
        extras = pick_row(extras, lax.axis_index("dp") // (shards // SHARDS))

        def pick(values):
            size = values.shape[-1] * SHARDS // shards
            return lax.dynamic_slice_in_dim(values, at * size, size, values.ndim - 1)

    one = width // SHARDS
    small_mine = jnp.where(flip, extras[8:16], extras[:8])
    grad_b_up = pick(small_mine[0:1, : ff_width // SHARDS])
    grad_b_qv = pick(small_mine[1:2, : 2 * one])
    rows = pick(small_mine[2:8, :one])
    grad_proj = extras[16:].reshape(-1, 3, 4 * proj_cols).transpose(1, 0, 2)
    grad_proj = grad_proj.reshape(one, 4 * proj_cols)
    grad_proj = lax.dynamic_slice_in_dim(grad_proj, at * share, share, 0).astype(BF)
    grad_proj = jnp.where(is_late, grad_proj, send(grad_proj, [(2, 0), (3, 1)])).astype(F32)
    grad_w_proj = lax.dynamic_slice_in_dim(grad_proj, section_at * proj_cols, proj_cols, 1)

    own_cols = jnp.where(is_late, pick_row(embedded_cols, section_at), straight_cols)
    other_cols = jnp.where(is_late, near_cols, crossed_cols)
    embedded_out = jnp.stack(
        [jnp.where(flip, other_cols, own_cols).T, jnp.where(flip, own_cols, other_cols).T]
    )

    mine = jnp.where(is_late, straight_grad, pick_row(quarters, core))
    others = jnp.where(is_late, crossed_grad, near_grad)
    grad_in = jnp.stack(
        [jnp.where(flip, others, mine), jnp.where(flip, mine, others)]
    ).astype(F32)

    return (
        embedded_out,
        grad_in,
        grad_w_qkv,
        grad_b_qv,
        grad_w_out,
        rows[0][None],
        rows[1:3][None],
        rows[3:5][None],
        grad_w_up,
        grad_b_up,
        grad_w_down,
        rows[5][None],
        grad_w_proj,
    )


def solution(mesh):
    in_specs = (
        P("dp", "section", None),
        P("dp", None),
        P("dp", None),
        P("section", None, None),
        P("section", None),
        P("section", None, None),
        P("section", None),
        P("section", None, None),
        P("section", None, None),
        P("section", None, None),
        P("section", None),
        P("section", None, None),
        P("section", None),
        P(None, "section"),
        P("dp", None, "section"),
    )
    out_specs = (
        P("dp", None, "section"),
        P("dp", "section", None),
        P("section", "dp", None),
        P("section", "dp"),
        P("section", "dp", None),
        P("section", "dp"),
        P("section", None, "dp"),
        P("section", None, "dp"),
        P("section", "dp", None),
        P("section", "dp"),
        P("section", "dp", None),
        P("section", "dp"),
        P("dp", "section"),
    )
    return jax.shard_map(body, mesh=mesh, in_specs=in_specs, out_specs=out_specs, check_vma=False)
```

```python
from functools import partial
import math

import jax
import jax.numpy as jnp
from jax import lax
from jax.experimental import pallas as pl
from jax.experimental.pallas import tpu as pltpu
from jax.sharding import PartitionSpec as P

HEAD = 64
PAIR = 2 * HEAD
QB = 128
KB = 512
KEYS = 256
EPS_NORM = 1e-05
EPS_PROJ = 1e-06
NEG_FILL = -1e30
PARAMS = pltpu.CompilerParams(vmem_limit_bytes=60 * 1024 * 1024)


def cost(micros):
    return pl.CostEstimate(flops=int(micros * 1e9), bytes_accessed=1024, transcendentals=0)


BF = jnp.bfloat16
F32 = jnp.float32

NT = (((1,), (1,)), ((), ()))
TN = (((0,), (0,)), ((), ()))


def dot(a, b):
    return jnp.dot(a, b, preferred_element_type=F32)


def dot_nt(a, b):
    return lax.dot_general(a, b, NT, preferred_element_type=F32)


def dot_tn(a, b):
    return lax.dot_general(a, b, TN, preferred_element_type=F32)


def pack_small(b_qv, b_out, gains, shifts, b_up, b_down):
    return jnp.concatenate(
        [b_up, b_qv, b_out, gains[0], gains[1], shifts[0], shifts[1], b_down]
    )


def small_spec(layer, width):
    return pl.BlockSpec((1, 1, width), lambda *_: (layer, 0, 0))


def attention_plan(starts, real_flags):
    length = real_flags.shape[0]
    places = jnp.arange(length, dtype=jnp.int32)
    segment = jnp.sum((starts[None, :] <= places[:, None]).astype(jnp.int32), axis=1)
    key_code = jnp.where(real_flags == 1, segment, -1).astype(F32)
    key_code = jnp.broadcast_to(key_code[:, None], (length, PAIR))
    query_code = segment.astype(F32).reshape(length // QB, QB)
    first = jnp.arange(length // QB, dtype=jnp.int32) * QB
    low = jnp.max(jnp.where(starts[None, :] <= first[:, None], starts[None, :], 0), axis=1)
    high = jnp.min(
        jnp.where(starts[None, :] > first[:, None] + (QB - 1), starts[None, :], length), axis=1
    )
    begin = (low // QB) * QB
    count = (high - begin + KEYS - 1) // KEYS
    begin = jnp.minimum(begin, length - KEYS * count)
    return (begin, count, key_code, query_code)


def pair_mask(rows):
    return lax.broadcasted_iota(jnp.int32, (rows, PAIR), 1) < HEAD


def stacked_heads(block):
    first = pair_mask(block.shape[0])
    zero = jnp.zeros_like(block)
    return jnp.concatenate([jnp.where(first, block, zero), jnp.where(first, zero, block)], axis=0)


def block_bias(key_code, query_code, key_at, query_at):
    shape = key_code.shape
    keys = lax.broadcasted_iota(jnp.int32, shape, 0) + (key_at - query_at)
    same = keys == lax.broadcasted_iota(jnp.int32, shape, 1)
    bias = jnp.where((key_code == query_code) | same, 0.0, NEG_FILL)
    return jnp.concatenate([bias, bias], axis=1)


def over_keys(begin, count, step, state):
    state = lax.fori_loop(
        0,
        lax.shift_right_logical(count, 1),
        lambda j, now: step(pl.multiple_of(begin + j * KB, QB), KB, now),
        state,
    )
    last = pl.multiple_of(begin + (count - 1) * KEYS, QB)
    return lax.fori_loop(
        0, jnp.bitwise_and(count, 1), lambda _, now: step(last, KEYS, now), state
    )


def unstack_heads(flat):
    rows = lax.broadcasted_iota(jnp.int32, (PAIR, QB), 0)
    return jnp.where(rows < HEAD, flat[:PAIR, :QB], flat[:PAIR, QB:]).T


SAFE_SCORE = 70.0


def score_bound(peak):
    lanes = lax.broadcasted_iota(jnp.int32, peak.shape, 1)
    return jnp.max(jnp.where(lanes < HEAD, peak, 0.0)) * jnp.max(jnp.where(lanes < HEAD, 0.0, peak))


def head_lanes(width):
    rows = lax.broadcasted_iota(jnp.int32, (2 * width, PAIR), 0)
    lanes = lax.broadcasted_iota(jnp.int32, (2 * width, PAIR), 1)
    head = lax.shift_right_logical(rows, 6)
    wanted = jnp.where(rows < width, head, head - width // HEAD + HEAD)
    return jnp.where(lanes == wanted, 1.0, 0.0).astype(BF)


def attend_forward(
    begin_ref, count_ref, qkv_ref, key_code_ref, query_code_ref, out_ref, logsum_ref,
    value_scr, query_scr, total_scr, is_safe,
):
    length = qkv_ref.shape[1]
    pairs = qkv_ref.shape[2] // PAIR
    every = range(pairs)
    cols = [slice(p * PAIR, (p + 1) * PAIR) for p in every]
    for p in every:
        value_scr[p, :PAIR, :] = qkv_ref[2, :, cols[p]].T
        value_scr[p, PAIR:, :] = jnp.ones((value_scr.shape[1] - PAIR, length), BF)

    def one_query_block(shifted, i, _):
        query_at = pl.multiple_of(i * QB, QB)
        begin, count = begin_ref[i], count_ref[i]
        query_code = query_code_ref[pl.ds(i, 1), :]
        for p in every:
            query_scr[p] = stacked_heads(qkv_ref[0, pl.ds(query_at, QB), cols[p]])
        total_scr[...] = jnp.zeros_like(total_scr)

        def one_key_block(key_at, size, tops):
            rows = pl.ds(key_at, size)
            bias = block_bias(key_code_ref[rows, :], query_code, key_at, query_at)
            scores = [dot_nt(qkv_ref[1, rows, cols[p]], query_scr[p]) + bias for p in every]
            if not shifted:
                probs = [jnp.exp(scores[p]).astype(BF) for p in every]
                for p in every:
                    total_scr[p] += dot(value_scr[p, :, rows], probs[p])
                return tops
            fresh = [
                jnp.maximum(tops[p], jnp.max(scores[p], axis=0, keepdims=True)) for p in every
            ]
            probs = [jnp.exp(scores[p] - fresh[p]).astype(BF) for p in every]
            for p in every:
                total_scr[p] = total_scr[p] * jnp.exp(tops[p] - fresh[p]) + dot(
                    value_scr[p, :, rows], probs[p]
                )
            return tuple(fresh)

        lowest = 2 * NEG_FILL if shifted else 0.0
        tops = tuple(jnp.full((1, 2 * QB), lowest, F32) for _ in every)
        tops = over_keys(begin, count, one_key_block, tops)
        for p in every:
            weight = total_scr[p, PAIR : PAIR + 1, :]
            logsum_ref[pl.ds(p * (length // QB) + i, 1), :] = tops[p] + jnp.log(weight)
            out_ref[pl.ds(query_at, QB), cols[p]] = unstack_heads(
                total_scr[p, :PAIR, :] * (1.0 / weight)
            ).astype(BF)
        return 0

    for wanted, shifted in ((is_safe, False), (jnp.logical_not(is_safe), True)):

        @pl.when(wanted)
        def _():
            lax.fori_loop(0, length // QB, partial(one_query_block, shifted), 0)


def attend_backward(
    begin_ref, count_ref, qkv, key_code_ref, query_code_ref, context, logsum_ref, grad, sums_ref,
    key_scr, query_scr, given_scr, down_scr, grad_key_scr, grad_value_scr,
):
    length = qkv.shape[1]
    pairs = qkv.shape[2] // PAIR
    every = range(pairs)
    blocks = length // QB
    cols = [slice(p * PAIR, (p + 1) * PAIR) for p in every]
    for p in every:
        key_scr[p] = qkv[1, :, cols[p]].T

    def one_query_block(i, _):
        query_at = pl.multiple_of(i * QB, QB)
        queries = pl.ds(query_at, QB)
        begin, count = begin_ref[i], count_ref[i]
        query_code = query_code_ref[pl.ds(i, 1), :]
        inner, logsum = [], []
        for p in every:
            query_scr[p] = stacked_heads(qkv[0, queries, cols[p]])
            given = grad[queries, cols[p]]
            given_scr[p] = stacked_heads(given)
            both = (given.astype(F32) * context[queries, cols[p]].astype(F32)).T
            inner.append(
                jnp.concatenate(
                    [
                        jnp.sum(both[:HEAD], axis=0, keepdims=True),
                        jnp.sum(both[HEAD:], axis=0, keepdims=True),
                    ],
                    axis=1,
                )
            )
            logsum.append(logsum_ref[pl.ds(p * blocks + i, 1), :])
        down_scr[...] = jnp.zeros_like(down_scr)

        def one_key_block(key_at, size, state):
            rows = pl.ds(key_at, size)
            bias = block_bias(key_code_ref[rows, :], query_code, key_at, query_at)
            parts, grads, probs, scores = {}, {}, {}, {}
            for p in range(pairs + 1):
                if p < pairs:
                    grads[p] = dot_nt(qkv[2, rows, cols[p]], given_scr[p]) - inner[p]
                    parts[p] = dot_nt(qkv[1, rows, cols[p]], query_scr[p]) + bias
                if 0 <= p - 1 < pairs:
                    q = p - 1
                    probs[q] = jnp.exp(parts.pop(q) - logsum[q])
                    scores[q] = (probs[q] * grads.pop(q)).astype(BF)
                    probs[q] = probs[q].astype(BF)
                if 0 <= p - 1 < pairs:
                    q = p - 1
                    grad_value_scr[rows, cols[q]] += dot(probs.pop(q), given_scr[q])
                    grad_key_scr[rows, cols[q]] += dot(scores[q], query_scr[q])
                    down_scr[q] += dot(key_scr[q, :, rows], scores.pop(q))
            return state

        over_keys(begin, count, one_key_block, 0)
        for p in every:
            grad_query = (unstack_heads(down_scr[p]) * (HEAD**-0.5)).astype(BF)
            qkv[0, queries, cols[p]] = grad_query
            sums_ref[0:1, cols[p]] += jnp.sum(grad_query.astype(F32), axis=0, keepdims=True)
        return 0

    lax.fori_loop(0, blocks, one_query_block, 0)
    qkv[1] = grad_key_scr[...].astype(BF)
    grad_value = grad_value_scr[...].astype(BF)
    qkv[2] = grad_value
    sums_ref[1:2, :] = jnp.sum(grad_value.astype(F32), axis=0, keepdims=True)


ANY = pl.BlockSpec(memory_space=pl.ANY)
ROWS = 256


class Held:
    def __init__(self, sel_ref, layer, pairs, held, sems, first=None):
        self.own = sel_ref[0] == layer
        self.items = list(zip(pairs, held, range(len(held))))
        self.sems = sems
        self.first = pl.program_id(0) == 0 if first is None else first

    def start(self):
        for pair, held, n in self.items:
            for wanted, source in zip((self.own, jnp.logical_not(self.own)), pair):

                @pl.when(self.first & wanted)
                def _():
                    pltpu.make_async_copy(source, held, self.sems.at[n]).start()

    def wait(self, n):
        pair, held, _ = self.items[n]

        @pl.when(self.first)
        def _():
            pltpu.make_async_copy(pair[0], held, self.sems.at[n]).wait()


def held_shapes(*weights):
    return [pltpu.VMEM(own.shape, own.dtype) for own, _ in weights]


def normalized(values):
    centred = values - jnp.mean(values, axis=-1, keepdims=True)
    inverse = lax.rsqrt(jnp.mean(centred * centred, axis=-1, keepdims=True) + EPS_NORM)
    return (centred * inverse, inverse)


def normalized_pull(grad_hat, hat, inverse):
    return inverse * (
        grad_hat
        - jnp.mean(grad_hat, axis=-1, keepdims=True)
        - hat * jnp.mean(grad_hat * hat, axis=-1, keepdims=True)
    )


ERF = (0.254829592, -0.284496736, 1.421413741, -1.453152027, 1.061405429)
ERF_SLOPE = 0.3275911


def gelu_parts(x):
    t = pl.reciprocal(1.0 + (ERF_SLOPE * math.sqrt(0.5)) * jnp.abs(x), approx=True)
    bell = jnp.exp(-0.5 * (x * x))
    tail = 0.5 * ERF[4]
    for term in ERF[3::-1]:
        tail = tail * t + 0.5 * term
    tail = tail * t * bell
    below = jnp.where(x >= 0, 1.0 - tail, tail)
    return (x * below, below + x * bell * (1.0 / math.sqrt(2.0 * math.pi)))


FB = 1024


def small_slices(width, ff_width):
    names = ("b_q", "b_v", "b_out", "gain1", "gain2", "shift1", "shift2", "b_down")
    at = {"b_up": slice(0, ff_width)}
    for n, name in enumerate(names):
        at[name] = slice(ff_width + n * width, ff_width + (n + 1) * width)
    return at


def refine_back_kernel(
    layer, sel_ref, grad_ref, hidden_ref, out_ref, scale1_ref, scale2_ref, slope_ref,
    out_own_ref, out_other_ref, up_own_ref, up_other_ref, down_own_ref, down_other_ref, small_ref,
    grad_low_ref, grad_raised_ref, grad_attn_ref, grad_context_ref, sums_ref, up_sums_ref,
    w_out, w_up, w_down, sems,
):
    pairs = [(out_own_ref, out_other_ref), (up_own_ref, up_other_ref), (down_own_ref, down_other_ref)]
    weights = Held(sel_ref, layer, pairs, [w_out, w_up, w_down], sems)
    weights.start()
    rows, width = grad_ref.shape
    ff_width = slope_ref.shape[1]
    at = small_slices(width, ff_width)

    @pl.when(pl.program_id(0) == 0)
    def _():
        sums_ref[...] = jnp.zeros_like(sums_ref)
        up_sums_ref[...] = jnp.zeros_like(up_sums_ref)

    def vector(name):
        return small_ref[0, :, at[name]]

    def add(row, values):
        sums_ref[row : row + 1, :] += jnp.sum(values, axis=0, keepdims=True)

    grad = grad_ref[...].astype(F32)
    hat = (out_ref[...].astype(F32) - vector("shift2")) * (1.0 / vector("gain2"))
    joined = normalized_pull(grad * vector("gain2"), hat, scale2_ref[:, :1])
    low = joined.astype(BF)
    grad_low_ref[...] = low
    add(2, grad * hat)
    add(4, grad)
    add(5, low.astype(F32))
    weights.wait(2)
    weights.wait(1)
    total = joined
    parts = [slice(f, f + FB) for f in range(0, ff_width, FB)]
    active = dot_nt(low, w_down[parts[0], :])
    for n, part in enumerate(parts):
        following = dot_nt(low, w_down[parts[n + 1], :]) if n + 1 < len(parts) else None
        raised = active * slope_ref[:, part].astype(F32)
        up_sums_ref[:, part] += jnp.sum(raised, axis=0, keepdims=True)
        raised = raised.astype(BF)
        grad_raised_ref[:, part] = raised
        total += dot_nt(raised, w_up[:, part])
        active = following
    hat = (hidden_ref[...].astype(F32) - vector("shift1")) * (1.0 / vector("gain1"))
    summed = normalized_pull(total * vector("gain1"), hat, scale1_ref[:, :1])
    attn = summed.astype(BF)
    grad_attn_ref[...] = attn
    weights.wait(0)
    grad_context_ref[...] = dot_nt(attn, w_out[...]).astype(BF)
    add(1, total * hat)
    add(3, total)
    add(0, attn.astype(F32))


def refine_back_second_kernel(layer, *refs):
    refine_back_kernel(layer, *refs[:14], *refs[18:])


def refine_back(sel, grad, kept, weights, layer, first=0, begun=()):
    w_out, w_up, w_down, small = weights
    hidden, out, scale1, scale2, slope = kept
    length, width = hidden.shape
    ff_width = w_up[0].shape[1]
    at = first // ROWS
    rows = pl.BlockSpec((ROWS, width), lambda n, _: (n + at, 0))
    lanes = pl.BlockSpec((ROWS, 128), lambda n, _: (n + at, 0))
    part = pl.BlockSpec((ROWS, ff_width), lambda n, _: (n + at, 0))
    row_shape = jax.ShapeDtypeStruct((length, width), BF)
    return pl.pallas_call(
        partial(refine_back_second_kernel if begun else refine_back_kernel, layer),
        name="refine_back",
        grid_spec=pltpu.PrefetchScalarGridSpec(
            num_scalar_prefetch=1,
            grid=(grad.shape[0] // ROWS,),
            in_specs=[
                pl.BlockSpec((ROWS, width), lambda n, _: (n, 0)),
                rows, rows, lanes, lanes, part,
            ]
            + [ANY] * 6
            + [small_spec(layer, small.shape[2])]
            + [ANY] * len(begun),
            out_specs=[
                rows, part, rows, rows,
                pl.BlockSpec((6, width), lambda n, _: (0, 0)),
                pl.BlockSpec((1, ff_width), lambda n, _: (0, 0)),
            ],
            scratch_shapes=[
                *held_shapes(w_out, w_up, w_down),
                pltpu.SemaphoreType.DMA((3,)),
            ],
        ),
        out_shape=[
            row_shape,
            jax.ShapeDtypeStruct((length, ff_width), BF),
            row_shape,
            row_shape,
            jax.ShapeDtypeStruct((6, width), F32),
            jax.ShapeDtypeStruct((1, ff_width), F32),
        ],
        input_output_aliases={14 + n: n for n in range(len(begun))},
        compiler_params=PARAMS,
        cost_estimate=cost(24),
    )(sel, grad, hidden, out, scale1, scale2, slope, *w_out, *w_up, *w_down, small, *begun)


def head_kernel(rows_ref, proj_ref, given_ref, embedded_ref, grad_proj_ref, grad_rows_ref):
    factor = math.sqrt(proj_ref.shape[0])
    columns = dot_nt(proj_ref[...], rows_ref[...])
    given = given_ref[...].astype(F32)
    inverse = lax.rsqrt(jnp.sum(columns * columns, axis=0, keepdims=True) + EPS_PROJ)
    cross = jnp.sum(columns * given, axis=0, keepdims=True)
    embedded_ref[...] = (factor * columns * inverse).astype(BF)
    grad = (factor * (given * inverse - columns * (cross * inverse * inverse * inverse))).astype(BF)
    grad_proj_ref[...] = dot(grad, rows_ref[...]).T.astype(BF)
    grad_rows_ref[...] = dot_tn(grad, proj_ref[...]).astype(BF)


def head(rows, proj, given):
    length, width = rows.shape
    cols = proj.shape[0]
    return pl.pallas_call(
        head_kernel,
        name="head",
        out_shape=[
            jax.ShapeDtypeStruct((cols, length), BF),
            jax.ShapeDtypeStruct((width, cols), BF),
            jax.ShapeDtypeStruct((length, width), BF),
        ],
        compiler_params=PARAMS,
        cost_estimate=cost(6),
    )(rows, proj, given)


HALF = 384
SHARDS = 8


def feed_grads_kernel(
    sel_ref, hidden_ref, raised_late_ref, raised_ref, active_ref, low_late_ref, low_ref, out_ref
):
    step = pl.program_id(0)
    shards, rows, _ = out_ref.shape
    blocks = raised_ref.shape[1] // HALF
    share = rows // blocks
    late = sel_ref[1] == 1

    def up(raised):
        part = dot_tn(hidden_ref[...], raised).astype(BF)
        for m in range(shards):
            for n in range(blocks):
                out_ref[m, n * share : (n + 1) * share, :] = part[
                    m * share : (m + 1) * share, n * HALF : (n + 1) * HALF
                ]

    def down(low):
        for m in range(shards):
            out_ref[m] = dot_tn(active_ref[:, m * rows : (m + 1) * rows], low).astype(BF)

    for wanted, raised_now, low_now in (
        (late, raised_late_ref, low_late_ref),
        (jnp.logical_not(late), raised_ref, low_ref),
    ):

        @pl.when(wanted & (step < 2))
        def _():
            up(raised_now[...])

        @pl.when(wanted & (step >= 2))
        def _():
            down(low_now[...])


def feed_grads(sel, hidden, raised_late, raised, active, low_late, low):
    length, width = hidden.shape
    ff_width = active.shape[1]
    half_ff = ff_width // 2

    def late_spec(shape, wanted):
        return pl.BlockSpec(shape, lambda n, sel: (0, jnp.where(sel[1] == wanted, sel[2], 0)))

    return pl.pallas_call(
        feed_grads_kernel,
        name="feed_grads",
        grid_spec=pltpu.PrefetchScalarGridSpec(
            num_scalar_prefetch=1,
            grid=(4,),
            in_specs=[
                pl.BlockSpec((length, width // 2), lambda n, _: (0, jnp.minimum(n, 1))),
                late_spec((length, half_ff), 1),
                late_spec((length, half_ff), 0),
                pl.BlockSpec((length, ff_width // 2), lambda n, _: (0, jnp.maximum(n - 2, 0))),
                late_spec((length, width // 2), 1),
                late_spec((length, width // 2), 0),
            ],
            out_specs=pl.BlockSpec(
                (SHARDS // 2, ff_width // SHARDS, HALF), lambda n, _: (lax.rem(n, 2), n // 2, 0)
            ),
        ),
        out_shape=jax.ShapeDtypeStruct((SHARDS, 2 * (ff_width // SHARDS), HALF), BF),
        compiler_params=PARAMS,
        cost_estimate=cost(12),
    )(sel, hidden, raised_late, raised, active, low_late, low)


def attend_grads_kernel(
    sel_ref, context_ref, x_ref, attn_late_ref, attn_ref, mixed_late_ref, mixed_ref, out_ref
):
    step = pl.program_id(0)
    late = sel_ref[1] == 1

    for wanted, attn_now, mixed_now in (
        (late, attn_late_ref, mixed_late_ref),
        (jnp.logical_not(late), attn_ref, mixed_ref),
    ):

        @pl.when(wanted & (step == 0))
        def _():
            part = dot_tn(context_ref[...], attn_now[...]).astype(BF)
            out_ref[...] = part.reshape(out_ref.shape)

        @pl.when(wanted & (step > 0))
        def _():
            part = dot_tn(x_ref[...], mixed_now[0]).astype(BF)
            out_ref[...] = part.reshape(out_ref.shape)


def attend_grads(sel, context, x, attn_late, attn, mixed_late, mixed):
    length, width = x.shape

    def late_spec(wanted):
        return pl.BlockSpec(
            (length, HALF), lambda n, sel: (0, jnp.where(sel[1] == wanted, sel[2], 0))
        )

    def mixed_spec(wanted):
        def at(n, sel):
            return (
                jnp.where(sel[1] == wanted, jnp.maximum(n - 1, 0), 0),
                0,
                jnp.where(sel[1] == wanted, sel[2], 0),
            )

        return pl.BlockSpec((1, length, HALF), at)

    whole = pl.BlockSpec((length, width), lambda n, _: (0, 0))
    share = width // SHARDS
    return pl.pallas_call(
        attend_grads_kernel,
        name="attend_grads",
        grid_spec=pltpu.PrefetchScalarGridSpec(
            num_scalar_prefetch=1,
            grid=(4,),
            in_specs=[whole, whole, late_spec(1), late_spec(0), mixed_spec(1), mixed_spec(0)],
            out_specs=pl.BlockSpec((SHARDS, share, HALF), lambda n, _: (0, n, 0)),
        ),
        out_shape=jax.ShapeDtypeStruct((SHARDS, 4 * share, HALF), BF),
        compiler_params=PARAMS,
        cost_estimate=cost(8),
    )(sel, context, x, attn_late, attn, mixed_late, mixed)


EXTRA_ROWS = 48


def pack_extras_kernel(
    sel_ref, proj_ref,
    late_sums_0, late_up_0, late_mix_0, late_sums_1, late_up_1, late_mix_1,
    sums_0, up_0, mix_0, sums_1, up_1, mix_1, out_ref,
):
    shards = out_ref.shape[0]
    width = sums_0.shape[1]
    share = width // shards
    third = share // 3
    cols = proj_ref.shape[1]
    out_ref[...] = jnp.zeros_like(out_ref)

    def layer(first, sums, up, mix):
        up_share = up.shape[1] // shards
        both = jnp.concatenate([mix[0:1, :], mix[1:2, :]], axis=1)
        for m in range(shards):
            rows = [up[0:1, m * up_share : (m + 1) * up_share]]
            rows += [both[:, 2 * m * share : 2 * (m + 1) * share]]
            rows += [sums[n : n + 1, m * share : (m + 1) * share] for n in range(6)]
            for n, row in enumerate(rows):
                out_ref[m, first + n : first + n + 1, : row.shape[1]] = row

    late = sel_ref[1] == 1
    for wanted, even, odd in (
        (late, (late_sums_0, late_up_0, late_mix_0), (late_sums_1, late_up_1, late_mix_1)),
        (jnp.logical_not(late), (sums_0, up_0, mix_0), (sums_1, up_1, mix_1)),
    ):

        @pl.when(wanted)
        def _():
            layer(0, *even)
            layer(8, *odd)

    for m in range(shards):
        for n in range(3):
            at = m * share + n * third
            out_ref[m, 16:, n * cols : (n + 1) * cols] = proj_ref[at : at + third, :].astype(F32)


def pack_extras(sel, proj, late_even, late_odd, even, odd):
    vmem = pl.BlockSpec(memory_space=pltpu.VMEM)
    return pl.pallas_call(
        pack_extras_kernel,
        name="pack_extras",
        in_specs=[pl.BlockSpec(memory_space=pltpu.SMEM)] + [vmem] * 13,
        out_specs=vmem,
        out_shape=jax.ShapeDtypeStruct((SHARDS, EXTRA_ROWS, HALF), F32),
        compiler_params=PARAMS,
        cost_estimate=cost(3),
    )(sel, proj, *late_even, *late_odd, *even, *odd)


def refine_block(
    rows, x, context, w_out, w_up, w_down, small_ref,
    hidden_rows, out_rows, scale1_ref, scale2_ref, active_rows, slope_rows,
):
    width, ff_width = w_up.shape
    at = small_slices(width, ff_width)

    def vector(name):
        return small_ref[0, :, at[name]]

    summed = x[rows, :].astype(F32) + dot(context[rows, :], w_out[...]) + vector("b_out")
    hat, inverse = normalized(summed)
    hidden = hat * vector("gain1") + vector("shift1")
    scale1_ref[rows, :] = jnp.broadcast_to(inverse, (ROWS, 128))
    hidden_low = hidden.astype(BF)
    hidden_rows[rows, :] = hidden_low
    total = hidden + vector("b_down")
    parts = [slice(f, f + FB) for f in range(0, ff_width, FB)]
    raised = dot(hidden_low, w_up[:, parts[0]])
    for m, part in enumerate(parts):
        following = dot(hidden_low, w_up[:, parts[m + 1]]) if m + 1 < len(parts) else None
        active, slope = gelu_parts(raised + small_ref[0, :, part])
        active = active.astype(BF)
        active_rows[rows, part] = active
        slope_rows[rows, part] = slope.astype(BF)
        total += dot(active, w_down[part, :])
        raised = following
    hat, inverse = normalized(total)
    scale2_ref[rows, :] = jnp.broadcast_to(inverse, (ROWS, 128))
    out_rows[rows, :] = (hat * vector("gain2") + vector("shift2")).astype(BF)


def refine_rest_kernel(
    layer, sel_ref, x_hbm, context_hbm,
    out_own_ref, out_other_ref, up_own_ref, up_other_ref, down_own_ref, down_other_ref, small_ref,
    hidden_begun, scale1_begun, scale2_begun, active_begun, slope_begun,
    out_hbm, hidden_hbm, scale1_ref, scale2_ref, active_hbm, slope_hbm,
    w_out, w_up, w_down, x, context, hidden_rows, out_rows, active_rows, slope_rows,
    weight_sems, in_sems, row_sems,
):
    pairs = [(out_own_ref, out_other_ref), (up_own_ref, up_other_ref), (down_own_ref, down_other_ref)]
    count = x.shape[0]
    first = x_hbm.shape[0] - count
    weights = Held(sel_ref, layer, pairs, [w_out, w_up, w_down], weight_sems, True)
    loads = [
        pltpu.make_async_copy(whole.at[pl.ds(first, count)], held, in_sems.at[n])
        for n, (whole, held) in enumerate(((x_hbm, x), (context_hbm, context)))
    ]
    for load in loads:
        load.start()
    weights.start()
    for load in loads:
        load.wait()
    for n in range(3):
        weights.wait(n)
    saved = [
        (hidden_rows, hidden_hbm, first), (out_rows, out_hbm, 0),
        (active_rows, active_hbm, first), (slope_rows, slope_hbm, first),
    ]

    def row_copies(n):
        return [
            pltpu.make_async_copy(
                rows.at[pl.ds(pl.multiple_of(n * ROWS, ROWS), ROWS)],
                whole.at[pl.ds(pl.multiple_of(n * ROWS + at, ROWS), ROWS)],
                row_sems.at[k, n],
            )
            for k, (rows, whole, at) in enumerate(saved)
        ]

    def refine_rows(n, _):
        refine_block(
            pl.ds(pl.multiple_of(n * ROWS, ROWS), ROWS), x, context, w_out, w_up, w_down,
            small_ref, hidden_rows, out_rows, scale1_ref, scale2_ref, active_rows, slope_rows,
        )
        for copy in row_copies(n):
            copy.start()
        return 0

    lax.fori_loop(0, count // ROWS, refine_rows, 0)
    for n in range(count // ROWS):
        for copy in row_copies(n):
            copy.wait()


def refine_rest(sel, x, context, weights, layer, begun, count):
    _, w_out, w_up, w_down, small = weights
    length, width = x.shape
    ff_width = w_up[0].shape[1]
    row = pltpu.VMEM((count, width), BF)
    wide = pltpu.VMEM((count, ff_width), BF)
    lanes = pl.BlockSpec((count, 128), lambda n, _: (length // count - 1, 0))
    return pl.pallas_call(
        partial(refine_rest_kernel, layer),
        name="refine_rest",
        grid_spec=pltpu.PrefetchScalarGridSpec(
            num_scalar_prefetch=1,
            grid=(1,),
            in_specs=[ANY] * 8 + [small_spec(layer, small.shape[2])] + [ANY] * 5,
            out_specs=[ANY, ANY, lanes, lanes, ANY, ANY],
            scratch_shapes=[
                *held_shapes(w_out, w_up, w_down),
                row, row, row, row, wide, wide,
                pltpu.SemaphoreType.DMA((3,)),
                pltpu.SemaphoreType.DMA((2,)),
                pltpu.SemaphoreType.DMA((4, count // ROWS)),
            ],
        ),
        out_shape=[jax.ShapeDtypeStruct((count, width), BF)]
        + [jax.ShapeDtypeStruct(part.shape, part.dtype) for part in begun],
        input_output_aliases={10 + n: 1 + n for n in range(5)},
        compiler_params=PARAMS,
        cost_estimate=cost(14),
    )(sel, x, context, *w_out, *w_up, *w_down, small, *begun)


def forward_kernel(
    layer, begin_ref, count_ref, sel_ref, x_hbm, key_code_ref, query_code_ref,
    mix_own_ref, mix_other_ref, out_own_ref, out_other_ref,
    up_own_ref, up_other_ref, down_own_ref, down_other_ref, small_ref,
    qkv_hbm, context_hbm, logsum_ref, out_hbm, hidden_hbm, scale1_ref, scale2_ref,
    active_hbm, slope_hbm,
    w_mix, w_out, w_up, w_down, x, qkv, context, hidden_rows, out_rows, active_rows, slope_rows,
    value_scr, query_scr, total_scr, peak, weight_sems, in_sems, qkv_sems, row_sems, context_sem,
):
    pairs = [
        (mix_own_ref, mix_other_ref), (out_own_ref, out_other_ref),
        (up_own_ref, up_other_ref), (down_own_ref, down_other_ref),
    ]
    length, width = x.shape
    ff_width = w_up.shape[1]
    blocks = length // ROWS
    at = small_slices(width, ff_width)

    def vector(name):
        return small_ref[0, :, at[name]]

    def rows_of(n):
        return pl.ds(pl.multiple_of(n * ROWS, ROWS), ROWS)

    def x_copy(n):
        return pltpu.make_async_copy(x_hbm.at[rows_of(n)], x.at[rows_of(n)], in_sems.at[n])

    def qkv_copy(n):
        return pltpu.make_async_copy(
            qkv.at[:, rows_of(n)], qkv_hbm.at[:, rows_of(n)], qkv_sems.at[n]
        )

    saved = [
        (hidden_rows, hidden_hbm), (out_rows, out_hbm),
        (active_rows, active_hbm), (slope_rows, slope_hbm),
    ]

    def row_copies(n):
        return [
            pltpu.make_async_copy(rows.at[rows_of(n)], whole.at[rows_of(n)], row_sems.at[k, n])
            for k, (rows, whole) in enumerate(saved)
        ]

    weights = Held(sel_ref, layer, pairs, [w_mix, w_out, w_up, w_down], weight_sems, True)
    for n in range(blocks):
        x_copy(n).start()
    weights.start()
    peak[...] = jnp.zeros_like(peak)
    lanes_of = head_lanes(width)
    weights.wait(0)

    def mix_rows(n, _):
        x_copy(n).wait()
        rows = rows_of(n)
        part = dot(x[rows, :], w_mix[...])
        queries = ((part[:, :width] + vector("b_q")) * HEAD**-0.5).astype(BF)
        keys = part[:, width : 2 * width].astype(BF)
        qkv[0, rows, :] = queries
        qkv[1, rows, :] = keys
        qkv[2, rows, :] = (part[:, 2 * width :] + vector("b_v")).astype(BF)
        lengths = dot(jnp.concatenate([queries * queries, keys * keys], axis=1), lanes_of)
        folded = lengths.reshape(ROWS // 8, 8, lengths.shape[1])
        peak[...] = jnp.maximum(peak[...], jnp.max(folded, axis=0))
        qkv_copy(n).start()
        return 0

    lax.fori_loop(0, blocks, mix_rows, 0)
    is_safe = score_bound(peak[...]) * 1.02 < SAFE_SCORE * SAFE_SCORE
    attend_forward(
        begin_ref, count_ref, qkv, key_code_ref, query_code_ref, context, logsum_ref,
        value_scr, query_scr, total_scr, is_safe,
    )
    context_copy = pltpu.make_async_copy(context, context_hbm, context_sem)
    context_copy.start()
    for n in (1, 2, 3):
        weights.wait(n)

    def refine_rows(n, _):
        refine_block(
            rows_of(n), x, context, w_out, w_up, w_down, small_ref,
            hidden_rows, out_rows, scale1_ref, scale2_ref, active_rows, slope_rows,
        )
        for copy in row_copies(n):
            copy.start()
        return 0

    last = out_hbm.shape[0] // ROWS
    lax.fori_loop(0, last, refine_rows, 0)
    context_copy.wait()
    for n in range(blocks):
        qkv_copy(n).wait()
    for n in range(last):
        for copy in row_copies(n):
            copy.wait()


def layer_forward(sel, x, weights, layer, plan, fed=None):
    w_qkv, w_out, w_up, w_down, small = weights
    begin, count, key_code, query_code = plan
    length, width = x.shape
    ff_width = w_up[0].shape[1]
    pairs = width // PAIR
    blocks = length // ROWS

    def whole(shape):
        return pl.BlockSpec(shape, lambda *_: (0,) * len(shape))

    row = jax.ShapeDtypeStruct((length, width), BF)
    lanes = jax.ShapeDtypeStruct((length, 128), F32)
    wide = jax.ShapeDtypeStruct((length, ff_width), BF)
    logsum_shape = (pairs * (length // QB), 2 * QB)
    qkv, context, logsum, out, hidden, scale1, scale2, active, slope = pl.pallas_call(
        partial(forward_kernel, layer),
        name="layer_forward",
        grid_spec=pltpu.PrefetchScalarGridSpec(
            num_scalar_prefetch=3,
            grid=(1,),
            in_specs=[ANY, whole(key_code.shape), whole(query_code.shape)]
            + [ANY] * 8
            + [small_spec(layer, small.shape[2])],
            out_specs=[
                ANY, ANY, whole(logsum_shape), ANY, ANY,
                whole((length, 128)), whole((length, 128)), ANY, ANY,
            ],
            scratch_shapes=[
                *held_shapes(w_qkv, w_out, w_up, w_down),
                pltpu.VMEM((length, width), BF),
                pltpu.VMEM((3, length, width), BF),
                pltpu.VMEM((length, width), BF),
                pltpu.VMEM((length, width), BF),
                pltpu.VMEM((length, width), BF),
                pltpu.VMEM((length, ff_width), BF),
                pltpu.VMEM((length, ff_width), BF),
                pltpu.VMEM((pairs, PAIR + 16, length), BF),
                pltpu.VMEM((pairs, 2 * QB, PAIR), BF),
                pltpu.VMEM((pairs, PAIR + 16, 2 * QB), F32),
                pltpu.VMEM((8, PAIR), F32),
                pltpu.SemaphoreType.DMA((4,)),
                pltpu.SemaphoreType.DMA((blocks,)),
                pltpu.SemaphoreType.DMA((blocks,)),
                pltpu.SemaphoreType.DMA((4, blocks)),
                pltpu.SemaphoreType.DMA,
            ],
        ),
        out_shape=[
            jax.ShapeDtypeStruct((3, length, width), BF), row,
            jax.ShapeDtypeStruct(logsum_shape, F32),
            jax.ShapeDtypeStruct((fed or length, width), BF),
            row, lanes, lanes, wide, wide,
        ],
        compiler_params=PARAMS,
        cost_estimate=cost(48),
    )(begin, count, sel, x, key_code, query_code, *w_qkv, *w_out, *w_up, *w_down, small)
    return (out, (x, qkv, context, logsum, hidden, out, scale1, scale2, slope, active))


def layer_forward_halves(sel, x, weights, layer, plan):
    half = x.shape[0] // 2
    first, kept = layer_forward(sel, x, weights, layer, plan, half)
    _, qkv, context, logsum, hidden, _, scale1, scale2, slope, active = kept
    second, hidden, scale1, scale2, active, slope = refine_rest(
        sel, x, context, weights, layer, (hidden, scale1, scale2, active, slope), half
    )
    out = jnp.concatenate([first, second], axis=0)
    return ((first, second), (x, qkv, context, logsum, hidden, out, scale1, scale2, slope, active))


def feed_backward(sel, grads, kept, weights, layer):
    first, begun, totals = 0, (), []
    for grad in grads:
        *begun, sums, up_sums = refine_back(
            sel, grad, kept[4:9], weights[1:], layer, first, tuple(begun)
        )
        first += grad.shape[0]
        totals.append((sums, up_sums))
    grad_low, grad_raised, grad_attn, grad_context = begun
    sums = tuple(sum(parts) for parts in zip(*totals))
    return (grad_context, (grad_low, grad_raised, grad_attn), sums)


def mixed_backward_kernel(
    layer, begin_ref, count_ref, sel_ref, qkv_hbm, key_code_ref, query_code_ref, context_hbm,
    logsum_ref, grad_hbm, skip_hbm, mix_own_ref, mix_other_ref,
    mixed_hbm, grad_x_hbm, sums_ref,
    w_mix, qkv, context, grad, skip, key_scr, query_scr, given_scr, down_scr,
    grad_key_scr, grad_value_scr, weight_sems, in_sems, mixed_sems, row_sems,
):
    length, width = skip.shape
    blocks = length // ROWS
    weights = Held(sel_ref, layer, [(mix_own_ref, mix_other_ref)], [w_mix], weight_sems, True)
    arrays = [(qkv_hbm, qkv), (context_hbm, context), (grad_hbm, grad), (skip_hbm, skip)]
    loads = [
        pltpu.make_async_copy(whole, held, in_sems.at[n]) for n, (whole, held) in enumerate(arrays)
    ]
    for load in loads:
        load.start()
    weights.start()
    grad_key_scr[...] = jnp.zeros_like(grad_key_scr)
    grad_value_scr[...] = jnp.zeros_like(grad_value_scr)
    sums_ref[...] = jnp.zeros_like(sums_ref)
    for load in loads:
        load.wait()
    attend_backward(
        begin_ref, count_ref, qkv, key_code_ref, query_code_ref, context, logsum_ref, grad,
        sums_ref, key_scr, query_scr, given_scr, down_scr, grad_key_scr, grad_value_scr,
    )
    store = pltpu.make_async_copy(qkv, mixed_hbm, mixed_sems.at[0])
    store.start()
    weights.wait(0)

    def rows_of(n):
        return pl.ds(pl.multiple_of(n * ROWS, ROWS), ROWS)

    def row_copy(n):
        return pltpu.make_async_copy(skip.at[rows_of(n)], grad_x_hbm.at[rows_of(n)], row_sems.at[n])

    def unmix_rows(n, _):
        rows = rows_of(n)
        total = skip[rows, :].astype(F32)
        for c in range(3):
            total += dot_nt(qkv[c, rows, :], w_mix[:, c * width : (c + 1) * width])
        skip[rows, :] = total.astype(BF)
        row_copy(n).start()
        return 0

    lax.fori_loop(0, blocks, unmix_rows, 0)
    store.wait()
    for n in range(blocks):
        row_copy(n).wait()


def mixed_backward(sel, grad_context, skip, kept, weights, layer, plan):
    _, qkv, context, logsum = kept[:4]
    begin, count, key_code, query_code = plan
    _, length, width = qkv.shape
    pairs = width // PAIR
    blocks = length // ROWS
    w_qkv = weights[0]

    def whole(shape):
        return pl.BlockSpec(shape, lambda *_: (0,) * len(shape))

    row = pltpu.VMEM((length, width), BF)
    return pl.pallas_call(
        partial(mixed_backward_kernel, layer),
        name="mixed_backward",
        grid_spec=pltpu.PrefetchScalarGridSpec(
            num_scalar_prefetch=3,
            grid=(1,),
            in_specs=[ANY, whole(key_code.shape), whole(query_code.shape), ANY, whole(logsum.shape)]
            + [ANY] * 4,
            out_specs=[ANY, ANY, whole((2, width))],
            scratch_shapes=[
                *held_shapes(w_qkv),
                pltpu.VMEM((3, length, width), BF),
                row, row, row,
                pltpu.VMEM((pairs, PAIR, length), BF),
                pltpu.VMEM((pairs, 2 * QB, PAIR), BF),
                pltpu.VMEM((pairs, 2 * QB, PAIR), BF),
                pltpu.VMEM((pairs, PAIR, 2 * QB), F32),
                pltpu.VMEM((length, width), F32),
                pltpu.VMEM((length, width), F32),
                pltpu.SemaphoreType.DMA((1,)),
                pltpu.SemaphoreType.DMA((4,)),
                pltpu.SemaphoreType.DMA((1,)),
                pltpu.SemaphoreType.DMA((blocks,)),
            ],
        ),
        out_shape=[
            jax.ShapeDtypeStruct((3, length, width), BF),
            jax.ShapeDtypeStruct((length, width), BF),
            jax.ShapeDtypeStruct((2, width), F32),
        ],
        compiler_params=PARAMS,
        cost_estimate=cost(38),
    )(begin, count, sel, qkv, key_code, query_code, context, logsum, grad_context, skip, *w_qkv)


def layer_backward(sel, grad, kept, weights, layer, plan):
    grad_context, grads, sums = feed_backward(sel, (grad,), kept, weights, layer)
    grad_mixed, grad_x, mix_sums = mixed_backward(
        sel, grad_context, grads[2], kept, weights, layer, plan
    )
    return (grad_x, grads + (grad_mixed,), sums + (mix_sums,))


def swap_cores(value):
    return send(value, ((0, 1), (1, 0), (2, 3), (3, 2)))


def send(value, routes):
    return lax.ppermute(value, "section", routes)


def pick_row(value, at, axis=0):
    return lax.dynamic_index_in_dim(value, at, axis, keepdims=False)


def plus(*values):
    return sum(value.astype(F32) for value in values).astype(BF)


class RowSum:
    def __init__(self, mine, arrived, blocks):
        self.terms, self.blocks, self.crossed, self.travelling = (mine, arrived), blocks, (), ()
        self.plain = lax.axis_size("dp") != SHARDS
        self.crossed_rows, self.ring_at = 0, 0
        if not self.plain:
            at = lax.axis_index("dp")
            self.z, self.x = at // 2, at % 2

    def state(self):
        return (self.terms, self.crossed, self.travelling)

    def set(self, state):
        self.terms, self.crossed, self.travelling = state

    def cross(self, rows=None):
        if self.plain:
            return
        first, last = self.crossed_rows, rows or self.terms[0].shape[1]
        self.crossed_rows = last
        others = []
        for term in self.terms:
            cut = term.reshape(4, 2, *term.shape[1:])[:, :, first:last]
            others.append(pick_row(cut, 1 - self.x, 1))
        pairs = [(n, n ^ 1) for n in range(8)]
        self.crossed += (lax.ppermute(plus(*others), "dp", pairs),)

    def part(self, z, *more):
        values = []
        for term in self.terms:
            _, rows, cols = term.shape
            cut = lax.dynamic_slice(
                term.reshape(4, 2, rows, cols), (z, self.x, 0, 0), (1, 1, rows, cols)
            )
            values.append(cut[0, 0])
        values.append(jnp.concatenate([pick_row(part, z) for part in self.crossed], axis=0))
        return plus(*values, *more)

    def ring(self):
        if self.plain:
            return
        self.ring_at += 1
        passing = self.part(lax.rem(self.z + 4 - self.ring_at, 4), *self.travelling)
        self.travelling = (lax.ppermute(passing, "dp", [(n, (n + 2) % 8) for n in range(8)]),)

    def direct(self):
        if self.plain:
            return
        arrived = []
        for far in (3, 2, 1):
            for way in (far, -far):
                part = self.part(jnp.clip(self.z + way, 0, 3))
                routes = [(n, n + 2 * way) for n in range(8) if 0 <= n + 2 * way < 8]
                arrived.append(lax.ppermute(part, "dp", routes))
        self.travelling = tuple(arrived)

    def result(self):
        if not self.plain:
            return self.part(self.z, *self.travelling)
        shards = lax.axis_size("dp")
        parts, at, value = [], 0, plus(*self.terms)
        for rows in self.blocks:
            part = value[:, at : at + rows].reshape(shards, -1, value.shape[2])
            parts, at = parts + [part], at + rows
        whole = jnp.concatenate(parts, axis=1)
        return lax.psum_scatter(whole, "dp", scatter_dimension=0, tiled=True)[0]


def body(
    tokens_in, seg_starts, pad_mask, w_qkv, b_qv, w_attn_out, b_attn_out, ln_gain, ln_bias,
    w_up, b_up, w_down, b_down, w_proj, cotangent,
):
    section_at = lax.axis_index("section")
    core = section_at % 2
    is_late = section_at >= 2
    flip = core == 1
    quarter = tokens_in.shape[1]
    length, width = 4 * quarter, tokens_in.shape[2]
    ff_width = w_up.shape[2]
    proj_cols = w_proj.shape[1]
    shards = lax.axis_size("dp")
    share = width // shards

    def sel_for(half):
        return jnp.stack([core, section_at // 2, half]).astype(jnp.int32)

    sel_mine, sel_theirs = sel_for(core), sel_for(1 - core)

    own = pick_row(tokens_in, core)
    other = pick_row(tokens_in, 1 - core)
    straight = send(own, [(2, 0), (3, 1)])
    crossed = send(other, [(2, 1), (3, 0)])
    near = swap_cores(other)
    small = pack_small(b_qv[0], b_attn_out[0], ln_gain[0], ln_bias[0], b_up[0], b_down[0])[None]
    small_other = swap_cores(small)
    small = jnp.stack([jnp.where(flip, small_other, small), jnp.where(flip, small, small_other)])
    weights = tuple((w[0], swap_cores(w[0])) for w in (w_qkv, w_attn_out, w_up, w_down)) + (small,)
    x = jnp.concatenate(
        [
            jnp.where(flip, near, own),
            jnp.where(flip, own, near),
            jnp.where(flip, crossed, straight),
            jnp.where(flip, straight, crossed),
        ],
        axis=0,
    )

    plan = attention_plan(pick_row(seg_starts, core), pick_row(pad_mask, core))

    def both_forward(rows):
        middle, kept_even = layer_forward(sel_mine, rows, weights, 0, plan)
        last, kept_odd = layer_forward(sel_mine, middle, weights, 1, plan)
        return (last, kept_even, kept_odd)

    middle, kept_even = layer_forward(sel_mine, x, weights, 0, plan)
    head_own = jnp.concatenate([w_proj.T, pick_row(cotangent, core).T], axis=1)
    head_other = jnp.concatenate([w_proj.T, pick_row(cotangent, 1 - core).T], axis=1)
    middle, head_own, head_other = lax.optimization_barrier((middle, head_own, head_other))
    head_late = send(head_other, [(2, 3), (3, 2)])
    head_straight = send(head_own, [(0, 2), (1, 3)])
    head_crossed = send(head_other, [(0, 3), (1, 2)])
    head_cols = jnp.concatenate(
        [
            jnp.where(flip, head_crossed, head_straight),
            jnp.where(flip, head_straight, head_crossed),
            jnp.where(flip, head_late, head_own),
            jnp.where(flip, head_own, head_late),
        ],
        axis=0,
    )
    proj_rows, given_rows = head_cols[:, :width], head_cols[:, width:]
    (first, second), kept_odd = layer_forward_halves(sel_mine, middle, weights, 1, plan)
    first, proj_rows, given_rows = lax.optimization_barrier((first, proj_rows, given_rows))
    arrived = send(first, [(0, 2), (1, 3)])
    arrived, second = lax.optimization_barrier((arrived, second))
    hopped = jnp.concatenate([arrived, send(second, [(0, 2), (1, 3)])], axis=0)

    def late_turn(rows, *_):
        last, kept_even, kept_odd = both_forward(rows)
        embedded, grad_proj, grad = head(last, proj_rows, given_rows)
        grad, grads_odd, sums_odd = layer_backward(sel_mine, grad, kept_odd, weights, 1, plan)
        grad, grads_even, sums_even = layer_backward(sel_mine, grad, kept_even, weights, 0, plan)
        return (
            kept_even, kept_odd, embedded, grad_proj, grad,
            grads_odd, sums_odd, grads_even, sums_even,
        )

    def early_turn(rows, kept_even, kept_odd):
        row, ff = jnp.zeros((length, width), BF), jnp.zeros((length, ff_width), BF)
        grads = (row, ff, row, jnp.zeros((3, length, width), BF))
        sums = (
            jnp.zeros((6, width), F32),
            jnp.zeros((1, ff_width), F32),
            jnp.zeros((2, width), F32),
        )
        return (
            kept_even, kept_odd, jnp.zeros((4 * proj_cols, length), BF),
            jnp.zeros((width, 4 * proj_cols), BF), row, grads, sums, grads, sums,
        )

    (
        kept_even, kept_odd, embedded, grad_proj, grad_mid,
        late_odd, late_sums_odd, late_even, late_sums_even,
    ) = lax.cond(is_late, late_turn, early_turn, hopped, kept_even, kept_odd)

    halfway = length // 2
    arriving = [
        send(grad_mid[at : at + halfway], [(2, 0), (3, 1)]) for at in (0, halfway)
    ]
    embedded_cols = embedded.reshape(4, proj_cols, length)

    rows_of_one = width // SHARDS
    attend_blocks = (rows_of_one,) * 4
    feed_blocks = (rows_of_one,) * (ff_width // (2 * HALF)) + (ff_width // SHARDS,)

    def tie(*values):
        return lax.optimization_barrier(values)

    def feed_args(kept, late, now):
        return (kept[4], late[1], now[1], kept[9], late[0], now[0])

    def attend_args(kept, late, now, mixed):
        return (kept[2], kept[0], late[2], now[2], late[3], mixed)

    def tie_sums(values, *sums):
        values, states = tie(values, [part.state() for part in sums])
        for part, state in zip(sums, states):
            part.set(state)
        return values

    grad_context, grads_odd, sums_odd = feed_backward(sel_mine, arriving, kept_odd, weights, 1)
    args = feed_args(kept_odd, late_odd, grads_odd)
    arrived = swap_cores(feed_grads(sel_theirs, *args))
    feed_odd = RowSum(feed_grads(sel_mine, *args), arrived, feed_blocks)
    grad_context = tie_sums(grad_context, feed_odd)
    feed_odd.cross(rows_of_one * 6)
    straight_cols = send(pick_row(embedded_cols, core), [(2, 0), (3, 1)])
    crossed_cols = send(pick_row(embedded_cols, 1 - core), [(2, 1), (3, 0)])
    near_cols = swap_cores(pick_row(embedded_cols, 3 - core))
    mixed_odd, grad, mix_sums = mixed_backward(
        sel_mine, grad_context, grads_odd[2], kept_odd, weights, 1, plan
    )
    sums_odd = sums_odd + (mix_sums,)
    args = attend_args(kept_odd, late_odd, grads_odd, mixed_odd)
    args, straight_cols, crossed_cols, near_cols = tie_sums(
        (args, straight_cols, crossed_cols, near_cols), feed_odd
    )
    feed_odd.cross()
    theirs = attend_grads(sel_theirs, *args)
    args, theirs = tie_sums((args, theirs), feed_odd)
    feed_odd.ring()
    arrived = swap_cores(theirs)
    attend_odd = RowSum(attend_grads(sel_mine, *args), arrived, attend_blocks)
    grad = tie_sums(grad, feed_odd, attend_odd)
    feed_odd.ring()
    attend_odd.cross()

    grad_context, grads_even, sums_even = feed_backward(sel_mine, (grad,), kept_even, weights, 0)
    args = tie_sums(feed_args(kept_even, late_even, grads_even), feed_odd, attend_odd)
    feed_odd.ring()
    theirs = feed_grads(sel_theirs, *args)
    args, theirs = tie_sums((args, theirs), feed_odd)
    attend_odd.ring()
    arrived = swap_cores(theirs)
    feed_even = RowSum(feed_grads(sel_mine, *args), arrived, feed_blocks)
    grad_context = tie_sums(grad_context, feed_even, attend_odd)
    feed_even.cross()
    attend_odd.ring()
    mixed_even, grad, mix_sums = mixed_backward(
        sel_mine, grad_context, grads_even[2], kept_even, weights, 0, plan
    )
    sums_even = sums_even + (mix_sums,)
    args = attend_args(kept_even, late_even, grads_even, mixed_even)
    args = tie_sums(args, feed_even, attend_odd)
    feed_even.ring()
    routes_odd, routes_even = ((0, 1), (2, 3)), ((1, 0), (3, 2))
    feed_odd = feed_odd.result()
    theirs = attend_grads(sel_theirs, *args)
    extras = pack_extras(sel_mine, grad_proj, late_sums_even, late_sums_odd, sums_even, sums_odd)
    theirs = jnp.concatenate([theirs, extras.astype(BF)], axis=1)
    args, theirs, extras = tie_sums((args, theirs, extras), feed_even)
    arrived = swap_cores(theirs)
    feed_even.ring()
    attend_odd.ring()
    quarters = grad.reshape(4, quarter, width)
    near_grad = swap_cores(pick_row(quarters, 1 - core))
    mine = jnp.concatenate([attend_grads(sel_mine, *args), extras.astype(BF)], axis=1)
    mine, quarters, near_grad = tie_sums((mine, quarters, near_grad), feed_even, attend_odd)
    attend_even = RowSum(mine, arrived, attend_blocks)
    attend_even.cross()
    feed_even.ring()
    attend_odd = attend_odd.result()
    sent_odd = [send(part, routes_odd) for part in (feed_odd, attend_odd)]
    straight_grad = send(pick_row(quarters, 2 + core), [(0, 2), (1, 3)])
    crossed_grad = send(pick_row(quarters, 3 - core), [(0, 3), (1, 2)])
    straight_grad, crossed_grad, sent_odd = tie_sums(
        (straight_grad, crossed_grad, sent_odd), feed_even, attend_even
    )
    attend_even.direct()
    feed_even = feed_even.result()
    if shards == SHARDS:
        tail = attend_even.result()
        attend_even, extras = tail[: 4 * share], tail[4 * share :].astype(F32)
    else:
        attend_even = attend_even.result()
        extras = plus(mine[:, -EXTRA_ROWS:], arrived[:, -EXTRA_ROWS:])
        extras = lax.psum(extras.astype(F32), "dp")

    def halves(even, odd, sent):
        arrived = jnp.where(flip, sent, send(even, routes_even))
        mine = jnp.where(flip, odd, even)
        return (jnp.where(flip, arrived, mine), jnp.where(flip, mine, arrived))

    blocks = ff_width // (2 * HALF)
    feed_halves = halves(feed_even, feed_odd, sent_odd[0])
    attend_halves = halves(attend_even, attend_odd, sent_odd[1])

    def columns(pair, first, count):
        parts = [part[n * share : (n + 1) * share] for part in pair for n in range(first, first + count)]
        return jnp.concatenate(parts, axis=1).astype(F32)

    grad_w_up = columns(feed_halves, 0, blocks)[None]
    grad_w_down = jnp.concatenate([part[blocks * share :] for part in feed_halves], axis=1)
    grad_w_down = grad_w_down.astype(F32)[None]
    grad_w_out = columns(attend_halves, 0, 1)[None]
    grad_w_qkv = jnp.concatenate([columns(attend_halves, 1 + c, 1) for c in range(3)], axis=1)[None]

    if shards == SHARDS:
        at, pick = 0, lambda values: values
    else:
        at = lax.axis_index("dp") % (shards // SHARDS)
        extras = pick_row(extras, lax.axis_index("dp") // (shards // SHARDS))

        def pick(values):
            size = values.shape[-1] * SHARDS // shards
            return lax.dynamic_slice_in_dim(values, at * size, size, values.ndim - 1)

    one = width // SHARDS
    small_mine = jnp.where(flip, extras[8:16], extras[:8])
    grad_b_up = pick(small_mine[0:1, : ff_width // SHARDS])
    grad_b_qv = pick(small_mine[1:2, : 2 * one])
    rows = pick(small_mine[2:8, :one])
    grad_proj = extras[16:].reshape(-1, 3, 4 * proj_cols).transpose(1, 0, 2)
    grad_proj = grad_proj.reshape(one, 4 * proj_cols)
    grad_proj = lax.dynamic_slice_in_dim(grad_proj, at * share, share, 0).astype(BF)
    grad_proj = jnp.where(is_late, grad_proj, send(grad_proj, [(2, 0), (3, 1)])).astype(F32)
    grad_w_proj = lax.dynamic_slice_in_dim(grad_proj, section_at * proj_cols, proj_cols, 1)

    own_cols = jnp.where(is_late, pick_row(embedded_cols, section_at), straight_cols)
    other_cols = jnp.where(is_late, near_cols, crossed_cols)
    embedded_out = jnp.stack(
        [jnp.where(flip, other_cols, own_cols).T, jnp.where(flip, own_cols, other_cols).T]
    )

    mine = jnp.where(is_late, straight_grad, pick_row(quarters, core))
    others = jnp.where(is_late, crossed_grad, near_grad)
    grad_in = jnp.stack(
        [jnp.where(flip, others, mine), jnp.where(flip, mine, others)]
    ).astype(F32)

    return (
        embedded_out,
        grad_in,
        grad_w_qkv,
        grad_b_qv,
        grad_w_out,
        rows[0][None],
        rows[1:3][None],
        rows[3:5][None],
        grad_w_up,
        grad_b_up,
        grad_w_down,
        rows[5][None],
        grad_w_proj,
    )


def solution(mesh):
    in_specs = (
        P("dp", "section", None),
        P("dp", None),
        P("dp", None),
        P("section", None, None),
        P("section", None),
        P("section", None, None),
        P("section", None),
        P("section", None, None),
        P("section", None, None),
        P("section", None, None),
        P("section", None),
        P("section", None, None),
        P("section", None),
        P(None, "section"),
        P("dp", None, "section"),
    )
    out_specs = (
        P("dp", None, "section"),
        P("dp", "section", None),
        P("section", "dp", None),
        P("section", "dp"),
        P("section", "dp", None),
        P("section", "dp"),
        P("section", None, "dp"),
        P("section", None, "dp"),
        P("section", "dp", None),
        P("section", "dp"),
        P("section", "dp", None),
        P("section", "dp"),
        P("dp", "section"),
    )
    return jax.shard_map(body, mesh=mesh, in_specs=in_specs, out_specs=out_specs, check_vma=False)
```

```python
from functools import partial
import math

import jax
import jax.numpy as jnp
from jax import lax
from jax.experimental import pallas as pl
from jax.experimental.pallas import tpu as pltpu
from jax.sharding import PartitionSpec as P

HEAD = 64
PAIR = 2 * HEAD
QB = 128
KB = 512
KEYS = 256
EPS_NORM = 1e-05
EPS_PROJ = 1e-06
NEG_FILL = -1e30
PARAMS = pltpu.CompilerParams(vmem_limit_bytes=60 * 1024 * 1024)


def cost(micros):
    return pl.CostEstimate(flops=int(micros * 1e9), bytes_accessed=1024, transcendentals=0)


BF = jnp.bfloat16
F32 = jnp.float32

NT = (((1,), (1,)), ((), ()))
TN = (((0,), (0,)), ((), ()))


def dot(a, b):
    return jnp.dot(a, b, preferred_element_type=F32)


def dot_nt(a, b):
    return lax.dot_general(a, b, NT, preferred_element_type=F32)


def dot_tn(a, b):
    return lax.dot_general(a, b, TN, preferred_element_type=F32)


def pack_small(b_qv, b_out, gains, shifts, b_up, b_down):
    return jnp.concatenate(
        [b_up, b_qv, b_out, gains[0], gains[1], shifts[0], shifts[1], b_down]
    )


def small_spec(layer, width):
    return pl.BlockSpec((1, 1, width), lambda *_: (layer, 0, 0))


def attention_plan(starts, real_flags):
    length = real_flags.shape[0]
    places = jnp.arange(length, dtype=jnp.int32)
    segment = jnp.sum((starts[None, :] <= places[:, None]).astype(jnp.int32), axis=1)
    key_code = jnp.where(real_flags == 1, segment, -1).astype(F32)
    key_code = jnp.broadcast_to(key_code[:, None], (length, PAIR))
    query_code = segment.astype(F32).reshape(length // QB, QB)
    first = jnp.arange(length // QB, dtype=jnp.int32) * QB
    low = jnp.max(jnp.where(starts[None, :] <= first[:, None], starts[None, :], 0), axis=1)
    high = jnp.min(
        jnp.where(starts[None, :] > first[:, None] + (QB - 1), starts[None, :], length), axis=1
    )
    begin = (low // QB) * QB
    count = (high - begin + KEYS - 1) // KEYS
    begin = jnp.minimum(begin, length - KEYS * count)
    return (begin, count, key_code, query_code)


def pair_mask(rows):
    return lax.broadcasted_iota(jnp.int32, (rows, PAIR), 1) < HEAD


def stacked_heads(block):
    first = pair_mask(block.shape[0])
    zero = jnp.zeros_like(block)
    return jnp.concatenate([jnp.where(first, block, zero), jnp.where(first, zero, block)], axis=0)


def block_bias(key_code, query_code, key_at, query_at):
    shape = key_code.shape
    keys = lax.broadcasted_iota(jnp.int32, shape, 0) + (key_at - query_at)
    same = keys == lax.broadcasted_iota(jnp.int32, shape, 1)
    bias = jnp.where((key_code == query_code) | same, 0.0, NEG_FILL)
    return jnp.concatenate([bias, bias], axis=1)


def over_keys(begin, count, step, state):
    state = lax.fori_loop(
        0,
        lax.shift_right_logical(count, 1),
        lambda j, now: step(pl.multiple_of(begin + j * KB, QB), KB, now),
        state,
    )
    last = pl.multiple_of(begin + (count - 1) * KEYS, QB)
    return lax.fori_loop(
        0, jnp.bitwise_and(count, 1), lambda _, now: step(last, KEYS, now), state
    )


def unstack_heads(flat):
    rows = lax.broadcasted_iota(jnp.int32, (PAIR, QB), 0)
    return jnp.where(rows < HEAD, flat[:PAIR, :QB], flat[:PAIR, QB:]).T


SAFE_SCORE = 70.0


def score_bound(peak):
    lanes = lax.broadcasted_iota(jnp.int32, peak.shape, 1)
    return jnp.max(jnp.where(lanes < HEAD, peak, 0.0)) * jnp.max(jnp.where(lanes < HEAD, 0.0, peak))


def head_lanes(width):
    rows = lax.broadcasted_iota(jnp.int32, (2 * width, PAIR), 0)
    lanes = lax.broadcasted_iota(jnp.int32, (2 * width, PAIR), 1)
    head = lax.shift_right_logical(rows, 6)
    wanted = jnp.where(rows < width, head, head - width // HEAD + HEAD)
    return jnp.where(lanes == wanted, 1.0, 0.0).astype(BF)


def attend_forward(
    begin_ref, count_ref, qkv_ref, key_code_ref, query_code_ref, out_ref, logsum_ref,
    value_scr, query_scr, total_scr, is_safe,
):
    length = qkv_ref.shape[1]
    pairs = qkv_ref.shape[2] // PAIR
    every = range(pairs)
    cols = [slice(p * PAIR, (p + 1) * PAIR) for p in every]
    for p in every:
        value_scr[p, :PAIR, :] = qkv_ref[2, :, cols[p]].T
        value_scr[p, PAIR:, :] = jnp.ones((value_scr.shape[1] - PAIR, length), BF)

    def one_query_block(shifted, i, _):
        query_at = pl.multiple_of(i * QB, QB)
        begin, count = begin_ref[i], count_ref[i]
        query_code = query_code_ref[pl.ds(i, 1), :]
        for p in every:
            query_scr[p] = stacked_heads(qkv_ref[0, pl.ds(query_at, QB), cols[p]])
        total_scr[...] = jnp.zeros_like(total_scr)

        def one_key_block(key_at, size, tops):
            rows = pl.ds(key_at, size)
            bias = block_bias(key_code_ref[rows, :], query_code, key_at, query_at)
            scores = [dot_nt(qkv_ref[1, rows, cols[p]], query_scr[p]) + bias for p in every]
            if not shifted:
                probs = [jnp.exp(scores[p]).astype(BF) for p in every]
                for p in every:
                    total_scr[p] += dot(value_scr[p, :, rows], probs[p])
                return tops
            fresh = [
                jnp.maximum(tops[p], jnp.max(scores[p], axis=0, keepdims=True)) for p in every
            ]
            probs = [jnp.exp(scores[p] - fresh[p]).astype(BF) for p in every]
            for p in every:
                total_scr[p] = total_scr[p] * jnp.exp(tops[p] - fresh[p]) + dot(
                    value_scr[p, :, rows], probs[p]
                )
            return tuple(fresh)

        lowest = 2 * NEG_FILL if shifted else 0.0
        tops = tuple(jnp.full((1, 2 * QB), lowest, F32) for _ in every)
        tops = over_keys(begin, count, one_key_block, tops)
        for p in every:
            weight = total_scr[p, PAIR : PAIR + 1, :]
            logsum_ref[pl.ds(p * (length // QB) + i, 1), :] = tops[p] + jnp.log(weight)
            out_ref[pl.ds(query_at, QB), cols[p]] = unstack_heads(
                total_scr[p, :PAIR, :] * (1.0 / weight)
            ).astype(BF)
        return 0

    for wanted, shifted in ((is_safe, False), (jnp.logical_not(is_safe), True)):

        @pl.when(wanted)
        def _():
            lax.fori_loop(0, length // QB, partial(one_query_block, shifted), 0)


def attend_backward(
    begin_ref, count_ref, qkv, key_code_ref, query_code_ref, context, logsum_ref, grad, sums_ref,
    key_scr, query_scr, given_scr, down_scr, grad_key_scr, grad_value_scr, ready,
):
    length = qkv.shape[1]
    pairs = qkv.shape[2] // PAIR
    every = range(pairs)
    blocks = length // QB
    cols = [slice(p * PAIR, (p + 1) * PAIR) for p in every]
    for p in every:
        key_scr[p] = qkv[1, :, cols[p]].T
    ready()

    def one_query_block(i, _):
        query_at = pl.multiple_of(i * QB, QB)
        queries = pl.ds(query_at, QB)
        begin, count = begin_ref[i], count_ref[i]
        query_code = query_code_ref[pl.ds(i, 1), :]
        inner, logsum = [], []
        for p in every:
            query_scr[p] = stacked_heads(qkv[0, queries, cols[p]])
            given = grad[queries, cols[p]]
            given_scr[p] = stacked_heads(given)
            both = (given.astype(F32) * context[queries, cols[p]].astype(F32)).T
            inner.append(
                jnp.concatenate(
                    [
                        jnp.sum(both[:HEAD], axis=0, keepdims=True),
                        jnp.sum(both[HEAD:], axis=0, keepdims=True),
                    ],
                    axis=1,
                )
            )
            logsum.append(logsum_ref[pl.ds(p * blocks + i, 1), :])
        down_scr[...] = jnp.zeros_like(down_scr)

        def one_key_block(key_at, size, state):
            rows = pl.ds(key_at, size)
            bias = block_bias(key_code_ref[rows, :], query_code, key_at, query_at)
            parts, grads, probs, scores = {}, {}, {}, {}
            for p in range(pairs + 1):
                if p < pairs:
                    grads[p] = dot_nt(qkv[2, rows, cols[p]], given_scr[p]) - inner[p]
                    parts[p] = dot_nt(qkv[1, rows, cols[p]], query_scr[p]) + bias
                if 0 <= p - 1 < pairs:
                    q = p - 1
                    probs[q] = jnp.exp(parts.pop(q) - logsum[q])
                    scores[q] = (probs[q] * grads.pop(q)).astype(BF)
                    probs[q] = probs[q].astype(BF)
                if 0 <= p - 1 < pairs:
                    q = p - 1
                    grad_value_scr[rows, cols[q]] += dot(probs.pop(q), given_scr[q])
                    grad_key_scr[rows, cols[q]] += dot(scores[q], query_scr[q])
                    down_scr[q] += dot(key_scr[q, :, rows], scores.pop(q))
            return state

        over_keys(begin, count, one_key_block, 0)
        for p in every:
            grad_query = (unstack_heads(down_scr[p]) * (HEAD**-0.5)).astype(BF)
            qkv[0, queries, cols[p]] = grad_query
            sums_ref[0:1, cols[p]] += jnp.sum(grad_query.astype(F32), axis=0, keepdims=True)
        return 0

    lax.fori_loop(0, blocks, one_query_block, 0)
    qkv[1] = grad_key_scr[...].astype(BF)
    grad_value = grad_value_scr[...].astype(BF)
    qkv[2] = grad_value
    sums_ref[1:2, :] = jnp.sum(grad_value.astype(F32), axis=0, keepdims=True)


ANY = pl.BlockSpec(memory_space=pl.ANY)
ROWS = 256


class Held:
    def __init__(self, sel_ref, layer, pairs, held, sems, first=None):
        self.own = sel_ref[0] == layer
        self.items = list(zip(pairs, held, range(len(held))))
        self.sems = sems
        self.first = pl.program_id(0) == 0 if first is None else first

    def start(self):
        for pair, held, n in self.items:
            for wanted, source in zip((self.own, jnp.logical_not(self.own)), pair):

                @pl.when(self.first & wanted)
                def _():
                    pltpu.make_async_copy(source, held, self.sems.at[n]).start()

    def wait(self, n):
        pair, held, _ = self.items[n]

        @pl.when(self.first)
        def _():
            pltpu.make_async_copy(pair[0], held, self.sems.at[n]).wait()


def held_shapes(*weights):
    return [pltpu.VMEM(own.shape, own.dtype) for own, _ in weights]


def normalized(values):
    centred = values - jnp.mean(values, axis=-1, keepdims=True)
    inverse = lax.rsqrt(jnp.mean(centred * centred, axis=-1, keepdims=True) + EPS_NORM)
    return (centred * inverse, inverse)


def normalized_pull(grad_hat, hat, inverse):
    return inverse * (
        grad_hat
        - jnp.mean(grad_hat, axis=-1, keepdims=True)
        - hat * jnp.mean(grad_hat * hat, axis=-1, keepdims=True)
    )


ERF = (0.254829592, -0.284496736, 1.421413741, -1.453152027, 1.061405429)
ERF_SLOPE = 0.3275911


def gelu_parts(x):
    t = pl.reciprocal(1.0 + (ERF_SLOPE * math.sqrt(0.5)) * jnp.abs(x), approx=True)
    bell = jnp.exp(-0.5 * (x * x))
    tail = 0.5 * ERF[4]
    for term in ERF[3::-1]:
        tail = tail * t + 0.5 * term
    tail = tail * t * bell
    below = jnp.where(x >= 0, 1.0 - tail, tail)
    return (x * below, below + x * bell * (1.0 / math.sqrt(2.0 * math.pi)))


FB = 1024


def small_slices(width, ff_width):
    names = ("b_q", "b_v", "b_out", "gain1", "gain2", "shift1", "shift2", "b_down")
    at = {"b_up": slice(0, ff_width)}
    for n, name in enumerate(names):
        at[name] = slice(ff_width + n * width, ff_width + (n + 1) * width)
    return at


def refine_back_kernel(
    layer, sel_ref, grad_ref, hidden_ref, out_ref, scale1_ref, scale2_ref, slope_ref,
    out_own_ref, out_other_ref, up_own_ref, up_other_ref, down_own_ref, down_other_ref, small_ref,
    grad_low_ref, grad_raised_ref, grad_attn_ref, grad_context_ref, sums_ref, up_sums_ref,
    w_out, w_up, w_down, sems,
):
    pairs = [(down_own_ref, down_other_ref), (up_own_ref, up_other_ref), (out_own_ref, out_other_ref)]
    weights = Held(sel_ref, layer, pairs, [w_down, w_up, w_out], sems)
    weights.start()
    rows, width = grad_ref.shape
    ff_width = slope_ref.shape[1]
    at = small_slices(width, ff_width)

    @pl.when(pl.program_id(0) == 0)
    def _():
        sums_ref[...] = jnp.zeros_like(sums_ref)
        up_sums_ref[...] = jnp.zeros_like(up_sums_ref)

    def vector(name):
        return small_ref[0, :, at[name]]

    def add(row, values):
        sums_ref[row : row + 1, :] += jnp.sum(values, axis=0, keepdims=True)

    grad = grad_ref[...].astype(F32)
    hat = (out_ref[...].astype(F32) - vector("shift2")) * (1.0 / vector("gain2"))
    joined = normalized_pull(grad * vector("gain2"), hat, scale2_ref[:, :1])
    low = joined.astype(BF)
    grad_low_ref[...] = low
    add(2, grad * hat)
    add(4, grad)
    add(5, low.astype(F32))
    weights.wait(0)
    weights.wait(1)
    total = joined
    parts = [slice(f, f + FB) for f in range(0, ff_width, FB)]
    active = dot_nt(low, w_down[parts[0], :])
    for n, part in enumerate(parts):
        following = dot_nt(low, w_down[parts[n + 1], :]) if n + 1 < len(parts) else None
        raised = active * slope_ref[:, part].astype(F32)
        up_sums_ref[:, part] += jnp.sum(raised, axis=0, keepdims=True)
        raised = raised.astype(BF)
        grad_raised_ref[:, part] = raised
        total += dot_nt(raised, w_up[:, part])
        active = following
    hat = (hidden_ref[...].astype(F32) - vector("shift1")) * (1.0 / vector("gain1"))
    summed = normalized_pull(total * vector("gain1"), hat, scale1_ref[:, :1])
    attn = summed.astype(BF)
    grad_attn_ref[...] = attn
    weights.wait(2)
    grad_context_ref[...] = dot_nt(attn, w_out[...]).astype(BF)
    add(1, total * hat)
    add(3, total)
    add(0, attn.astype(F32))


def refine_back_second_kernel(layer, *refs):
    refine_back_kernel(layer, *refs[:14], *refs[18:])


def refine_back(sel, grad, kept, weights, layer, first=0, begun=()):
    w_out, w_up, w_down, small = weights
    hidden, out, scale1, scale2, slope = kept
    length, width = hidden.shape
    ff_width = w_up[0].shape[1]
    at = first // ROWS
    rows = pl.BlockSpec((ROWS, width), lambda n, _: (n + at, 0))
    lanes = pl.BlockSpec((ROWS, 128), lambda n, _: (n + at, 0))
    part = pl.BlockSpec((ROWS, ff_width), lambda n, _: (n + at, 0))
    row_shape = jax.ShapeDtypeStruct((length, width), BF)
    return pl.pallas_call(
        partial(refine_back_second_kernel if begun else refine_back_kernel, layer),
        name="refine_back",
        grid_spec=pltpu.PrefetchScalarGridSpec(
            num_scalar_prefetch=1,
            grid=(grad.shape[0] // ROWS,),
            in_specs=[
                pl.BlockSpec((ROWS, width), lambda n, _: (n, 0)),
                rows, rows, lanes, lanes, part,
            ]
            + [ANY] * 6
            + [small_spec(layer, small.shape[2])]
            + [ANY] * len(begun),
            out_specs=[
                rows, part, rows, rows,
                pl.BlockSpec((6, width), lambda n, _: (0, 0)),
                pl.BlockSpec((1, ff_width), lambda n, _: (0, 0)),
            ],
            scratch_shapes=[
                *held_shapes(w_out, w_up, w_down),
                pltpu.SemaphoreType.DMA((3,)),
            ],
        ),
        out_shape=[
            row_shape,
            jax.ShapeDtypeStruct((length, ff_width), BF),
            row_shape,
            row_shape,
            jax.ShapeDtypeStruct((6, width), F32),
            jax.ShapeDtypeStruct((1, ff_width), F32),
        ],
        input_output_aliases={14 + n: n for n in range(len(begun))},
        compiler_params=PARAMS,
        cost_estimate=cost(24),
    )(sel, grad, hidden, out, scale1, scale2, slope, *w_out, *w_up, *w_down, small, *begun)


def head_kernel(rows_ref, proj_ref, given_ref, embedded_ref, grad_proj_ref, grad_rows_ref):
    factor = math.sqrt(proj_ref.shape[0])
    columns = dot_nt(proj_ref[...], rows_ref[...])
    given = given_ref[...].astype(F32)
    inverse = lax.rsqrt(jnp.sum(columns * columns, axis=0, keepdims=True) + EPS_PROJ)
    cross = jnp.sum(columns * given, axis=0, keepdims=True)
    embedded_ref[...] = (factor * columns * inverse).astype(BF)
    grad = (factor * (given * inverse - columns * (cross * inverse * inverse * inverse))).astype(BF)
    grad_proj_ref[...] = dot(grad, rows_ref[...]).T.astype(BF)
    grad_rows_ref[...] = dot_tn(grad, proj_ref[...]).astype(BF)


def head(rows, proj, given):
    length, width = rows.shape
    cols = proj.shape[0]
    return pl.pallas_call(
        head_kernel,
        name="head",
        out_shape=[
            jax.ShapeDtypeStruct((cols, length), BF),
            jax.ShapeDtypeStruct((width, cols), BF),
            jax.ShapeDtypeStruct((length, width), BF),
        ],
        compiler_params=PARAMS,
        cost_estimate=cost(6),
    )(rows, proj, given)


HALF = 384
SHARDS = 8


def feed_grads_kernel(
    sel_ref, hidden_ref, raised_late_ref, raised_ref, active_ref, low_late_ref, low_ref, out_ref
):
    step = pl.program_id(0)
    shards, rows, _ = out_ref.shape
    blocks = raised_ref.shape[1] // HALF
    share = rows // blocks
    late = sel_ref[1] == 1

    def up(raised):
        part = dot_tn(hidden_ref[...], raised).astype(BF)
        for m in range(shards):
            for n in range(blocks):
                out_ref[m, n * share : (n + 1) * share, :] = part[
                    m * share : (m + 1) * share, n * HALF : (n + 1) * HALF
                ]

    def down(low):
        for m in range(shards):
            out_ref[m] = dot_tn(active_ref[:, m * rows : (m + 1) * rows], low).astype(BF)

    for wanted, raised_now, low_now in (
        (late, raised_late_ref, low_late_ref),
        (jnp.logical_not(late), raised_ref, low_ref),
    ):

        @pl.when(wanted & (step < 2))
        def _():
            up(raised_now[...])

        @pl.when(wanted & (step >= 2))
        def _():
            down(low_now[...])


def feed_grads(sel, hidden, raised_late, raised, active, low_late, low):
    length, width = hidden.shape
    ff_width = active.shape[1]
    half_ff = ff_width // 2

    def late_spec(shape, wanted):
        return pl.BlockSpec(shape, lambda n, sel: (0, jnp.where(sel[1] == wanted, sel[2], 0)))

    return pl.pallas_call(
        feed_grads_kernel,
        name="feed_grads",
        grid_spec=pltpu.PrefetchScalarGridSpec(
            num_scalar_prefetch=1,
            grid=(4,),
            in_specs=[
                pl.BlockSpec((length, width // 2), lambda n, _: (0, jnp.minimum(n, 1))),
                late_spec((length, half_ff), 1),
                late_spec((length, half_ff), 0),
                pl.BlockSpec((length, ff_width // 2), lambda n, _: (0, jnp.maximum(n - 2, 0))),
                late_spec((length, width // 2), 1),
                late_spec((length, width // 2), 0),
            ],
            out_specs=pl.BlockSpec(
                (SHARDS // 2, ff_width // SHARDS, HALF), lambda n, _: (lax.rem(n, 2), n // 2, 0)
            ),
        ),
        out_shape=jax.ShapeDtypeStruct((SHARDS, 2 * (ff_width // SHARDS), HALF), BF),
        compiler_params=PARAMS,
        cost_estimate=cost(12),
    )(sel, hidden, raised_late, raised, active, low_late, low)


def attend_grads_kernel(
    sel_ref, context_ref, x_ref, attn_late_ref, attn_ref, mixed_late_ref, mixed_ref, out_ref
):
    step = pl.program_id(0)
    late = sel_ref[1] == 1

    for wanted, attn_now, mixed_now in (
        (late, attn_late_ref, mixed_late_ref),
        (jnp.logical_not(late), attn_ref, mixed_ref),
    ):

        @pl.when(wanted & (step == 0))
        def _():
            part = dot_tn(context_ref[...], attn_now[...]).astype(BF)
            out_ref[...] = part.reshape(out_ref.shape)

        @pl.when(wanted & (step > 0))
        def _():
            part = dot_tn(x_ref[...], mixed_now[0]).astype(BF)
            out_ref[...] = part.reshape(out_ref.shape)


def attend_grads(sel, context, x, attn_late, attn, mixed_late, mixed):
    length, width = x.shape

    def late_spec(wanted):
        return pl.BlockSpec(
            (length, HALF), lambda n, sel: (0, jnp.where(sel[1] == wanted, sel[2], 0))
        )

    def mixed_spec(wanted):
        def at(n, sel):
            return (
                jnp.where(sel[1] == wanted, jnp.maximum(n - 1, 0), 0),
                0,
                jnp.where(sel[1] == wanted, sel[2], 0),
            )

        return pl.BlockSpec((1, length, HALF), at)

    whole = pl.BlockSpec((length, width), lambda n, _: (0, 0))
    share = width // SHARDS
    return pl.pallas_call(
        attend_grads_kernel,
        name="attend_grads",
        grid_spec=pltpu.PrefetchScalarGridSpec(
            num_scalar_prefetch=1,
            grid=(4,),
            in_specs=[whole, whole, late_spec(1), late_spec(0), mixed_spec(1), mixed_spec(0)],
            out_specs=pl.BlockSpec((SHARDS, share, HALF), lambda n, _: (0, n, 0)),
        ),
        out_shape=jax.ShapeDtypeStruct((SHARDS, 4 * share, HALF), BF),
        compiler_params=PARAMS,
        cost_estimate=cost(8),
    )(sel, context, x, attn_late, attn, mixed_late, mixed)


EXTRA_ROWS = 48


def pack_extras_kernel(
    sel_ref, proj_ref,
    late_sums_0, late_up_0, late_mix_0, late_sums_1, late_up_1, late_mix_1,
    sums_0, up_0, mix_0, sums_1, up_1, mix_1, out_ref,
):
    shards = out_ref.shape[0]
    width = sums_0.shape[1]
    share = width // shards
    third = share // 3
    cols = proj_ref.shape[1]
    out_ref[...] = jnp.zeros_like(out_ref)

    def layer(first, sums, up, mix):
        up_share = up.shape[1] // shards
        both = jnp.concatenate([mix[0:1, :], mix[1:2, :]], axis=1)
        for m in range(shards):
            rows = [up[0:1, m * up_share : (m + 1) * up_share]]
            rows += [both[:, 2 * m * share : 2 * (m + 1) * share]]
            rows += [sums[n : n + 1, m * share : (m + 1) * share] for n in range(6)]
            for n, row in enumerate(rows):
                out_ref[m, first + n : first + n + 1, : row.shape[1]] = row

    late = sel_ref[1] == 1
    for wanted, even, odd in (
        (late, (late_sums_0, late_up_0, late_mix_0), (late_sums_1, late_up_1, late_mix_1)),
        (jnp.logical_not(late), (sums_0, up_0, mix_0), (sums_1, up_1, mix_1)),
    ):

        @pl.when(wanted)
        def _():
            layer(0, *even)
            layer(8, *odd)

    for m in range(shards):
        for n in range(3):
            at = m * share + n * third
            out_ref[m, 16:, n * cols : (n + 1) * cols] = proj_ref[at : at + third, :].astype(F32)


def pack_extras(sel, proj, late_even, late_odd, even, odd):
    vmem = pl.BlockSpec(memory_space=pltpu.VMEM)
    return pl.pallas_call(
        pack_extras_kernel,
        name="pack_extras",
        in_specs=[pl.BlockSpec(memory_space=pltpu.SMEM)] + [vmem] * 13,
        out_specs=vmem,
        out_shape=jax.ShapeDtypeStruct((SHARDS, EXTRA_ROWS, HALF), F32),
        compiler_params=PARAMS,
        cost_estimate=cost(3),
    )(sel, proj, *late_even, *late_odd, *even, *odd)


def refine_block(
    rows, x, context, w_out, w_up, w_down, small_ref,
    hidden_rows, out_rows, scale1_ref, scale2_ref, active_rows, slope_rows,
):
    width, ff_width = w_up.shape
    at = small_slices(width, ff_width)

    def vector(name):
        return small_ref[0, :, at[name]]

    summed = x[rows, :].astype(F32) + dot(context[rows, :], w_out[...]) + vector("b_out")
    hat, inverse = normalized(summed)
    hidden = hat * vector("gain1") + vector("shift1")
    scale1_ref[rows, :] = jnp.broadcast_to(inverse, (ROWS, 128))
    hidden_low = hidden.astype(BF)
    hidden_rows[rows, :] = hidden_low
    total = hidden + vector("b_down")
    parts = [slice(f, f + FB) for f in range(0, ff_width, FB)]
    raised = dot(hidden_low, w_up[:, parts[0]])
    for m, part in enumerate(parts):
        following = dot(hidden_low, w_up[:, parts[m + 1]]) if m + 1 < len(parts) else None
        active, slope = gelu_parts(raised + small_ref[0, :, part])
        active = active.astype(BF)
        active_rows[rows, part] = active
        slope_rows[rows, part] = slope.astype(BF)
        total += dot(active, w_down[part, :])
        raised = following
    hat, inverse = normalized(total)
    scale2_ref[rows, :] = jnp.broadcast_to(inverse, (ROWS, 128))
    out_rows[rows, :] = (hat * vector("gain2") + vector("shift2")).astype(BF)


def refine_rest_kernel(
    layer, sel_ref, x_hbm, context_hbm,
    out_own_ref, out_other_ref, up_own_ref, up_other_ref, down_own_ref, down_other_ref, small_ref,
    hidden_begun, scale1_begun, scale2_begun, active_begun, slope_begun,
    out_hbm, hidden_hbm, scale1_ref, scale2_ref, active_hbm, slope_hbm,
    w_out, w_up, w_down, x, context, hidden_rows, out_rows, active_rows, slope_rows,
    weight_sems, in_sems, row_sems,
):
    pairs = [(out_own_ref, out_other_ref), (up_own_ref, up_other_ref), (down_own_ref, down_other_ref)]
    count = x.shape[0]
    first = x_hbm.shape[0] - count
    weights = Held(sel_ref, layer, pairs, [w_out, w_up, w_down], weight_sems, True)
    loads = [
        pltpu.make_async_copy(whole.at[pl.ds(first, count)], held, in_sems.at[n])
        for n, (whole, held) in enumerate(((x_hbm, x), (context_hbm, context)))
    ]
    for load in loads:
        load.start()
    weights.start()
    for load in loads:
        load.wait()
    for n in range(3):
        weights.wait(n)
    saved = [
        (hidden_rows, hidden_hbm, first), (out_rows, out_hbm, 0),
        (active_rows, active_hbm, first), (slope_rows, slope_hbm, first),
    ]

    def row_copies(n):
        return [
            pltpu.make_async_copy(
                rows.at[pl.ds(pl.multiple_of(n * ROWS, ROWS), ROWS)],
                whole.at[pl.ds(pl.multiple_of(n * ROWS + at, ROWS), ROWS)],
                row_sems.at[k, n],
            )
            for k, (rows, whole, at) in enumerate(saved)
        ]

    def refine_rows(n, _):
        refine_block(
            pl.ds(pl.multiple_of(n * ROWS, ROWS), ROWS), x, context, w_out, w_up, w_down,
            small_ref, hidden_rows, out_rows, scale1_ref, scale2_ref, active_rows, slope_rows,
        )
        for copy in row_copies(n):
            copy.start()
        return 0

    lax.fori_loop(0, count // ROWS, refine_rows, 0)
    for n in range(count // ROWS):
        for copy in row_copies(n):
            copy.wait()


def refine_rest(sel, x, context, weights, layer, begun, count):
    _, w_out, w_up, w_down, small = weights
    length, width = x.shape
    ff_width = w_up[0].shape[1]
    row = pltpu.VMEM((count, width), BF)
    wide = pltpu.VMEM((count, ff_width), BF)
    lanes = pl.BlockSpec((count, 128), lambda n, _: (length // count - 1, 0))
    return pl.pallas_call(
        partial(refine_rest_kernel, layer),
        name="refine_rest",
        grid_spec=pltpu.PrefetchScalarGridSpec(
            num_scalar_prefetch=1,
            grid=(1,),
            in_specs=[ANY] * 8 + [small_spec(layer, small.shape[2])] + [ANY] * 5,
            out_specs=[ANY, ANY, lanes, lanes, ANY, ANY],
            scratch_shapes=[
                *held_shapes(w_out, w_up, w_down),
                row, row, row, row, wide, wide,
                pltpu.SemaphoreType.DMA((3,)),
                pltpu.SemaphoreType.DMA((2,)),
                pltpu.SemaphoreType.DMA((4, count // ROWS)),
            ],
        ),
        out_shape=[jax.ShapeDtypeStruct((count, width), BF)]
        + [jax.ShapeDtypeStruct(part.shape, part.dtype) for part in begun],
        input_output_aliases={10 + n: 1 + n for n in range(5)},
        compiler_params=PARAMS,
        cost_estimate=cost(14),
    )(sel, x, context, *w_out, *w_up, *w_down, small, *begun)


def forward_kernel(
    layer, begin_ref, count_ref, sel_ref, x_hbm, key_code_ref, query_code_ref,
    mix_own_ref, mix_other_ref, out_own_ref, out_other_ref,
    up_own_ref, up_other_ref, down_own_ref, down_other_ref, small_ref,
    qkv_hbm, context_hbm, logsum_ref, out_hbm, hidden_hbm, scale1_ref, scale2_ref,
    active_hbm, slope_hbm,
    w_mix, w_out, w_up, w_down, x, qkv, context, hidden_rows, out_rows, active_rows, slope_rows,
    value_scr, query_scr, total_scr, peak, weight_sems, in_sems, qkv_sems, row_sems, context_sem,
):
    pairs = [
        (mix_own_ref, mix_other_ref), (out_own_ref, out_other_ref),
        (up_own_ref, up_other_ref), (down_own_ref, down_other_ref),
    ]
    length, width = x.shape
    ff_width = w_up.shape[1]
    blocks = length // ROWS
    at = small_slices(width, ff_width)

    def vector(name):
        return small_ref[0, :, at[name]]

    def rows_of(n):
        return pl.ds(pl.multiple_of(n * ROWS, ROWS), ROWS)

    def x_copy(n):
        return pltpu.make_async_copy(x_hbm.at[rows_of(n)], x.at[rows_of(n)], in_sems.at[n])

    def qkv_copy(n):
        return pltpu.make_async_copy(
            qkv.at[:, rows_of(n)], qkv_hbm.at[:, rows_of(n)], qkv_sems.at[n]
        )

    saved = [
        (hidden_rows, hidden_hbm), (out_rows, out_hbm),
        (active_rows, active_hbm), (slope_rows, slope_hbm),
    ]

    def row_copies(n):
        return [
            pltpu.make_async_copy(rows.at[rows_of(n)], whole.at[rows_of(n)], row_sems.at[k, n])
            for k, (rows, whole) in enumerate(saved)
        ]

    weights = Held(sel_ref, layer, pairs, [w_mix, w_out, w_up, w_down], weight_sems, True)
    for n in range(blocks):
        x_copy(n).start()
    weights.start()
    peak[...] = jnp.zeros_like(peak)
    lanes_of = head_lanes(width)
    weights.wait(0)

    def mix_rows(n, _):
        x_copy(n).wait()
        rows = rows_of(n)
        part = dot(x[rows, :], w_mix[...])
        queries = ((part[:, :width] + vector("b_q")) * HEAD**-0.5).astype(BF)
        keys = part[:, width : 2 * width].astype(BF)
        qkv[0, rows, :] = queries
        qkv[1, rows, :] = keys
        qkv[2, rows, :] = (part[:, 2 * width :] + vector("b_v")).astype(BF)
        lengths = dot(jnp.concatenate([queries * queries, keys * keys], axis=1), lanes_of)
        folded = lengths.reshape(ROWS // 8, 8, lengths.shape[1])
        peak[...] = jnp.maximum(peak[...], jnp.max(folded, axis=0))
        qkv_copy(n).start()
        return 0

    lax.fori_loop(0, blocks, mix_rows, 0)
    is_safe = score_bound(peak[...]) * 1.02 < SAFE_SCORE * SAFE_SCORE
    attend_forward(
        begin_ref, count_ref, qkv, key_code_ref, query_code_ref, context, logsum_ref,
        value_scr, query_scr, total_scr, is_safe,
    )
    context_copy = pltpu.make_async_copy(context, context_hbm, context_sem)
    context_copy.start()
    for n in (1, 2, 3):
        weights.wait(n)

    def refine_rows(n, _):
        refine_block(
            rows_of(n), x, context, w_out, w_up, w_down, small_ref,
            hidden_rows, out_rows, scale1_ref, scale2_ref, active_rows, slope_rows,
        )
        for copy in row_copies(n):
            copy.start()
        return 0

    last = out_hbm.shape[0] // ROWS
    lax.fori_loop(0, last, refine_rows, 0)
    context_copy.wait()
    for n in range(blocks):
        qkv_copy(n).wait()
    for n in range(last):
        for copy in row_copies(n):
            copy.wait()


def layer_forward(sel, x, weights, layer, plan, fed=None):
    w_qkv, w_out, w_up, w_down, small = weights
    begin, count, key_code, query_code = plan
    length, width = x.shape
    ff_width = w_up[0].shape[1]
    pairs = width // PAIR
    blocks = length // ROWS

    def whole(shape):
        return pl.BlockSpec(shape, lambda *_: (0,) * len(shape))

    row = jax.ShapeDtypeStruct((length, width), BF)
    lanes = jax.ShapeDtypeStruct((length, 128), F32)
    wide = jax.ShapeDtypeStruct((length, ff_width), BF)
    logsum_shape = (pairs * (length // QB), 2 * QB)
    qkv, context, logsum, out, hidden, scale1, scale2, active, slope = pl.pallas_call(
        partial(forward_kernel, layer),
        name="layer_forward",
        grid_spec=pltpu.PrefetchScalarGridSpec(
            num_scalar_prefetch=3,
            grid=(1,),
            in_specs=[ANY, whole(key_code.shape), whole(query_code.shape)]
            + [ANY] * 8
            + [small_spec(layer, small.shape[2])],
            out_specs=[
                ANY, ANY, whole(logsum_shape), ANY, ANY,
                whole((length, 128)), whole((length, 128)), ANY, ANY,
            ],
            scratch_shapes=[
                *held_shapes(w_qkv, w_out, w_up, w_down),
                pltpu.VMEM((length, width), BF),
                pltpu.VMEM((3, length, width), BF),
                pltpu.VMEM((length, width), BF),
                pltpu.VMEM((length, width), BF),
                pltpu.VMEM((length, width), BF),
                pltpu.VMEM((length, ff_width), BF),
                pltpu.VMEM((length, ff_width), BF),
                pltpu.VMEM((pairs, PAIR + 16, length), BF),
                pltpu.VMEM((pairs, 2 * QB, PAIR), BF),
                pltpu.VMEM((pairs, PAIR + 16, 2 * QB), F32),
                pltpu.VMEM((8, PAIR), F32),
                pltpu.SemaphoreType.DMA((4,)),
                pltpu.SemaphoreType.DMA((blocks,)),
                pltpu.SemaphoreType.DMA((blocks,)),
                pltpu.SemaphoreType.DMA((4, blocks)),
                pltpu.SemaphoreType.DMA,
            ],
        ),
        out_shape=[
            jax.ShapeDtypeStruct((3, length, width), BF), row,
            jax.ShapeDtypeStruct(logsum_shape, F32),
            jax.ShapeDtypeStruct((fed or length, width), BF),
            row, lanes, lanes, wide, wide,
        ],
        compiler_params=PARAMS,
        cost_estimate=cost(48),
    )(begin, count, sel, x, key_code, query_code, *w_qkv, *w_out, *w_up, *w_down, small)
    return (out, (x, qkv, context, logsum, hidden, out, scale1, scale2, slope, active))


def layer_forward_halves(sel, x, weights, layer, plan):
    half = x.shape[0] // 2
    first, kept = layer_forward(sel, x, weights, layer, plan, half)
    _, qkv, context, logsum, hidden, _, scale1, scale2, slope, active = kept
    second, hidden, scale1, scale2, active, slope = refine_rest(
        sel, x, context, weights, layer, (hidden, scale1, scale2, active, slope), half
    )
    out = jnp.concatenate([first, second], axis=0)
    return ((first, second), (x, qkv, context, logsum, hidden, out, scale1, scale2, slope, active))


def feed_backward(sel, grads, kept, weights, layer):
    first, begun, totals = 0, (), []
    for grad in grads:
        *begun, sums, up_sums = refine_back(
            sel, grad, kept[4:9], weights[1:], layer, first, tuple(begun)
        )
        first += grad.shape[0]
        totals.append((sums, up_sums))
    grad_low, grad_raised, grad_attn, grad_context = begun
    sums = tuple(sum(parts) for parts in zip(*totals))
    return (grad_context, (grad_low, grad_raised, grad_attn), sums)


def mixed_backward_kernel(
    layer, begin_ref, count_ref, sel_ref, qkv_hbm, key_code_ref, query_code_ref, context_hbm,
    logsum_ref, grad_hbm, skip_hbm, mix_own_ref, mix_other_ref,
    mixed_hbm, grad_x_hbm, sums_ref,
    w_mix, qkv, context, grad, skip, key_scr, query_scr, given_scr, down_scr,
    grad_key_scr, grad_value_scr, weight_sems, in_sems, mixed_sems, row_sems,
):
    length, width = skip.shape
    blocks = length // ROWS
    weights = Held(sel_ref, layer, [(mix_own_ref, mix_other_ref)], [w_mix], weight_sems, True)
    arrays = [(qkv_hbm, qkv), (context_hbm, context), (grad_hbm, grad), (skip_hbm, skip)]
    loads = [
        pltpu.make_async_copy(whole, held, in_sems.at[n]) for n, (whole, held) in enumerate(arrays)
    ]
    for load in loads:
        load.start()
    weights.start()
    grad_key_scr[...] = jnp.zeros_like(grad_key_scr)
    grad_value_scr[...] = jnp.zeros_like(grad_value_scr)
    sums_ref[...] = jnp.zeros_like(sums_ref)
    loads[0].wait()

    def ready():
        loads[1].wait()
        loads[2].wait()

    attend_backward(
        begin_ref, count_ref, qkv, key_code_ref, query_code_ref, context, logsum_ref, grad,
        sums_ref, key_scr, query_scr, given_scr, down_scr, grad_key_scr, grad_value_scr, ready,
    )
    loads[3].wait()
    store = pltpu.make_async_copy(qkv, mixed_hbm, mixed_sems.at[0])
    store.start()
    weights.wait(0)

    def rows_of(n):
        return pl.ds(pl.multiple_of(n * ROWS, ROWS), ROWS)

    def row_copy(n):
        return pltpu.make_async_copy(skip.at[rows_of(n)], grad_x_hbm.at[rows_of(n)], row_sems.at[n])

    def unmix_rows(n, _):
        rows = rows_of(n)
        total = skip[rows, :].astype(F32)
        for c in range(3):
            total += dot_nt(qkv[c, rows, :], w_mix[:, c * width : (c + 1) * width])
        skip[rows, :] = total.astype(BF)
        row_copy(n).start()
        return 0

    lax.fori_loop(0, blocks, unmix_rows, 0)
    store.wait()
    for n in range(blocks):
        row_copy(n).wait()


def mixed_backward(sel, grad_context, skip, kept, weights, layer, plan):
    _, qkv, context, logsum = kept[:4]
    begin, count, key_code, query_code = plan
    _, length, width = qkv.shape
    pairs = width // PAIR
    blocks = length // ROWS
    w_qkv = weights[0]

    def whole(shape):
        return pl.BlockSpec(shape, lambda *_: (0,) * len(shape))

    row = pltpu.VMEM((length, width), BF)
    return pl.pallas_call(
        partial(mixed_backward_kernel, layer),
        name="mixed_backward",
        grid_spec=pltpu.PrefetchScalarGridSpec(
            num_scalar_prefetch=3,
            grid=(1,),
            in_specs=[ANY, whole(key_code.shape), whole(query_code.shape), ANY, whole(logsum.shape)]
            + [ANY] * 4,
            out_specs=[ANY, ANY, whole((2, width))],
            scratch_shapes=[
                *held_shapes(w_qkv),
                pltpu.VMEM((3, length, width), BF),
                row, row, row,
                pltpu.VMEM((pairs, PAIR, length), BF),
                pltpu.VMEM((pairs, 2 * QB, PAIR), BF),
                pltpu.VMEM((pairs, 2 * QB, PAIR), BF),
                pltpu.VMEM((pairs, PAIR, 2 * QB), F32),
                pltpu.VMEM((length, width), F32),
                pltpu.VMEM((length, width), F32),
                pltpu.SemaphoreType.DMA((1,)),
                pltpu.SemaphoreType.DMA((4,)),
                pltpu.SemaphoreType.DMA((1,)),
                pltpu.SemaphoreType.DMA((blocks,)),
            ],
        ),
        out_shape=[
            jax.ShapeDtypeStruct((3, length, width), BF),
            jax.ShapeDtypeStruct((length, width), BF),
            jax.ShapeDtypeStruct((2, width), F32),
        ],
        compiler_params=PARAMS,
        cost_estimate=cost(38),
    )(begin, count, sel, qkv, key_code, query_code, context, logsum, grad_context, skip, *w_qkv)


def layer_backward(sel, grad, kept, weights, layer, plan):
    grad_context, grads, sums = feed_backward(sel, (grad,), kept, weights, layer)
    grad_mixed, grad_x, mix_sums = mixed_backward(
        sel, grad_context, grads[2], kept, weights, layer, plan
    )
    return (grad_x, grads + (grad_mixed,), sums + (mix_sums,))


def swap_cores(value):
    return send(value, ((0, 1), (1, 0), (2, 3), (3, 2)))


def send(value, routes):
    return lax.ppermute(value, "section", routes)


def pick_row(value, at, axis=0):
    return lax.dynamic_index_in_dim(value, at, axis, keepdims=False)


def plus(*values):
    return sum(value.astype(F32) for value in values).astype(BF)


class RowSum:
    def __init__(self, mine, arrived, blocks):
        self.terms, self.blocks, self.crossed, self.travelling = (mine, arrived), blocks, (), ()
        self.plain = lax.axis_size("dp") != SHARDS
        self.crossed_rows, self.ring_at = 0, 0
        if not self.plain:
            at = lax.axis_index("dp")
            self.z, self.x = at // 2, at % 2

    def state(self):
        return (self.terms, self.crossed, self.travelling)

    def set(self, state):
        self.terms, self.crossed, self.travelling = state

    def cross(self, rows=None):
        if self.plain:
            return
        first, last = self.crossed_rows, rows or self.terms[0].shape[1]
        self.crossed_rows = last
        others = []
        for term in self.terms:
            cols = term.shape[2]
            cut = lax.dynamic_slice(
                term.reshape(4, 2, *term.shape[1:]),
                (0, 1 - self.x, first, 0),
                (4, 1, last - first, cols),
            )
            others.append(cut[:, 0])
        pairs = [(n, n ^ 1) for n in range(8)]
        self.crossed += (lax.ppermute(plus(*others), "dp", pairs),)

    def part(self, z, *more):
        values = []
        for term in self.terms:
            _, rows, cols = term.shape
            cut = lax.dynamic_slice(
                term.reshape(4, 2, rows, cols), (z, self.x, 0, 0), (1, 1, rows, cols)
            )
            values.append(cut[0, 0])
        values.append(jnp.concatenate([pick_row(part, z) for part in self.crossed], axis=0))
        return plus(*values, *more)

    def ring(self):
        if self.plain:
            return
        self.ring_at += 1
        passing = self.part(lax.rem(self.z + 4 - self.ring_at, 4), *self.travelling)
        self.travelling = (lax.ppermute(passing, "dp", [(n, (n + 2) % 8) for n in range(8)]),)

    def direct(self):
        if self.plain:
            return
        arrived = []
        for far in (3, 2, 1):
            for way in (far, -far):
                part = self.part(jnp.clip(self.z + way, 0, 3))
                routes = [(n, n + 2 * way) for n in range(8) if 0 <= n + 2 * way < 8]
                arrived.append(lax.ppermute(part, "dp", routes))
        self.travelling = tuple(arrived)

    def result(self):
        if not self.plain:
            return self.part(self.z, *self.travelling)
        shards = lax.axis_size("dp")
        parts, at, value = [], 0, plus(*self.terms)
        for rows in self.blocks:
            part = value[:, at : at + rows].reshape(shards, -1, value.shape[2])
            parts, at = parts + [part], at + rows
        whole = jnp.concatenate(parts, axis=1)
        return lax.psum_scatter(whole, "dp", scatter_dimension=0, tiled=True)[0]


def body(
    tokens_in, seg_starts, pad_mask, w_qkv, b_qv, w_attn_out, b_attn_out, ln_gain, ln_bias,
    w_up, b_up, w_down, b_down, w_proj, cotangent,
):
    section_at = lax.axis_index("section")
    core = section_at % 2
    is_late = section_at >= 2
    flip = core == 1
    quarter = tokens_in.shape[1]
    length, width = 4 * quarter, tokens_in.shape[2]
    ff_width = w_up.shape[2]
    proj_cols = w_proj.shape[1]
    shards = lax.axis_size("dp")
    share = width // shards

    def sel_for(half):
        return jnp.stack([core, section_at // 2, half]).astype(jnp.int32)

    sel_mine, sel_theirs = sel_for(core), sel_for(1 - core)

    own = pick_row(tokens_in, core)
    other = pick_row(tokens_in, 1 - core)
    straight = send(own, [(2, 0), (3, 1)])
    crossed = send(other, [(2, 1), (3, 0)])
    near = swap_cores(other)
    small = pack_small(b_qv[0], b_attn_out[0], ln_gain[0], ln_bias[0], b_up[0], b_down[0])[None]
    small_other = swap_cores(small)
    small = jnp.stack([jnp.where(flip, small_other, small), jnp.where(flip, small, small_other)])
    weights = tuple((w[0], swap_cores(w[0])) for w in (w_qkv, w_attn_out, w_up, w_down)) + (small,)
    x = jnp.concatenate(
        [
            jnp.where(flip, near, own),
            jnp.where(flip, own, near),
            jnp.where(flip, crossed, straight),
            jnp.where(flip, straight, crossed),
        ],
        axis=0,
    )

    plan = attention_plan(pick_row(seg_starts, core), pick_row(pad_mask, core))

    def both_forward(rows):
        middle, kept_even = layer_forward(sel_mine, rows, weights, 0, plan)
        last, kept_odd = layer_forward(sel_mine, middle, weights, 1, plan)
        return (last, kept_even, kept_odd)

    middle, kept_even = layer_forward(sel_mine, x, weights, 0, plan)
    head_own = jnp.concatenate([w_proj.T, pick_row(cotangent, core).T], axis=1)
    head_other = jnp.concatenate([w_proj.T, pick_row(cotangent, 1 - core).T], axis=1)
    middle, head_own, head_other = lax.optimization_barrier((middle, head_own, head_other))
    head_late = send(head_other, [(2, 3), (3, 2)])
    head_straight = send(head_own, [(0, 2), (1, 3)])
    head_crossed = send(head_other, [(0, 3), (1, 2)])
    head_cols = jnp.concatenate(
        [
            jnp.where(flip, head_crossed, head_straight),
            jnp.where(flip, head_straight, head_crossed),
            jnp.where(flip, head_late, head_own),
            jnp.where(flip, head_own, head_late),
        ],
        axis=0,
    )
    proj_rows, given_rows = head_cols[:, :width], head_cols[:, width:]
    (first, second), kept_odd = layer_forward_halves(sel_mine, middle, weights, 1, plan)
    first, proj_rows, given_rows = lax.optimization_barrier((first, proj_rows, given_rows))
    arrived = send(first, [(0, 2), (1, 3)])
    arrived, second = lax.optimization_barrier((arrived, second))
    hopped = jnp.concatenate([arrived, send(second, [(0, 2), (1, 3)])], axis=0)

    def late_turn(rows, *_):
        last, kept_even, kept_odd = both_forward(rows)
        embedded, grad_proj, grad = head(last, proj_rows, given_rows)
        grad, grads_odd, sums_odd = layer_backward(sel_mine, grad, kept_odd, weights, 1, plan)
        grad, grads_even, sums_even = layer_backward(sel_mine, grad, kept_even, weights, 0, plan)
        return (
            kept_even, kept_odd, embedded, grad_proj, grad,
            grads_odd, sums_odd, grads_even, sums_even,
        )

    def early_turn(rows, kept_even, kept_odd):
        row, ff = jnp.zeros((length, width), BF), jnp.zeros((length, ff_width), BF)
        grads = (row, ff, row, jnp.zeros((3, length, width), BF))
        sums = (
            jnp.zeros((6, width), F32),
            jnp.zeros((1, ff_width), F32),
            jnp.zeros((2, width), F32),
        )
        return (
            kept_even, kept_odd, jnp.zeros((4 * proj_cols, length), BF),
            jnp.zeros((width, 4 * proj_cols), BF), row, grads, sums, grads, sums,
        )

    (
        kept_even, kept_odd, embedded, grad_proj, grad_mid,
        late_odd, late_sums_odd, late_even, late_sums_even,
    ) = lax.cond(is_late, late_turn, early_turn, hopped, kept_even, kept_odd)

    halfway = length // 2
    arriving = [
        send(grad_mid[at : at + halfway], [(2, 0), (3, 1)]) for at in (0, halfway)
    ]
    embedded_cols = embedded.reshape(4, proj_cols, length)

    rows_of_one = width // SHARDS
    attend_blocks = (rows_of_one,) * 4
    feed_blocks = (rows_of_one,) * (ff_width // (2 * HALF)) + (ff_width // SHARDS,)

    def tie(*values):
        return lax.optimization_barrier(values)

    def feed_args(kept, late, now):
        return (kept[4], late[1], now[1], kept[9], late[0], now[0])

    def attend_args(kept, late, now, mixed):
        return (kept[2], kept[0], late[2], now[2], late[3], mixed)

    def tie_sums(values, *sums):
        values, states = tie(values, [part.state() for part in sums])
        for part, state in zip(sums, states):
            part.set(state)
        return values

    grad_context, grads_odd, sums_odd = feed_backward(sel_mine, arriving, kept_odd, weights, 1)
    args = feed_args(kept_odd, late_odd, grads_odd)
    arrived = swap_cores(feed_grads(sel_theirs, *args))
    feed_odd = RowSum(feed_grads(sel_mine, *args), arrived, feed_blocks)
    grad_context = tie_sums(grad_context, feed_odd)
    feed_odd.cross(rows_of_one * 6)
    straight_cols = send(pick_row(embedded_cols, core), [(2, 0), (3, 1)])
    crossed_cols = send(pick_row(embedded_cols, 1 - core), [(2, 1), (3, 0)])
    near_cols = swap_cores(pick_row(embedded_cols, 3 - core))
    mixed_odd, grad, mix_sums = mixed_backward(
        sel_mine, grad_context, grads_odd[2], kept_odd, weights, 1, plan
    )
    sums_odd = sums_odd + (mix_sums,)
    args = attend_args(kept_odd, late_odd, grads_odd, mixed_odd)
    args, straight_cols, crossed_cols, near_cols = tie_sums(
        (args, straight_cols, crossed_cols, near_cols), feed_odd
    )
    feed_odd.cross()
    theirs = attend_grads(sel_theirs, *args)
    args, theirs = tie_sums((args, theirs), feed_odd)
    feed_odd.ring()
    arrived = swap_cores(theirs)
    attend_odd = RowSum(attend_grads(sel_mine, *args), arrived, attend_blocks)
    grad = tie_sums(grad, feed_odd, attend_odd)
    feed_odd.ring()
    attend_odd.cross()

    grad_context, grads_even, sums_even = feed_backward(sel_mine, (grad,), kept_even, weights, 0)
    args = tie_sums(feed_args(kept_even, late_even, grads_even), feed_odd, attend_odd)
    feed_odd.ring()
    theirs = feed_grads(sel_theirs, *args)
    args, theirs = tie_sums((args, theirs), feed_odd)
    attend_odd.ring()
    arrived = swap_cores(theirs)
    feed_even = RowSum(feed_grads(sel_mine, *args), arrived, feed_blocks)
    grad_context = tie_sums(grad_context, feed_even, attend_odd)
    feed_even.cross()
    attend_odd.ring()
    mixed_even, grad, mix_sums = mixed_backward(
        sel_mine, grad_context, grads_even[2], kept_even, weights, 0, plan
    )
    sums_even = sums_even + (mix_sums,)
    args = attend_args(kept_even, late_even, grads_even, mixed_even)
    args = tie_sums(args, feed_even, attend_odd)
    feed_even.ring()
    routes_odd, routes_even = ((0, 1), (2, 3)), ((1, 0), (3, 2))
    feed_odd = feed_odd.result()
    theirs = attend_grads(sel_theirs, *args)
    extras = pack_extras(sel_mine, grad_proj, late_sums_even, late_sums_odd, sums_even, sums_odd)
    theirs = jnp.concatenate([theirs, extras.astype(BF)], axis=1)
    args, theirs, extras = tie_sums((args, theirs, extras), feed_even)
    arrived = swap_cores(theirs)
    feed_even.ring()
    quarters = grad.reshape(4, quarter, width)
    near_grad = swap_cores(pick_row(quarters, 1 - core))
    mine = jnp.concatenate([attend_grads(sel_mine, *args), extras.astype(BF)], axis=1)
    mine, quarters, near_grad = tie_sums((mine, quarters, near_grad), feed_even, attend_odd)
    attend_even = RowSum(mine, arrived, attend_blocks)
    attend_even.cross()
    feed_even.ring()
    attend_odd.ring()
    straight_grad = send(pick_row(quarters, 2 + core), [(0, 2), (1, 3)])
    crossed_grad = send(pick_row(quarters, 3 - core), [(0, 3), (1, 2)])
    straight_grad, crossed_grad = tie_sums(
        (straight_grad, crossed_grad), feed_even, attend_even, attend_odd
    )
    attend_even.direct()
    feed_even, attend_odd = feed_even.result(), attend_odd.result()
    sent_odd = [send(part, routes_odd) for part in (feed_odd, attend_odd)]
    if shards == SHARDS:
        tail = attend_even.result()
        attend_even, extras = tail[: 4 * share], tail[4 * share :].astype(F32)
    else:
        attend_even = attend_even.result()
        extras = plus(mine[:, -EXTRA_ROWS:], arrived[:, -EXTRA_ROWS:])
        extras = lax.psum(extras.astype(F32), "dp")

    def halves(even, odd, sent):
        arrived = jnp.where(flip, sent, send(even, routes_even))
        mine = jnp.where(flip, odd, even)
        return (jnp.where(flip, arrived, mine), jnp.where(flip, mine, arrived))

    blocks = ff_width // (2 * HALF)
    feed_halves = halves(feed_even, feed_odd, sent_odd[0])
    attend_halves = halves(attend_even, attend_odd, sent_odd[1])

    def columns(pair, first, count):
        parts = [part[n * share : (n + 1) * share] for part in pair for n in range(first, first + count)]
        return jnp.concatenate(parts, axis=1).astype(F32)

    grad_w_up = columns(feed_halves, 0, blocks)[None]
    grad_w_down = jnp.concatenate([part[blocks * share :] for part in feed_halves], axis=1)
    grad_w_down = grad_w_down.astype(F32)[None]
    grad_w_out = columns(attend_halves, 0, 1)[None]
    grad_w_qkv = jnp.concatenate([columns(attend_halves, 1 + c, 1) for c in range(3)], axis=1)[None]

    if shards == SHARDS:
        at, pick = 0, lambda values: values
    else:
        at = lax.axis_index("dp") % (shards // SHARDS)
        extras = pick_row(extras, lax.axis_index("dp") // (shards // SHARDS))

        def pick(values):
            size = values.shape[-1] * SHARDS // shards
            return lax.dynamic_slice_in_dim(values, at * size, size, values.ndim - 1)

    one = width // SHARDS
    small_mine = jnp.where(flip, extras[8:16], extras[:8])
    grad_b_up = pick(small_mine[0:1, : ff_width // SHARDS])
    grad_b_qv = pick(small_mine[1:2, : 2 * one])
    rows = pick(small_mine[2:8, :one])
    grad_proj = extras[16:].reshape(-1, 3, 4 * proj_cols).transpose(1, 0, 2)
    grad_proj = grad_proj.reshape(one, 4 * proj_cols)
    grad_proj = lax.dynamic_slice_in_dim(grad_proj, at * share, share, 0).astype(BF)
    grad_proj = jnp.where(is_late, grad_proj, send(grad_proj, [(2, 0), (3, 1)])).astype(F32)
    grad_w_proj = lax.dynamic_slice_in_dim(grad_proj, section_at * proj_cols, proj_cols, 1)

    own_cols = jnp.where(is_late, pick_row(embedded_cols, section_at), straight_cols)
    other_cols = jnp.where(is_late, near_cols, crossed_cols)
    embedded_out = jnp.stack(
        [jnp.where(flip, other_cols, own_cols).T, jnp.where(flip, own_cols, other_cols).T]
    )

    mine = jnp.where(is_late, straight_grad, pick_row(quarters, core))
    others = jnp.where(is_late, crossed_grad, near_grad)
    grad_in = jnp.stack(
        [jnp.where(flip, others, mine), jnp.where(flip, mine, others)]
    ).astype(F32)

    return (
        embedded_out,
        grad_in,
        grad_w_qkv,
        grad_b_qv,
        grad_w_out,
        rows[0][None],
        rows[1:3][None],
        rows[3:5][None],
        grad_w_up,
        grad_b_up,
        grad_w_down,
        rows[5][None],
        grad_w_proj,
    )


def solution(mesh):
    in_specs = (
        P("dp", "section", None),
        P("dp", None),
        P("dp", None),
        P("section", None, None),
        P("section", None),
        P("section", None, None),
        P("section", None),
        P("section", None, None),
        P("section", None, None),
        P("section", None, None),
        P("section", None),
        P("section", None, None),
        P("section", None),
        P(None, "section"),
        P("dp", None, "section"),
    )
    out_specs = (
        P("dp", None, "section"),
        P("dp", "section", None),
        P("section", "dp", None),
        P("section", "dp"),
        P("section", "dp", None),
        P("section", "dp"),
        P("section", None, "dp"),
        P("section", None, "dp"),
        P("section", "dp", None),
        P("section", "dp"),
        P("section", "dp", None),
        P("section", "dp"),
        P("dp", "section"),
    )
    return jax.shard_map(body, mesh=mesh, in_specs=in_specs, out_specs=out_specs, check_vma=False)
```

```python
from functools import partial
import math

import jax
import jax.numpy as jnp
from jax import lax
from jax.experimental import pallas as pl
from jax.experimental.pallas import tpu as pltpu
from jax.sharding import PartitionSpec as P

HEAD = 64
PAIR = 2 * HEAD
QB = 128
KB = 512
KEYS = 256
EPS_NORM = 1e-05
EPS_PROJ = 1e-06
NEG_FILL = -1e30
PARAMS = pltpu.CompilerParams(vmem_limit_bytes=60 * 1024 * 1024)


def cost(micros):
    return pl.CostEstimate(flops=int(micros * 1e9), bytes_accessed=1024, transcendentals=0)


BF = jnp.bfloat16
F32 = jnp.float32

NT = (((1,), (1,)), ((), ()))
TN = (((0,), (0,)), ((), ()))


def dot(a, b):
    return jnp.dot(a, b, preferred_element_type=F32)


def dot_nt(a, b):
    return lax.dot_general(a, b, NT, preferred_element_type=F32)


def dot_tn(a, b):
    return lax.dot_general(a, b, TN, preferred_element_type=F32)


def pack_small(b_qv, b_out, gains, shifts, b_up, b_down):
    return jnp.concatenate(
        [b_up, b_qv, b_out, gains[0], gains[1], shifts[0], shifts[1], b_down]
    )


def small_spec(layer, width):
    return pl.BlockSpec((1, 1, width), lambda *_: (layer, 0, 0))


def attention_plan(starts, real_flags):
    length = real_flags.shape[0]
    places = jnp.arange(length, dtype=jnp.int32)
    segment = jnp.sum((starts[None, :] <= places[:, None]).astype(jnp.int32), axis=1)
    key_code = jnp.where(real_flags == 1, segment, -1).astype(F32)
    key_code = jnp.broadcast_to(key_code[:, None], (length, PAIR))
    query_code = segment.astype(F32).reshape(length // QB, QB)
    first = jnp.arange(length // QB, dtype=jnp.int32) * QB
    low = jnp.max(jnp.where(starts[None, :] <= first[:, None], starts[None, :], 0), axis=1)
    high = jnp.min(
        jnp.where(starts[None, :] > first[:, None] + (QB - 1), starts[None, :], length), axis=1
    )
    begin = (low // QB) * QB
    count = (high - begin + KEYS - 1) // KEYS
    begin = jnp.minimum(begin, length - KEYS * count)
    return (begin, count, key_code, query_code)


def pair_mask(rows):
    return lax.broadcasted_iota(jnp.int32, (rows, PAIR), 1) < HEAD


def stacked_heads(block):
    first = pair_mask(block.shape[0])
    zero = jnp.zeros_like(block)
    return jnp.concatenate([jnp.where(first, block, zero), jnp.where(first, zero, block)], axis=0)


def block_bias(key_code, query_code, key_at, query_at):
    shape = key_code.shape
    keys = lax.broadcasted_iota(jnp.int32, shape, 0) + (key_at - query_at)
    same = keys == lax.broadcasted_iota(jnp.int32, shape, 1)
    bias = jnp.where((key_code == query_code) | same, 0.0, NEG_FILL)
    return jnp.concatenate([bias, bias], axis=1)


def over_keys(begin, count, step, state):
    state = lax.fori_loop(
        0,
        lax.shift_right_logical(count, 1),
        lambda j, now: step(pl.multiple_of(begin + j * KB, QB), KB, now),
        state,
    )
    last = pl.multiple_of(begin + (count - 1) * KEYS, QB)
    return lax.fori_loop(
        0, jnp.bitwise_and(count, 1), lambda _, now: step(last, KEYS, now), state
    )


def unstack_heads(flat):
    rows = lax.broadcasted_iota(jnp.int32, (PAIR, QB), 0)
    return jnp.where(rows < HEAD, flat[:PAIR, :QB], flat[:PAIR, QB:]).T


SAFE_SCORE = 70.0


def score_bound(peak):
    lanes = lax.broadcasted_iota(jnp.int32, peak.shape, 1)
    return jnp.max(jnp.where(lanes < HEAD, peak, 0.0)) * jnp.max(jnp.where(lanes < HEAD, 0.0, peak))


def head_lanes(width):
    rows = lax.broadcasted_iota(jnp.int32, (2 * width, PAIR), 0)
    lanes = lax.broadcasted_iota(jnp.int32, (2 * width, PAIR), 1)
    head = lax.shift_right_logical(rows, 6)
    wanted = jnp.where(rows < width, head, head - width // HEAD + HEAD)
    return jnp.where(lanes == wanted, 1.0, 0.0).astype(BF)


def attend_forward(
    begin_ref, count_ref, qkv_ref, key_code_ref, query_code_ref, out_ref, logsum_ref,
    value_scr, query_scr, total_scr, is_safe,
):
    length = qkv_ref.shape[1]
    pairs = qkv_ref.shape[2] // PAIR
    every = range(pairs)
    cols = [slice(p * PAIR, (p + 1) * PAIR) for p in every]
    for p in every:
        value_scr[p, :PAIR, :] = qkv_ref[2, :, cols[p]].T
        value_scr[p, PAIR:, :] = jnp.ones((value_scr.shape[1] - PAIR, length), BF)

    def one_query_block(shifted, i, _):
        query_at = pl.multiple_of(i * QB, QB)
        begin, count = begin_ref[i], count_ref[i]
        query_code = query_code_ref[pl.ds(i, 1), :]
        for p in every:
            query_scr[p] = stacked_heads(qkv_ref[0, pl.ds(query_at, QB), cols[p]])
        total_scr[...] = jnp.zeros_like(total_scr)

        def one_key_block(key_at, size, tops):
            rows = pl.ds(key_at, size)
            bias = block_bias(key_code_ref[rows, :], query_code, key_at, query_at)
            scores = [dot_nt(qkv_ref[1, rows, cols[p]], query_scr[p]) + bias for p in every]
            if not shifted:
                probs = [jnp.exp(scores[p]).astype(BF) for p in every]
                for p in every:
                    total_scr[p] += dot(value_scr[p, :, rows], probs[p])
                return tops
            fresh = [
                jnp.maximum(tops[p], jnp.max(scores[p], axis=0, keepdims=True)) for p in every
            ]
            probs = [jnp.exp(scores[p] - fresh[p]).astype(BF) for p in every]
            for p in every:
                total_scr[p] = total_scr[p] * jnp.exp(tops[p] - fresh[p]) + dot(
                    value_scr[p, :, rows], probs[p]
                )
            return tuple(fresh)

        lowest = 2 * NEG_FILL if shifted else 0.0
        tops = tuple(jnp.full((1, 2 * QB), lowest, F32) for _ in every)
        tops = over_keys(begin, count, one_key_block, tops)
        for p in every:
            weight = total_scr[p, PAIR : PAIR + 1, :]
            logsum_ref[pl.ds(p * (length // QB) + i, 1), :] = tops[p] + jnp.log(weight)
            out_ref[pl.ds(query_at, QB), cols[p]] = unstack_heads(
                total_scr[p, :PAIR, :] * (1.0 / weight)
            ).astype(BF)
        return 0

    for wanted, shifted in ((is_safe, False), (jnp.logical_not(is_safe), True)):

        @pl.when(wanted)
        def _():
            lax.fori_loop(0, length // QB, partial(one_query_block, shifted), 0)


def attend_backward(
    begin_ref, count_ref, qkv, key_code_ref, query_code_ref, context, logsum_ref, grad, sums_ref,
    key_scr, query_scr, given_scr, down_scr, grad_key_scr, grad_value_scr, ready,
):
    length = qkv.shape[1]
    pairs = qkv.shape[2] // PAIR
    every = range(pairs)
    blocks = length // QB
    cols = [slice(p * PAIR, (p + 1) * PAIR) for p in every]
    for p in every:
        key_scr[p] = qkv[1, :, cols[p]].T
    ready()

    def one_query_block(i, _):
        query_at = pl.multiple_of(i * QB, QB)
        queries = pl.ds(query_at, QB)
        begin, count = begin_ref[i], count_ref[i]
        query_code = query_code_ref[pl.ds(i, 1), :]
        inner, logsum = [], []
        for p in every:
            query_scr[p] = stacked_heads(qkv[0, queries, cols[p]])
            given = grad[queries, cols[p]]
            given_scr[p] = stacked_heads(given)
            both = (given.astype(F32) * context[queries, cols[p]].astype(F32)).T
            inner.append(
                jnp.concatenate(
                    [
                        jnp.sum(both[:HEAD], axis=0, keepdims=True),
                        jnp.sum(both[HEAD:], axis=0, keepdims=True),
                    ],
                    axis=1,
                )
            )
            logsum.append(logsum_ref[pl.ds(p * blocks + i, 1), :])
        down_scr[...] = jnp.zeros_like(down_scr)

        def one_key_block(key_at, size, state):
            rows = pl.ds(key_at, size)
            bias = block_bias(key_code_ref[rows, :], query_code, key_at, query_at)
            parts, grads, probs, scores = {}, {}, {}, {}
            for p in range(pairs + 1):
                if p < pairs:
                    grads[p] = dot_nt(qkv[2, rows, cols[p]], given_scr[p]) - inner[p]
                    parts[p] = dot_nt(qkv[1, rows, cols[p]], query_scr[p]) + bias
                if 0 <= p - 1 < pairs:
                    q = p - 1
                    probs[q] = jnp.exp(parts.pop(q) - logsum[q])
                    scores[q] = (probs[q] * grads.pop(q)).astype(BF)
                    probs[q] = probs[q].astype(BF)
                if 0 <= p - 1 < pairs:
                    q = p - 1
                    grad_value_scr[rows, cols[q]] += dot(probs.pop(q), given_scr[q])
                    grad_key_scr[rows, cols[q]] += dot(scores[q], query_scr[q])
                    down_scr[q] += dot(key_scr[q, :, rows], scores.pop(q))
            return state

        over_keys(begin, count, one_key_block, 0)
        for p in every:
            grad_query = (unstack_heads(down_scr[p]) * (HEAD**-0.5)).astype(BF)
            qkv[0, queries, cols[p]] = grad_query
            sums_ref[0:1, cols[p]] += jnp.sum(grad_query.astype(F32), axis=0, keepdims=True)
        return 0

    lax.fori_loop(0, blocks, one_query_block, 0)
    qkv[1] = grad_key_scr[...].astype(BF)
    grad_value = grad_value_scr[...].astype(BF)
    qkv[2] = grad_value
    sums_ref[1:2, :] = jnp.sum(grad_value.astype(F32), axis=0, keepdims=True)


ANY = pl.BlockSpec(memory_space=pl.ANY)
ROWS = 256


class Held:
    def __init__(self, sel_ref, layer, pairs, held, sems, first=None):
        self.own = sel_ref[0] == layer
        self.items = list(zip(pairs, held, range(len(held))))
        self.sems = sems
        self.first = pl.program_id(0) == 0 if first is None else first

    def start(self):
        for pair, held, n in self.items:
            for wanted, source in zip((self.own, jnp.logical_not(self.own)), pair):

                @pl.when(self.first & wanted)
                def _():
                    pltpu.make_async_copy(source, held, self.sems.at[n]).start()

    def wait(self, n):
        pair, held, _ = self.items[n]

        @pl.when(self.first)
        def _():
            pltpu.make_async_copy(pair[0], held, self.sems.at[n]).wait()


def held_shapes(*weights):
    return [pltpu.VMEM(own.shape, own.dtype) for own, _ in weights]


def normalized(values):
    centred = values - jnp.mean(values, axis=-1, keepdims=True)
    inverse = lax.rsqrt(jnp.mean(centred * centred, axis=-1, keepdims=True) + EPS_NORM)
    return (centred * inverse, inverse)


def normalized_pull(grad_hat, hat, inverse):
    return inverse * (
        grad_hat
        - jnp.mean(grad_hat, axis=-1, keepdims=True)
        - hat * jnp.mean(grad_hat * hat, axis=-1, keepdims=True)
    )


ERF = (0.254829592, -0.284496736, 1.421413741, -1.453152027, 1.061405429)
ERF_SLOPE = 0.3275911


def gelu_parts(x):
    t = pl.reciprocal(1.0 + (ERF_SLOPE * math.sqrt(0.5)) * jnp.abs(x), approx=True)
    bell = jnp.exp(-0.5 * (x * x))
    tail = 0.5 * ERF[4]
    for term in ERF[3::-1]:
        tail = tail * t + 0.5 * term
    tail = tail * t * bell
    below = jnp.where(x >= 0, 1.0 - tail, tail)
    return (x * below, below + x * bell * (1.0 / math.sqrt(2.0 * math.pi)))


FB = 1024


def small_slices(width, ff_width):
    names = ("b_q", "b_v", "b_out", "gain1", "gain2", "shift1", "shift2", "b_down")
    at = {"b_up": slice(0, ff_width)}
    for n, name in enumerate(names):
        at[name] = slice(ff_width + n * width, ff_width + (n + 1) * width)
    return at


def refine_back_kernel(
    layer, sel_ref, grad_ref, hidden_ref, out_ref, scale1_ref, scale2_ref, slope_ref,
    out_own_ref, out_other_ref, up_own_ref, up_other_ref, down_own_ref, down_other_ref, small_ref,
    grad_low_ref, grad_raised_ref, grad_attn_ref, grad_context_ref, sums_ref, up_sums_ref,
    w_out, w_up, w_down, sems,
):
    pairs = [(down_own_ref, down_other_ref), (up_own_ref, up_other_ref), (out_own_ref, out_other_ref)]
    weights = Held(sel_ref, layer, pairs, [w_down, w_up, w_out], sems)
    weights.start()
    rows, width = grad_ref.shape
    ff_width = slope_ref.shape[1]
    at = small_slices(width, ff_width)

    @pl.when(pl.program_id(0) == 0)
    def _():
        sums_ref[...] = jnp.zeros_like(sums_ref)
        up_sums_ref[...] = jnp.zeros_like(up_sums_ref)

    def vector(name):
        return small_ref[0, :, at[name]]

    def add(row, values):
        sums_ref[row : row + 1, :] += jnp.sum(values, axis=0, keepdims=True)

    grad = grad_ref[...].astype(F32)
    hat = (out_ref[...].astype(F32) - vector("shift2")) * (1.0 / vector("gain2"))
    joined = normalized_pull(grad * vector("gain2"), hat, scale2_ref[:, :1])
    low = joined.astype(BF)
    grad_low_ref[...] = low
    add(2, grad * hat)
    add(4, grad)
    add(5, low.astype(F32))
    weights.wait(0)
    weights.wait(1)
    total = joined
    parts = [slice(f, f + FB) for f in range(0, ff_width, FB)]
    active = dot_nt(low, w_down[parts[0], :])
    for n, part in enumerate(parts):
        following = dot_nt(low, w_down[parts[n + 1], :]) if n + 1 < len(parts) else None
        raised = active * slope_ref[:, part].astype(F32)
        up_sums_ref[:, part] += jnp.sum(raised, axis=0, keepdims=True)
        raised = raised.astype(BF)
        grad_raised_ref[:, part] = raised
        total += dot_nt(raised, w_up[:, part])
        active = following
    hat = (hidden_ref[...].astype(F32) - vector("shift1")) * (1.0 / vector("gain1"))
    summed = normalized_pull(total * vector("gain1"), hat, scale1_ref[:, :1])
    attn = summed.astype(BF)
    grad_attn_ref[...] = attn
    weights.wait(2)
    grad_context_ref[...] = dot_nt(attn, w_out[...]).astype(BF)
    add(1, total * hat)
    add(3, total)
    add(0, attn.astype(F32))


def refine_back_second_kernel(layer, *refs):
    refine_back_kernel(layer, *refs[:14], *refs[18:])


def refine_back(sel, grad, kept, weights, layer, first=0, begun=()):
    w_out, w_up, w_down, small = weights
    hidden, out, scale1, scale2, slope = kept
    length, width = hidden.shape
    ff_width = w_up[0].shape[1]
    at = first // ROWS
    rows = pl.BlockSpec((ROWS, width), lambda n, _: (n + at, 0))
    lanes = pl.BlockSpec((ROWS, 128), lambda n, _: (n + at, 0))
    part = pl.BlockSpec((ROWS, ff_width), lambda n, _: (n + at, 0))
    row_shape = jax.ShapeDtypeStruct((length, width), BF)
    return pl.pallas_call(
        partial(refine_back_second_kernel if begun else refine_back_kernel, layer),
        name="refine_back",
        grid_spec=pltpu.PrefetchScalarGridSpec(
            num_scalar_prefetch=1,
            grid=(grad.shape[0] // ROWS,),
            in_specs=[
                pl.BlockSpec((ROWS, width), lambda n, _: (n, 0)),
                rows, rows, lanes, lanes, part,
            ]
            + [ANY] * 6
            + [small_spec(layer, small.shape[2])]
            + [ANY] * len(begun),
            out_specs=[
                rows, part, rows, rows,
                pl.BlockSpec((6, width), lambda n, _: (0, 0)),
                pl.BlockSpec((1, ff_width), lambda n, _: (0, 0)),
            ],
            scratch_shapes=[
                *held_shapes(w_out, w_up, w_down),
                pltpu.SemaphoreType.DMA((3,)),
            ],
        ),
        out_shape=[
            row_shape,
            jax.ShapeDtypeStruct((length, ff_width), BF),
            row_shape,
            row_shape,
            jax.ShapeDtypeStruct((6, width), F32),
            jax.ShapeDtypeStruct((1, ff_width), F32),
        ],
        input_output_aliases={14 + n: n for n in range(len(begun))},
        compiler_params=PARAMS,
        cost_estimate=cost(24),
    )(sel, grad, hidden, out, scale1, scale2, slope, *w_out, *w_up, *w_down, small, *begun)


def head_kernel(rows_ref, proj_ref, given_ref, embedded_ref, grad_proj_ref, grad_rows_ref):
    factor = math.sqrt(proj_ref.shape[0])
    columns = dot_nt(proj_ref[...], rows_ref[...])
    given = given_ref[...].astype(F32)
    inverse = lax.rsqrt(jnp.sum(columns * columns, axis=0, keepdims=True) + EPS_PROJ)
    cross = jnp.sum(columns * given, axis=0, keepdims=True)
    embedded_ref[...] = (factor * columns * inverse).astype(BF)
    grad = (factor * (given * inverse - columns * (cross * inverse * inverse * inverse))).astype(BF)
    grad_proj_ref[...] = dot(grad, rows_ref[...]).T.astype(BF)
    grad_rows_ref[...] = dot_tn(grad, proj_ref[...]).astype(BF)


def head(rows, proj, given):
    length, width = rows.shape
    cols = proj.shape[0]
    return pl.pallas_call(
        head_kernel,
        name="head",
        out_shape=[
            jax.ShapeDtypeStruct((cols, length), BF),
            jax.ShapeDtypeStruct((width, cols), BF),
            jax.ShapeDtypeStruct((length, width), BF),
        ],
        compiler_params=PARAMS,
        cost_estimate=cost(6),
    )(rows, proj, given)


HALF = 384
SHARDS = 8


def feed_grads_kernel(
    sel_ref, hidden_ref, raised_late_ref, raised_ref, active_ref, low_late_ref, low_ref, out_ref
):
    step = pl.program_id(0)
    shards, rows, _ = out_ref.shape
    blocks = raised_ref.shape[1] // HALF
    share = rows // blocks
    late = sel_ref[1] == 1

    def up(raised):
        part = dot_tn(hidden_ref[...], raised).astype(BF)
        for m in range(shards):
            for n in range(blocks):
                out_ref[m, n * share : (n + 1) * share, :] = part[
                    m * share : (m + 1) * share, n * HALF : (n + 1) * HALF
                ]

    def down(low):
        for m in range(shards):
            out_ref[m] = dot_tn(active_ref[:, m * rows : (m + 1) * rows], low).astype(BF)

    for wanted, raised_now, low_now in (
        (late, raised_late_ref, low_late_ref),
        (jnp.logical_not(late), raised_ref, low_ref),
    ):

        @pl.when(wanted & (step < 2))
        def _():
            up(raised_now[...])

        @pl.when(wanted & (step >= 2))
        def _():
            down(low_now[...])


def feed_grads(sel, hidden, raised_late, raised, active, low_late, low):
    length, width = hidden.shape
    ff_width = active.shape[1]
    half_ff = ff_width // 2

    def late_spec(shape, wanted):
        return pl.BlockSpec(shape, lambda n, sel: (0, jnp.where(sel[1] == wanted, sel[2], 0)))

    return pl.pallas_call(
        feed_grads_kernel,
        name="feed_grads",
        grid_spec=pltpu.PrefetchScalarGridSpec(
            num_scalar_prefetch=1,
            grid=(4,),
            in_specs=[
                pl.BlockSpec((length, width // 2), lambda n, _: (0, jnp.minimum(n, 1))),
                late_spec((length, half_ff), 1),
                late_spec((length, half_ff), 0),
                pl.BlockSpec((length, ff_width // 2), lambda n, _: (0, jnp.maximum(n - 2, 0))),
                late_spec((length, width // 2), 1),
                late_spec((length, width // 2), 0),
            ],
            out_specs=pl.BlockSpec(
                (SHARDS // 2, ff_width // SHARDS, HALF), lambda n, _: (lax.rem(n, 2), n // 2, 0)
            ),
        ),
        out_shape=jax.ShapeDtypeStruct((SHARDS, 2 * (ff_width // SHARDS), HALF), BF),
        compiler_params=PARAMS,
        cost_estimate=cost(12),
    )(sel, hidden, raised_late, raised, active, low_late, low)


def attend_grads_kernel(
    sel_ref, context_ref, x_ref, attn_late_ref, attn_ref, mixed_late_ref, mixed_ref, *rest
):
    step = pl.program_id(0)
    late = sel_ref[1] == 1
    out_ref = rest[-1]
    shards = out_ref.shape[0]
    share = x_ref.shape[1] // shards

    def store(n, rows, cols):
        part = dot_tn(rows, cols).astype(BF).reshape(shards, share, cols.shape[1])
        if len(rest) == 1:
            out_ref[...] = part
        else:
            out_ref[:, n * share : (n + 1) * share, :] = part

    if len(rest) > 1:

        @pl.when(step == 0)
        def _():
            out_ref[:, 4 * share :, :] = rest[0][...].astype(BF)

    for wanted, attn_now, mixed_now in (
        (late, attn_late_ref, mixed_late_ref),
        (jnp.logical_not(late), attn_ref, mixed_ref),
    ):

        @pl.when(wanted & (step == 0))
        def _():
            store(0, context_ref[...], attn_now[...])

        for n in (1, 2, 3):

            @pl.when(wanted & (step == n))
            def _():
                store(n, x_ref[...], mixed_now[0])


def attend_grads(sel, context, x, attn_late, attn, mixed_late, mixed, extras=None):
    length, width = x.shape

    def late_spec(wanted):
        return pl.BlockSpec(
            (length, HALF), lambda n, sel: (0, jnp.where(sel[1] == wanted, sel[2], 0))
        )

    def mixed_spec(wanted):
        def at(n, sel):
            return (
                jnp.where(sel[1] == wanted, jnp.maximum(n - 1, 0), 0),
                0,
                jnp.where(sel[1] == wanted, sel[2], 0),
            )

        return pl.BlockSpec((1, length, HALF), at)

    whole = pl.BlockSpec((length, width), lambda n, _: (0, 0))
    share = width // SHARDS
    more = () if extras is None else (extras,)
    rows = 4 * share + sum(part.shape[1] for part in more)
    out_spec = pl.BlockSpec((SHARDS, share, HALF), lambda n, _: (0, n, 0))
    if more:
        out_spec = pl.BlockSpec((SHARDS, rows, HALF), lambda n, _: (0, 0, 0))
    return pl.pallas_call(
        attend_grads_kernel,
        name="attend_grads",
        grid_spec=pltpu.PrefetchScalarGridSpec(
            num_scalar_prefetch=1,
            grid=(4,),
            in_specs=[whole, whole, late_spec(1), late_spec(0), mixed_spec(1), mixed_spec(0)]
            + [pl.BlockSpec(part.shape, lambda n, _: (0, 0, 0)) for part in more],
            out_specs=out_spec,
        ),
        out_shape=jax.ShapeDtypeStruct((SHARDS, rows, HALF), BF),
        compiler_params=PARAMS,
        cost_estimate=cost(8),
    )(sel, context, x, attn_late, attn, mixed_late, mixed, *more)


EXTRA_ROWS = 48


def pack_extras_kernel(
    sel_ref, proj_ref,
    late_sums_0, late_up_0, late_mix_0, late_sums_1, late_up_1, late_mix_1,
    sums_0, up_0, mix_0, sums_1, up_1, mix_1, out_ref,
):
    shards = out_ref.shape[0]
    width = sums_0.shape[1]
    share = width // shards
    third = share // 3
    cols = proj_ref.shape[1]
    out_ref[...] = jnp.zeros_like(out_ref)

    def layer(first, sums, up, mix):
        up_share = up.shape[1] // shards
        both = jnp.concatenate([mix[0:1, :], mix[1:2, :]], axis=1)
        for m in range(shards):
            rows = [up[0:1, m * up_share : (m + 1) * up_share]]
            rows += [both[:, 2 * m * share : 2 * (m + 1) * share]]
            rows += [sums[n : n + 1, m * share : (m + 1) * share] for n in range(6)]
            for n, row in enumerate(rows):
                out_ref[m, first + n : first + n + 1, : row.shape[1]] = row

    late = sel_ref[1] == 1
    for wanted, even, odd in (
        (late, (late_sums_0, late_up_0, late_mix_0), (late_sums_1, late_up_1, late_mix_1)),
        (jnp.logical_not(late), (sums_0, up_0, mix_0), (sums_1, up_1, mix_1)),
    ):

        @pl.when(wanted)
        def _():
            layer(0, *even)
            layer(8, *odd)

    for m in range(shards):
        for n in range(3):
            at = m * share + n * third
            out_ref[m, 16:, n * cols : (n + 1) * cols] = proj_ref[at : at + third, :].astype(F32)


def pack_extras(sel, proj, late_even, late_odd, even, odd):
    vmem = pl.BlockSpec(memory_space=pltpu.VMEM)
    return pl.pallas_call(
        pack_extras_kernel,
        name="pack_extras",
        in_specs=[pl.BlockSpec(memory_space=pltpu.SMEM)] + [vmem] * 13,
        out_specs=vmem,
        out_shape=jax.ShapeDtypeStruct((SHARDS, EXTRA_ROWS, HALF), F32),
        compiler_params=PARAMS,
        cost_estimate=cost(3),
    )(sel, proj, *late_even, *late_odd, *even, *odd)


def refine_block(
    rows, x, context, w_out, w_up, w_down, small_ref,
    hidden_rows, out_rows, scale1_ref, scale2_ref, active_rows, slope_rows,
):
    width, ff_width = w_up.shape
    at = small_slices(width, ff_width)

    def vector(name):
        return small_ref[0, :, at[name]]

    summed = x[rows, :].astype(F32) + dot(context[rows, :], w_out[...]) + vector("b_out")
    hat, inverse = normalized(summed)
    hidden = hat * vector("gain1") + vector("shift1")
    scale1_ref[rows, :] = jnp.broadcast_to(inverse, (ROWS, 128))
    hidden_low = hidden.astype(BF)
    hidden_rows[rows, :] = hidden_low
    total = hidden + vector("b_down")
    parts = [slice(f, f + FB) for f in range(0, ff_width, FB)]
    raised = dot(hidden_low, w_up[:, parts[0]])
    for m, part in enumerate(parts):
        following = dot(hidden_low, w_up[:, parts[m + 1]]) if m + 1 < len(parts) else None
        active, slope = gelu_parts(raised + small_ref[0, :, part])
        active = active.astype(BF)
        active_rows[rows, part] = active
        slope_rows[rows, part] = slope.astype(BF)
        total += dot(active, w_down[part, :])
        raised = following
    hat, inverse = normalized(total)
    scale2_ref[rows, :] = jnp.broadcast_to(inverse, (ROWS, 128))
    out_rows[rows, :] = (hat * vector("gain2") + vector("shift2")).astype(BF)


def refine_rest_kernel(
    layer, sel_ref, x_hbm, context_hbm,
    out_own_ref, out_other_ref, up_own_ref, up_other_ref, down_own_ref, down_other_ref, small_ref,
    hidden_begun, scale1_begun, scale2_begun, active_begun, slope_begun,
    out_hbm, hidden_hbm, scale1_ref, scale2_ref, active_hbm, slope_hbm,
    w_out, w_up, w_down, x, context, hidden_rows, out_rows, active_rows, slope_rows,
    weight_sems, in_sems, row_sems,
):
    pairs = [(out_own_ref, out_other_ref), (up_own_ref, up_other_ref), (down_own_ref, down_other_ref)]
    count = x.shape[0]
    first = x_hbm.shape[0] - count
    weights = Held(sel_ref, layer, pairs, [w_out, w_up, w_down], weight_sems, True)
    loads = [
        pltpu.make_async_copy(whole.at[pl.ds(first, count)], held, in_sems.at[n])
        for n, (whole, held) in enumerate(((x_hbm, x), (context_hbm, context)))
    ]
    for load in loads:
        load.start()
    weights.start()
    for load in loads:
        load.wait()
    for n in range(3):
        weights.wait(n)
    saved = [
        (hidden_rows, hidden_hbm, first), (out_rows, out_hbm, 0),
        (active_rows, active_hbm, first), (slope_rows, slope_hbm, first),
    ]

    def row_copies(n):
        return [
            pltpu.make_async_copy(
                rows.at[pl.ds(pl.multiple_of(n * ROWS, ROWS), ROWS)],
                whole.at[pl.ds(pl.multiple_of(n * ROWS + at, ROWS), ROWS)],
                row_sems.at[k, n],
            )
            for k, (rows, whole, at) in enumerate(saved)
        ]

    def refine_rows(n, _):
        refine_block(
            pl.ds(pl.multiple_of(n * ROWS, ROWS), ROWS), x, context, w_out, w_up, w_down,
            small_ref, hidden_rows, out_rows, scale1_ref, scale2_ref, active_rows, slope_rows,
        )
        for copy in row_copies(n):
            copy.start()
        return 0

    lax.fori_loop(0, count // ROWS, refine_rows, 0)
    for n in range(count // ROWS):
        for copy in row_copies(n):
            copy.wait()


def refine_rest(sel, x, context, weights, layer, begun, count):
    _, w_out, w_up, w_down, small = weights
    length, width = x.shape
    ff_width = w_up[0].shape[1]
    row = pltpu.VMEM((count, width), BF)
    wide = pltpu.VMEM((count, ff_width), BF)
    lanes = pl.BlockSpec((count, 128), lambda n, _: (length // count - 1, 0))
    return pl.pallas_call(
        partial(refine_rest_kernel, layer),
        name="refine_rest",
        grid_spec=pltpu.PrefetchScalarGridSpec(
            num_scalar_prefetch=1,
            grid=(1,),
            in_specs=[ANY] * 8 + [small_spec(layer, small.shape[2])] + [ANY] * 5,
            out_specs=[ANY, ANY, lanes, lanes, ANY, ANY],
            scratch_shapes=[
                *held_shapes(w_out, w_up, w_down),
                row, row, row, row, wide, wide,
                pltpu.SemaphoreType.DMA((3,)),
                pltpu.SemaphoreType.DMA((2,)),
                pltpu.SemaphoreType.DMA((4, count // ROWS)),
            ],
        ),
        out_shape=[jax.ShapeDtypeStruct((count, width), BF)]
        + [jax.ShapeDtypeStruct(part.shape, part.dtype) for part in begun],
        input_output_aliases={10 + n: 1 + n for n in range(5)},
        compiler_params=PARAMS,
        cost_estimate=cost(14),
    )(sel, x, context, *w_out, *w_up, *w_down, small, *begun)


def forward_kernel(
    layer, begin_ref, count_ref, sel_ref, x_hbm, key_code_ref, query_code_ref,
    mix_own_ref, mix_other_ref, out_own_ref, out_other_ref,
    up_own_ref, up_other_ref, down_own_ref, down_other_ref, small_ref,
    qkv_hbm, context_hbm, logsum_ref, out_hbm, hidden_hbm, scale1_ref, scale2_ref,
    active_hbm, slope_hbm,
    w_mix, w_out, w_up, w_down, x, qkv, context, hidden_rows, out_rows, active_rows, slope_rows,
    value_scr, query_scr, total_scr, peak, weight_sems, in_sems, qkv_sems, row_sems, context_sem,
):
    pairs = [
        (mix_own_ref, mix_other_ref), (out_own_ref, out_other_ref),
        (up_own_ref, up_other_ref), (down_own_ref, down_other_ref),
    ]
    length, width = x.shape
    ff_width = w_up.shape[1]
    blocks = length // ROWS
    at = small_slices(width, ff_width)

    def vector(name):
        return small_ref[0, :, at[name]]

    def rows_of(n):
        return pl.ds(pl.multiple_of(n * ROWS, ROWS), ROWS)

    def x_copy(n):
        return pltpu.make_async_copy(x_hbm.at[rows_of(n)], x.at[rows_of(n)], in_sems.at[n])

    def qkv_copy(n):
        return pltpu.make_async_copy(
            qkv.at[:, rows_of(n)], qkv_hbm.at[:, rows_of(n)], qkv_sems.at[n]
        )

    saved = [
        (hidden_rows, hidden_hbm), (out_rows, out_hbm),
        (active_rows, active_hbm), (slope_rows, slope_hbm),
    ]

    def row_copies(n):
        return [
            pltpu.make_async_copy(rows.at[rows_of(n)], whole.at[rows_of(n)], row_sems.at[k, n])
            for k, (rows, whole) in enumerate(saved)
        ]

    weights = Held(sel_ref, layer, pairs, [w_mix, w_out, w_up, w_down], weight_sems, True)
    for n in range(blocks):
        x_copy(n).start()
    weights.start()
    peak[...] = jnp.zeros_like(peak)
    lanes_of = head_lanes(width)
    weights.wait(0)

    def mix_rows(n, _):
        x_copy(n).wait()
        rows = rows_of(n)
        part = dot(x[rows, :], w_mix[...])
        queries = ((part[:, :width] + vector("b_q")) * HEAD**-0.5).astype(BF)
        keys = part[:, width : 2 * width].astype(BF)
        qkv[0, rows, :] = queries
        qkv[1, rows, :] = keys
        qkv[2, rows, :] = (part[:, 2 * width :] + vector("b_v")).astype(BF)
        lengths = dot(jnp.concatenate([queries * queries, keys * keys], axis=1), lanes_of)
        folded = lengths.reshape(ROWS // 8, 8, lengths.shape[1])
        peak[...] = jnp.maximum(peak[...], jnp.max(folded, axis=0))
        qkv_copy(n).start()
        return 0

    lax.fori_loop(0, blocks, mix_rows, 0)
    is_safe = score_bound(peak[...]) * 1.02 < SAFE_SCORE * SAFE_SCORE
    attend_forward(
        begin_ref, count_ref, qkv, key_code_ref, query_code_ref, context, logsum_ref,
        value_scr, query_scr, total_scr, is_safe,
    )
    context_copy = pltpu.make_async_copy(context, context_hbm, context_sem)
    context_copy.start()
    for n in (1, 2, 3):
        weights.wait(n)

    def refine_rows(n, _):
        refine_block(
            rows_of(n), x, context, w_out, w_up, w_down, small_ref,
            hidden_rows, out_rows, scale1_ref, scale2_ref, active_rows, slope_rows,
        )
        for copy in row_copies(n):
            copy.start()
        return 0

    last = out_hbm.shape[0] // ROWS
    lax.fori_loop(0, last, refine_rows, 0)
    context_copy.wait()
    for n in range(blocks):
        qkv_copy(n).wait()
    for n in range(last):
        for copy in row_copies(n):
            copy.wait()


def layer_forward(sel, x, weights, layer, plan, fed=None):
    w_qkv, w_out, w_up, w_down, small = weights
    begin, count, key_code, query_code = plan
    length, width = x.shape
    ff_width = w_up[0].shape[1]
    pairs = width // PAIR
    blocks = length // ROWS

    def whole(shape):
        return pl.BlockSpec(shape, lambda *_: (0,) * len(shape))

    row = jax.ShapeDtypeStruct((length, width), BF)
    lanes = jax.ShapeDtypeStruct((length, 128), F32)
    wide = jax.ShapeDtypeStruct((length, ff_width), BF)
    logsum_shape = (pairs * (length // QB), 2 * QB)
    qkv, context, logsum, out, hidden, scale1, scale2, active, slope = pl.pallas_call(
        partial(forward_kernel, layer),
        name="layer_forward",
        grid_spec=pltpu.PrefetchScalarGridSpec(
            num_scalar_prefetch=3,
            grid=(1,),
            in_specs=[ANY, whole(key_code.shape), whole(query_code.shape)]
            + [ANY] * 8
            + [small_spec(layer, small.shape[2])],
            out_specs=[
                ANY, ANY, whole(logsum_shape), ANY, ANY,
                whole((length, 128)), whole((length, 128)), ANY, ANY,
            ],
            scratch_shapes=[
                *held_shapes(w_qkv, w_out, w_up, w_down),
                pltpu.VMEM((length, width), BF),
                pltpu.VMEM((3, length, width), BF),
                pltpu.VMEM((length, width), BF),
                pltpu.VMEM((length, width), BF),
                pltpu.VMEM((length, width), BF),
                pltpu.VMEM((length, ff_width), BF),
                pltpu.VMEM((length, ff_width), BF),
                pltpu.VMEM((pairs, PAIR + 16, length), BF),
                pltpu.VMEM((pairs, 2 * QB, PAIR), BF),
                pltpu.VMEM((pairs, PAIR + 16, 2 * QB), F32),
                pltpu.VMEM((8, PAIR), F32),
                pltpu.SemaphoreType.DMA((4,)),
                pltpu.SemaphoreType.DMA((blocks,)),
                pltpu.SemaphoreType.DMA((blocks,)),
                pltpu.SemaphoreType.DMA((4, blocks)),
                pltpu.SemaphoreType.DMA,
            ],
        ),
        out_shape=[
            jax.ShapeDtypeStruct((3, length, width), BF), row,
            jax.ShapeDtypeStruct(logsum_shape, F32),
            jax.ShapeDtypeStruct((fed or length, width), BF),
            row, lanes, lanes, wide, wide,
        ],
        compiler_params=PARAMS,
        cost_estimate=cost(48),
    )(begin, count, sel, x, key_code, query_code, *w_qkv, *w_out, *w_up, *w_down, small)
    return (out, (x, qkv, context, logsum, hidden, out, scale1, scale2, slope, active))


def layer_forward_halves(sel, x, weights, layer, plan):
    half = x.shape[0] // 2
    first, kept = layer_forward(sel, x, weights, layer, plan, half)
    _, qkv, context, logsum, hidden, _, scale1, scale2, slope, active = kept
    second, hidden, scale1, scale2, active, slope = refine_rest(
        sel, x, context, weights, layer, (hidden, scale1, scale2, active, slope), half
    )
    out = jnp.concatenate([first, second], axis=0)
    return ((first, second), (x, qkv, context, logsum, hidden, out, scale1, scale2, slope, active))


def feed_backward(sel, grads, kept, weights, layer):
    first, begun, totals = 0, (), []
    for grad in grads:
        *begun, sums, up_sums = refine_back(
            sel, grad, kept[4:9], weights[1:], layer, first, tuple(begun)
        )
        first += grad.shape[0]
        totals.append((sums, up_sums))
    grad_low, grad_raised, grad_attn, grad_context = begun
    sums = tuple(sum(parts) for parts in zip(*totals))
    return (grad_context, (grad_low, grad_raised, grad_attn), sums)


def mixed_backward_kernel(
    layer, begin_ref, count_ref, sel_ref, qkv_hbm, key_code_ref, query_code_ref, context_hbm,
    logsum_ref, grad_hbm, skip_hbm, mix_own_ref, mix_other_ref,
    mixed_hbm, grad_x_hbm, sums_ref,
    w_mix, qkv, context, grad, skip, key_scr, query_scr, given_scr, down_scr,
    grad_key_scr, grad_value_scr, weight_sems, in_sems, mixed_sems, row_sems,
):
    length, width = skip.shape
    blocks = length // ROWS
    weights = Held(sel_ref, layer, [(mix_own_ref, mix_other_ref)], [w_mix], weight_sems, True)
    arrays = [(qkv_hbm, qkv), (context_hbm, context), (grad_hbm, grad), (skip_hbm, skip)]
    loads = [
        pltpu.make_async_copy(whole, held, in_sems.at[n]) for n, (whole, held) in enumerate(arrays)
    ]
    for load in loads:
        load.start()
    weights.start()
    grad_key_scr[...] = jnp.zeros_like(grad_key_scr)
    grad_value_scr[...] = jnp.zeros_like(grad_value_scr)
    sums_ref[...] = jnp.zeros_like(sums_ref)
    loads[0].wait()

    def ready():
        loads[1].wait()
        loads[2].wait()

    attend_backward(
        begin_ref, count_ref, qkv, key_code_ref, query_code_ref, context, logsum_ref, grad,
        sums_ref, key_scr, query_scr, given_scr, down_scr, grad_key_scr, grad_value_scr, ready,
    )
    loads[3].wait()
    store = pltpu.make_async_copy(qkv, mixed_hbm, mixed_sems.at[0])
    store.start()
    weights.wait(0)

    def rows_of(n):
        return pl.ds(pl.multiple_of(n * ROWS, ROWS), ROWS)

    def row_copy(n):
        return pltpu.make_async_copy(skip.at[rows_of(n)], grad_x_hbm.at[rows_of(n)], row_sems.at[n])

    def unmix_rows(n, _):
        rows = rows_of(n)
        total = skip[rows, :].astype(F32)
        for c in range(3):
            total += dot_nt(qkv[c, rows, :], w_mix[:, c * width : (c + 1) * width])
        skip[rows, :] = total.astype(BF)
        row_copy(n).start()
        return 0

    lax.fori_loop(0, blocks, unmix_rows, 0)
    store.wait()
    for n in range(blocks):
        row_copy(n).wait()


def mixed_backward(sel, grad_context, skip, kept, weights, layer, plan):
    _, qkv, context, logsum = kept[:4]
    begin, count, key_code, query_code = plan
    _, length, width = qkv.shape
    pairs = width // PAIR
    blocks = length // ROWS
    w_qkv = weights[0]

    def whole(shape):
        return pl.BlockSpec(shape, lambda *_: (0,) * len(shape))

    row = pltpu.VMEM((length, width), BF)
    return pl.pallas_call(
        partial(mixed_backward_kernel, layer),
        name="mixed_backward",
        grid_spec=pltpu.PrefetchScalarGridSpec(
            num_scalar_prefetch=3,
            grid=(1,),
            in_specs=[ANY, whole(key_code.shape), whole(query_code.shape), ANY, whole(logsum.shape)]
            + [ANY] * 4,
            out_specs=[ANY, ANY, whole((2, width))],
            scratch_shapes=[
                *held_shapes(w_qkv),
                pltpu.VMEM((3, length, width), BF),
                row, row, row,
                pltpu.VMEM((pairs, PAIR, length), BF),
                pltpu.VMEM((pairs, 2 * QB, PAIR), BF),
                pltpu.VMEM((pairs, 2 * QB, PAIR), BF),
                pltpu.VMEM((pairs, PAIR, 2 * QB), F32),
                pltpu.VMEM((length, width), F32),
                pltpu.VMEM((length, width), F32),
                pltpu.SemaphoreType.DMA((1,)),
                pltpu.SemaphoreType.DMA((4,)),
                pltpu.SemaphoreType.DMA((1,)),
                pltpu.SemaphoreType.DMA((blocks,)),
            ],
        ),
        out_shape=[
            jax.ShapeDtypeStruct((3, length, width), BF),
            jax.ShapeDtypeStruct((length, width), BF),
            jax.ShapeDtypeStruct((2, width), F32),
        ],
        compiler_params=PARAMS,
        cost_estimate=cost(38),
    )(begin, count, sel, qkv, key_code, query_code, context, logsum, grad_context, skip, *w_qkv)


def layer_backward(sel, grad, kept, weights, layer, plan):
    grad_context, grads, sums = feed_backward(sel, (grad,), kept, weights, layer)
    grad_mixed, grad_x, mix_sums = mixed_backward(
        sel, grad_context, grads[2], kept, weights, layer, plan
    )
    return (grad_x, grads + (grad_mixed,), sums + (mix_sums,))


def swap_cores(value):
    return send(value, ((0, 1), (1, 0), (2, 3), (3, 2)))


def send(value, routes):
    return lax.ppermute(value, "section", routes)


def pick_row(value, at, axis=0):
    return lax.dynamic_index_in_dim(value, at, axis, keepdims=False)


def plus(*values):
    return sum(value.astype(F32) for value in values).astype(BF)


class RowSum:
    def __init__(self, mine, arrived, blocks):
        self.terms, self.blocks, self.crossed, self.travelling = (mine, arrived), blocks, (), ()
        self.plain = lax.axis_size("dp") != SHARDS
        self.crossed_rows, self.ring_at = 0, 0
        if not self.plain:
            at = lax.axis_index("dp")
            self.z, self.x = at // 2, at % 2

    def state(self):
        return (self.terms, self.crossed, self.travelling)

    def set(self, state):
        self.terms, self.crossed, self.travelling = state

    def cross(self, rows=None):
        if self.plain:
            return
        first, last = self.crossed_rows, rows or self.terms[0].shape[1]
        self.crossed_rows = last
        others = []
        for term in self.terms:
            cols = term.shape[2]
            cut = lax.dynamic_slice(
                term.reshape(4, 2, *term.shape[1:]),
                (0, 1 - self.x, first, 0),
                (4, 1, last - first, cols),
            )
            others.append(cut[:, 0])
        pairs = [(n, n ^ 1) for n in range(8)]
        self.crossed += (lax.ppermute(plus(*others), "dp", pairs),)

    def part(self, z, *more):
        values = []
        for term in self.terms:
            _, rows, cols = term.shape
            cut = lax.dynamic_slice(
                term.reshape(4, 2, rows, cols), (z, self.x, 0, 0), (1, 1, rows, cols)
            )
            values.append(cut[0, 0])
        values.append(jnp.concatenate([pick_row(part, z) for part in self.crossed], axis=0))
        return plus(*values, *more)

    def ring(self):
        if self.plain:
            return
        self.ring_at += 1
        passing = self.part(lax.rem(self.z + 4 - self.ring_at, 4), *self.travelling)
        self.travelling = (lax.ppermute(passing, "dp", [(n, (n + 2) % 8) for n in range(8)]),)

    def direct(self):
        if self.plain:
            return
        arrived = []
        for far in (3, 2, 1):
            for way in (far, -far):
                part = self.part(jnp.clip(self.z + way, 0, 3))
                routes = [(n, n + 2 * way) for n in range(8) if 0 <= n + 2 * way < 8]
                arrived.append(lax.ppermute(part, "dp", routes))
        self.travelling = tuple(arrived)

    def result(self):
        if not self.plain:
            return self.part(self.z, *self.travelling)
        shards = lax.axis_size("dp")
        parts, at, value = [], 0, plus(*self.terms)
        for rows in self.blocks:
            part = value[:, at : at + rows].reshape(shards, -1, value.shape[2])
            parts, at = parts + [part], at + rows
        whole = jnp.concatenate(parts, axis=1)
        return lax.psum_scatter(whole, "dp", scatter_dimension=0, tiled=True)[0]


def body(
    tokens_in, seg_starts, pad_mask, w_qkv, b_qv, w_attn_out, b_attn_out, ln_gain, ln_bias,
    w_up, b_up, w_down, b_down, w_proj, cotangent,
):
    section_at = lax.axis_index("section")
    core = section_at % 2
    is_late = section_at >= 2
    flip = core == 1
    quarter = tokens_in.shape[1]
    length, width = 4 * quarter, tokens_in.shape[2]
    ff_width = w_up.shape[2]
    proj_cols = w_proj.shape[1]
    shards = lax.axis_size("dp")
    share = width // shards

    def sel_for(half):
        return jnp.stack([core, section_at // 2, half]).astype(jnp.int32)

    sel_mine, sel_theirs = sel_for(core), sel_for(1 - core)

    own = pick_row(tokens_in, core)
    other = pick_row(tokens_in, 1 - core)
    straight = send(own, [(2, 0), (3, 1)])
    crossed = send(other, [(2, 1), (3, 0)])
    near = swap_cores(other)
    small = pack_small(b_qv[0], b_attn_out[0], ln_gain[0], ln_bias[0], b_up[0], b_down[0])[None]
    small_other = swap_cores(small)
    small = jnp.stack([jnp.where(flip, small_other, small), jnp.where(flip, small, small_other)])
    weights = tuple((w[0], swap_cores(w[0])) for w in (w_qkv, w_attn_out, w_up, w_down)) + (small,)
    x = jnp.concatenate(
        [
            jnp.where(flip, near, own),
            jnp.where(flip, own, near),
            jnp.where(flip, crossed, straight),
            jnp.where(flip, straight, crossed),
        ],
        axis=0,
    )

    plan = attention_plan(pick_row(seg_starts, core), pick_row(pad_mask, core))

    def both_forward(rows):
        middle, kept_even = layer_forward(sel_mine, rows, weights, 0, plan)
        last, kept_odd = layer_forward(sel_mine, middle, weights, 1, plan)
        return (last, kept_even, kept_odd)

    middle, kept_even = layer_forward(sel_mine, x, weights, 0, plan)
    head_own = jnp.concatenate([w_proj.T, pick_row(cotangent, core).T], axis=1)
    head_other = jnp.concatenate([w_proj.T, pick_row(cotangent, 1 - core).T], axis=1)
    middle, head_own, head_other = lax.optimization_barrier((middle, head_own, head_other))
    head_late = send(head_other, [(2, 3), (3, 2)])
    head_straight = send(head_own, [(0, 2), (1, 3)])
    head_crossed = send(head_other, [(0, 3), (1, 2)])
    head_cols = jnp.concatenate(
        [
            jnp.where(flip, head_crossed, head_straight),
            jnp.where(flip, head_straight, head_crossed),
            jnp.where(flip, head_late, head_own),
            jnp.where(flip, head_own, head_late),
        ],
        axis=0,
    )
    proj_rows, given_rows = head_cols[:, :width], head_cols[:, width:]
    (first, second), kept_odd = layer_forward_halves(sel_mine, middle, weights, 1, plan)
    first, proj_rows, given_rows = lax.optimization_barrier((first, proj_rows, given_rows))
    arrived = send(first, [(0, 2), (1, 3)])
    arrived, second = lax.optimization_barrier((arrived, second))
    hopped = jnp.concatenate([arrived, send(second, [(0, 2), (1, 3)])], axis=0)

    def late_turn(rows, *_):
        last, kept_even, kept_odd = both_forward(rows)
        embedded, grad_proj, grad = head(last, proj_rows, given_rows)
        grad, grads_odd, sums_odd = layer_backward(sel_mine, grad, kept_odd, weights, 1, plan)
        grad, grads_even, sums_even = layer_backward(sel_mine, grad, kept_even, weights, 0, plan)
        return (
            kept_even, kept_odd, embedded, grad_proj, grad,
            grads_odd, sums_odd, grads_even, sums_even,
        )

    def early_turn(rows, kept_even, kept_odd):
        row, ff = jnp.zeros((length, width), BF), jnp.zeros((length, ff_width), BF)
        grads = (row, ff, row, jnp.zeros((3, length, width), BF))
        sums = (
            jnp.zeros((6, width), F32),
            jnp.zeros((1, ff_width), F32),
            jnp.zeros((2, width), F32),
        )
        return (
            kept_even, kept_odd, jnp.zeros((4 * proj_cols, length), BF),
            jnp.zeros((width, 4 * proj_cols), BF), row, grads, sums, grads, sums,
        )

    (
        kept_even, kept_odd, embedded, grad_proj, grad_mid,
        late_odd, late_sums_odd, late_even, late_sums_even,
    ) = lax.cond(is_late, late_turn, early_turn, hopped, kept_even, kept_odd)

    halfway = length // 2
    arriving = [
        send(grad_mid[at : at + halfway], [(2, 0), (3, 1)]) for at in (0, halfway)
    ]
    embedded_cols = embedded.reshape(4, proj_cols, length)

    rows_of_one = width // SHARDS
    attend_blocks = (rows_of_one,) * 4
    feed_blocks = (rows_of_one,) * (ff_width // (2 * HALF)) + (ff_width // SHARDS,)

    def tie(*values):
        return lax.optimization_barrier(values)

    def feed_args(kept, late, now):
        return (kept[4], late[1], now[1], kept[9], late[0], now[0])

    def attend_args(kept, late, now, mixed):
        return (kept[2], kept[0], late[2], now[2], late[3], mixed)

    def tie_sums(values, *sums):
        values, states = tie(values, [part.state() for part in sums])
        for part, state in zip(sums, states):
            part.set(state)
        return values

    grad_context, grads_odd, sums_odd = feed_backward(sel_mine, arriving, kept_odd, weights, 1)
    args = feed_args(kept_odd, late_odd, grads_odd)
    arrived = swap_cores(feed_grads(sel_theirs, *args))
    feed_odd = RowSum(feed_grads(sel_mine, *args), arrived, feed_blocks)
    grad_context = tie_sums(grad_context, feed_odd)
    feed_odd.cross(rows_of_one * 6)
    straight_cols = send(pick_row(embedded_cols, core), [(2, 0), (3, 1)])
    crossed_cols = send(pick_row(embedded_cols, 1 - core), [(2, 1), (3, 0)])
    near_cols = swap_cores(pick_row(embedded_cols, 3 - core))
    mixed_odd, grad, mix_sums = mixed_backward(
        sel_mine, grad_context, grads_odd[2], kept_odd, weights, 1, plan
    )
    sums_odd = sums_odd + (mix_sums,)
    args = attend_args(kept_odd, late_odd, grads_odd, mixed_odd)
    args, straight_cols, crossed_cols, near_cols = tie_sums(
        (args, straight_cols, crossed_cols, near_cols), feed_odd
    )
    feed_odd.cross()
    theirs = attend_grads(sel_theirs, *args)
    args, theirs = tie_sums((args, theirs), feed_odd)
    feed_odd.ring()
    arrived = swap_cores(theirs)
    attend_odd = RowSum(attend_grads(sel_mine, *args), arrived, attend_blocks)
    grad = tie_sums(grad, feed_odd, attend_odd)
    feed_odd.ring()
    attend_odd.cross()

    grad_context, grads_even, sums_even = feed_backward(sel_mine, (grad,), kept_even, weights, 0)
    args = tie_sums(feed_args(kept_even, late_even, grads_even), feed_odd, attend_odd)
    feed_odd.ring()
    theirs = feed_grads(sel_theirs, *args)
    args, theirs = tie_sums((args, theirs), feed_odd)
    attend_odd.ring()
    arrived = swap_cores(theirs)
    feed_even = RowSum(feed_grads(sel_mine, *args), arrived, feed_blocks)
    grad_context = tie_sums(grad_context, feed_even, attend_odd)
    feed_even.cross()
    attend_odd.ring()
    mixed_even, grad, mix_sums = mixed_backward(
        sel_mine, grad_context, grads_even[2], kept_even, weights, 0, plan
    )
    sums_even = sums_even + (mix_sums,)
    args = attend_args(kept_even, late_even, grads_even, mixed_even)
    args = tie_sums(args, feed_even, attend_odd)
    feed_even.ring()
    routes_odd, routes_even = ((0, 1), (2, 3)), ((1, 0), (3, 2))
    feed_odd = feed_odd.result()
    extras = pack_extras(sel_mine, grad_proj, late_sums_even, late_sums_odd, sums_even, sums_odd)
    theirs = attend_grads(sel_theirs, *args, extras)
    args, theirs, extras = tie_sums((args, theirs, extras), feed_even)
    arrived = swap_cores(theirs)
    feed_even.ring()
    quarters = grad.reshape(4, quarter, width)
    near_grad = swap_cores(pick_row(quarters, 1 - core))
    mine = attend_grads(sel_mine, *args, extras)
    mine, quarters, near_grad = tie_sums((mine, quarters, near_grad), feed_even, attend_odd)
    attend_even = RowSum(mine, arrived, attend_blocks)
    attend_even.cross()
    feed_even.ring()
    attend_odd.ring()
    straight_grad = send(pick_row(quarters, 2 + core), [(0, 2), (1, 3)])
    crossed_grad = send(pick_row(quarters, 3 - core), [(0, 3), (1, 2)])
    straight_grad, crossed_grad = tie_sums(
        (straight_grad, crossed_grad), feed_even, attend_even, attend_odd
    )
    attend_even.direct()
    feed_even, attend_odd = feed_even.result(), attend_odd.result()
    sent_odd = [send(part, routes_odd) for part in (feed_odd, attend_odd)]
    if shards == SHARDS:
        tail = attend_even.result()
        attend_even, extras = tail[: 4 * share], tail[4 * share :].astype(F32)
    else:
        attend_even = attend_even.result()
        extras = plus(mine[:, -EXTRA_ROWS:], arrived[:, -EXTRA_ROWS:])
        extras = lax.psum(extras.astype(F32), "dp")

    def halves(even, odd, sent):
        arrived = jnp.where(flip, sent, send(even, routes_even))
        mine = jnp.where(flip, odd, even)
        return (jnp.where(flip, arrived, mine), jnp.where(flip, mine, arrived))

    blocks = ff_width // (2 * HALF)
    feed_halves = halves(feed_even, feed_odd, sent_odd[0])
    attend_halves = halves(attend_even, attend_odd, sent_odd[1])

    def columns(pair, first, count):
        parts = [part[n * share : (n + 1) * share] for part in pair for n in range(first, first + count)]
        return jnp.concatenate(parts, axis=1).astype(F32)

    grad_w_up = columns(feed_halves, 0, blocks)[None]
    grad_w_down = jnp.concatenate([part[blocks * share :] for part in feed_halves], axis=1)
    grad_w_down = grad_w_down.astype(F32)[None]
    grad_w_out = columns(attend_halves, 0, 1)[None]
    grad_w_qkv = jnp.concatenate([columns(attend_halves, 1 + c, 1) for c in range(3)], axis=1)[None]

    if shards == SHARDS:
        at, pick = 0, lambda values: values
    else:
        at = lax.axis_index("dp") % (shards // SHARDS)
        extras = pick_row(extras, lax.axis_index("dp") // (shards // SHARDS))

        def pick(values):
            size = values.shape[-1] * SHARDS // shards
            return lax.dynamic_slice_in_dim(values, at * size, size, values.ndim - 1)

    one = width // SHARDS
    small_mine = jnp.where(flip, extras[8:16], extras[:8])
    grad_b_up = pick(small_mine[0:1, : ff_width // SHARDS])
    grad_b_qv = pick(small_mine[1:2, : 2 * one])
    rows = pick(small_mine[2:8, :one])
    grad_proj = extras[16:].reshape(-1, 3, 4 * proj_cols).transpose(1, 0, 2)
    grad_proj = grad_proj.reshape(one, 4 * proj_cols)
    grad_proj = lax.dynamic_slice_in_dim(grad_proj, at * share, share, 0).astype(BF)
    grad_proj = jnp.where(is_late, grad_proj, send(grad_proj, [(2, 0), (3, 1)])).astype(F32)
    grad_w_proj = lax.dynamic_slice_in_dim(grad_proj, section_at * proj_cols, proj_cols, 1)

    own_cols = jnp.where(is_late, pick_row(embedded_cols, section_at), straight_cols)
    other_cols = jnp.where(is_late, near_cols, crossed_cols)
    embedded_out = jnp.stack(
        [jnp.where(flip, other_cols, own_cols).T, jnp.where(flip, own_cols, other_cols).T]
    )

    mine = jnp.where(is_late, straight_grad, pick_row(quarters, core))
    others = jnp.where(is_late, crossed_grad, near_grad)
    grad_in = jnp.stack(
        [jnp.where(flip, others, mine), jnp.where(flip, mine, others)]
    ).astype(F32)

    return (
        embedded_out,
        grad_in,
        grad_w_qkv,
        grad_b_qv,
        grad_w_out,
        rows[0][None],
        rows[1:3][None],
        rows[3:5][None],
        grad_w_up,
        grad_b_up,
        grad_w_down,
        rows[5][None],
        grad_w_proj,
    )


def solution(mesh):
    in_specs = (
        P("dp", "section", None),
        P("dp", None),
        P("dp", None),
        P("section", None, None),
        P("section", None),
        P("section", None, None),
        P("section", None),
        P("section", None, None),
        P("section", None, None),
        P("section", None, None),
        P("section", None),
        P("section", None, None),
        P("section", None),
        P(None, "section"),
        P("dp", None, "section"),
    )
    out_specs = (
        P("dp", None, "section"),
        P("dp", "section", None),
        P("section", "dp", None),
        P("section", "dp"),
        P("section", "dp", None),
        P("section", "dp"),
        P("section", None, "dp"),
        P("section", None, "dp"),
        P("section", "dp", None),
        P("section", "dp"),
        P("section", "dp", None),
        P("section", "dp"),
        P("dp", "section"),
    )
    return jax.shard_map(body, mesh=mesh, in_specs=in_specs, out_specs=out_specs, check_vma=False)
```
